32 devices in a mesh: bin: 4 (over x, core), sens: 8 (over z, y).
Axes of the slice: x: 2, y: 2, z: 4, core: 2. Of those that a mesh axis runs over, the one named last changes fastest.
Arguments:
- spectra: bfloat16 [512, 512], P('bin', 'sens'), parts along dimension 0, may hold values from -6 to 6
- valid_mask: int32 [64, 512], P(None, 'sens'), may hold values from 0 to 1, as said below
- pairing: int32 [2, 32], replicated, may hold values from 0 to 31, each once within a row
- positions: float32 [2, 512], replicated, may hold values from -136 to 136
- wavenumber: float32 [4], P('bin'), parts along dimension 0, may hold values from 4 to 6
Outputs:
- early_resp: float32 [512, 1024], P('sens', 'bin'), parts along dimension 1
- final_resp: float32 [512, 1024], P('sens', 'bin'), parts along dimension 1
The draws below stay inside these ranges and needn't reach their ends.
There are 4 independent parts, one for each index of `bin`. The reference program is written for one: setup_inputs(seed, part) draws one part's arguments, and reference() takes and returns one part's arrays. A program takes and returns all parts, laid end to end along the dimension named above; an argument that names none is the same for every part. Nothing has to cross between parts.
Inputs may be any that keep to these rules, and one draw needn't show every extreme that they name: `valid_mask`: every sensor has at least one valid segment. `pairing`: each row holds every number 0 to 31 once.
All inputs are finite; a program needn't handle non-finite values.
Results may differ from the reference program's by a relative error of at most 0.0083.
The reference program's roundings to bfloat16 on the way (of `scaled` and `table`) count: a program that leaves them out, or rounds other values in their place, can miss the bound.
Values may be sent and summed in bfloat16 or wider, within the bound.
No kernel may reach another device: no remote copies, remote signals or barrier semaphores. Data moves between devices by JAX's collectives and lax.ppermute only.
A program may use at most 64 MiB of HBM per device.

```python
import jax
import jax.numpy as jnp
from jax import lax

S_DEV = 64
SEGS = 64
BEAMS = 256
ROUNDS = 2
PANEL = 32
BLOCKS = 8
SENSORS = 512


def draw_valid_mask(key, part):
    level_key = jax.random.fold_in(key, 11)
    choice_key = jax.random.fold_in(key, 12)
    levels = jax.random.randint(level_key, (SENSORS,), 1, 9)
    random_bits = jax.random.randint(choice_key, (SEGS, SENSORS), 0, 8)
    segment_ids = jnp.arange(SEGS, dtype=jnp.int32)[:, None]
    sensor_ids = jnp.arange(SENSORS, dtype=jnp.int32)[None, :]
    forced = segment_ids == sensor_ids % SEGS
    return jnp.where((random_bits < levels[None, :]) | forced, 1, 0).astype(jnp.int32)


def draw_positions(key, part):
    jitter_key = jax.random.fold_in(key, 21)
    lateral_key = jax.random.fold_in(key, 22)
    bow_key = jax.random.fold_in(key, 23)
    index = jnp.arange(SENSORS, dtype=jnp.float32)
    along = 0.5 * (index - SENSORS // 2) + jax.random.uniform(jitter_key, (SENSORS,), jnp.float32, -0.1, 0.1)
    bow_size = jax.random.uniform(bow_key, (), jnp.float32, 2.0, 5.0)
    lateral = bow_size * jnp.sin(jnp.pi * index / SENSORS) + jax.random.uniform(lateral_key, (SENSORS,), jnp.float32, -0.5, 0.5)
    return jnp.stack([along, lateral]).astype(jnp.float32)


def block_scale(stream_key, shape, pieces, low, high):
    level = 1.0
    for axis_at, parts in pieces:
        steps = jax.random.uniform(jax.random.fold_in(jax.random.fold_in(stream_key, 6), axis_at), (parts,), jnp.float32, low / len(pieces), high / len(pieces))
        level = level * jnp.repeat(jnp.exp(steps), shape[axis_at] // parts).reshape((-1,) + (1,) * (len(shape) - 1 - axis_at))
    return level


def scatter_about(own_key, shape, deviation, reach, cuts=(), kind=jnp.bfloat16):
    array = deviation * jax.random.normal(own_key, shape, jnp.float32)
    if cuts:
        array = array * block_scale(own_key, shape, cuts, -0.22, 0.18)
    return jnp.clip(array, -reach, reach).astype(kind)


def setup_inputs(seed: int = 0, part: int = 0) -> dict:
    arg_keys = jax.random.split(jax.random.key(seed), 6)
    own_keys = jax.random.split(jax.random.fold_in(arg_keys[5], part), 6)
    spectra = scatter_about(own_keys[0], (2 * SEGS, SENSORS), 1.0, 6.0, ((1, 8),))
    valid_mask = draw_valid_mask(jax.random.fold_in(arg_keys[5], 71), part)
    pairing = jax.vmap(lambda own: jax.random.permutation(own, PANEL))(jax.random.split(arg_keys[2], ROUNDS)).reshape((ROUNDS, PANEL)).astype(jnp.int32)
    positions = draw_positions(jax.random.fold_in(arg_keys[5], 71), part)
    wavenumber = jnp.clip(jax.random.uniform(own_keys[4], (1,), jnp.float32, 4.0, 6.0), 4.0, 6.0)
    return {"spectra": spectra, "valid_mask": valid_mask, "pairing": pairing, "positions": positions, "wavenumber": wavenumber}


LOAD = 0.5

def scale_spectra(spectra, valid_mask):
    validity = valid_mask.astype(jnp.float32)
    counts = lax.optimization_barrier(jnp.sum(valid_mask, axis=0))
    scaling = 1.0 / jnp.sqrt(counts.astype(jnp.float32))
    doubled = jnp.concatenate([validity, validity], axis=0)
    return (spectra.astype(jnp.float32) * doubled * scaling[None, :]).astype(jnp.bfloat16)

def taper_matrix(positions, width):
    delta_along = positions[0][:, None] - positions[0][None, :]
    delta_side = positions[1][:, None] - positions[1][None, :]
    distance = jnp.sqrt(delta_along * delta_along + delta_side * delta_side)
    return jnp.sinc(width * distance / jnp.pi)

def rotate_pair(upper_panel, bottom):
    left_re, left_im = (upper_panel[0], upper_panel[1])
    right_re, right_im = (bottom[0], bottom[1])
    norm_left = lax.optimization_barrier(jnp.sum(left_re * left_re + left_im * left_im, axis=-1, keepdims=True))
    norm_right = lax.optimization_barrier(jnp.sum(right_re * right_re + right_im * right_im, axis=-1, keepdims=True))
    gamma_re = lax.optimization_barrier(jnp.sum(left_re * right_re + left_im * right_im, axis=-1, keepdims=True))
    gamma_im = lax.optimization_barrier(jnp.sum(left_re * right_im - left_im * right_re, axis=-1, keepdims=True))
    spread = norm_right - norm_left
    radius = jnp.sqrt(spread * spread + 4.0 * (gamma_re * gamma_re + gamma_im * gamma_im) + 1e-30)
    leading = jnp.sqrt((radius + jnp.abs(spread)) / (2.0 * radius))
    factor = 1.0 / (radius * leading)
    gleft_re = factor * (gamma_re * left_re - gamma_im * left_im)
    gleft_im = factor * (gamma_re * left_im + gamma_im * left_re)
    cright_re = factor * (gamma_re * right_re + gamma_im * right_im)
    cright_im = factor * (gamma_re * right_im - gamma_im * right_re)
    rising = spread >= 0.0
    new_left_re = jnp.where(rising, leading * left_re - cright_re, gleft_re - leading * right_re)
    new_left_im = jnp.where(rising, leading * left_im - cright_im, gleft_im - leading * right_im)
    new_right_re = jnp.where(rising, gleft_re + leading * right_re, leading * left_re + cright_re)
    new_right_im = jnp.where(rising, gleft_im + leading * right_im, leading * left_im + cright_im)
    return (jnp.stack([new_left_re, new_left_im]), jnp.stack([new_right_re, new_right_im]))

def steer_table(positions, wavenumber, beams):
    bearing = jnp.pi * (jnp.arange(beams, dtype=jnp.float32) + 0.5) / beams
    phases = wavenumber[0] * (jnp.cos(bearing)[:, None] * positions[0][None, :] + jnp.sin(bearing)[:, None] * positions[1][None, :])
    cos_part = jnp.cos(phases).astype(jnp.bfloat16)
    sin_part = jnp.sin(phases).astype(jnp.bfloat16)
    return jnp.stack([jnp.concatenate([cos_part, -sin_part], axis=0), jnp.concatenate([sin_part, cos_part], axis=0)])

def responses(upper_panel, bottom, table):
    stacked = jnp.stack([upper_panel, bottom], axis=2).reshape(2, SENSORS, SENSORS)
    col_norms = lax.optimization_barrier(jnp.sum(stacked[0] * stacked[0] + stacked[1] * stacked[1], axis=-1))
    rounded = stacked.astype(jnp.bfloat16).astype(jnp.float32)
    projected = jnp.einsum('kcs,kbs->cb', rounded, table.astype(jnp.float32))
    energy = projected[:, :BEAMS] * projected[:, :BEAMS] + projected[:, BEAMS:] * projected[:, BEAMS:]
    return energy / col_norms[:, None]

def reference(spectra, valid_mask, pairing, positions, wavenumber):
    scaled = scale_spectra(spectra, valid_mask)
    turned = jnp.concatenate([scaled[SEGS:], -scaled[:SEGS]], axis=0)
    weights = jnp.concatenate([scaled, turned], axis=1)
    columns = jnp.dot(weights.T, scaled, preferred_element_type=jnp.float32).reshape(2, SENSORS, SENSORS)
    taper = taper_matrix(positions, 3.0 / S_DEV)
    loading = jnp.eye(SENSORS, dtype=jnp.float32) * LOAD
    columns = jnp.stack([columns[0] * taper + loading, columns[1] * taper])
    blocked = columns.reshape(2, BLOCKS, 2, PANEL, SENSORS)
    upper_panel = blocked[:, :, 0]
    bottom = jnp.take(blocked[:, :, 1], pairing[0], axis=2)
    upper_panel, bottom = rotate_pair(upper_panel, bottom)
    table = steer_table(positions, wavenumber, BEAMS)
    early_resp = responses(upper_panel, bottom, table)
    moved_top = jnp.concatenate([upper_panel[:, :1], bottom[:, :1], upper_panel[:, 1:-1]], axis=1)
    moved_bottom = jnp.concatenate([bottom[:, 1:], upper_panel[:, -1:]], axis=1)
    moved_bottom = jnp.take(moved_bottom, pairing[1], axis=2)
    upper_panel, bottom = rotate_pair(moved_top, moved_bottom)
    final_resp = responses(upper_panel, bottom, table)
    return (early_resp, final_resp)
```

```python
import jax
import jax.numpy as jnp
from jax import lax
from jax.sharding import PartitionSpec as P

BEAMS = 256
LOAD = 0.5


def scale_spectra(spectra, valid_mask):
    validity = valid_mask.astype(jnp.float32)
    counts = jnp.sum(valid_mask, axis=0)
    scaling = 1.0 / jnp.sqrt(counts.astype(jnp.float32))
    doubled = jnp.concatenate([validity, validity], axis=0)
    return (spectra.astype(jnp.float32) * doubled * scaling[None, :]).astype(jnp.bfloat16)


def pair_terms(left, right):
    left_re, left_im = left
    right_re, right_im = right
    norm_left = jnp.sum(left_re * left_re + left_im * left_im, axis=-1, keepdims=True)
    norm_right = jnp.sum(right_re * right_re + right_im * right_im, axis=-1, keepdims=True)
    gamma_re = jnp.sum(left_re * right_re + left_im * right_im, axis=-1, keepdims=True)
    gamma_im = jnp.sum(left_re * right_im - left_im * right_re, axis=-1, keepdims=True)
    spread = norm_right - norm_left
    radius = jnp.sqrt(spread * spread + 4.0 * (gamma_re * gamma_re + gamma_im * gamma_im) + 1e-30)
    leading = jnp.sqrt((radius + jnp.abs(spread)) / (2.0 * radius))
    factor = 1.0 / (radius * leading)
    return spread >= 0.0, leading, factor * gamma_re, factor * gamma_im


def rotate_side(left, right, side):
    rising, leading, b_re, b_im = pair_terms(left, right)
    plain = jnp.logical_xor(rising, side)
    sign = jnp.where(side, 1.0, -1.0)
    u_re, u_im = (jnp.where(plain, left[i], right[i]) for i in (0, 1))
    v_re, v_im = (jnp.where(plain, right[i], left[i]) for i in (0, 1))
    lead = jnp.where(plain, leading, sign * leading)
    c_re = jnp.where(plain, sign * b_re, b_re)
    c_im = jnp.where(plain, -sign * b_im, b_im)
    return lead * u_re + c_re * v_re - c_im * v_im, lead * u_im + c_re * v_im + c_im * v_re


def rotate_both(left, right):
    rising, leading, b_re, b_im = pair_terms(left, right)
    sign = jnp.where(rising, -1.0, 1.0)
    x_re = leading * left[0] + sign * (b_re * right[0] + b_im * right[1])
    x_im = leading * left[1] + sign * (b_re * right[1] - b_im * right[0])
    y_re = b_re * left[0] - b_im * left[1] - sign * leading * right[0]
    y_im = b_re * left[1] + b_im * left[0] - sign * leading * right[1]
    new_left = jnp.where(rising, x_re, y_re), jnp.where(rising, x_im, y_im)
    new_right = jnp.where(rising, y_re, x_re), jnp.where(rising, y_im, x_im)
    return new_left, new_right


def steer_table(positions, wavenumber, beams):
    bearing = jnp.pi * (jnp.arange(beams, dtype=jnp.float32) + 0.5) / beams
    phases = wavenumber[0] * (
        jnp.cos(bearing)[:, None] * positions[0][None, :]
        + jnp.sin(bearing)[:, None] * positions[1][None, :]
    )
    return jnp.concatenate(
        [jnp.cos(phases).astype(jnp.bfloat16), jnp.sin(phases).astype(jnp.bfloat16)], axis=0
    )


def respond(left, right, table, beams):
    re = jnp.concatenate([left[0], right[0]], axis=0)
    im = jnp.concatenate([left[1], right[1]], axis=0)
    rows = re.shape[0]
    norms = jnp.sum(re * re + im * im, axis=-1, keepdims=True)
    rounded = jnp.concatenate([re, im], axis=0).astype(jnp.bfloat16)
    projected = jnp.einsum("cs,bs->cb", rounded, table, preferred_element_type=jnp.float32)
    z_re = projected[:rows, :beams] + projected[rows:, beams:]
    z_im = projected[rows:, :beams] - projected[:rows, beams:]
    return (z_re * z_re + z_im * z_im) / norms


def gather_blocks(own):
    return lax.all_gather(own, "sens", axis=0, tiled=True)


def per_device(spectra, valid_mask, pairing, positions, wavenumber):
    blocks = lax.axis_size("sens")
    position = lax.axis_index("sens")
    segments, block_size = valid_mask.shape
    panel_size = block_size // 2
    sensors = positions.shape[1]
    width = 3.0 / block_size
    order = jnp.concatenate([jnp.arange(panel_size), panel_size + pairing[0]])
    pick = (order[:, None] == jnp.arange(block_size)[None, :]).astype(jnp.bfloat16)
    scaled = scale_spectra(spectra, valid_mask)
    own = jnp.einsum("kj,rj->kr", pick, scaled, preferred_element_type=jnp.float32).astype(jnp.bfloat16)
    gathered = gather_blocks(own)

    places = jnp.take(positions.reshape(2, blocks, block_size), order, axis=2).reshape(2, sensors)
    table = steer_table(places, wavenumber, BEAMS)

    lower = jnp.maximum(position - 1, 0)
    upper = jnp.minimum(position + 1, blocks - 1)
    inner = jnp.arange(block_size)
    turned_order = jnp.concatenate([pairing[1], panel_size + pairing[1]])
    rows = jnp.concatenate(
        [position * block_size + inner, lower * block_size + inner, upper * block_size + turned_order]
    )
    row_places = jnp.take(places, rows, axis=1)
    delta_along = row_places[0][:, None] - places[0][None, :]
    delta_side = row_places[1][:, None] - places[1][None, :]
    distance = jnp.sqrt(delta_along * delta_along + delta_side * delta_side)
    taper = jnp.sinc(width * distance / jnp.pi)
    loading = jnp.where(rows[:, None] == jnp.arange(sensors)[None, :], LOAD, 0.0)

    chosen = jnp.take(gathered, rows, axis=0)
    turned = jnp.concatenate([chosen[:, segments:], -chosen[:, :segments]], axis=1)
    weights = jnp.concatenate([chosen, turned], axis=0)
    tile = jnp.einsum("cr,mr->cm", weights, gathered, preferred_element_type=jnp.float32)
    col_re = tile[: rows.shape[0]] * taper + loading
    col_im = tile[rows.shape[0] :] * taper
    panels = [
        (col_re[at : at + panel_size], col_im[at : at + panel_size])
        for at in range(0, 3 * block_size, panel_size)
    ]
    top, bottom = rotate_both(panels[0], panels[1])
    early_resp = respond(top, bottom, table, BEAMS)
    moved_top = rotate_side(panels[2], panels[3], position == 1)
    moved_bottom = rotate_side(panels[4], panels[5], position < blocks - 1)
    top, bottom = rotate_both(moved_top, moved_bottom)
    final_resp = respond(top, bottom, table, BEAMS)
    return (early_resp, final_resp)


def solution(mesh):
    in_specs = (P("bin", "sens"), P(None, "sens"), P(), P(), P("bin"))
    out_specs = (P("sens", "bin"), P("sens", "bin"))
    return jax.shard_map(
        per_device, mesh=mesh, in_specs=in_specs, out_specs=out_specs, check_vma=False
    )
```

```python
import jax
import jax.numpy as jnp
from jax import lax
from jax.sharding import PartitionSpec as P

BEAMS = 256
LOAD = 0.5


def scale_spectra(spectra, valid_mask):
    validity = valid_mask.astype(jnp.float32)
    counts = jnp.sum(valid_mask, axis=0)
    scaling = 1.0 / jnp.sqrt(counts.astype(jnp.float32))
    doubled = jnp.concatenate([validity, validity], axis=0)
    return (spectra.astype(jnp.float32) * doubled * scaling[None, :]).astype(jnp.bfloat16)


def pair_terms(left, right):
    left_re, left_im = left
    right_re, right_im = right
    norm_left = jnp.sum(left_re * left_re + left_im * left_im, axis=-1, keepdims=True)
    norm_right = jnp.sum(right_re * right_re + right_im * right_im, axis=-1, keepdims=True)
    gamma_re = jnp.sum(left_re * right_re + left_im * right_im, axis=-1, keepdims=True)
    gamma_im = jnp.sum(left_re * right_im - left_im * right_re, axis=-1, keepdims=True)
    spread = norm_right - norm_left
    radius = jnp.sqrt(spread * spread + 4.0 * (gamma_re * gamma_re + gamma_im * gamma_im) + 1e-30)
    leading = jnp.sqrt((radius + jnp.abs(spread)) / (2.0 * radius))
    factor = 1.0 / (radius * leading)
    return spread >= 0.0, leading, factor * gamma_re, factor * gamma_im


def rotate_side(left, right, side):
    rising, leading, b_re, b_im = pair_terms(left, right)
    plain = jnp.logical_xor(rising, side)
    sign = jnp.where(side, 1.0, -1.0)
    u_re, u_im = (jnp.where(plain, left[i], right[i]) for i in (0, 1))
    v_re, v_im = (jnp.where(plain, right[i], left[i]) for i in (0, 1))
    lead = jnp.where(plain, leading, sign * leading)
    c_re = jnp.where(plain, sign * b_re, b_re)
    c_im = jnp.where(plain, -sign * b_im, b_im)
    return lead * u_re + c_re * v_re - c_im * v_im, lead * u_im + c_re * v_im + c_im * v_re


def rotate_both(left, right):
    rising, leading, b_re, b_im = pair_terms(left, right)
    sign = jnp.where(rising, -1.0, 1.0)
    x_re = leading * left[0] + sign * (b_re * right[0] + b_im * right[1])
    x_im = leading * left[1] + sign * (b_re * right[1] - b_im * right[0])
    y_re = b_re * left[0] - b_im * left[1] - sign * leading * right[0]
    y_im = b_re * left[1] + b_im * left[0] - sign * leading * right[1]
    new_left = jnp.where(rising, x_re, y_re), jnp.where(rising, x_im, y_im)
    new_right = jnp.where(rising, y_re, x_re), jnp.where(rising, y_im, x_im)
    return new_left, new_right


def steer_table(positions, wavenumber, beams):
    bearing = jnp.pi * (jnp.arange(beams, dtype=jnp.float32) + 0.5) / beams
    phases = wavenumber[0] * (
        jnp.cos(bearing)[:, None] * positions[0][None, :]
        + jnp.sin(bearing)[:, None] * positions[1][None, :]
    )
    return jnp.concatenate(
        [jnp.cos(phases).astype(jnp.bfloat16), jnp.sin(phases).astype(jnp.bfloat16)], axis=0
    )


def respond(left, right, table, beams):
    re = jnp.concatenate([left[0], right[0]], axis=0)
    im = jnp.concatenate([left[1], right[1]], axis=0)
    rows = re.shape[0]
    norms = jnp.sum(re * re + im * im, axis=-1, keepdims=True)
    rounded = jnp.concatenate([re, im], axis=0).astype(jnp.bfloat16)
    projected = jnp.einsum("cs,bs->cb", rounded, table, preferred_element_type=jnp.float32)
    z_re = projected[:rows, :beams] + projected[rows:, beams:]
    z_im = projected[rows:, :beams] - projected[:rows, beams:]
    return (z_re * z_re + z_im * z_im) / norms


def gather_blocks(own):
    peers = lax.axis_size("sens")
    copies = jnp.broadcast_to(own[None], (peers, *own.shape))
    return lax.all_to_all(copies, "sens", split_axis=0, concat_axis=0).reshape(-1, own.shape[1])


def per_device(spectra, valid_mask, pairing, positions, wavenumber):
    blocks = lax.axis_size("sens")
    position = lax.axis_index("sens")
    segments, block_size = valid_mask.shape
    panel_size = block_size // 2
    sensors = positions.shape[1]
    width = 3.0 / block_size
    order = jnp.concatenate([jnp.arange(panel_size), panel_size + pairing[0]])
    pick = (order[:, None] == jnp.arange(block_size)[None, :]).astype(jnp.bfloat16)
    scaled = scale_spectra(spectra, valid_mask)
    own = jnp.einsum("kj,rj->kr", pick, scaled, preferred_element_type=jnp.float32).astype(jnp.bfloat16)
    gathered = gather_blocks(own)

    places = jnp.take(positions.reshape(2, blocks, block_size), order, axis=2).reshape(2, sensors)
    table = steer_table(places, wavenumber, BEAMS)

    lower = jnp.maximum(position - 1, 0)
    upper = jnp.minimum(position + 1, blocks - 1)
    inner = jnp.arange(block_size)
    turned_order = jnp.concatenate([pairing[1], panel_size + pairing[1]])
    rows = jnp.concatenate(
        [position * block_size + inner, lower * block_size + inner, upper * block_size + turned_order]
    )
    row_places = jnp.take(places, rows, axis=1)
    delta_along = row_places[0][:, None] - places[0][None, :]
    delta_side = row_places[1][:, None] - places[1][None, :]
    distance = jnp.sqrt(delta_along * delta_along + delta_side * delta_side)
    taper = jnp.sinc(width * distance / jnp.pi)
    loading = jnp.where(rows[:, None] == jnp.arange(sensors)[None, :], LOAD, 0.0)

    chosen = jnp.take(gathered, rows, axis=0)
    turned = jnp.concatenate([chosen[:, segments:], -chosen[:, :segments]], axis=1)
    weights = jnp.concatenate([chosen, turned], axis=0)
    tile = jnp.einsum("cr,mr->cm", weights, gathered, preferred_element_type=jnp.float32)
    col_re = tile[: rows.shape[0]] * taper + loading
    col_im = tile[rows.shape[0] :] * taper
    panels = [
        (col_re[at : at + panel_size], col_im[at : at + panel_size])
        for at in range(0, 3 * block_size, panel_size)
    ]
    top, bottom = rotate_both(panels[0], panels[1])
    early_resp = respond(top, bottom, table, BEAMS)
    moved_top = rotate_side(panels[2], panels[3], position == 1)
    moved_bottom = rotate_side(panels[4], panels[5], position < blocks - 1)
    top, bottom = rotate_both(moved_top, moved_bottom)
    final_resp = respond(top, bottom, table, BEAMS)
    return (early_resp, final_resp)


def solution(mesh):
    in_specs = (P("bin", "sens"), P(None, "sens"), P(), P(), P("bin"))
    out_specs = (P("sens", "bin"), P("sens", "bin"))
    return jax.shard_map(
        per_device, mesh=mesh, in_specs=in_specs, out_specs=out_specs, check_vma=False
    )
```

```python
import functools
import math

import jax
import jax.numpy as jnp
from jax import lax
from jax.experimental import pallas as pl
from jax.experimental.pallas import tpu as pltpu
from jax.sharding import PartitionSpec as P

BEAMS = 256
LOAD = 0.5
LANES = 128
ROWS = 8
GROUP = 16
VMEM = pl.BlockSpec(memory_space=pltpu.VMEM)
SMEM = pl.BlockSpec(memory_space=pltpu.SMEM)

COS = (0.99999921, -19.73898036, 64.92865742, -85.27162153, 58.79049212, -21.07110563)
SIN = (6.28318492, -41.34158923, 81.59994333, -76.61447253, 41.34288235, -12.47124354)
SIN_FINE = (6.2831853, -41.34170041, 81.60513139, -76.70301535, 42.02592699, -14.89984667, 3.23813751)


def horner(coefficients, at):
    value = coefficients[-1]
    for coefficient in coefficients[-2::-1]:
        value = value * at + coefficient
    return value


def dot(left, right, contract):
    return lax.dot_general(left, right, ((contract[:1], contract[1:]), ((), ())), preferred_element_type=jnp.float32)


def spread_kernel(spectra_ref, mask_ref, copies_ref):
    segments, block = mask_ref.shape
    validity = mask_ref[...].astype(jnp.float32)
    counts = jnp.sum(validity, axis=0, keepdims=True)
    scaling = 1.0 / jnp.sqrt(counts)
    halves = [
        (spectra_ref[at : at + segments, :].astype(jnp.float32) * validity * scaling).astype(jnp.bfloat16)
        for at in (0, segments)
    ]
    scaled = jnp.concatenate(halves, axis=0)
    eye = lax.broadcasted_iota(jnp.int32, (block, block), 0) == lax.broadcasted_iota(jnp.int32, (block, block), 1)
    turned = dot(eye.astype(jnp.bfloat16), scaled, (1, 1)).astype(jnp.bfloat16)
    for peer in range(copies_ref.shape[0]):
        copies_ref[peer] = turned


def prepare_kernel(block, meta_ref, pairing_ref, wavenumber_ref, positions_ref, table_ref, taper_ref, load_ref, pick_ref):
    sensors = positions_ref.shape[1]
    half = block // 2
    width = 3.0 / block

    beam = lax.broadcasted_iota(jnp.int32, (ROWS, BEAMS), 1).astype(jnp.float32)
    turns = (beam + 0.5) * (0.5 / BEAMS)
    square = turns * turns
    cos_beam = horner(COS_FINE, square)
    sin_beam = turns * horner(SIN_FINE, square)
    scale = wavenumber_ref[0] * (0.5 / math.pi)
    for at in range(0, sensors, LANES):
        along, side = (
            jnp.transpose(jnp.broadcast_to(positions_ref[axis : axis + 1, at : at + LANES] * scale, (LANES, LANES)))
            for axis in (0, 1)
        )
        for row in range(0, LANES, GROUP):
            for lane in range(0, BEAMS, LANES):
                cos_part = cos_beam[:1, lane : lane + LANES]
                sin_part = sin_beam[:1, lane : lane + LANES]
                phase = along[row : row + GROUP] * cos_part + side[row : row + GROUP] * sin_part
                phase = phase - jnp.round(phase)
                square = phase * phase
                rows = slice(at + row, at + row + GROUP)
                table_ref[rows, lane : lane + LANES] = horner(COS, square).astype(jnp.bfloat16)
                table_ref[rows, BEAMS + lane : BEAMS + lane + LANES] = (phase * horner(SIN, square)).astype(jnp.bfloat16)

    sub = lax.broadcasted_iota(jnp.int32, (ROWS, LANES), 0)
    lane = lax.broadcasted_iota(jnp.int32, (ROWS, LANES), 1)

    def column(numbers):
        value = jnp.zeros((ROWS, LANES), jnp.int32)
        for i, number in enumerate(numbers):
            value = jnp.where(sub == i, number, value)
        return value

    order, later = [], []
    for at in range(0, half, ROWS):
        order.append(sub + at)
        later.append(column([pairing_ref[1, at + i] for i in range(ROWS)]))
    for at in range(0, half, ROWS):
        order.append(column([half + pairing_ref[0, at + i] for i in range(ROWS)]))
        later.append(column([half + pairing_ref[0, pairing_ref[1, at + i]] for i in range(ROWS)]))
    for which, rows in enumerate((order, later)):
        for at in range(0, len(rows), 2):
            pair = jnp.concatenate(rows[at : at + 2], axis=0)
            lanes = jnp.concatenate([lane, lane], axis=0)
            start = which * block + at * ROWS
            pick_ref[start : start + GROUP, :] = jnp.where(pair == lanes, 1.0, 0.0)[:, :block].astype(jnp.bfloat16)

    for which, rows in enumerate((order, order, later)):
        number = meta_ref[which]
        chunk = number // (LANES // block)
        shift = (number - chunk * (LANES // block)) * block
        for at, row in enumerate(rows):
            start = which * block + at * ROWS
            hit = row + shift == lane
            load_ref[start : start + ROWS, :] = jnp.where(hit, LOAD, 0.0)
            near = positions_ref[:, pl.ds(pl.multiple_of(chunk * LANES, LANES), LANES)]
            own_along = jnp.sum(jnp.where(hit, near[0:1], 0.0), axis=1, keepdims=True)
            own_side = jnp.sum(jnp.where(hit, near[1:2], 0.0), axis=1, keepdims=True)
            for to in range(0, sensors, LANES):
                delta_along = own_along - positions_ref[0:1, to : to + LANES]
                delta_side = own_side - positions_ref[1:2, to : to + LANES]
                square = jnp.maximum(delta_along * delta_along + delta_side * delta_side, 1e-30)
                inverse = lax.rsqrt(square)
                turn = (square * inverse) * (0.5 * width / math.pi)
                turn = turn - jnp.round(turn)
                value = turn * horner(SIN_FINE, turn * turn) * (inverse * (1.0 / width))
                taper_ref[start : start + ROWS, to : to + LANES] = value


COS_FINE = (0.99999999, -19.7392045, 64.93911746, -85.45013953, 60.16763095, -25.96759925, 6.52865816)


def sums(left, right):
    left_re, left_im = left
    right_re, right_im = right
    norm_left = jnp.sum(left_re * left_re + left_im * left_im, axis=1, keepdims=True)
    norm_right = jnp.sum(right_re * right_re + right_im * right_im, axis=1, keepdims=True)
    gamma_re = jnp.sum(left_re * right_re + left_im * right_im, axis=1, keepdims=True)
    gamma_im = jnp.sum(left_re * right_im - left_im * right_re, axis=1, keepdims=True)
    spread = norm_right - norm_left
    radius = jnp.sqrt(spread * spread + 4.0 * (gamma_re * gamma_re + gamma_im * gamma_im) + 1e-30)
    leading = jnp.sqrt((radius + jnp.abs(spread)) / (2.0 * radius))
    factor = 1.0 / (radius * leading)
    return spread >= 0.0, leading, factor * gamma_re, factor * gamma_im


def rotate_side(left, right, side, sign):
    rising, leading, b_re, b_im = sums(left, right)
    plain = jnp.where(rising, 1, 0) != side
    left_re = jnp.where(plain, leading, b_re)
    left_im = jnp.where(plain, 0.0, b_im)
    right_re = sign * jnp.where(plain, b_re, leading)
    right_im = sign * jnp.where(plain, -b_im, 0.0)
    return (
        left_re * left[0] - left_im * left[1] + right_re * right[0] - right_im * right[1],
        left_re * left[1] + left_im * left[0] + right_re * right[1] + right_im * right[0],
    )


def rotate_both(left, right):
    rising, leading, b_re, b_im = sums(left, right)
    zero = jnp.zeros_like(b_im)

    def combine(left_re, left_im, right_re, right_im):
        return (
            left_re * left[0] - left_im * left[1] + right_re * right[0] - right_im * right[1],
            left_re * left[1] + left_im * left[0] + right_re * right[1] + right_im * right[0],
        )

    new_left = combine(
        jnp.where(rising, leading, b_re),
        jnp.where(rising, zero, b_im),
        jnp.where(rising, -b_re, -leading),
        jnp.where(rising, b_im, zero),
    )
    new_right = combine(
        jnp.where(rising, b_re, leading),
        jnp.where(rising, b_im, zero),
        jnp.where(rising, leading, b_re),
        jnp.where(rising, zero, -b_im),
    )
    return new_left, new_right


def respond_kernel(
    meta_ref, blocks_ref, table_ref, taper_ref, load_ref, pick_ref, early_ref, final_ref, re_ref, im_ref, turn_ref, norm_ref
):
    block, depth = blocks_ref.shape[1:]
    sensors = table_ref.shape[0]
    half = block // 2
    everything = blocks_ref[...].reshape(sensors, depth)
    sign = jnp.where(lax.broadcasted_iota(jnp.int32, (block, depth), 1) < depth // 2, 1.0, -1.0)
    for which in range(3):
        number = meta_ref[which]
        pick = pick_ref[block:, :] if which == 2 else pick_ref[:block, :]
        rows = dot(pick, blocks_ref[number], (1, 0))
        weights = jnp.concatenate([rows, pltpu.roll(rows, depth // 2, 1) * sign], axis=0).astype(jnp.bfloat16)
        tile = dot(weights, everything, (1, 1))
        part = slice(which * block, (which + 1) * block)
        taper = taper_ref[part, :]
        re_ref[part, :] = tile[:block] * taper
        im_ref[part, :] = tile[block:] * taper
        lanes = pl.ds(pl.multiple_of(number // (LANES // block) * LANES, LANES), LANES)
        re_ref[part, lanes] += load_ref[part, :]

    def rows_at(start):
        return re_ref[start : start + GROUP, :], im_ref[start : start + GROUP, :]

    def keep(start, column):
        turn_ref[start : start + GROUP, :] = column[0].astype(jnp.bfloat16)
        turn_ref[2 * block + start : 2 * block + start + GROUP, :] = column[1].astype(jnp.bfloat16)
        total = jnp.sum(column[0] * column[0] + column[1] * column[1], axis=1, keepdims=True)
        norm_ref[start : start + GROUP, :] = jnp.broadcast_to(1.0 / total, (GROUP, LANES))

    for at in range(0, half, GROUP):
        top, bottom = rotate_both(rows_at(at), rows_at(half + at))
        keep(at, top)
        keep(half + at, bottom)
    lower_side, upper_side = meta_ref[3], meta_ref[4]
    lower_sign = (2 * lower_side - 1).astype(jnp.float32)
    upper_sign = (2 * upper_side - 1).astype(jnp.float32)
    for at in range(0, half, GROUP):
        moved_top = rotate_side(rows_at(block + at), rows_at(block + half + at), lower_side, lower_sign)
        moved_bottom = rotate_side(rows_at(2 * block + at), rows_at(2 * block + half + at), upper_side, upper_sign)
        top, bottom = rotate_both(moved_top, moved_bottom)
        keep(block + at, top)
        keep(block + half + at, bottom)

    projected = dot(turn_ref[...], table_ref[...], (1, 0))
    rows = 2 * block
    z_re = projected[:rows, :BEAMS] + projected[rows:, BEAMS:]
    z_im = projected[rows:, :BEAMS] - projected[:rows, BEAMS:]
    inverse = jnp.concatenate([norm_ref[...]] * (BEAMS // LANES), axis=1)
    response = (z_re * z_re + z_im * z_im) * inverse
    early_ref[...] = response[:block]
    final_ref[...] = response[block:]


def per_device(spectra, valid_mask, pairing, positions, wavenumber):
    blocks = lax.axis_size("sens")
    position = lax.axis_index("sens")
    block = valid_mask.shape[1]
    depth = spectra.shape[0]
    sensors = positions.shape[1]
    meta = jnp.stack(
        [
            position,
            jnp.maximum(position - 1, 0),
            jnp.minimum(position + 1, blocks - 1),
            (position == 1).astype(jnp.int32),
            (position < blocks - 1).astype(jnp.int32),
        ]
    ).astype(jnp.int32)
    copies = pl.pallas_call(
        spread_kernel,
        out_shape=jax.ShapeDtypeStruct((blocks, block, depth), jnp.bfloat16),
        in_specs=[VMEM, VMEM],
        out_specs=VMEM,
        name="spread",
    )(spectra, valid_mask)
    gathered = lax.all_to_all(copies, "sens", split_axis=0, concat_axis=0)
    table, taper, load, pick = pl.pallas_call(
        functools.partial(prepare_kernel, block),
        out_shape=(
            jax.ShapeDtypeStruct((sensors, 2 * BEAMS), jnp.bfloat16),
            jax.ShapeDtypeStruct((3 * block, sensors), jnp.float32),
            jax.ShapeDtypeStruct((3 * block, LANES), jnp.float32),
            jax.ShapeDtypeStruct((2 * block, block), jnp.bfloat16),
        ),
        in_specs=[SMEM, SMEM, SMEM, VMEM],
        out_specs=(VMEM, VMEM, VMEM, VMEM),
        name="prepare",
    )(meta, pairing, wavenumber, positions)
    out = jax.ShapeDtypeStruct((block, BEAMS), jnp.float32)
    return pl.pallas_call(
        respond_kernel,
        out_shape=(out, out),
        in_specs=[SMEM, VMEM, VMEM, VMEM, VMEM, VMEM],
        out_specs=(VMEM, VMEM),
        scratch_shapes=[
            pltpu.VMEM((3 * block, sensors), jnp.float32),
            pltpu.VMEM((3 * block, sensors), jnp.float32),
            pltpu.VMEM((4 * block, sensors), jnp.bfloat16),
            pltpu.VMEM((2 * block, LANES), jnp.float32),
        ],
        compiler_params=pltpu.CompilerParams(vmem_limit_bytes=24 * 2**20),
        name="respond",
    )(meta, gathered, table, taper, load, pick)


def solution(mesh):
    in_specs = (P("bin", "sens"), P(None, "sens"), P(), P(), P("bin"))
    out_specs = (P("sens", "bin"), P("sens", "bin"))
    return jax.shard_map(
        per_device, mesh=mesh, in_specs=in_specs, out_specs=out_specs, check_vma=False
    )
```

```python
import functools
import math

import jax
import jax.numpy as jnp
from jax import lax
from jax.experimental import pallas as pl
from jax.experimental.pallas import tpu as pltpu
from jax.sharding import PartitionSpec as P

BEAMS = 256
LOAD = 0.5
LANES = 128
ROWS = 8
GROUP = 16
VMEM = pl.BlockSpec(memory_space=pltpu.VMEM)
SMEM = pl.BlockSpec(memory_space=pltpu.SMEM)

COS = (0.99999921, -19.73898036, 64.92865742, -85.27162153, 58.79049212, -21.07110563)
SIN = (6.28318492, -41.34158923, 81.59994333, -76.61447253, 41.34288235, -12.47124354)
SIN_FINE = (6.2831853, -41.34170041, 81.60513139, -76.70301535, 42.02592699, -14.89984667, 3.23813751)


def small(mebibytes):
    return pltpu.CompilerParams(vmem_limit_bytes=mebibytes * 2**20)


def horner(coefficients, at):
    value = coefficients[-1]
    for coefficient in coefficients[-2::-1]:
        value = value * at + coefficient
    return value


def dot(left, right, contract):
    return lax.dot_general(left, right, ((contract[:1], contract[1:]), ((), ())), preferred_element_type=jnp.float32)


def spread_kernel(spectra_ref, mask_ref, copies_ref):
    segments, block = mask_ref.shape
    depth = spectra_ref.shape[1]
    row = lax.broadcasted_iota(jnp.int32, (segments, depth), 0)
    lane = lax.broadcasted_iota(jnp.int32, (segments, depth), 1)
    twice = jnp.where((row == lane) | (row + segments == lane), 1.0, 0.0).astype(jnp.bfloat16)
    validity = dot(mask_ref[...].astype(jnp.float32).astype(jnp.bfloat16), twice, (0, 0))
    counts = 0.5 * jnp.sum(validity, axis=1, keepdims=True)
    scaled = (spectra_ref[...].astype(jnp.float32) * validity * (1.0 / jnp.sqrt(counts))).astype(jnp.bfloat16)
    for peer in range(copies_ref.shape[0]):
        copies_ref[peer] = scaled


def prepare_kernel(block, meta_ref, pairing_ref, wavenumber_ref, positions_ref, table_ref, taper_ref, load_ref, pick_ref):
    sensors = positions_ref.shape[1]
    half = block // 2
    width = 3.0 / block

    beam = lax.broadcasted_iota(jnp.int32, (ROWS, BEAMS), 1).astype(jnp.float32)
    turns = (beam + 0.5) * (0.5 / BEAMS)
    square = turns * turns
    cos_beam = horner(COS_FINE, square)
    sin_beam = turns * horner(SIN_FINE, square)
    scale = wavenumber_ref[0] * (0.5 / math.pi)
    for at in range(0, sensors, LANES):
        along, side = (
            jnp.transpose(jnp.broadcast_to(positions_ref[axis : axis + 1, at : at + LANES] * scale, (LANES, LANES)))
            for axis in (0, 1)
        )
        for row in range(0, LANES, GROUP):
            for lane in range(0, BEAMS, LANES):
                cos_part = cos_beam[:1, lane : lane + LANES]
                sin_part = sin_beam[:1, lane : lane + LANES]
                phase = along[row : row + GROUP] * cos_part + side[row : row + GROUP] * sin_part
                phase = phase - jnp.round(phase)
                square = phase * phase
                rows = slice(at + row, at + row + GROUP)
                table_ref[rows, lane : lane + LANES] = horner(COS, square).astype(jnp.bfloat16)
                table_ref[rows, BEAMS + lane : BEAMS + lane + LANES] = (phase * horner(SIN, square)).astype(jnp.bfloat16)

    sub = lax.broadcasted_iota(jnp.int32, (ROWS, LANES), 0)
    lane = lax.broadcasted_iota(jnp.int32, (ROWS, LANES), 1)

    def column(numbers):
        value = jnp.zeros((ROWS, LANES), jnp.int32)
        for i, number in enumerate(numbers):
            value = jnp.where(sub == i, number, value)
        return value

    order, later = [], []
    for at in range(0, half, ROWS):
        order.append(sub + at)
        later.append(column([pairing_ref[1, at + i] for i in range(ROWS)]))
    for at in range(0, half, ROWS):
        order.append(column([half + pairing_ref[0, at + i] for i in range(ROWS)]))
        later.append(column([half + pairing_ref[0, pairing_ref[1, at + i]] for i in range(ROWS)]))
    for which, rows in enumerate((order, later)):
        for at in range(0, len(rows), 2):
            pair = jnp.concatenate(rows[at : at + 2], axis=0)
            lanes = jnp.concatenate([lane, lane], axis=0)
            start = which * block + at * ROWS
            pick_ref[start : start + GROUP, :] = jnp.where(pair == lanes, 1.0, 0.0)[:, :block].astype(jnp.bfloat16)

    for which, rows in enumerate((order, order, later)):
        number = meta_ref[which]
        chunk = number // (LANES // block)
        shift = (number - chunk * (LANES // block)) * block
        for at, row in enumerate(rows):
            start = which * block + at * ROWS
            hit = row + shift == lane
            load_ref[start : start + ROWS, :] = jnp.where(hit, LOAD, 0.0)
            near = positions_ref[:, pl.ds(pl.multiple_of(chunk * LANES, LANES), LANES)]
            own_along = jnp.sum(jnp.where(hit, near[0:1], 0.0), axis=1, keepdims=True)
            own_side = jnp.sum(jnp.where(hit, near[1:2], 0.0), axis=1, keepdims=True)
            for to in range(0, sensors, LANES):
                delta_along = own_along - positions_ref[0:1, to : to + LANES]
                delta_side = own_side - positions_ref[1:2, to : to + LANES]
                square = jnp.maximum(delta_along * delta_along + delta_side * delta_side, 1e-30)
                inverse = lax.rsqrt(square)
                turn = (square * inverse) * (0.5 * width / math.pi)
                turn = turn - jnp.round(turn)
                value = turn * horner(SIN_FINE, turn * turn) * (inverse * (1.0 / width))
                taper_ref[start : start + ROWS, to : to + LANES] = value


COS_FINE = (0.99999999, -19.7392045, 64.93911746, -85.45013953, 60.16763095, -25.96759925, 6.52865816)


def sums(left, right):
    left_re, left_im = left
    right_re, right_im = right
    norm_left = jnp.sum(left_re * left_re + left_im * left_im, axis=1, keepdims=True)
    norm_right = jnp.sum(right_re * right_re + right_im * right_im, axis=1, keepdims=True)
    gamma_re = jnp.sum(left_re * right_re + left_im * right_im, axis=1, keepdims=True)
    gamma_im = jnp.sum(left_re * right_im - left_im * right_re, axis=1, keepdims=True)
    spread = norm_right - norm_left
    radius = jnp.sqrt(spread * spread + 4.0 * (gamma_re * gamma_re + gamma_im * gamma_im) + 1e-30)
    leading = jnp.sqrt((radius + jnp.abs(spread)) / (2.0 * radius))
    factor = 1.0 / (radius * leading)
    return spread >= 0.0, leading, factor * gamma_re, factor * gamma_im


def rotate_side(left, right, side, sign):
    rising, leading, b_re, b_im = sums(left, right)
    plain = jnp.where(rising, 1, 0) != side
    left_re = jnp.where(plain, leading, b_re)
    left_im = jnp.where(plain, 0.0, b_im)
    right_re = sign * jnp.where(plain, b_re, leading)
    right_im = sign * jnp.where(plain, -b_im, 0.0)
    return (
        left_re * left[0] - left_im * left[1] + right_re * right[0] - right_im * right[1],
        left_re * left[1] + left_im * left[0] + right_re * right[1] + right_im * right[0],
    )


def rotate_both(left, right):
    rising, leading, b_re, b_im = sums(left, right)
    zero = jnp.zeros_like(b_im)

    def combine(left_re, left_im, right_re, right_im):
        return (
            left_re * left[0] - left_im * left[1] + right_re * right[0] - right_im * right[1],
            left_re * left[1] + left_im * left[0] + right_re * right[1] + right_im * right[0],
        )

    new_left = combine(
        jnp.where(rising, leading, b_re),
        jnp.where(rising, zero, b_im),
        jnp.where(rising, -b_re, -leading),
        jnp.where(rising, b_im, zero),
    )
    new_right = combine(
        jnp.where(rising, b_re, leading),
        jnp.where(rising, b_im, zero),
        jnp.where(rising, leading, b_re),
        jnp.where(rising, zero, -b_im),
    )
    return new_left, new_right


def respond_kernel(
    meta_ref, blocks_ref, table_ref, taper_ref, load_ref, pick_ref, early_ref, final_ref, re_ref, im_ref, turn_ref, norm_ref
):
    block, depth = blocks_ref.shape[1:]
    sensors = table_ref.shape[0]
    half = block // 2
    everything = blocks_ref[...].reshape(sensors, depth)
    sign = jnp.where(lax.broadcasted_iota(jnp.int32, (block, depth), 1) < depth // 2, 1.0, -1.0)
    for which in range(3):
        number = meta_ref[which]
        pick = pick_ref[block:, :] if which == 2 else pick_ref[:block, :]
        rows = dot(pick, blocks_ref[number], (1, 0))
        weights = jnp.concatenate([rows, pltpu.roll(rows, depth // 2, 1) * sign], axis=0).astype(jnp.bfloat16)
        tile = dot(weights, everything, (1, 1))
        part = slice(which * block, (which + 1) * block)
        taper = taper_ref[part, :]
        re_ref[part, :] = tile[:block] * taper
        im_ref[part, :] = tile[block:] * taper
        lanes = pl.ds(pl.multiple_of(number // (LANES // block) * LANES, LANES), LANES)
        re_ref[part, lanes] += load_ref[part, :]

    def rows_at(start):
        return re_ref[start : start + GROUP, :], im_ref[start : start + GROUP, :]

    def keep(start, column):
        turn_ref[start : start + GROUP, :] = column[0].astype(jnp.bfloat16)
        turn_ref[2 * block + start : 2 * block + start + GROUP, :] = column[1].astype(jnp.bfloat16)
        total = jnp.sum(column[0] * column[0] + column[1] * column[1], axis=1, keepdims=True)
        norm_ref[start : start + GROUP, :] = jnp.broadcast_to(1.0 / total, (GROUP, LANES))

    for at in range(0, half, GROUP):
        top, bottom = rotate_both(rows_at(at), rows_at(half + at))
        keep(at, top)
        keep(half + at, bottom)
    lower_side, upper_side = meta_ref[3], meta_ref[4]
    lower_sign = (2 * lower_side - 1).astype(jnp.float32)
    upper_sign = (2 * upper_side - 1).astype(jnp.float32)
    for at in range(0, half, GROUP):
        moved_top = rotate_side(rows_at(block + at), rows_at(block + half + at), lower_side, lower_sign)
        moved_bottom = rotate_side(rows_at(2 * block + at), rows_at(2 * block + half + at), upper_side, upper_sign)
        top, bottom = rotate_both(moved_top, moved_bottom)
        keep(block + at, top)
        keep(block + half + at, bottom)

    projected = dot(turn_ref[...], table_ref[...], (1, 0))
    rows = 2 * block
    z_re = projected[:rows, :BEAMS] + projected[rows:, BEAMS:]
    z_im = projected[rows:, :BEAMS] - projected[:rows, BEAMS:]
    inverse = jnp.concatenate([norm_ref[...]] * (BEAMS // LANES), axis=1)
    response = (z_re * z_re + z_im * z_im) * inverse
    early_ref[...] = response[:block]
    final_ref[...] = response[block:]


def per_device(spectra, valid_mask, pairing, positions, wavenumber):
    blocks = lax.axis_size("sens")
    position = lax.axis_index("sens")
    block = valid_mask.shape[1]
    depth = spectra.shape[0]
    sensors = positions.shape[1]
    meta = jnp.stack(
        [
            position,
            jnp.maximum(position - 1, 0),
            jnp.minimum(position + 1, blocks - 1),
            (position == 1).astype(jnp.int32),
            (position < blocks - 1).astype(jnp.int32),
        ]
    ).astype(jnp.int32)
    copies = pl.pallas_call(
        spread_kernel,
        out_shape=jax.ShapeDtypeStruct((blocks, block, depth), jnp.bfloat16),
        in_specs=[VMEM, VMEM],
        out_specs=VMEM,
        compiler_params=small(2),
        name="spread",
    )(spectra.T, valid_mask)
    gathered = lax.all_to_all(copies, "sens", split_axis=0, concat_axis=0)
    table, taper, load, pick = pl.pallas_call(
        functools.partial(prepare_kernel, block),
        out_shape=(
            jax.ShapeDtypeStruct((sensors, 2 * BEAMS), jnp.bfloat16),
            jax.ShapeDtypeStruct((3 * block, sensors), jnp.float32),
            jax.ShapeDtypeStruct((3 * block, LANES), jnp.float32),
            jax.ShapeDtypeStruct((2 * block, block), jnp.bfloat16),
        ),
        in_specs=[SMEM, SMEM, SMEM, VMEM],
        out_specs=(VMEM, VMEM, VMEM, VMEM),
        compiler_params=small(4),
        name="prepare",
    )(meta, pairing, wavenumber, positions)
    out = jax.ShapeDtypeStruct((block, BEAMS), jnp.float32)
    return pl.pallas_call(
        respond_kernel,
        out_shape=(out, out),
        in_specs=[SMEM, VMEM, VMEM, VMEM, VMEM, VMEM],
        out_specs=(VMEM, VMEM),
        scratch_shapes=[
            pltpu.VMEM((3 * block, sensors), jnp.float32),
            pltpu.VMEM((3 * block, sensors), jnp.float32),
            pltpu.VMEM((4 * block, sensors), jnp.bfloat16),
            pltpu.VMEM((2 * block, LANES), jnp.float32),
        ],
        compiler_params=small(4 + sensors * block // 2**13),
        name="respond",
    )(meta, gathered, table, taper, load, pick)


def solution(mesh):
    in_specs = (P("bin", "sens"), P(None, "sens"), P(), P(), P("bin"))
    out_specs = (P("sens", "bin"), P("sens", "bin"))
    return jax.shard_map(
        per_device, mesh=mesh, in_specs=in_specs, out_specs=out_specs, check_vma=False
    )
```

```python
import functools
import math

import jax
import jax.numpy as jnp
from jax import lax
from jax.experimental import pallas as pl
from jax.experimental.pallas import tpu as pltpu
from jax.sharding import PartitionSpec as P

BEAMS = 256
LOAD = 0.5
LANES = 128
ROWS = 8
GROUP = 16
VMEM = pl.BlockSpec(memory_space=pltpu.VMEM)
SMEM = pl.BlockSpec(memory_space=pltpu.SMEM)

COS = (0.99999921, -19.73898036, 64.92865742, -85.27162153, 58.79049212, -21.07110563)
SIN = (6.28318492, -41.34158923, 81.59994333, -76.61447253, 41.34288235, -12.47124354)
SIN_FINE = (6.2831853, -41.34170041, 81.60513139, -76.70301535, 42.02592699, -14.89984667, 3.23813751)


def small(mebibytes):
    return pltpu.CompilerParams(vmem_limit_bytes=mebibytes * 2**20)


def horner(coefficients, at):
    value = coefficients[-1]
    for coefficient in coefficients[-2::-1]:
        value = value * at + coefficient
    return value


def dot(left, right, contract):
    return lax.dot_general(left, right, ((contract[:1], contract[1:]), ((), ())), preferred_element_type=jnp.float32)


def spread_kernel(spectra_ref, mask_ref, scaled_ref):
    segments, block = mask_ref.shape
    depth = spectra_ref.shape[1]
    row = lax.broadcasted_iota(jnp.int32, (segments, depth), 0)
    lane = lax.broadcasted_iota(jnp.int32, (segments, depth), 1)
    twice = jnp.where((row == lane) | (row + segments == lane), 1.0, 0.0).astype(jnp.bfloat16)
    validity = dot(mask_ref[...].astype(jnp.float32).astype(jnp.bfloat16), twice, (0, 0))
    counts = 0.5 * jnp.sum(validity, axis=1, keepdims=True)
    scaled = (spectra_ref[...].astype(jnp.float32) * validity * (1.0 / jnp.sqrt(counts))).astype(jnp.bfloat16)
    scaled_ref[0] = scaled


def prepare_kernel(block, meta_ref, pairing_ref, wavenumber_ref, positions_ref, table_ref, taper_ref, load_ref, pick_ref):
    sensors = positions_ref.shape[1]
    half = block // 2
    width = 3.0 / block

    beam = lax.broadcasted_iota(jnp.int32, (ROWS, BEAMS), 1).astype(jnp.float32)
    turns = (beam + 0.5) * (0.5 / BEAMS)
    square = turns * turns
    cos_beam = horner(COS_FINE, square)
    sin_beam = turns * horner(SIN_FINE, square)
    scale = wavenumber_ref[0] * (0.5 / math.pi)
    for at in range(0, sensors, LANES):
        along, side = (
            jnp.transpose(jnp.broadcast_to(positions_ref[axis : axis + 1, at : at + LANES] * scale, (LANES, LANES)))
            for axis in (0, 1)
        )
        for row in range(0, LANES, GROUP):
            for lane in range(0, BEAMS, LANES):
                cos_part = cos_beam[:1, lane : lane + LANES]
                sin_part = sin_beam[:1, lane : lane + LANES]
                phase = along[row : row + GROUP] * cos_part + side[row : row + GROUP] * sin_part
                phase = phase - jnp.round(phase)
                square = phase * phase
                rows = slice(at + row, at + row + GROUP)
                table_ref[rows, lane : lane + LANES] = horner(COS, square).astype(jnp.bfloat16)
                table_ref[rows, BEAMS + lane : BEAMS + lane + LANES] = (phase * horner(SIN, square)).astype(jnp.bfloat16)

    sub = lax.broadcasted_iota(jnp.int32, (ROWS, LANES), 0)
    lane = lax.broadcasted_iota(jnp.int32, (ROWS, LANES), 1)

    def column(numbers):
        value = jnp.zeros((ROWS, LANES), jnp.int32)
        for i, number in enumerate(numbers):
            value = jnp.where(sub == i, number, value)
        return value

    order, later = [], []
    for at in range(0, half, ROWS):
        order.append(sub + at)
        later.append(column([pairing_ref[1, at + i] for i in range(ROWS)]))
    for at in range(0, half, ROWS):
        order.append(column([half + pairing_ref[0, at + i] for i in range(ROWS)]))
        later.append(column([half + pairing_ref[0, pairing_ref[1, at + i]] for i in range(ROWS)]))
    for which, rows in enumerate((order, later)):
        for at in range(0, len(rows), 2):
            pair = jnp.concatenate(rows[at : at + 2], axis=0)
            lanes = jnp.concatenate([lane, lane], axis=0)
            start = which * block + at * ROWS
            pick_ref[start : start + GROUP, :] = jnp.where(pair == lanes, 1.0, 0.0)[:, :block].astype(jnp.bfloat16)

    for which, rows in enumerate((order, order, later)):
        number = meta_ref[which]
        chunk = number // (LANES // block)
        shift = (number - chunk * (LANES // block)) * block
        for at, row in enumerate(rows):
            start = which * block + at * ROWS
            hit = row + shift == lane
            load_ref[start : start + ROWS, :] = jnp.where(hit, LOAD, 0.0)
            near = positions_ref[:, pl.ds(pl.multiple_of(chunk * LANES, LANES), LANES)]
            own_along = jnp.sum(jnp.where(hit, near[0:1], 0.0), axis=1, keepdims=True)
            own_side = jnp.sum(jnp.where(hit, near[1:2], 0.0), axis=1, keepdims=True)
            for to in range(0, sensors, LANES):
                delta_along = own_along - positions_ref[0:1, to : to + LANES]
                delta_side = own_side - positions_ref[1:2, to : to + LANES]
                square = jnp.maximum(delta_along * delta_along + delta_side * delta_side, 1e-30)
                inverse = lax.rsqrt(square)
                turn = (square * inverse) * (0.5 * width / math.pi)
                turn = turn - jnp.round(turn)
                value = turn * horner(SIN_FINE, turn * turn) * (inverse * (1.0 / width))
                taper_ref[start : start + ROWS, to : to + LANES] = value


COS_FINE = (0.99999999, -19.7392045, 64.93911746, -85.45013953, 60.16763095, -25.96759925, 6.52865816)


def sums(left, right):
    left_re, left_im = left
    right_re, right_im = right
    norm_left = jnp.sum(left_re * left_re + left_im * left_im, axis=1, keepdims=True)
    norm_right = jnp.sum(right_re * right_re + right_im * right_im, axis=1, keepdims=True)
    gamma_re = jnp.sum(left_re * right_re + left_im * right_im, axis=1, keepdims=True)
    gamma_im = jnp.sum(left_re * right_im - left_im * right_re, axis=1, keepdims=True)
    spread = norm_right - norm_left
    radius = jnp.sqrt(spread * spread + 4.0 * (gamma_re * gamma_re + gamma_im * gamma_im) + 1e-30)
    leading = jnp.sqrt((radius + jnp.abs(spread)) / (2.0 * radius))
    factor = 1.0 / (radius * leading)
    return spread >= 0.0, leading, factor * gamma_re, factor * gamma_im


def rotate_side(left, right, side, sign):
    rising, leading, b_re, b_im = sums(left, right)
    plain = jnp.where(rising, 1, 0) != side
    left_re = jnp.where(plain, leading, b_re)
    left_im = jnp.where(plain, 0.0, b_im)
    right_re = sign * jnp.where(plain, b_re, leading)
    right_im = sign * jnp.where(plain, -b_im, 0.0)
    return (
        left_re * left[0] - left_im * left[1] + right_re * right[0] - right_im * right[1],
        left_re * left[1] + left_im * left[0] + right_re * right[1] + right_im * right[0],
    )


def rotate_both(left, right):
    rising, leading, b_re, b_im = sums(left, right)
    zero = jnp.zeros_like(b_im)

    def combine(left_re, left_im, right_re, right_im):
        return (
            left_re * left[0] - left_im * left[1] + right_re * right[0] - right_im * right[1],
            left_re * left[1] + left_im * left[0] + right_re * right[1] + right_im * right[0],
        )

    new_left = combine(
        jnp.where(rising, leading, b_re),
        jnp.where(rising, zero, b_im),
        jnp.where(rising, -b_re, -leading),
        jnp.where(rising, b_im, zero),
    )
    new_right = combine(
        jnp.where(rising, b_re, leading),
        jnp.where(rising, b_im, zero),
        jnp.where(rising, leading, b_re),
        jnp.where(rising, zero, -b_im),
    )
    return new_left, new_right


def respond_kernel(
    meta_ref, held_ref, came_ref, table_ref, taper_ref, load_ref, pick_ref, early_ref, final_ref, all_ref, re_ref, im_ref, turn_ref, norm_ref
):
    block, depth = held_ref.shape[1:]
    half = block // 2
    count = held_ref.shape[0]
    for at in range(count):
        for ref, start in ((held_ref, 0), (came_ref, count)):
            source = meta_ref[5 + start + at]
            all_ref[pl.ds(pl.multiple_of(source * block, block), block), :] = ref[at]
    everything = all_ref[...]
    sign = jnp.where(lax.broadcasted_iota(jnp.int32, (block, depth), 1) < depth // 2, 1.0, -1.0)
    for which in range(3):
        number = meta_ref[which]
        pick = pick_ref[block:, :] if which == 2 else pick_ref[:block, :]
        rows = dot(pick, all_ref[pl.ds(pl.multiple_of(number * block, block), block), :], (1, 0))
        weights = jnp.concatenate([rows, pltpu.roll(rows, depth // 2, 1) * sign], axis=0).astype(jnp.bfloat16)
        tile = dot(weights, everything, (1, 1))
        part = slice(which * block, (which + 1) * block)
        taper = taper_ref[part, :]
        re_ref[part, :] = tile[:block] * taper
        im_ref[part, :] = tile[block:] * taper
        lanes = pl.ds(pl.multiple_of(number // (LANES // block) * LANES, LANES), LANES)
        re_ref[part, lanes] += load_ref[part, :]

    def rows_at(start):
        return re_ref[start : start + GROUP, :], im_ref[start : start + GROUP, :]

    def keep(start, column):
        turn_ref[start : start + GROUP, :] = column[0].astype(jnp.bfloat16)
        turn_ref[2 * block + start : 2 * block + start + GROUP, :] = column[1].astype(jnp.bfloat16)
        total = jnp.sum(column[0] * column[0] + column[1] * column[1], axis=1, keepdims=True)
        norm_ref[start : start + GROUP, :] = jnp.broadcast_to(1.0 / total, (GROUP, LANES))

    for at in range(0, half, GROUP):
        top, bottom = rotate_both(rows_at(at), rows_at(half + at))
        keep(at, top)
        keep(half + at, bottom)
    lower_side, upper_side = meta_ref[3], meta_ref[4]
    lower_sign = (2 * lower_side - 1).astype(jnp.float32)
    upper_sign = (2 * upper_side - 1).astype(jnp.float32)
    for at in range(0, half, GROUP):
        moved_top = rotate_side(rows_at(block + at), rows_at(block + half + at), lower_side, lower_sign)
        moved_bottom = rotate_side(rows_at(2 * block + at), rows_at(2 * block + half + at), upper_side, upper_sign)
        top, bottom = rotate_both(moved_top, moved_bottom)
        keep(block + at, top)
        keep(block + half + at, bottom)

    projected = dot(turn_ref[...], table_ref[...], (1, 0))
    rows = 2 * block
    z_re = projected[:rows, :BEAMS] + projected[rows:, BEAMS:]
    z_im = projected[rows:, :BEAMS] - projected[:rows, BEAMS:]
    inverse = jnp.concatenate([norm_ref[...]] * (BEAMS // LANES), axis=1)
    response = (z_re * z_re + z_im * z_im) * inverse
    early_ref[...] = response[:block]
    final_ref[...] = response[block:]


def gather_blocks(own):
    peers = lax.axis_size("sens")
    held, sources = own, [0]
    step = peers // 2
    while True:
        came = lax.ppermute(held, "sens", [(i, i ^ step) for i in range(peers)])
        sources = sources + [source ^ step for source in sources]
        if step == 1:
            return held, came, sources
        held = jnp.concatenate([held, came], axis=0)
        step //= 2


def per_device(spectra, valid_mask, pairing, positions, wavenumber):
    blocks = lax.axis_size("sens")
    position = lax.axis_index("sens")
    block = valid_mask.shape[1]
    depth = spectra.shape[0]
    sensors = positions.shape[1]
    own = pl.pallas_call(
        spread_kernel,
        out_shape=jax.ShapeDtypeStruct((1, block, depth), jnp.bfloat16),
        in_specs=[VMEM, VMEM],
        out_specs=VMEM,
        compiler_params=small(2),
        name="spread",
    )(spectra.T, valid_mask)
    held, came, sources = gather_blocks(own)
    numbers = [
        position,
        jnp.maximum(position - 1, 0),
        jnp.minimum(position + 1, blocks - 1),
        position == 1,
        position < blocks - 1,
    ]
    numbers += [position ^ source for source in sources]
    meta = jnp.stack([jnp.asarray(number, jnp.int32) for number in numbers])
    table, taper, load, pick = pl.pallas_call(
        functools.partial(prepare_kernel, block),
        out_shape=(
            jax.ShapeDtypeStruct((sensors, 2 * BEAMS), jnp.bfloat16),
            jax.ShapeDtypeStruct((3 * block, sensors), jnp.float32),
            jax.ShapeDtypeStruct((3 * block, LANES), jnp.float32),
            jax.ShapeDtypeStruct((2 * block, block), jnp.bfloat16),
        ),
        in_specs=[SMEM, SMEM, SMEM, VMEM],
        out_specs=(VMEM, VMEM, VMEM, VMEM),
        compiler_params=small(4),
        name="prepare",
    )(meta, pairing, wavenumber, positions)
    out = jax.ShapeDtypeStruct((block, BEAMS), jnp.float32)
    return pl.pallas_call(
        respond_kernel,
        out_shape=(out, out),
        in_specs=[SMEM, VMEM, VMEM, VMEM, VMEM, VMEM, VMEM],
        out_specs=(VMEM, VMEM),
        scratch_shapes=[
            pltpu.VMEM((sensors, depth), jnp.bfloat16),
            pltpu.VMEM((3 * block, sensors), jnp.float32),
            pltpu.VMEM((3 * block, sensors), jnp.float32),
            pltpu.VMEM((4 * block, sensors), jnp.bfloat16),
            pltpu.VMEM((2 * block, LANES), jnp.float32),
        ],
        compiler_params=small(4 + sensors * block // 2**13),
        name="respond",
    )(meta, held, came, table, taper, load, pick)


def solution(mesh):
    in_specs = (P("bin", "sens"), P(None, "sens"), P(), P(), P("bin"))
    out_specs = (P("sens", "bin"), P("sens", "bin"))
    return jax.shard_map(
        per_device, mesh=mesh, in_specs=in_specs, out_specs=out_specs, check_vma=False
    )
```

```python
import functools
import math

import jax
import jax.numpy as jnp
from jax import lax
from jax.experimental import pallas as pl
from jax.experimental.pallas import tpu as pltpu
from jax.sharding import PartitionSpec as P

BEAMS = 256
LOAD = 0.5
LANES = 128
ROWS = 8
GROUP = 16
VMEM = pl.BlockSpec(memory_space=pltpu.VMEM)
SMEM = pl.BlockSpec(memory_space=pltpu.SMEM)
HBM = pl.BlockSpec(memory_space=pltpu.HBM)

COS = (0.99999921, -19.73898036, 64.92865742, -85.27162153, 58.79049212, -21.07110563)
SIN = (6.28318492, -41.34158923, 81.59994333, -76.61447253, 41.34288235, -12.47124354)
SIN_FINE = (6.2831853, -41.34170041, 81.60513139, -76.70301535, 42.02592699, -14.89984667, 3.23813751)


def small(mebibytes):
    return pltpu.CompilerParams(vmem_limit_bytes=mebibytes * 2**20)


def fetch(pairs, semaphores):
    copies = [pltpu.make_async_copy(*pair, semaphores.at[i]) for i, pair in enumerate(pairs)]
    for copy in copies:
        copy.start()
    for copy in copies:
        copy.wait()


def horner(coefficients, at):
    value = coefficients[-1]
    for coefficient in coefficients[-2::-1]:
        value = value * at + coefficient
    return value


def dot(left, right, contract):
    return lax.dot_general(left, right, ((contract[:1], contract[1:]), ((), ())), preferred_element_type=jnp.float32)


def spread_kernel(spectra_hbm, mask_hbm, scaled_ref, spectra_ref, mask_ref, semaphores):
    fetch(((spectra_hbm, spectra_ref), (mask_hbm, mask_ref)), semaphores)
    segments, block = mask_ref.shape
    depth = spectra_ref.shape[1]
    row = lax.broadcasted_iota(jnp.int32, (segments, depth), 0)
    lane = lax.broadcasted_iota(jnp.int32, (segments, depth), 1)
    twice = jnp.where((row == lane) | (row + segments == lane), 1.0, 0.0).astype(jnp.bfloat16)
    validity = dot(mask_ref[...].astype(jnp.float32).astype(jnp.bfloat16), twice, (0, 0))
    counts = 0.5 * jnp.sum(validity, axis=1, keepdims=True)
    scaled = (spectra_ref[...].astype(jnp.float32) * validity * (1.0 / jnp.sqrt(counts))).astype(jnp.bfloat16)
    scaled_ref[0] = scaled


def prepare_kernel(
    block, meta_ref, pairing_hbm, wavenumber_hbm, positions_hbm, table_ref, taper_ref, load_ref, pick_ref,
    pairing_ref, wavenumber_ref, positions_ref, semaphores
):
    fetch(((pairing_hbm, pairing_ref), (wavenumber_hbm, wavenumber_ref), (positions_hbm, positions_ref)), semaphores)
    sensors = positions_ref.shape[1]
    half = block // 2
    width = 3.0 / block

    beam = lax.broadcasted_iota(jnp.int32, (ROWS, BEAMS), 1).astype(jnp.float32)
    turns = (beam + 0.5) * (0.5 / BEAMS)
    square = turns * turns
    cos_beam = horner(COS_FINE, square)
    sin_beam = turns * horner(SIN_FINE, square)
    scale = wavenumber_ref[0] * (0.5 / math.pi)
    for at in range(0, sensors, LANES):
        along, side = (
            jnp.transpose(jnp.broadcast_to(positions_ref[axis : axis + 1, at : at + LANES] * scale, (LANES, LANES)))
            for axis in (0, 1)
        )
        for row in range(0, LANES, GROUP):
            for lane in range(0, BEAMS, LANES):
                cos_part = cos_beam[:1, lane : lane + LANES]
                sin_part = sin_beam[:1, lane : lane + LANES]
                phase = along[row : row + GROUP] * cos_part + side[row : row + GROUP] * sin_part
                phase = phase - jnp.round(phase)
                square = phase * phase
                rows = slice(at + row, at + row + GROUP)
                table_ref[rows, lane : lane + LANES] = horner(COS, square).astype(jnp.bfloat16)
                table_ref[rows, BEAMS + lane : BEAMS + lane + LANES] = (phase * horner(SIN, square)).astype(jnp.bfloat16)

    sub = lax.broadcasted_iota(jnp.int32, (ROWS, LANES), 0)
    lane = lax.broadcasted_iota(jnp.int32, (ROWS, LANES), 1)

    def column(numbers):
        value = jnp.zeros((ROWS, LANES), jnp.int32)
        for i, number in enumerate(numbers):
            value = jnp.where(sub == i, number, value)
        return value

    order, later = [], []
    for at in range(0, half, ROWS):
        order.append(sub + at)
        later.append(column([pairing_ref[1, at + i] for i in range(ROWS)]))
    for at in range(0, half, ROWS):
        order.append(column([half + pairing_ref[0, at + i] for i in range(ROWS)]))
        later.append(column([half + pairing_ref[0, pairing_ref[1, at + i]] for i in range(ROWS)]))
    for which, rows in enumerate((order, later)):
        for at in range(0, len(rows), 2):
            pair = jnp.concatenate(rows[at : at + 2], axis=0)
            lanes = jnp.concatenate([lane, lane], axis=0)
            start = which * block + at * ROWS
            pick_ref[start : start + GROUP, :] = jnp.where(pair == lanes, 1.0, 0.0)[:, :block].astype(jnp.bfloat16)

    for which, rows in enumerate((order, order, later)):
        number = meta_ref[which]
        chunk = number // (LANES // block)
        shift = (number - chunk * (LANES // block)) * block
        for at, row in enumerate(rows):
            start = which * block + at * ROWS
            hit = row + shift == lane
            load_ref[start : start + ROWS, :] = jnp.where(hit, LOAD, 0.0)
            near = positions_ref[:, pl.ds(pl.multiple_of(chunk * LANES, LANES), LANES)]
            own_along = jnp.sum(jnp.where(hit, near[0:1], 0.0), axis=1, keepdims=True)
            own_side = jnp.sum(jnp.where(hit, near[1:2], 0.0), axis=1, keepdims=True)
            for to in range(0, sensors, LANES):
                delta_along = own_along - positions_ref[0:1, to : to + LANES]
                delta_side = own_side - positions_ref[1:2, to : to + LANES]
                square = jnp.maximum(delta_along * delta_along + delta_side * delta_side, 1e-30)
                inverse = lax.rsqrt(square)
                turn = (square * inverse) * (0.5 * width / math.pi)
                turn = turn - jnp.round(turn)
                value = turn * horner(SIN_FINE, turn * turn) * (inverse * (1.0 / width))
                taper_ref[start : start + ROWS, to : to + LANES] = value


COS_FINE = (0.99999999, -19.7392045, 64.93911746, -85.45013953, 60.16763095, -25.96759925, 6.52865816)


def sums(left, right):
    left_re, left_im = left
    right_re, right_im = right
    norm_left = jnp.sum(left_re * left_re + left_im * left_im, axis=1, keepdims=True)
    norm_right = jnp.sum(right_re * right_re + right_im * right_im, axis=1, keepdims=True)
    gamma_re = jnp.sum(left_re * right_re + left_im * right_im, axis=1, keepdims=True)
    gamma_im = jnp.sum(left_re * right_im - left_im * right_re, axis=1, keepdims=True)
    spread = norm_right - norm_left
    radius = jnp.sqrt(spread * spread + 4.0 * (gamma_re * gamma_re + gamma_im * gamma_im) + 1e-30)
    leading = jnp.sqrt((radius + jnp.abs(spread)) / (2.0 * radius))
    factor = 1.0 / (radius * leading)
    return spread >= 0.0, leading, factor * gamma_re, factor * gamma_im


def rotate_side(left, right, side, sign):
    rising, leading, b_re, b_im = sums(left, right)
    plain = jnp.where(rising, 1, 0) != side
    left_re = jnp.where(plain, leading, b_re)
    left_im = jnp.where(plain, 0.0, b_im)
    right_re = sign * jnp.where(plain, b_re, leading)
    right_im = sign * jnp.where(plain, -b_im, 0.0)
    return (
        left_re * left[0] - left_im * left[1] + right_re * right[0] - right_im * right[1],
        left_re * left[1] + left_im * left[0] + right_re * right[1] + right_im * right[0],
    )


def rotate_both(left, right):
    rising, leading, b_re, b_im = sums(left, right)
    zero = jnp.zeros_like(b_im)

    def combine(left_re, left_im, right_re, right_im):
        return (
            left_re * left[0] - left_im * left[1] + right_re * right[0] - right_im * right[1],
            left_re * left[1] + left_im * left[0] + right_re * right[1] + right_im * right[0],
        )

    new_left = combine(
        jnp.where(rising, leading, b_re),
        jnp.where(rising, zero, b_im),
        jnp.where(rising, -b_re, -leading),
        jnp.where(rising, b_im, zero),
    )
    new_right = combine(
        jnp.where(rising, b_re, leading),
        jnp.where(rising, b_im, zero),
        jnp.where(rising, leading, b_re),
        jnp.where(rising, zero, -b_im),
    )
    return new_left, new_right


def respond_kernel(
    meta_ref, held_ref, came_ref, table_ref, taper_ref, load_ref, pick_ref, early_hbm, final_hbm, all_ref, re_ref, im_ref, turn_ref, norm_ref, response_ref, semaphores
):
    block, depth = held_ref.shape[1:]
    half = block // 2
    count = held_ref.shape[0]
    for at in range(count):
        for ref, start in ((held_ref, 0), (came_ref, count)):
            source = meta_ref[5 + start + at]
            all_ref[pl.ds(pl.multiple_of(source * block, block), block), :] = ref[at]
    everything = all_ref[...]
    sign = jnp.where(lax.broadcasted_iota(jnp.int32, (block, depth), 1) < depth // 2, 1.0, -1.0)
    for which in range(3):
        number = meta_ref[which]
        pick = pick_ref[block:, :] if which == 2 else pick_ref[:block, :]
        rows = dot(pick, all_ref[pl.ds(pl.multiple_of(number * block, block), block), :], (1, 0))
        weights = jnp.concatenate([rows, pltpu.roll(rows, depth // 2, 1) * sign], axis=0).astype(jnp.bfloat16)
        tile = dot(weights, everything, (1, 1))
        part = slice(which * block, (which + 1) * block)
        taper = taper_ref[part, :]
        re_ref[part, :] = tile[:block] * taper
        im_ref[part, :] = tile[block:] * taper
        lanes = pl.ds(pl.multiple_of(number // (LANES // block) * LANES, LANES), LANES)
        re_ref[part, lanes] += load_ref[part, :]

    def rows_at(start):
        return re_ref[start : start + GROUP, :], im_ref[start : start + GROUP, :]

    def keep(which, start, column):
        turn_ref[which, start : start + GROUP, :] = column[0].astype(jnp.bfloat16)
        turn_ref[which, block + start : block + start + GROUP, :] = column[1].astype(jnp.bfloat16)
        total = jnp.sum(column[0] * column[0] + column[1] * column[1], axis=1, keepdims=True)
        norm_ref[which, start : start + GROUP, :] = jnp.broadcast_to(1.0 / total, (GROUP, LANES))

    def respond(which, result_hbm):
        projected = dot(turn_ref[which], table_ref[...], (1, 0))
        z_re = projected[:block, :BEAMS] + projected[block:, BEAMS:]
        z_im = projected[block:, :BEAMS] - projected[:block, BEAMS:]
        inverse = jnp.concatenate([norm_ref[which]] * (BEAMS // LANES), axis=1)
        response_ref[which] = (z_re * z_re + z_im * z_im) * inverse
        copy = pltpu.make_async_copy(response_ref.at[which], result_hbm, semaphores.at[which])
        copy.start()
        return copy

    for at in range(0, half, GROUP):
        top, bottom = rotate_both(rows_at(at), rows_at(half + at))
        keep(0, at, top)
        keep(0, half + at, bottom)
    early_copy = respond(0, early_hbm)
    lower_side, upper_side = meta_ref[3], meta_ref[4]
    lower_sign = (2 * lower_side - 1).astype(jnp.float32)
    upper_sign = (2 * upper_side - 1).astype(jnp.float32)
    for at in range(0, half, GROUP):
        moved_top = rotate_side(rows_at(block + at), rows_at(block + half + at), lower_side, lower_sign)
        moved_bottom = rotate_side(rows_at(2 * block + at), rows_at(2 * block + half + at), upper_side, upper_sign)
        top, bottom = rotate_both(moved_top, moved_bottom)
        keep(1, at, top)
        keep(1, half + at, bottom)
    final_copy = respond(1, final_hbm)
    early_copy.wait()
    final_copy.wait()


def order_of_arrival(peers):
    sources, step = [0], peers // 2
    while step:
        sources = sources + [source ^ step for source in sources]
        step //= 2
    return sources


def gather_blocks(own, beside):
    peers = lax.axis_size("sens")
    held, step = own, peers // 2
    while True:
        came = lax.ppermute(held, "sens", [(i, i ^ step) for i in range(peers)])
        if step == 1:
            return held, came, beside
        held = jnp.concatenate([held, came], axis=0)
        if step == peers // 2:
            held, beside = lax.optimization_barrier((held, beside))
        step //= 2


def per_device(spectra, valid_mask, pairing, positions, wavenumber):
    blocks = lax.axis_size("sens")
    position = lax.axis_index("sens")
    block = valid_mask.shape[1]
    depth = spectra.shape[0]
    sensors = positions.shape[1]
    own = pl.pallas_call(
        spread_kernel,
        out_shape=jax.ShapeDtypeStruct((1, block, depth), jnp.bfloat16),
        in_specs=[HBM, HBM],
        out_specs=VMEM,
        scratch_shapes=[
            pltpu.VMEM((block, depth), spectra.dtype),
            pltpu.VMEM(valid_mask.shape, valid_mask.dtype),
            pltpu.SemaphoreType.DMA((2,)),
        ],
        compiler_params=small(2),
        name="spread",
    )(spectra.T, valid_mask)
    numbers = [
        position,
        jnp.maximum(position - 1, 0),
        jnp.minimum(position + 1, blocks - 1),
        position == 1,
        position < blocks - 1,
    ]
    numbers += [position ^ source for source in order_of_arrival(blocks)]
    meta = jnp.stack([jnp.asarray(number, jnp.int32) for number in numbers])
    prepared = pl.pallas_call(
        functools.partial(prepare_kernel, block),
        out_shape=(
            jax.ShapeDtypeStruct((sensors, 2 * BEAMS), jnp.bfloat16),
            jax.ShapeDtypeStruct((3 * block, sensors), jnp.float32),
            jax.ShapeDtypeStruct((3 * block, LANES), jnp.float32),
            jax.ShapeDtypeStruct((2 * block, block), jnp.bfloat16),
        ),
        in_specs=[SMEM, HBM, HBM, HBM],
        out_specs=(VMEM, VMEM, VMEM, VMEM),
        scratch_shapes=[
            pltpu.SMEM(pairing.shape, pairing.dtype),
            pltpu.SMEM(wavenumber.shape, wavenumber.dtype),
            pltpu.VMEM(positions.shape, positions.dtype),
            pltpu.SemaphoreType.DMA((3,)),
        ],
        compiler_params=small(4),
        name="prepare",
    )(meta, pairing, wavenumber, positions)
    held, came, prepared = gather_blocks(own, prepared)
    out = jax.ShapeDtypeStruct((block, BEAMS), jnp.float32)
    return pl.pallas_call(
        respond_kernel,
        out_shape=(out, out),
        in_specs=[SMEM, VMEM, VMEM, VMEM, VMEM, VMEM, VMEM],
        out_specs=(HBM, HBM),
        scratch_shapes=[
            pltpu.VMEM((sensors, depth), jnp.bfloat16),
            pltpu.VMEM((3 * block, sensors), jnp.float32),
            pltpu.VMEM((3 * block, sensors), jnp.float32),
            pltpu.VMEM((2, 2 * block, sensors), jnp.bfloat16),
            pltpu.VMEM((2, block, LANES), jnp.float32),
            pltpu.VMEM((2, block, BEAMS), jnp.float32),
            pltpu.SemaphoreType.DMA((2,)),
        ],
        compiler_params=small(4 + sensors * block // 2**13),
        name="respond",
    )(meta, held, came, *prepared)


def solution(mesh):
    in_specs = (P("bin", "sens"), P(None, "sens"), P(), P(), P("bin"))
    out_specs = (P("sens", "bin"), P("sens", "bin"))
    return jax.shard_map(
        per_device, mesh=mesh, in_specs=in_specs, out_specs=out_specs, check_vma=False
    )
```

```python
import functools
import math

import jax
import jax.numpy as jnp
from jax import lax
from jax.experimental import pallas as pl
from jax.experimental.pallas import tpu as pltpu
from jax.sharding import PartitionSpec as P

BEAMS = 256
LOAD = 0.5
LANES = 128
ROWS = 8
GROUP = 16
VMEM = pl.BlockSpec(memory_space=pltpu.VMEM)
SMEM = pl.BlockSpec(memory_space=pltpu.SMEM)
HBM = pl.BlockSpec(memory_space=pltpu.HBM)

COS = (0.99999921, -19.73898036, 64.92865742, -85.27162153, 58.79049212, -21.07110563)
SIN = (6.28318492, -41.34158923, 81.59994333, -76.61447253, 41.34288235, -12.47124354)
SIN_FINE = (6.2831853, -41.34170041, 81.60513139, -76.70301535, 42.02592699, -14.89984667, 3.23813751)


def small(mebibytes):
    return pltpu.CompilerParams(vmem_limit_bytes=mebibytes * 2**20)


def fetch(pairs, semaphores):
    copies = [pltpu.make_async_copy(*pair, semaphores.at[i]) for i, pair in enumerate(pairs)]
    for copy in copies:
        copy.start()
    for copy in copies:
        copy.wait()


def horner(coefficients, at):
    value = coefficients[-1]
    for coefficient in coefficients[-2::-1]:
        value = value * at + coefficient
    return value


def dot(left, right, contract):
    return lax.dot_general(left, right, ((contract[:1], contract[1:]), ((), ())), preferred_element_type=jnp.float32)


def spread_kernel(spectra_hbm, mask_hbm, copies_ref, spectra_ref, mask_ref, semaphores):
    fetch(((spectra_hbm, spectra_ref), (mask_hbm, mask_ref)), semaphores)
    segments, block = mask_ref.shape
    depth = spectra_ref.shape[1]
    row = lax.broadcasted_iota(jnp.int32, (segments, depth), 0)
    lane = lax.broadcasted_iota(jnp.int32, (segments, depth), 1)
    twice = jnp.where((row == lane) | (row + segments == lane), 1.0, 0.0).astype(jnp.bfloat16)
    validity = dot(mask_ref[...].astype(jnp.float32).astype(jnp.bfloat16), twice, (0, 0))
    counts = 0.5 * jnp.sum(validity, axis=1, keepdims=True)
    scaled = (spectra_ref[...].astype(jnp.float32) * validity * (1.0 / jnp.sqrt(counts))).astype(jnp.bfloat16)
    for peer in range(copies_ref.shape[0]):
        copies_ref[peer] = scaled


def prepare_kernel(
    block, meta_ref, wavenumber_ref, pairing_hbm, positions_hbm, table_ref, taper_ref, load_ref, pick_ref,
    pairing_ref, positions_ref, semaphores
):
    fetch(((pairing_hbm, pairing_ref), (positions_hbm, positions_ref)), semaphores)
    sensors = positions_ref.shape[1]
    half = block // 2
    width = 3.0 / block

    beam = lax.broadcasted_iota(jnp.int32, (ROWS, BEAMS), 1).astype(jnp.float32)
    turns = (beam + 0.5) * (0.5 / BEAMS)
    square = turns * turns
    cos_beam = horner(COS_FINE, square)
    sin_beam = turns * horner(SIN_FINE, square)
    scale = wavenumber_ref[0] * (0.5 / math.pi)
    for at in range(0, sensors, LANES):
        along, side = (
            jnp.transpose(jnp.broadcast_to(positions_ref[axis : axis + 1, at : at + LANES] * scale, (LANES, LANES)))
            for axis in (0, 1)
        )
        for row in range(0, LANES, GROUP):
            for lane in range(0, BEAMS, LANES):
                cos_part = cos_beam[:1, lane : lane + LANES]
                sin_part = sin_beam[:1, lane : lane + LANES]
                phase = along[row : row + GROUP] * cos_part + side[row : row + GROUP] * sin_part
                phase = phase - jnp.round(phase)
                square = phase * phase
                rows = slice(at + row, at + row + GROUP)
                table_ref[rows, lane : lane + LANES] = horner(COS, square).astype(jnp.bfloat16)
                table_ref[rows, BEAMS + lane : BEAMS + lane + LANES] = (phase * horner(SIN, square)).astype(jnp.bfloat16)

    sub = lax.broadcasted_iota(jnp.int32, (ROWS, LANES), 0)
    lane = lax.broadcasted_iota(jnp.int32, (ROWS, LANES), 1)

    def column(numbers):
        value = jnp.zeros((ROWS, LANES), jnp.int32)
        for i, number in enumerate(numbers):
            value = jnp.where(sub == i, number, value)
        return value

    order, later = [], []
    for at in range(0, half, ROWS):
        order.append(sub + at)
        later.append(column([pairing_ref[1, at + i] for i in range(ROWS)]))
    for at in range(0, half, ROWS):
        order.append(column([half + pairing_ref[0, at + i] for i in range(ROWS)]))
        later.append(column([half + pairing_ref[0, pairing_ref[1, at + i]] for i in range(ROWS)]))
    for which, rows in enumerate((order, later)):
        for at in range(0, len(rows), 2):
            pair = jnp.concatenate(rows[at : at + 2], axis=0)
            lanes = jnp.concatenate([lane, lane], axis=0)
            start = which * block + at * ROWS
            pick_ref[start : start + GROUP, :] = jnp.where(pair == lanes, 1.0, 0.0)[:, :block].astype(jnp.bfloat16)

    for which, rows in enumerate((order, order, later)):
        number = meta_ref[which]
        chunk = number // (LANES // block)
        shift = (number - chunk * (LANES // block)) * block
        for at, row in enumerate(rows):
            start = which * block + at * ROWS
            hit = row + shift == lane
            load_ref[start : start + ROWS, :] = jnp.where(hit, LOAD, 0.0)
            near = positions_ref[:, pl.ds(pl.multiple_of(chunk * LANES, LANES), LANES)]
            own_along = jnp.sum(jnp.where(hit, near[0:1], 0.0), axis=1, keepdims=True)
            own_side = jnp.sum(jnp.where(hit, near[1:2], 0.0), axis=1, keepdims=True)
            for to in range(0, sensors, LANES):
                delta_along = own_along - positions_ref[0:1, to : to + LANES]
                delta_side = own_side - positions_ref[1:2, to : to + LANES]
                square = jnp.maximum(delta_along * delta_along + delta_side * delta_side, 1e-30)
                inverse = lax.rsqrt(square)
                turn = (square * inverse) * (0.5 * width / math.pi)
                turn = turn - jnp.round(turn)
                value = turn * horner(SIN_FINE, turn * turn) * (inverse * (1.0 / width))
                taper_ref[start : start + ROWS, to : to + LANES] = value


COS_FINE = (0.99999999, -19.7392045, 64.93911746, -85.45013953, 60.16763095, -25.96759925, 6.52865816)


def sums(left, right):
    left_re, left_im = left
    right_re, right_im = right
    norm_left = jnp.sum(left_re * left_re + left_im * left_im, axis=1, keepdims=True)
    norm_right = jnp.sum(right_re * right_re + right_im * right_im, axis=1, keepdims=True)
    gamma_re = jnp.sum(left_re * right_re + left_im * right_im, axis=1, keepdims=True)
    gamma_im = jnp.sum(left_re * right_im - left_im * right_re, axis=1, keepdims=True)
    spread = norm_right - norm_left
    radius = jnp.sqrt(spread * spread + 4.0 * (gamma_re * gamma_re + gamma_im * gamma_im) + 1e-30)
    leading = jnp.sqrt((radius + jnp.abs(spread)) / (2.0 * radius))
    factor = 1.0 / (radius * leading)
    return spread >= 0.0, leading, factor * gamma_re, factor * gamma_im


def rotate_side(left, right, side, sign):
    rising, leading, b_re, b_im = sums(left, right)
    plain = jnp.where(rising, 1, 0) != side
    left_re = jnp.where(plain, leading, b_re)
    left_im = jnp.where(plain, 0.0, b_im)
    right_re = sign * jnp.where(plain, b_re, leading)
    right_im = sign * jnp.where(plain, -b_im, 0.0)
    return (
        left_re * left[0] - left_im * left[1] + right_re * right[0] - right_im * right[1],
        left_re * left[1] + left_im * left[0] + right_re * right[1] + right_im * right[0],
    )


def rotate_both(left, right):
    rising, leading, b_re, b_im = sums(left, right)
    zero = jnp.zeros_like(b_im)

    def combine(left_re, left_im, right_re, right_im):
        return (
            left_re * left[0] - left_im * left[1] + right_re * right[0] - right_im * right[1],
            left_re * left[1] + left_im * left[0] + right_re * right[1] + right_im * right[0],
        )

    new_left = combine(
        jnp.where(rising, leading, b_re),
        jnp.where(rising, zero, b_im),
        jnp.where(rising, -b_re, -leading),
        jnp.where(rising, b_im, zero),
    )
    new_right = combine(
        jnp.where(rising, b_re, leading),
        jnp.where(rising, b_im, zero),
        jnp.where(rising, leading, b_re),
        jnp.where(rising, zero, -b_im),
    )
    return new_left, new_right


def respond_kernel(
    order, meta_ref, blocks_ref, table_ref, taper_ref, load_ref, pick_ref, early_hbm, final_hbm, all_ref, re_ref, im_ref, turn_ref, norm_ref, response_ref, semaphores
):
    block, depth = blocks_ref.shape[1:]
    half = block // 2
    for at, source in enumerate(order):
        all_ref[source * block : (source + 1) * block, :] = blocks_ref[at]
    everything = all_ref[...]
    sign = jnp.where(lax.broadcasted_iota(jnp.int32, (block, depth), 1) < depth // 2, 1.0, -1.0)
    for which in range(3):
        number = meta_ref[which]
        pick = pick_ref[block:, :] if which == 2 else pick_ref[:block, :]
        rows = dot(pick, all_ref[pl.ds(pl.multiple_of(number * block, block), block), :], (1, 0))
        weights = jnp.concatenate([rows, pltpu.roll(rows, depth // 2, 1) * sign], axis=0).astype(jnp.bfloat16)
        tile = dot(weights, everything, (1, 1))
        part = slice(which * block, (which + 1) * block)
        taper = taper_ref[part, :]
        re_ref[part, :] = tile[:block] * taper
        im_ref[part, :] = tile[block:] * taper
        lanes = pl.ds(pl.multiple_of(number // (LANES // block) * LANES, LANES), LANES)
        re_ref[part, lanes] += load_ref[part, :]

    def rows_at(start):
        return re_ref[start : start + GROUP, :], im_ref[start : start + GROUP, :]

    def keep(which, start, column):
        turn_ref[which, start : start + GROUP, :] = column[0].astype(jnp.bfloat16)
        turn_ref[which, block + start : block + start + GROUP, :] = column[1].astype(jnp.bfloat16)
        total = jnp.sum(column[0] * column[0] + column[1] * column[1], axis=1, keepdims=True)
        norm_ref[which, start : start + GROUP, :] = jnp.broadcast_to(1.0 / total, (GROUP, LANES))

    def respond(which, result_hbm):
        projected = dot(turn_ref[which], table_ref[...], (1, 0))
        z_re = projected[:block, :BEAMS] + projected[block:, BEAMS:]
        z_im = projected[block:, :BEAMS] - projected[:block, BEAMS:]
        inverse = jnp.concatenate([norm_ref[which]] * (BEAMS // LANES), axis=1)
        response_ref[which] = (z_re * z_re + z_im * z_im) * inverse
        copy = pltpu.make_async_copy(response_ref.at[which], result_hbm, semaphores.at[which])
        copy.start()
        return copy

    for at in range(0, half, GROUP):
        top, bottom = rotate_both(rows_at(at), rows_at(half + at))
        keep(0, at, top)
        keep(0, half + at, bottom)
    early_copy = respond(0, early_hbm)
    lower_side, upper_side = meta_ref[3], meta_ref[4]
    lower_sign = (2 * lower_side - 1).astype(jnp.float32)
    upper_sign = (2 * upper_side - 1).astype(jnp.float32)
    for at in range(0, half, GROUP):
        moved_top = rotate_side(rows_at(block + at), rows_at(block + half + at), lower_side, lower_sign)
        moved_bottom = rotate_side(rows_at(2 * block + at), rows_at(2 * block + half + at), upper_side, upper_sign)
        top, bottom = rotate_both(moved_top, moved_bottom)
        keep(1, at, top)
        keep(1, half + at, bottom)
    final_copy = respond(1, final_hbm)
    early_copy.wait()
    final_copy.wait()


def send_order(peers):
    return [at // 2 if at % 2 == 0 else peers - 1 - at // 2 for at in range(peers)]


def pinned(array):
    return pltpu.with_memory_space_constraint(array, pltpu.HBM)


def per_device(spectra, valid_mask, pairing, positions, wavenumber):
    blocks = lax.axis_size("sens")
    position = lax.axis_index("sens")
    block = valid_mask.shape[1]
    depth = spectra.shape[0]
    sensors = positions.shape[1]
    copies = pl.pallas_call(
        spread_kernel,
        out_shape=jax.ShapeDtypeStruct((blocks, block, depth), jnp.bfloat16),
        in_specs=[HBM, HBM],
        out_specs=VMEM,
        scratch_shapes=[
            pltpu.VMEM((block, depth), spectra.dtype),
            pltpu.VMEM(valid_mask.shape, valid_mask.dtype),
            pltpu.SemaphoreType.DMA((2,)),
        ],
        compiler_params=small(2),
        name="spread",
    )(pinned(spectra.T), pinned(valid_mask))
    order = send_order(blocks)
    numbers = [
        position,
        jnp.maximum(position - 1, 0),
        jnp.minimum(position + 1, blocks - 1),
        position == 1,
        position < blocks - 1,
    ]
    meta = jnp.stack([jnp.asarray(number, jnp.int32) for number in numbers])
    prepared = pl.pallas_call(
        functools.partial(prepare_kernel, block),
        out_shape=(
            jax.ShapeDtypeStruct((sensors, 2 * BEAMS), jnp.bfloat16),
            jax.ShapeDtypeStruct((3 * block, sensors), jnp.float32),
            jax.ShapeDtypeStruct((3 * block, LANES), jnp.float32),
            jax.ShapeDtypeStruct((2 * block, block), jnp.bfloat16),
        ),
        in_specs=[SMEM, SMEM, HBM, HBM],
        out_specs=(VMEM, VMEM, VMEM, VMEM),
        scratch_shapes=[
            pltpu.SMEM(pairing.shape, pairing.dtype),
            pltpu.VMEM(positions.shape, positions.dtype),
            pltpu.SemaphoreType.DMA((2,)),
        ],
        compiler_params=small(4),
        name="prepare",
    )(meta, wavenumber, pinned(pairing), pinned(positions))
    gathered = lax.all_to_all(copies, "sens", split_axis=0, concat_axis=0, axis_index_groups=[order])
    out = jax.ShapeDtypeStruct((block, BEAMS), jnp.float32)
    return pl.pallas_call(
        functools.partial(respond_kernel, order),
        out_shape=(out, out),
        in_specs=[SMEM, VMEM, VMEM, VMEM, VMEM, VMEM],
        out_specs=(HBM, HBM),
        scratch_shapes=[
            pltpu.VMEM((sensors, depth), jnp.bfloat16),
            pltpu.VMEM((3 * block, sensors), jnp.float32),
            pltpu.VMEM((3 * block, sensors), jnp.float32),
            pltpu.VMEM((2, 2 * block, sensors), jnp.bfloat16),
            pltpu.VMEM((2, block, LANES), jnp.float32),
            pltpu.VMEM((2, block, BEAMS), jnp.float32),
            pltpu.SemaphoreType.DMA((2,)),
        ],
        compiler_params=small(4 + sensors * block // 2**13),
        name="respond",
    )(meta, gathered, *prepared)


def solution(mesh):
    in_specs = (P("bin", "sens"), P(None, "sens"), P(), P(), P("bin"))
    out_specs = (P("sens", "bin"), P("sens", "bin"))
    return jax.shard_map(
        per_device, mesh=mesh, in_specs=in_specs, out_specs=out_specs, check_vma=False
    )
```

```python
import functools
import math

import jax
import jax.numpy as jnp
from jax import lax
from jax.experimental import pallas as pl
from jax.experimental.pallas import tpu as pltpu
from jax.sharding import PartitionSpec as P

BEAMS = 256
LOAD = 0.5
LANES = 128
ROWS = 8
GROUP = 16
VMEM = pl.BlockSpec(memory_space=pltpu.VMEM)
SMEM = pl.BlockSpec(memory_space=pltpu.SMEM)
HBM = pl.BlockSpec(memory_space=pltpu.HBM)

COS = (0.99999921, -19.73898036, 64.92865742, -85.27162153, 58.79049212, -21.07110563)
SIN = (6.28318492, -41.34158923, 81.59994333, -76.61447253, 41.34288235, -12.47124354)
SIN_FINE = (6.2831853, -41.34170041, 81.60513139, -76.70301535, 42.02592699, -14.89984667, 3.23813751)


def small(mebibytes):
    return pltpu.CompilerParams(vmem_limit_bytes=mebibytes * 2**20)


def fetch(pairs, semaphores):
    copies = [pltpu.make_async_copy(*pair, semaphores.at[i]) for i, pair in enumerate(pairs)]
    for copy in copies:
        copy.start()
    for copy in copies:
        copy.wait()


def horner(coefficients, at):
    value = coefficients[-1]
    for coefficient in coefficients[-2::-1]:
        value = value * at + coefficient
    return value


def dot(left, right, contract):
    return lax.dot_general(left, right, ((contract[:1], contract[1:]), ((), ())), preferred_element_type=jnp.float32)


def spread_kernel(spectra_hbm, mask_hbm, copies_ref, spectra_ref, mask_ref, semaphores):
    fetch(((spectra_hbm, spectra_ref), (mask_hbm, mask_ref)), semaphores)
    segments, block = mask_ref.shape
    depth = spectra_ref.shape[1]
    row = lax.broadcasted_iota(jnp.int32, (segments, depth), 0)
    lane = lax.broadcasted_iota(jnp.int32, (segments, depth), 1)
    twice = jnp.where((row == lane) | (row + segments == lane), 1.0, 0.0).astype(jnp.bfloat16)
    validity = dot(mask_ref[...].astype(jnp.float32).astype(jnp.bfloat16), twice, (0, 0))
    counts = 0.5 * jnp.sum(validity, axis=1, keepdims=True)
    scaled = (spectra_ref[...].astype(jnp.float32) * validity * (1.0 / jnp.sqrt(counts))).astype(jnp.bfloat16)
    for peer in range(copies_ref.shape[0]):
        copies_ref[peer] = scaled


def prepare_kernel(
    block, meta_ref, wavenumber_ref, pairing_hbm, positions_hbm, table_ref, taper_ref, load_ref, pick_ref,
    pairing_ref, positions_ref, semaphores
):
    fetch(((pairing_hbm, pairing_ref), (positions_hbm, positions_ref)), semaphores)
    sensors = positions_ref.shape[1]
    half = block // 2
    width = 3.0 / block

    beam = lax.broadcasted_iota(jnp.int32, (ROWS, BEAMS), 1).astype(jnp.float32)
    turns = (beam + 0.5) * (0.5 / BEAMS)
    square = turns * turns
    cos_beam = horner(COS_FINE, square)
    sin_beam = turns * horner(SIN_FINE, square)
    scale = wavenumber_ref[0] * (0.5 / math.pi)
    for at in range(0, sensors, LANES):
        along, side = (
            jnp.transpose(jnp.broadcast_to(positions_ref[axis : axis + 1, at : at + LANES] * scale, (LANES, LANES)))
            for axis in (0, 1)
        )
        for row in range(0, LANES, GROUP):
            for lane in range(0, BEAMS, LANES):
                cos_part = cos_beam[:1, lane : lane + LANES]
                sin_part = sin_beam[:1, lane : lane + LANES]
                phase = along[row : row + GROUP] * cos_part + side[row : row + GROUP] * sin_part
                phase = phase - jnp.round(phase)
                square = phase * phase
                rows = slice(at + row, at + row + GROUP)
                table_ref[rows, lane : lane + LANES] = horner(COS, square).astype(jnp.bfloat16)
                table_ref[rows, BEAMS + lane : BEAMS + lane + LANES] = (phase * horner(SIN, square)).astype(jnp.bfloat16)

    sub = lax.broadcasted_iota(jnp.int32, (ROWS, LANES), 0)
    lane = lax.broadcasted_iota(jnp.int32, (ROWS, LANES), 1)

    def column(numbers):
        value = jnp.zeros((ROWS, LANES), jnp.int32)
        for i, number in enumerate(numbers):
            value = jnp.where(sub == i, number, value)
        return value

    order, later = [], []
    for at in range(0, half, ROWS):
        order.append(sub + at)
        later.append(column([pairing_ref[1, at + i] for i in range(ROWS)]))
    for at in range(0, half, ROWS):
        order.append(column([half + pairing_ref[0, at + i] for i in range(ROWS)]))
        later.append(column([half + pairing_ref[0, pairing_ref[1, at + i]] for i in range(ROWS)]))
    for which, rows in enumerate((order, later)):
        for at in range(0, len(rows), 2):
            pair = jnp.concatenate(rows[at : at + 2], axis=0)
            lanes = jnp.concatenate([lane, lane], axis=0)
            start = which * block + at * ROWS
            pick_ref[start : start + GROUP, :] = jnp.where(pair == lanes, 1.0, 0.0)[:, :block].astype(jnp.bfloat16)

    for which, rows in enumerate((order, order, later)):
        number = meta_ref[which]
        chunk = number // (LANES // block)
        shift = (number - chunk * (LANES // block)) * block
        for at, row in enumerate(rows):
            start = which * block + at * ROWS
            hit = row + shift == lane
            load_ref[start : start + ROWS, :] = jnp.where(hit, LOAD, 0.0)
            near = positions_ref[:, pl.ds(pl.multiple_of(chunk * LANES, LANES), LANES)]
            own_along = jnp.sum(jnp.where(hit, near[0:1], 0.0), axis=1, keepdims=True)
            own_side = jnp.sum(jnp.where(hit, near[1:2], 0.0), axis=1, keepdims=True)
            for to in range(0, sensors, LANES):
                delta_along = own_along - positions_ref[0:1, to : to + LANES]
                delta_side = own_side - positions_ref[1:2, to : to + LANES]
                square = jnp.maximum(delta_along * delta_along + delta_side * delta_side, 1e-30)
                inverse = lax.rsqrt(square)
                turn = (square * inverse) * (0.5 * width / math.pi)
                turn = turn - jnp.round(turn)
                value = turn * horner(SIN_FINE, turn * turn) * (inverse * (1.0 / width))
                taper_ref[start : start + ROWS, to : to + LANES] = value


COS_FINE = (0.99999999, -19.7392045, 64.93911746, -85.45013953, 60.16763095, -25.96759925, 6.52865816)


def sums(left, right):
    left_re, left_im = left
    right_re, right_im = right
    norm_left = jnp.sum(left_re * left_re + left_im * left_im, axis=1, keepdims=True)
    norm_right = jnp.sum(right_re * right_re + right_im * right_im, axis=1, keepdims=True)
    gamma_re = jnp.sum(left_re * right_re + left_im * right_im, axis=1, keepdims=True)
    gamma_im = jnp.sum(left_re * right_im - left_im * right_re, axis=1, keepdims=True)
    spread = norm_right - norm_left
    radius = jnp.sqrt(spread * spread + 4.0 * (gamma_re * gamma_re + gamma_im * gamma_im) + 1e-30)
    leading = jnp.sqrt((radius + jnp.abs(spread)) / (2.0 * radius))
    factor = 1.0 / (radius * leading)
    return spread >= 0.0, leading, factor * gamma_re, factor * gamma_im


def rotate_side(left, right, side, sign):
    rising, leading, b_re, b_im = sums(left, right)
    plain = jnp.where(rising, 1, 0) != side
    left_re = jnp.where(plain, leading, b_re)
    left_im = jnp.where(plain, 0.0, b_im)
    right_re = sign * jnp.where(plain, b_re, leading)
    right_im = sign * jnp.where(plain, -b_im, 0.0)
    return (
        left_re * left[0] - left_im * left[1] + right_re * right[0] - right_im * right[1],
        left_re * left[1] + left_im * left[0] + right_re * right[1] + right_im * right[0],
    )


def rotate_both(left, right):
    rising, leading, b_re, b_im = sums(left, right)
    zero = jnp.zeros_like(b_im)

    def combine(left_re, left_im, right_re, right_im):
        return (
            left_re * left[0] - left_im * left[1] + right_re * right[0] - right_im * right[1],
            left_re * left[1] + left_im * left[0] + right_re * right[1] + right_im * right[0],
        )

    new_left = combine(
        jnp.where(rising, leading, b_re),
        jnp.where(rising, zero, b_im),
        jnp.where(rising, -b_re, -leading),
        jnp.where(rising, b_im, zero),
    )
    new_right = combine(
        jnp.where(rising, b_re, leading),
        jnp.where(rising, b_im, zero),
        jnp.where(rising, leading, b_re),
        jnp.where(rising, zero, -b_im),
    )
    return new_left, new_right


def respond_kernel(
    order, meta_ref, blocks_ref, table_ref, taper_ref, load_ref, pick_ref, early_hbm, final_hbm, all_ref, re_ref, im_ref, turn_ref, norm_ref, response_ref, semaphores
):
    block, depth = blocks_ref.shape[1:]
    half = block // 2
    for at, source in enumerate(order):
        all_ref[source * block : (source + 1) * block, :] = blocks_ref[at]
    everything = all_ref[...]
    sign = jnp.where(lax.broadcasted_iota(jnp.int32, (block, depth), 1) < depth // 2, 1.0, -1.0)
    for which in range(3):
        number = meta_ref[which]
        pick = pick_ref[block:, :] if which == 2 else pick_ref[:block, :]
        rows = dot(pick, all_ref[pl.ds(pl.multiple_of(number * block, block), block), :], (1, 0))
        weights = jnp.concatenate([rows, pltpu.roll(rows, depth // 2, 1) * sign], axis=0).astype(jnp.bfloat16)
        tile = dot(weights, everything, (1, 1))
        part = slice(which * block, (which + 1) * block)
        taper = taper_ref[part, :]
        re_ref[part, :] = tile[:block] * taper
        im_ref[part, :] = tile[block:] * taper
        lanes = pl.ds(pl.multiple_of(number // (LANES // block) * LANES, LANES), LANES)
        re_ref[part, lanes] += load_ref[part, :]

    def rows_at(start):
        return re_ref[start : start + GROUP, :], im_ref[start : start + GROUP, :]

    def keep(which, start, column):
        turn_ref[which, start : start + GROUP, :] = column[0].astype(jnp.bfloat16)
        turn_ref[which, block + start : block + start + GROUP, :] = column[1].astype(jnp.bfloat16)
        total = jnp.sum(column[0] * column[0] + column[1] * column[1], axis=1, keepdims=True)
        norm_ref[which, start : start + GROUP, :] = jnp.broadcast_to(1.0 / total, (GROUP, LANES))

    def respond(which, result_hbm):
        projected = dot(turn_ref[which], table_ref[...], (1, 0))
        z_re = projected[:block, :BEAMS] + projected[block:, BEAMS:]
        z_im = projected[block:, :BEAMS] - projected[:block, BEAMS:]
        inverse = jnp.concatenate([norm_ref[which]] * (BEAMS // LANES), axis=1)
        response_ref[which] = (z_re * z_re + z_im * z_im) * inverse
        copy = pltpu.make_async_copy(response_ref.at[which], result_hbm, semaphores.at[which])
        copy.start()
        return copy

    for at in range(0, half, GROUP):
        top, bottom = rotate_both(rows_at(at), rows_at(half + at))
        keep(0, at, top)
        keep(0, half + at, bottom)
    early_copy = respond(0, early_hbm)
    lower_side, upper_side = meta_ref[3], meta_ref[4]
    lower_sign = (2 * lower_side - 1).astype(jnp.float32)
    upper_sign = (2 * upper_side - 1).astype(jnp.float32)
    for at in range(0, half, GROUP):
        moved_top = rotate_side(rows_at(block + at), rows_at(block + half + at), lower_side, lower_sign)
        moved_bottom = rotate_side(rows_at(2 * block + at), rows_at(2 * block + half + at), upper_side, upper_sign)
        top, bottom = rotate_both(moved_top, moved_bottom)
        keep(1, at, top)
        keep(1, half + at, bottom)
    final_copy = respond(1, final_hbm)
    early_copy.wait()
    final_copy.wait()


def send_order(peers):
    return [at // 2 if at % 2 == 0 else peers - 1 - at // 2 for at in range(peers)][::-1]


def pinned(array):
    return pltpu.with_memory_space_constraint(array, pltpu.HBM)


def per_device(spectra, valid_mask, pairing, positions, wavenumber):
    blocks = lax.axis_size("sens")
    position = lax.axis_index("sens")
    block = valid_mask.shape[1]
    depth = spectra.shape[0]
    sensors = positions.shape[1]
    copies = pl.pallas_call(
        spread_kernel,
        out_shape=jax.ShapeDtypeStruct((blocks, block, depth), jnp.bfloat16),
        in_specs=[HBM, HBM],
        out_specs=VMEM,
        scratch_shapes=[
            pltpu.VMEM((block, depth), spectra.dtype),
            pltpu.VMEM(valid_mask.shape, valid_mask.dtype),
            pltpu.SemaphoreType.DMA((2,)),
        ],
        compiler_params=small(2),
        name="spread",
    )(pinned(spectra.T), pinned(valid_mask))
    order = send_order(blocks)
    numbers = [
        position,
        jnp.maximum(position - 1, 0),
        jnp.minimum(position + 1, blocks - 1),
        position == 1,
        position < blocks - 1,
    ]
    meta = jnp.stack([jnp.asarray(number, jnp.int32) for number in numbers])
    prepared = pl.pallas_call(
        functools.partial(prepare_kernel, block),
        out_shape=(
            jax.ShapeDtypeStruct((sensors, 2 * BEAMS), jnp.bfloat16),
            jax.ShapeDtypeStruct((3 * block, sensors), jnp.float32),
            jax.ShapeDtypeStruct((3 * block, LANES), jnp.float32),
            jax.ShapeDtypeStruct((2 * block, block), jnp.bfloat16),
        ),
        in_specs=[SMEM, SMEM, HBM, HBM],
        out_specs=(VMEM, VMEM, VMEM, VMEM),
        scratch_shapes=[
            pltpu.SMEM(pairing.shape, pairing.dtype),
            pltpu.VMEM(positions.shape, positions.dtype),
            pltpu.SemaphoreType.DMA((2,)),
        ],
        compiler_params=small(4),
        name="prepare",
    )(meta, wavenumber, pinned(pairing), pinned(positions))
    gathered = lax.all_to_all(copies, "sens", split_axis=0, concat_axis=0, axis_index_groups=[order])
    out = jax.ShapeDtypeStruct((block, BEAMS), jnp.float32)
    return pl.pallas_call(
        functools.partial(respond_kernel, order),
        out_shape=(out, out),
        in_specs=[SMEM, VMEM, VMEM, VMEM, VMEM, VMEM],
        out_specs=(HBM, HBM),
        scratch_shapes=[
            pltpu.VMEM((sensors, depth), jnp.bfloat16),
            pltpu.VMEM((3 * block, sensors), jnp.float32),
            pltpu.VMEM((3 * block, sensors), jnp.float32),
            pltpu.VMEM((2, 2 * block, sensors), jnp.bfloat16),
            pltpu.VMEM((2, block, LANES), jnp.float32),
            pltpu.VMEM((2, block, BEAMS), jnp.float32),
            pltpu.SemaphoreType.DMA((2,)),
        ],
        compiler_params=small(4 + sensors * block // 2**13),
        name="respond",
    )(meta, gathered, *prepared)


def solution(mesh):
    in_specs = (P("bin", "sens"), P(None, "sens"), P(), P(), P("bin"))
    out_specs = (P("sens", "bin"), P("sens", "bin"))
    return jax.shard_map(
        per_device, mesh=mesh, in_specs=in_specs, out_specs=out_specs, check_vma=False
    )
```

```python
import functools
import math

import jax
import jax.numpy as jnp
from jax import lax
from jax.experimental import pallas as pl
from jax.experimental.pallas import tpu as pltpu
from jax.sharding import PartitionSpec as P

BEAMS = 256
LOAD = 0.5
LANES = 128
ROWS = 8
GROUP = 16
VMEM = pl.BlockSpec(memory_space=pltpu.VMEM)
SMEM = pl.BlockSpec(memory_space=pltpu.SMEM)
HBM = pl.BlockSpec(memory_space=pltpu.HBM)

COS = (0.99999921, -19.73898036, 64.92865742, -85.27162153, 58.79049212, -21.07110563)
SIN = (6.28318492, -41.34158923, 81.59994333, -76.61447253, 41.34288235, -12.47124354)
SIN_FINE = (6.2831853, -41.34170041, 81.60513139, -76.70301535, 42.02592699, -14.89984667, 3.23813751)


def small(mebibytes):
    return pltpu.CompilerParams(vmem_limit_bytes=mebibytes * 2**20)


def fetch(pairs, semaphores):
    copies = [pltpu.make_async_copy(*pair, semaphores.at[i]) for i, pair in enumerate(pairs)]
    for copy in copies:
        copy.start()
    for copy in copies:
        copy.wait()


def horner(coefficients, at):
    value = coefficients[-1]
    for coefficient in coefficients[-2::-1]:
        value = value * at + coefficient
    return value


def dot(left, right, contract):
    return lax.dot_general(left, right, ((contract[:1], contract[1:]), ((), ())), preferred_element_type=jnp.float32)


def spread_kernel(spectra_hbm, mask_hbm, copies_ref, spectra_ref, mask_ref, semaphores):
    fetch(((spectra_hbm, spectra_ref), (mask_hbm, mask_ref)), semaphores)
    segments, block = mask_ref.shape
    depth = spectra_ref.shape[1]
    row = lax.broadcasted_iota(jnp.int32, (segments, depth), 0)
    lane = lax.broadcasted_iota(jnp.int32, (segments, depth), 1)
    twice = jnp.where((row == lane) | (row + segments == lane), 1.0, 0.0).astype(jnp.bfloat16)
    validity = dot(mask_ref[...].astype(jnp.float32).astype(jnp.bfloat16), twice, (0, 0))
    counts = 0.5 * jnp.sum(validity, axis=1, keepdims=True)
    scaled = (spectra_ref[...].astype(jnp.float32) * validity * (1.0 / jnp.sqrt(counts))).astype(jnp.bfloat16)
    for peer in range(copies_ref.shape[0]):
        copies_ref[peer] = scaled


def prepare_kernel(
    block, meta_ref, wavenumber_ref, pairing_hbm, positions_hbm, table_ref, taper_ref, load_ref, pick_ref,
    pairing_ref, positions_ref, semaphores
):
    fetch(((pairing_hbm, pairing_ref), (positions_hbm, positions_ref)), semaphores)
    sensors = positions_ref.shape[1]
    half = block // 2
    width = 3.0 / block

    beam = lax.broadcasted_iota(jnp.int32, (ROWS, BEAMS), 1).astype(jnp.float32)
    turns = (beam + 0.5) * (0.5 / BEAMS)
    square = turns * turns
    cos_beam = horner(COS_FINE, square)
    sin_beam = turns * horner(SIN_FINE, square)
    scale = wavenumber_ref[0] * (0.5 / math.pi)
    for at in range(0, sensors, LANES):
        along, side = (
            jnp.transpose(jnp.broadcast_to(positions_ref[axis : axis + 1, at : at + LANES] * scale, (LANES, LANES)))
            for axis in (0, 1)
        )
        for row in range(0, LANES, GROUP):
            for lane in range(0, BEAMS, LANES):
                cos_part = cos_beam[:1, lane : lane + LANES]
                sin_part = sin_beam[:1, lane : lane + LANES]
                phase = along[row : row + GROUP] * cos_part + side[row : row + GROUP] * sin_part
                phase = phase - jnp.round(phase)
                square = phase * phase
                rows = slice(at + row, at + row + GROUP)
                table_ref[rows, lane : lane + LANES] = horner(COS, square).astype(jnp.bfloat16)
                table_ref[rows, BEAMS + lane : BEAMS + lane + LANES] = (phase * horner(SIN, square)).astype(jnp.bfloat16)

    sub = lax.broadcasted_iota(jnp.int32, (ROWS, LANES), 0)
    lane = lax.broadcasted_iota(jnp.int32, (ROWS, LANES), 1)

    def column(numbers):
        value = jnp.zeros((ROWS, LANES), jnp.int32)
        for i, number in enumerate(numbers):
            value = jnp.where(sub == i, number, value)
        return value

    order, later = [], []
    for at in range(0, half, ROWS):
        order.append(sub + at)
        later.append(column([pairing_ref[1, at + i] for i in range(ROWS)]))
    for at in range(0, half, ROWS):
        order.append(column([half + pairing_ref[0, at + i] for i in range(ROWS)]))
        later.append(column([half + pairing_ref[0, pairing_ref[1, at + i]] for i in range(ROWS)]))
    for which, rows in enumerate((order, later)):
        for at in range(0, len(rows), 2):
            pair = jnp.concatenate(rows[at : at + 2], axis=0)
            lanes = jnp.concatenate([lane, lane], axis=0)
            start = which * block + at * ROWS
            pick_ref[start : start + GROUP, :] = jnp.where(pair == lanes, 1.0, 0.0)[:, :block].astype(jnp.bfloat16)

    for which, rows in enumerate((order, order, later)):
        number = meta_ref[which]
        chunk = number // (LANES // block)
        shift = (number - chunk * (LANES // block)) * block
        for at, row in enumerate(rows):
            start = which * block + at * ROWS
            hit = row + shift == lane
            load_ref[start : start + ROWS, :] = jnp.where(hit, LOAD, 0.0)
            near = positions_ref[:, pl.ds(pl.multiple_of(chunk * LANES, LANES), LANES)]
            own_along = jnp.sum(jnp.where(hit, near[0:1], 0.0), axis=1, keepdims=True)
            own_side = jnp.sum(jnp.where(hit, near[1:2], 0.0), axis=1, keepdims=True)
            for to in range(0, sensors, LANES):
                delta_along = own_along - positions_ref[0:1, to : to + LANES]
                delta_side = own_side - positions_ref[1:2, to : to + LANES]
                square = jnp.maximum(delta_along * delta_along + delta_side * delta_side, 1e-30)
                inverse = lax.rsqrt(square)
                turn = (square * inverse) * (0.5 * width / math.pi)
                turn = turn - jnp.round(turn)
                value = turn * horner(SIN_FINE, turn * turn) * (inverse * (1.0 / width))
                taper_ref[start : start + ROWS, to : to + LANES] = value


COS_FINE = (0.99999999, -19.7392045, 64.93911746, -85.45013953, 60.16763095, -25.96759925, 6.52865816)


def sums(left, right):
    left_re, left_im = left
    right_re, right_im = right
    norm_left = jnp.sum(left_re * left_re + left_im * left_im, axis=1, keepdims=True)
    norm_right = jnp.sum(right_re * right_re + right_im * right_im, axis=1, keepdims=True)
    gamma_re = jnp.sum(left_re * right_re + left_im * right_im, axis=1, keepdims=True)
    gamma_im = jnp.sum(left_re * right_im - left_im * right_re, axis=1, keepdims=True)
    spread = norm_right - norm_left
    radius = jnp.sqrt(spread * spread + 4.0 * (gamma_re * gamma_re + gamma_im * gamma_im) + 1e-30)
    leading = jnp.sqrt((radius + jnp.abs(spread)) / (2.0 * radius))
    factor = 1.0 / (radius * leading)
    return spread >= 0.0, leading, factor * gamma_re, factor * gamma_im


def rotate_side(left, right, side, sign):
    rising, leading, b_re, b_im = sums(left, right)
    plain = jnp.where(rising, 1, 0) != side
    left_re = jnp.where(plain, leading, b_re)
    left_im = jnp.where(plain, 0.0, b_im)
    right_re = sign * jnp.where(plain, b_re, leading)
    right_im = sign * jnp.where(plain, -b_im, 0.0)
    return (
        left_re * left[0] - left_im * left[1] + right_re * right[0] - right_im * right[1],
        left_re * left[1] + left_im * left[0] + right_re * right[1] + right_im * right[0],
    )


def rotate_both(left, right):
    rising, leading, b_re, b_im = sums(left, right)
    zero = jnp.zeros_like(b_im)

    def combine(left_re, left_im, right_re, right_im):
        return (
            left_re * left[0] - left_im * left[1] + right_re * right[0] - right_im * right[1],
            left_re * left[1] + left_im * left[0] + right_re * right[1] + right_im * right[0],
        )

    new_left = combine(
        jnp.where(rising, leading, b_re),
        jnp.where(rising, zero, b_im),
        jnp.where(rising, -b_re, -leading),
        jnp.where(rising, b_im, zero),
    )
    new_right = combine(
        jnp.where(rising, b_re, leading),
        jnp.where(rising, b_im, zero),
        jnp.where(rising, leading, b_re),
        jnp.where(rising, zero, -b_im),
    )
    return new_left, new_right


def respond_kernel(
    order, meta_ref, blocks_ref, table_ref, taper_ref, load_ref, pick_ref, early_hbm, final_hbm, all_ref, re_ref, im_ref, turn_ref, norm_ref, response_ref, semaphores
):
    block, depth = blocks_ref.shape[1:]
    half = block // 2
    for at, source in enumerate(order):
        all_ref[source * block : (source + 1) * block, :] = blocks_ref[at]
    everything = all_ref[...]
    sign = jnp.where(lax.broadcasted_iota(jnp.int32, (block, depth), 1) < depth // 2, 1.0, -1.0)
    for which in range(3):
        number = meta_ref[which]
        pick = pick_ref[block:, :] if which == 2 else pick_ref[:block, :]
        rows = dot(pick, all_ref[pl.ds(pl.multiple_of(number * block, block), block), :], (1, 0))
        weights = jnp.concatenate([rows, pltpu.roll(rows, depth // 2, 1) * sign], axis=0).astype(jnp.bfloat16)
        tile = dot(weights, everything, (1, 1))
        part = slice(which * block, (which + 1) * block)
        taper = taper_ref[part, :]
        re_ref[part, :] = tile[:block] * taper
        im_ref[part, :] = tile[block:] * taper
        lanes = pl.ds(pl.multiple_of(number // (LANES // block) * LANES, LANES), LANES)
        re_ref[part, lanes] += load_ref[part, :]

    def rows_at(start):
        return re_ref[start : start + GROUP, :], im_ref[start : start + GROUP, :]

    def keep(which, start, column):
        turn_ref[which, start : start + GROUP, :] = column[0].astype(jnp.bfloat16)
        turn_ref[which, block + start : block + start + GROUP, :] = column[1].astype(jnp.bfloat16)
        total = jnp.sum(column[0] * column[0] + column[1] * column[1], axis=1, keepdims=True)
        norm_ref[which, start : start + GROUP, :] = jnp.broadcast_to(1.0 / total, (GROUP, LANES))

    def respond(which, result_hbm):
        projected = dot(turn_ref[which], table_ref[...], (1, 0))
        z_re = projected[:block, :BEAMS] + projected[block:, BEAMS:]
        z_im = projected[block:, :BEAMS] - projected[:block, BEAMS:]
        inverse = jnp.concatenate([norm_ref[which]] * (BEAMS // LANES), axis=1)
        response_ref[which] = (z_re * z_re + z_im * z_im) * inverse
        copy = pltpu.make_async_copy(response_ref.at[which], result_hbm, semaphores.at[which])
        copy.start()
        return copy

    for at in range(0, half, GROUP):
        top, bottom = rotate_both(rows_at(at), rows_at(half + at))
        keep(0, at, top)
        keep(0, half + at, bottom)
    early_copy = respond(0, early_hbm)
    lower_side, upper_side = meta_ref[3], meta_ref[4]
    lower_sign = (2 * lower_side - 1).astype(jnp.float32)
    upper_sign = (2 * upper_side - 1).astype(jnp.float32)
    for at in range(0, half, GROUP):
        moved_top = rotate_side(rows_at(block + at), rows_at(block + half + at), lower_side, lower_sign)
        moved_bottom = rotate_side(rows_at(2 * block + at), rows_at(2 * block + half + at), upper_side, upper_sign)
        top, bottom = rotate_both(moved_top, moved_bottom)
        keep(1, at, top)
        keep(1, half + at, bottom)
    final_copy = respond(1, final_hbm)
    early_copy.wait()
    final_copy.wait()


def send_order(peers):
    return list(range(peers))[::-1]


def pinned(array):
    return pltpu.with_memory_space_constraint(array, pltpu.HBM)


def per_device(spectra, valid_mask, pairing, positions, wavenumber):
    blocks = lax.axis_size("sens")
    position = lax.axis_index("sens")
    block = valid_mask.shape[1]
    depth = spectra.shape[0]
    sensors = positions.shape[1]
    copies = pl.pallas_call(
        spread_kernel,
        out_shape=jax.ShapeDtypeStruct((blocks, block, depth), jnp.bfloat16),
        in_specs=[HBM, HBM],
        out_specs=VMEM,
        scratch_shapes=[
            pltpu.VMEM((block, depth), spectra.dtype),
            pltpu.VMEM(valid_mask.shape, valid_mask.dtype),
            pltpu.SemaphoreType.DMA((2,)),
        ],
        compiler_params=small(2),
        name="spread",
    )(pinned(spectra.T), pinned(valid_mask))
    order = send_order(blocks)
    numbers = [
        position,
        jnp.maximum(position - 1, 0),
        jnp.minimum(position + 1, blocks - 1),
        position == 1,
        position < blocks - 1,
    ]
    meta = jnp.stack([jnp.asarray(number, jnp.int32) for number in numbers])
    prepared = pl.pallas_call(
        functools.partial(prepare_kernel, block),
        out_shape=(
            jax.ShapeDtypeStruct((sensors, 2 * BEAMS), jnp.bfloat16),
            jax.ShapeDtypeStruct((3 * block, sensors), jnp.float32),
            jax.ShapeDtypeStruct((3 * block, LANES), jnp.float32),
            jax.ShapeDtypeStruct((2 * block, block), jnp.bfloat16),
        ),
        in_specs=[SMEM, SMEM, HBM, HBM],
        out_specs=(VMEM, VMEM, VMEM, VMEM),
        scratch_shapes=[
            pltpu.SMEM(pairing.shape, pairing.dtype),
            pltpu.VMEM(positions.shape, positions.dtype),
            pltpu.SemaphoreType.DMA((2,)),
        ],
        compiler_params=small(4),
        name="prepare",
    )(meta, wavenumber, pinned(pairing), pinned(positions))
    gathered = lax.all_to_all(copies, "sens", split_axis=0, concat_axis=0, axis_index_groups=[order])
    out = jax.ShapeDtypeStruct((block, BEAMS), jnp.float32)
    return pl.pallas_call(
        functools.partial(respond_kernel, order),
        out_shape=(out, out),
        in_specs=[SMEM, VMEM, VMEM, VMEM, VMEM, VMEM],
        out_specs=(HBM, HBM),
        scratch_shapes=[
            pltpu.VMEM((sensors, depth), jnp.bfloat16),
            pltpu.VMEM((3 * block, sensors), jnp.float32),
            pltpu.VMEM((3 * block, sensors), jnp.float32),
            pltpu.VMEM((2, 2 * block, sensors), jnp.bfloat16),
            pltpu.VMEM((2, block, LANES), jnp.float32),
            pltpu.VMEM((2, block, BEAMS), jnp.float32),
            pltpu.SemaphoreType.DMA((2,)),
        ],
        compiler_params=small(4 + sensors * block // 2**13),
        name="respond",
    )(meta, gathered, *prepared)


def solution(mesh):
    in_specs = (P("bin", "sens"), P(None, "sens"), P(), P(), P("bin"))
    out_specs = (P("sens", "bin"), P("sens", "bin"))
    return jax.shard_map(
        per_device, mesh=mesh, in_specs=in_specs, out_specs=out_specs, check_vma=False
    )
```

```python
import functools
import math

import jax
import jax.numpy as jnp
from jax import lax
from jax.experimental import pallas as pl
from jax.experimental.pallas import tpu as pltpu
from jax.sharding import PartitionSpec as P

BEAMS = 256
LOAD = 0.5
LANES = 128
ROWS = 8
GROUP = 16
VMEM = pl.BlockSpec(memory_space=pltpu.VMEM)
SMEM = pl.BlockSpec(memory_space=pltpu.SMEM)
HBM = pl.BlockSpec(memory_space=pltpu.HBM)

COS = (0.99999921, -19.73898036, 64.92865742, -85.27162153, 58.79049212, -21.07110563)
SIN = (6.28318492, -41.34158923, 81.59994333, -76.61447253, 41.34288235, -12.47124354)
SIN_FINE = (6.2831853, -41.34170041, 81.60513139, -76.70301535, 42.02592699, -14.89984667, 3.23813751)


def small(mebibytes):
    return pltpu.CompilerParams(vmem_limit_bytes=mebibytes * 2**20)


def fetch(pairs, semaphores):
    copies = [pltpu.make_async_copy(*pair, semaphores.at[i]) for i, pair in enumerate(pairs)]
    for copy in copies:
        copy.start()
    for copy in copies:
        copy.wait()


def horner(coefficients, at):
    value = coefficients[-1]
    for coefficient in coefficients[-2::-1]:
        value = value * at + coefficient
    return value


def dot(left, right, contract):
    return lax.dot_general(left, right, ((contract[:1], contract[1:]), ((), ())), preferred_element_type=jnp.float32)


def spread_kernel(spectra_hbm, mask_hbm, copies_ref, spectra_ref, mask_ref, semaphores):
    fetch(((spectra_hbm, spectra_ref), (mask_hbm, mask_ref)), semaphores)
    segments, block = mask_ref.shape
    depth = spectra_ref.shape[1]
    row = lax.broadcasted_iota(jnp.int32, (segments, depth), 0)
    lane = lax.broadcasted_iota(jnp.int32, (segments, depth), 1)
    twice = jnp.where((row == lane) | (row + segments == lane), 1.0, 0.0).astype(jnp.bfloat16)
    validity = dot(mask_ref[...].astype(jnp.float32).astype(jnp.bfloat16), twice, (0, 0))
    counts = 0.5 * jnp.sum(validity, axis=1, keepdims=True)
    scaled = (spectra_ref[...].astype(jnp.float32) * validity * (1.0 / jnp.sqrt(counts))).astype(jnp.bfloat16)
    for peer in range(copies_ref.shape[0]):
        copies_ref[peer] = scaled


def prepare_kernel(
    block, meta_ref, wavenumber_ref, pairing_hbm, positions_hbm, table_ref, taper_ref, load_ref, pick_ref,
    pairing_ref, positions_ref, semaphores
):
    fetch(((pairing_hbm, pairing_ref), (positions_hbm, positions_ref)), semaphores)
    sensors = positions_ref.shape[1]
    half = block // 2
    width = 3.0 / block

    beam = lax.broadcasted_iota(jnp.int32, (ROWS, BEAMS), 1).astype(jnp.float32)
    turns = (beam + 0.5) * (0.5 / BEAMS)
    square = turns * turns
    cos_beam = horner(COS_FINE, square)
    sin_beam = turns * horner(SIN_FINE, square)
    scale = wavenumber_ref[0] * (0.5 / math.pi)
    for at in range(0, sensors, LANES):
        along, side = (
            jnp.transpose(jnp.broadcast_to(positions_ref[axis : axis + 1, at : at + LANES] * scale, (LANES, LANES)))
            for axis in (0, 1)
        )
        for row in range(0, LANES, GROUP):
            for lane in range(0, BEAMS, LANES):
                cos_part = cos_beam[:1, lane : lane + LANES]
                sin_part = sin_beam[:1, lane : lane + LANES]
                phase = along[row : row + GROUP] * cos_part + side[row : row + GROUP] * sin_part
                phase = phase - jnp.round(phase)
                square = phase * phase
                rows = slice(at + row, at + row + GROUP)
                table_ref[rows, lane : lane + LANES] = horner(COS, square).astype(jnp.bfloat16)
                table_ref[rows, BEAMS + lane : BEAMS + lane + LANES] = (phase * horner(SIN, square)).astype(jnp.bfloat16)

    sub = lax.broadcasted_iota(jnp.int32, (ROWS, LANES), 0)
    lane = lax.broadcasted_iota(jnp.int32, (ROWS, LANES), 1)

    def column(numbers):
        value = jnp.zeros((ROWS, LANES), jnp.int32)
        for i, number in enumerate(numbers):
            value = jnp.where(sub == i, number, value)
        return value

    order, later = [], []
    for at in range(0, half, ROWS):
        order.append(sub + at)
        later.append(column([pairing_ref[1, at + i] for i in range(ROWS)]))
    for at in range(0, half, ROWS):
        order.append(column([half + pairing_ref[0, at + i] for i in range(ROWS)]))
        later.append(column([half + pairing_ref[0, pairing_ref[1, at + i]] for i in range(ROWS)]))
    for which, rows in enumerate((order, later)):
        for at in range(0, len(rows), 2):
            pair = jnp.concatenate(rows[at : at + 2], axis=0)
            lanes = jnp.concatenate([lane, lane], axis=0)
            start = which * block + at * ROWS
            pick_ref[start : start + GROUP, :] = jnp.where(pair == lanes, 1.0, 0.0)[:, :block].astype(jnp.bfloat16)

    for which, rows in enumerate((order, order, later)):
        number = meta_ref[which]
        chunk = number // (LANES // block)
        shift = (number - chunk * (LANES // block)) * block
        for at, row in enumerate(rows):
            start = which * block + at * ROWS
            hit = row + shift == lane
            load_ref[start : start + ROWS, :] = jnp.where(hit, LOAD, 0.0)
            near = positions_ref[:, pl.ds(pl.multiple_of(chunk * LANES, LANES), LANES)]
            own_along = jnp.sum(jnp.where(hit, near[0:1], 0.0), axis=1, keepdims=True)
            own_side = jnp.sum(jnp.where(hit, near[1:2], 0.0), axis=1, keepdims=True)
            for to in range(0, sensors, LANES):
                delta_along = own_along - positions_ref[0:1, to : to + LANES]
                delta_side = own_side - positions_ref[1:2, to : to + LANES]
                square = jnp.maximum(delta_along * delta_along + delta_side * delta_side, 1e-30)
                inverse = lax.rsqrt(square)
                turn = (square * inverse) * (0.5 * width / math.pi)
                turn = turn - jnp.round(turn)
                value = turn * horner(SIN_FINE, turn * turn) * (inverse * (1.0 / width))
                taper_ref[start : start + ROWS, to : to + LANES] = value


COS_FINE = (0.99999999, -19.7392045, 64.93911746, -85.45013953, 60.16763095, -25.96759925, 6.52865816)


def sums(left, right):
    left_re, left_im = left
    right_re, right_im = right
    norm_left = jnp.sum(left_re * left_re + left_im * left_im, axis=1, keepdims=True)
    norm_right = jnp.sum(right_re * right_re + right_im * right_im, axis=1, keepdims=True)
    gamma_re = jnp.sum(left_re * right_re + left_im * right_im, axis=1, keepdims=True)
    gamma_im = jnp.sum(left_re * right_im - left_im * right_re, axis=1, keepdims=True)
    spread = norm_right - norm_left
    radius = jnp.sqrt(spread * spread + 4.0 * (gamma_re * gamma_re + gamma_im * gamma_im) + 1e-30)
    leading = jnp.sqrt((radius + jnp.abs(spread)) / (2.0 * radius))
    factor = 1.0 / (radius * leading)
    return spread >= 0.0, leading, factor * gamma_re, factor * gamma_im


def rotate_side(left, right, side, sign):
    rising, leading, b_re, b_im = sums(left, right)
    plain = jnp.where(rising, 1, 0) != side
    left_re = jnp.where(plain, leading, b_re)
    left_im = jnp.where(plain, 0.0, b_im)
    right_re = sign * jnp.where(plain, b_re, leading)
    right_im = sign * jnp.where(plain, -b_im, 0.0)
    return (
        left_re * left[0] - left_im * left[1] + right_re * right[0] - right_im * right[1],
        left_re * left[1] + left_im * left[0] + right_re * right[1] + right_im * right[0],
    )


def rotate_both(left, right):
    rising, leading, b_re, b_im = sums(left, right)
    zero = jnp.zeros_like(b_im)

    def combine(left_re, left_im, right_re, right_im):
        return (
            left_re * left[0] - left_im * left[1] + right_re * right[0] - right_im * right[1],
            left_re * left[1] + left_im * left[0] + right_re * right[1] + right_im * right[0],
        )

    new_left = combine(
        jnp.where(rising, leading, b_re),
        jnp.where(rising, zero, b_im),
        jnp.where(rising, -b_re, -leading),
        jnp.where(rising, b_im, zero),
    )
    new_right = combine(
        jnp.where(rising, b_re, leading),
        jnp.where(rising, b_im, zero),
        jnp.where(rising, leading, b_re),
        jnp.where(rising, zero, -b_im),
    )
    return new_left, new_right


def respond_kernel(
    order, meta_ref, blocks_ref, table_ref, taper_ref, load_ref, pick_ref, early_hbm, final_hbm, all_ref, re_ref, im_ref, turn_ref, norm_ref, response_ref, semaphores
):
    block, depth = blocks_ref.shape[1:]
    half = block // 2
    for at, source in enumerate(order):
        all_ref[source * block : (source + 1) * block, :] = blocks_ref[at]
    everything = all_ref[...]
    sign = jnp.where(lax.broadcasted_iota(jnp.int32, (block, depth), 1) < depth // 2, 1.0, -1.0)
    for which in range(3):
        number = meta_ref[which]
        pick = pick_ref[block:, :] if which == 2 else pick_ref[:block, :]
        rows = dot(pick, all_ref[pl.ds(pl.multiple_of(number * block, block), block), :], (1, 0))
        weights = jnp.concatenate([rows, pltpu.roll(rows, depth // 2, 1) * sign], axis=0).astype(jnp.bfloat16)
        tile = dot(weights, everything, (1, 1))
        part = slice(which * block, (which + 1) * block)
        taper = taper_ref[part, :]
        re_ref[part, :] = tile[:block] * taper
        im_ref[part, :] = tile[block:] * taper
        lanes = pl.ds(pl.multiple_of(number // (LANES // block) * LANES, LANES), LANES)
        re_ref[part, lanes] += load_ref[part, :]

    def rows_at(start):
        return re_ref[start : start + GROUP, :], im_ref[start : start + GROUP, :]

    def keep(which, start, column):
        turn_ref[which, start : start + GROUP, :] = column[0].astype(jnp.bfloat16)
        turn_ref[which, block + start : block + start + GROUP, :] = column[1].astype(jnp.bfloat16)
        total = jnp.sum(column[0] * column[0] + column[1] * column[1], axis=1, keepdims=True)
        norm_ref[which, start : start + GROUP, :] = jnp.broadcast_to(1.0 / total, (GROUP, LANES))

    def respond(which, result_hbm):
        projected = dot(turn_ref[which], table_ref[...], (1, 0))
        z_re = projected[:block, :BEAMS] + projected[block:, BEAMS:]
        z_im = projected[block:, :BEAMS] - projected[:block, BEAMS:]
        inverse = jnp.concatenate([norm_ref[which]] * (BEAMS // LANES), axis=1)
        response_ref[which] = (z_re * z_re + z_im * z_im) * inverse
        copy = pltpu.make_async_copy(response_ref.at[which], result_hbm, semaphores.at[which])
        copy.start()
        return copy

    for at in range(0, half, GROUP):
        top, bottom = rotate_both(rows_at(at), rows_at(half + at))
        keep(0, at, top)
        keep(0, half + at, bottom)
    early_copy = respond(0, early_hbm)
    lower_side, upper_side = meta_ref[3], meta_ref[4]
    lower_sign = (2 * lower_side - 1).astype(jnp.float32)
    upper_sign = (2 * upper_side - 1).astype(jnp.float32)
    for at in range(0, half, GROUP):
        moved_top = rotate_side(rows_at(block + at), rows_at(block + half + at), lower_side, lower_sign)
        moved_bottom = rotate_side(rows_at(2 * block + at), rows_at(2 * block + half + at), upper_side, upper_sign)
        top, bottom = rotate_both(moved_top, moved_bottom)
        keep(1, at, top)
        keep(1, half + at, bottom)
    final_copy = respond(1, final_hbm)
    early_copy.wait()
    final_copy.wait()


def send_order(peers):
    return [peers - 1 - at // 2 if at % 2 == 0 else at // 2 for at in range(peers)]


def pinned(array):
    return pltpu.with_memory_space_constraint(array, pltpu.HBM)


def per_device(spectra, valid_mask, pairing, positions, wavenumber):
    blocks = lax.axis_size("sens")
    position = lax.axis_index("sens")
    block = valid_mask.shape[1]
    depth = spectra.shape[0]
    sensors = positions.shape[1]
    copies = pl.pallas_call(
        spread_kernel,
        out_shape=jax.ShapeDtypeStruct((blocks, block, depth), jnp.bfloat16),
        in_specs=[HBM, HBM],
        out_specs=VMEM,
        scratch_shapes=[
            pltpu.VMEM((block, depth), spectra.dtype),
            pltpu.VMEM(valid_mask.shape, valid_mask.dtype),
            pltpu.SemaphoreType.DMA((2,)),
        ],
        compiler_params=small(2),
        name="spread",
    )(pinned(spectra.T), pinned(valid_mask))
    order = send_order(blocks)
    numbers = [
        position,
        jnp.maximum(position - 1, 0),
        jnp.minimum(position + 1, blocks - 1),
        position == 1,
        position < blocks - 1,
    ]
    meta = jnp.stack([jnp.asarray(number, jnp.int32) for number in numbers])
    prepared = pl.pallas_call(
        functools.partial(prepare_kernel, block),
        out_shape=(
            jax.ShapeDtypeStruct((sensors, 2 * BEAMS), jnp.bfloat16),
            jax.ShapeDtypeStruct((3 * block, sensors), jnp.float32),
            jax.ShapeDtypeStruct((3 * block, LANES), jnp.float32),
            jax.ShapeDtypeStruct((2 * block, block), jnp.bfloat16),
        ),
        in_specs=[SMEM, SMEM, HBM, HBM],
        out_specs=(VMEM, VMEM, VMEM, VMEM),
        scratch_shapes=[
            pltpu.SMEM(pairing.shape, pairing.dtype),
            pltpu.VMEM(positions.shape, positions.dtype),
            pltpu.SemaphoreType.DMA((2,)),
        ],
        compiler_params=small(4),
        name="prepare",
    )(meta, wavenumber, pinned(pairing), pinned(positions))
    gathered = lax.all_to_all(copies, "sens", split_axis=0, concat_axis=0, axis_index_groups=[order])
    out = jax.ShapeDtypeStruct((block, BEAMS), jnp.float32)
    return pl.pallas_call(
        functools.partial(respond_kernel, order),
        out_shape=(out, out),
        in_specs=[SMEM, VMEM, VMEM, VMEM, VMEM, VMEM],
        out_specs=(HBM, HBM),
        scratch_shapes=[
            pltpu.VMEM((sensors, depth), jnp.bfloat16),
            pltpu.VMEM((3 * block, sensors), jnp.float32),
            pltpu.VMEM((3 * block, sensors), jnp.float32),
            pltpu.VMEM((2, 2 * block, sensors), jnp.bfloat16),
            pltpu.VMEM((2, block, LANES), jnp.float32),
            pltpu.VMEM((2, block, BEAMS), jnp.float32),
            pltpu.SemaphoreType.DMA((2,)),
        ],
        compiler_params=small(4 + sensors * block // 2**13),
        name="respond",
    )(meta, gathered, *prepared)


def solution(mesh):
    in_specs = (P("bin", "sens"), P(None, "sens"), P(), P(), P("bin"))
    out_specs = (P("sens", "bin"), P("sens", "bin"))
    return jax.shard_map(
        per_device, mesh=mesh, in_specs=in_specs, out_specs=out_specs, check_vma=False
    )
```

```python
import functools
import math

import jax
import jax.numpy as jnp
from jax import lax
from jax.experimental import pallas as pl
from jax.experimental.pallas import tpu as pltpu
from jax.sharding import PartitionSpec as P

BEAMS = 256
LOAD = 0.5
LANES = 128
ROWS = 8
GROUP = 16
VMEM = pl.BlockSpec(memory_space=pltpu.VMEM)
SMEM = pl.BlockSpec(memory_space=pltpu.SMEM)
HBM = pl.BlockSpec(memory_space=pltpu.HBM)

COS = (0.99999921, -19.73898036, 64.92865742, -85.27162153, 58.79049212, -21.07110563)
SIN = (6.28318492, -41.34158923, 81.59994333, -76.61447253, 41.34288235, -12.47124354)
SIN_FINE = (6.2831853, -41.34170041, 81.60513139, -76.70301535, 42.02592699, -14.89984667, 3.23813751)


def small(mebibytes):
    return pltpu.CompilerParams(vmem_limit_bytes=mebibytes * 2**20)


def fetch(pairs, semaphores):
    copies = [pltpu.make_async_copy(*pair, semaphores.at[i]) for i, pair in enumerate(pairs)]
    for copy in copies:
        copy.start()
    for copy in copies:
        copy.wait()


def horner(coefficients, at):
    value = coefficients[-1]
    for coefficient in coefficients[-2::-1]:
        value = value * at + coefficient
    return value


def dot(left, right, contract):
    return lax.dot_general(left, right, ((contract[:1], contract[1:]), ((), ())), preferred_element_type=jnp.float32)


def spread_kernel(spectra_hbm, mask_hbm, copies_ref, spectra_ref, mask_ref, semaphores):
    fetch(((spectra_hbm, spectra_ref), (mask_hbm, mask_ref)), semaphores)
    segments, block = mask_ref.shape
    depth = spectra_ref.shape[1]
    row = lax.broadcasted_iota(jnp.int32, (segments, depth), 0)
    lane = lax.broadcasted_iota(jnp.int32, (segments, depth), 1)
    twice = jnp.where((row == lane) | (row + segments == lane), 1.0, 0.0).astype(jnp.bfloat16)
    validity = dot(mask_ref[...].astype(jnp.float32).astype(jnp.bfloat16), twice, (0, 0))
    counts = 0.5 * jnp.sum(validity, axis=1, keepdims=True)
    scaled = (spectra_ref[...].astype(jnp.float32) * validity * (1.0 / jnp.sqrt(counts))).astype(jnp.bfloat16)
    for peer in range(copies_ref.shape[0]):
        copies_ref[peer] = scaled


def prepare_kernel(
    block, meta_ref, wavenumber_ref, pairing_hbm, positions_hbm, table_ref, taper_ref, load_ref, pick_ref,
    pairing_ref, positions_ref, semaphores
):
    fetch(((pairing_hbm, pairing_ref), (positions_hbm, positions_ref)), semaphores)
    sensors = positions_ref.shape[1]
    half = block // 2
    width = 3.0 / block

    beam = lax.broadcasted_iota(jnp.int32, (ROWS, BEAMS), 1).astype(jnp.float32)
    turns = (beam + 0.5) * (0.5 / BEAMS)
    square = turns * turns
    cos_beam = horner(COS_FINE, square)
    sin_beam = turns * horner(SIN_FINE, square)
    scale = wavenumber_ref[0] * (0.5 / math.pi)
    for at in range(0, sensors, LANES):
        along, side = (
            jnp.transpose(jnp.broadcast_to(positions_ref[axis : axis + 1, at : at + LANES] * scale, (LANES, LANES)))
            for axis in (0, 1)
        )
        for row in range(0, LANES, GROUP):
            for lane in range(0, BEAMS, LANES):
                cos_part = cos_beam[:1, lane : lane + LANES]
                sin_part = sin_beam[:1, lane : lane + LANES]
                phase = along[row : row + GROUP] * cos_part + side[row : row + GROUP] * sin_part
                phase = phase - jnp.round(phase)
                square = phase * phase
                rows = slice(at + row, at + row + GROUP)
                table_ref[rows, lane : lane + LANES] = horner(COS, square).astype(jnp.bfloat16)
                table_ref[rows, BEAMS + lane : BEAMS + lane + LANES] = (phase * horner(SIN, square)).astype(jnp.bfloat16)

    sub = lax.broadcasted_iota(jnp.int32, (ROWS, LANES), 0)
    lane = lax.broadcasted_iota(jnp.int32, (ROWS, LANES), 1)

    def column(numbers):
        value = jnp.zeros((ROWS, LANES), jnp.int32)
        for i, number in enumerate(numbers):
            value = jnp.where(sub == i, number, value)
        return value

    order, later = [], []
    for at in range(0, half, ROWS):
        order.append(sub + at)
        later.append(column([pairing_ref[1, at + i] for i in range(ROWS)]))
    for at in range(0, half, ROWS):
        order.append(column([half + pairing_ref[0, at + i] for i in range(ROWS)]))
        later.append(column([half + pairing_ref[0, pairing_ref[1, at + i]] for i in range(ROWS)]))
    for which, rows in enumerate((order, later)):
        for at in range(0, len(rows), 2):
            pair = jnp.concatenate(rows[at : at + 2], axis=0)
            lanes = jnp.concatenate([lane, lane], axis=0)
            start = which * block + at * ROWS
            pick_ref[start : start + GROUP, :] = jnp.where(pair == lanes, 1.0, 0.0)[:, :block].astype(jnp.bfloat16)

    for which, rows in enumerate((order, order, later)):
        number = meta_ref[which]
        chunk = number // (LANES // block)
        shift = (number - chunk * (LANES // block)) * block
        for at, row in enumerate(rows):
            start = which * block + at * ROWS
            hit = row + shift == lane
            load_ref[start : start + ROWS, :] = jnp.where(hit, LOAD, 0.0)
            near = positions_ref[:, pl.ds(pl.multiple_of(chunk * LANES, LANES), LANES)]
            own_along = jnp.sum(jnp.where(hit, near[0:1], 0.0), axis=1, keepdims=True)
            own_side = jnp.sum(jnp.where(hit, near[1:2], 0.0), axis=1, keepdims=True)
            for to in range(0, sensors, LANES):
                delta_along = own_along - positions_ref[0:1, to : to + LANES]
                delta_side = own_side - positions_ref[1:2, to : to + LANES]
                square = jnp.maximum(delta_along * delta_along + delta_side * delta_side, 1e-30)
                inverse = lax.rsqrt(square)
                turn = (square * inverse) * (0.5 * width / math.pi)
                turn = turn - jnp.round(turn)
                value = turn * horner(SIN_FINE, turn * turn) * (inverse * (1.0 / width))
                taper_ref[start : start + ROWS, to : to + LANES] = value


COS_FINE = (0.99999999, -19.7392045, 64.93911746, -85.45013953, 60.16763095, -25.96759925, 6.52865816)


def sums(left, right):
    left_re, left_im = left
    right_re, right_im = right
    norm_left = jnp.sum(left_re * left_re + left_im * left_im, axis=1, keepdims=True)
    norm_right = jnp.sum(right_re * right_re + right_im * right_im, axis=1, keepdims=True)
    gamma_re = jnp.sum(left_re * right_re + left_im * right_im, axis=1, keepdims=True)
    gamma_im = jnp.sum(left_re * right_im - left_im * right_re, axis=1, keepdims=True)
    spread = norm_right - norm_left
    radius = jnp.sqrt(spread * spread + 4.0 * (gamma_re * gamma_re + gamma_im * gamma_im) + 1e-30)
    leading = jnp.sqrt((radius + jnp.abs(spread)) / (2.0 * radius))
    factor = 1.0 / (radius * leading)
    return spread >= 0.0, leading, factor * gamma_re, factor * gamma_im


def rotate_side(left, right, side, sign):
    rising, leading, b_re, b_im = sums(left, right)
    plain = jnp.where(rising, 1, 0) != side
    left_re = jnp.where(plain, leading, b_re)
    left_im = jnp.where(plain, 0.0, b_im)
    right_re = sign * jnp.where(plain, b_re, leading)
    right_im = sign * jnp.where(plain, -b_im, 0.0)
    return (
        left_re * left[0] - left_im * left[1] + right_re * right[0] - right_im * right[1],
        left_re * left[1] + left_im * left[0] + right_re * right[1] + right_im * right[0],
    )


def rotate_both(left, right):
    rising, leading, b_re, b_im = sums(left, right)
    zero = jnp.zeros_like(b_im)

    def combine(left_re, left_im, right_re, right_im):
        return (
            left_re * left[0] - left_im * left[1] + right_re * right[0] - right_im * right[1],
            left_re * left[1] + left_im * left[0] + right_re * right[1] + right_im * right[0],
        )

    new_left = combine(
        jnp.where(rising, leading, b_re),
        jnp.where(rising, zero, b_im),
        jnp.where(rising, -b_re, -leading),
        jnp.where(rising, b_im, zero),
    )
    new_right = combine(
        jnp.where(rising, b_re, leading),
        jnp.where(rising, b_im, zero),
        jnp.where(rising, leading, b_re),
        jnp.where(rising, zero, -b_im),
    )
    return new_left, new_right


def respond_kernel(
    order, meta_ref, blocks_ref, table_ref, taper_ref, load_ref, pick_ref, early_hbm, final_hbm, all_ref, re_ref, im_ref, turn_ref, norm_ref, response_ref, semaphores
):
    block, depth = blocks_ref.shape[1:]
    half = block // 2
    for at, source in enumerate(order):
        all_ref[source * block : (source + 1) * block, :] = blocks_ref[at]
    everything = all_ref[...]
    sign = jnp.where(lax.broadcasted_iota(jnp.int32, (block, depth), 1) < depth // 2, 1.0, -1.0)
    for which in range(3):
        number = meta_ref[which]
        pick = pick_ref[block:, :] if which == 2 else pick_ref[:block, :]
        rows = dot(pick, all_ref[pl.ds(pl.multiple_of(number * block, block), block), :], (1, 0))
        weights = jnp.concatenate([rows, pltpu.roll(rows, depth // 2, 1) * sign], axis=0).astype(jnp.bfloat16)
        tile = dot(weights, everything, (1, 1))
        part = slice(which * block, (which + 1) * block)
        taper = taper_ref[part, :]
        re_ref[part, :] = tile[:block] * taper
        im_ref[part, :] = tile[block:] * taper
        lanes = pl.ds(pl.multiple_of(number // (LANES // block) * LANES, LANES), LANES)
        re_ref[part, lanes] += load_ref[part, :]

    def rows_at(start):
        return re_ref[start : start + GROUP, :], im_ref[start : start + GROUP, :]

    def keep(which, start, column):
        turn_ref[which, start : start + GROUP, :] = column[0].astype(jnp.bfloat16)
        turn_ref[which, block + start : block + start + GROUP, :] = column[1].astype(jnp.bfloat16)
        total = jnp.sum(column[0] * column[0] + column[1] * column[1], axis=1, keepdims=True)
        norm_ref[which, start : start + GROUP, :] = jnp.broadcast_to(1.0 / total, (GROUP, LANES))

    def respond(which, result_hbm):
        projected = dot(turn_ref[which], table_ref[...], (1, 0))
        z_re = projected[:block, :BEAMS] + projected[block:, BEAMS:]
        z_im = projected[block:, :BEAMS] - projected[:block, BEAMS:]
        inverse = jnp.concatenate([norm_ref[which]] * (BEAMS // LANES), axis=1)
        response_ref[which] = (z_re * z_re + z_im * z_im) * inverse
        copy = pltpu.make_async_copy(response_ref.at[which], result_hbm, semaphores.at[which])
        copy.start()
        return copy

    for at in range(0, half, GROUP):
        top, bottom = rotate_both(rows_at(at), rows_at(half + at))
        keep(0, at, top)
        keep(0, half + at, bottom)
    early_copy = respond(0, early_hbm)
    lower_side, upper_side = meta_ref[3], meta_ref[4]
    lower_sign = (2 * lower_side - 1).astype(jnp.float32)
    upper_sign = (2 * upper_side - 1).astype(jnp.float32)
    for at in range(0, half, GROUP):
        moved_top = rotate_side(rows_at(block + at), rows_at(block + half + at), lower_side, lower_sign)
        moved_bottom = rotate_side(rows_at(2 * block + at), rows_at(2 * block + half + at), upper_side, upper_sign)
        top, bottom = rotate_both(moved_top, moved_bottom)
        keep(1, at, top)
        keep(1, half + at, bottom)
    final_copy = respond(1, final_hbm)
    early_copy.wait()
    final_copy.wait()


def send_order(peers):
    ends = [at // 2 if at % 2 == 0 else peers - 1 - at // 2 for at in range(peers)]
    return [peers // 2] + [peer for peer in ends if peer != peers // 2]


def pinned(array):
    return pltpu.with_memory_space_constraint(array, pltpu.HBM)


def per_device(spectra, valid_mask, pairing, positions, wavenumber):
    blocks = lax.axis_size("sens")
    position = lax.axis_index("sens")
    block = valid_mask.shape[1]
    depth = spectra.shape[0]
    sensors = positions.shape[1]
    copies = pl.pallas_call(
        spread_kernel,
        out_shape=pltpu.VMEM((blocks, block, depth), jnp.bfloat16),
        in_specs=[HBM, HBM],
        out_specs=VMEM,
        scratch_shapes=[
            pltpu.VMEM((block, depth), spectra.dtype),
            pltpu.VMEM(valid_mask.shape, valid_mask.dtype),
            pltpu.SemaphoreType.DMA((2,)),
        ],
        compiler_params=small(2),
        name="spread",
    )(pinned(spectra.T), pinned(valid_mask))
    order = send_order(blocks)
    numbers = [
        position,
        jnp.maximum(position - 1, 0),
        jnp.minimum(position + 1, blocks - 1),
        position == 1,
        position < blocks - 1,
    ]
    meta = jnp.stack([jnp.asarray(number, jnp.int32) for number in numbers])
    prepared = pl.pallas_call(
        functools.partial(prepare_kernel, block),
        out_shape=(
            jax.ShapeDtypeStruct((sensors, 2 * BEAMS), jnp.bfloat16),
            jax.ShapeDtypeStruct((3 * block, sensors), jnp.float32),
            jax.ShapeDtypeStruct((3 * block, LANES), jnp.float32),
            jax.ShapeDtypeStruct((2 * block, block), jnp.bfloat16),
        ),
        in_specs=[SMEM, SMEM, HBM, HBM],
        out_specs=(VMEM, VMEM, VMEM, VMEM),
        scratch_shapes=[
            pltpu.SMEM(pairing.shape, pairing.dtype),
            pltpu.VMEM(positions.shape, positions.dtype),
            pltpu.SemaphoreType.DMA((2,)),
        ],
        compiler_params=small(4),
        name="prepare",
    )(meta, wavenumber, pinned(pairing), pinned(positions))
    gathered = lax.all_to_all(copies, "sens", split_axis=0, concat_axis=0, axis_index_groups=[order])
    out = jax.ShapeDtypeStruct((block, BEAMS), jnp.float32)
    return pl.pallas_call(
        functools.partial(respond_kernel, order),
        out_shape=(out, out),
        in_specs=[SMEM, VMEM, VMEM, VMEM, VMEM, VMEM],
        out_specs=(HBM, HBM),
        scratch_shapes=[
            pltpu.VMEM((sensors, depth), jnp.bfloat16),
            pltpu.VMEM((3 * block, sensors), jnp.float32),
            pltpu.VMEM((3 * block, sensors), jnp.float32),
            pltpu.VMEM((2, 2 * block, sensors), jnp.bfloat16),
            pltpu.VMEM((2, block, LANES), jnp.float32),
            pltpu.VMEM((2, block, BEAMS), jnp.float32),
            pltpu.SemaphoreType.DMA((2,)),
        ],
        compiler_params=small(4 + sensors * block // 2**13),
        name="respond",
    )(meta, gathered, *prepared)


def solution(mesh):
    in_specs = (P("bin", "sens"), P(None, "sens"), P(), P(), P("bin"))
    out_specs = (P("sens", "bin"), P("sens", "bin"))
    return jax.shard_map(
        per_device, mesh=mesh, in_specs=in_specs, out_specs=out_specs, check_vma=False
    )
```

```python
import functools
import math

import jax
import jax.numpy as jnp
from jax import lax
from jax.experimental import pallas as pl
from jax.experimental.pallas import tpu as pltpu
from jax.sharding import PartitionSpec as P

BEAMS = 256
LOAD = 0.5
LANES = 128
ROWS = 8
GROUP = 16
VMEM = pl.BlockSpec(memory_space=pltpu.VMEM)
SMEM = pl.BlockSpec(memory_space=pltpu.SMEM)
HBM = pl.BlockSpec(memory_space=pltpu.HBM)

COS = (0.99999921, -19.73898036, 64.92865742, -85.27162153, 58.79049212, -21.07110563)
SIN = (6.28318492, -41.34158923, 81.59994333, -76.61447253, 41.34288235, -12.47124354)
SIN_FINE = (6.2831853, -41.34170041, 81.60513139, -76.70301535, 42.02592699, -14.89984667, 3.23813751)


def small(mebibytes):
    return pltpu.CompilerParams(vmem_limit_bytes=mebibytes * 2**20)


def fetch(pairs, semaphores):
    copies = [pltpu.make_async_copy(*pair, semaphores.at[i]) for i, pair in enumerate(pairs)]
    for copy in copies:
        copy.start()
    for copy in copies:
        copy.wait()


def horner(coefficients, at):
    value = coefficients[-1]
    for coefficient in coefficients[-2::-1]:
        value = value * at + coefficient
    return value


def dot(left, right, contract):
    return lax.dot_general(left, right, ((contract[:1], contract[1:]), ((), ())), preferred_element_type=jnp.float32)


def spread_kernel(spectra_hbm, mask_hbm, copies_ref, spectra_ref, mask_ref, semaphores):
    fetch(((spectra_hbm, spectra_ref), (mask_hbm, mask_ref)), semaphores)
    segments, block = mask_ref.shape
    depth = spectra_ref.shape[1]
    row = lax.broadcasted_iota(jnp.int32, (segments, depth), 0)
    lane = lax.broadcasted_iota(jnp.int32, (segments, depth), 1)
    twice = jnp.where((row == lane) | (row + segments == lane), 1.0, 0.0).astype(jnp.bfloat16)
    validity = dot(mask_ref[...].astype(jnp.float32).astype(jnp.bfloat16), twice, (0, 0))
    counts = 0.5 * jnp.sum(validity, axis=1, keepdims=True)
    scaled = (spectra_ref[...].astype(jnp.float32) * validity * (1.0 / jnp.sqrt(counts))).astype(jnp.bfloat16)
    for peer in range(copies_ref.shape[0]):
        copies_ref[peer] = scaled


def prepare_kernel(
    block, meta_ref, wavenumber_ref, pairing_hbm, positions_hbm, table_ref, taper_ref, load_ref, pick_ref,
    pairing_ref, positions_ref, semaphores
):
    fetch(((pairing_hbm, pairing_ref), (positions_hbm, positions_ref)), semaphores)
    sensors = positions_ref.shape[1]
    half = block // 2
    width = 3.0 / block

    beam = lax.broadcasted_iota(jnp.int32, (ROWS, BEAMS), 1).astype(jnp.float32)
    turns = (beam + 0.5) * (0.5 / BEAMS)
    square = turns * turns
    cos_beam = horner(COS_FINE, square)
    sin_beam = turns * horner(SIN_FINE, square)
    scale = wavenumber_ref[0] * (0.5 / math.pi)
    for at in range(0, sensors, LANES):
        along, side = (
            jnp.transpose(jnp.broadcast_to(positions_ref[axis : axis + 1, at : at + LANES] * scale, (LANES, LANES)))
            for axis in (0, 1)
        )
        for row in range(0, LANES, GROUP):
            for lane in range(0, BEAMS, LANES):
                cos_part = cos_beam[:1, lane : lane + LANES]
                sin_part = sin_beam[:1, lane : lane + LANES]
                phase = along[row : row + GROUP] * cos_part + side[row : row + GROUP] * sin_part
                phase = phase - jnp.round(phase)
                square = phase * phase
                rows = slice(at + row, at + row + GROUP)
                table_ref[rows, lane : lane + LANES] = horner(COS, square).astype(jnp.bfloat16)
                table_ref[rows, BEAMS + lane : BEAMS + lane + LANES] = (phase * horner(SIN, square)).astype(jnp.bfloat16)

    sub = lax.broadcasted_iota(jnp.int32, (ROWS, LANES), 0)
    lane = lax.broadcasted_iota(jnp.int32, (ROWS, LANES), 1)

    def column(numbers):
        value = jnp.zeros((ROWS, LANES), jnp.int32)
        for i, number in enumerate(numbers):
            value = jnp.where(sub == i, number, value)
        return value

    order, later = [], []
    for at in range(0, half, ROWS):
        order.append(sub + at)
        later.append(column([pairing_ref[1, at + i] for i in range(ROWS)]))
    for at in range(0, half, ROWS):
        order.append(column([half + pairing_ref[0, at + i] for i in range(ROWS)]))
        later.append(column([half + pairing_ref[0, pairing_ref[1, at + i]] for i in range(ROWS)]))
    for which, rows in enumerate((order, later)):
        for at in range(0, len(rows), 2):
            pair = jnp.concatenate(rows[at : at + 2], axis=0)
            lanes = jnp.concatenate([lane, lane], axis=0)
            start = which * block + at * ROWS
            pick_ref[start : start + GROUP, :] = jnp.where(pair == lanes, 1.0, 0.0)[:, :block].astype(jnp.bfloat16)

    for which, rows in enumerate((order, order, later)):
        number = meta_ref[which]
        chunk = number // (LANES // block)
        shift = (number - chunk * (LANES // block)) * block
        for at, row in enumerate(rows):
            start = which * block + at * ROWS
            hit = row + shift == lane
            near = positions_ref[:, pl.ds(pl.multiple_of(chunk * LANES, LANES), LANES)]
            own_along = jnp.sum(jnp.where(hit, near[0:1], 0.0), axis=1, keepdims=True)
            own_side = jnp.sum(jnp.where(hit, near[1:2], 0.0), axis=1, keepdims=True)
            for to in range(0, sensors, LANES):
                delta_along = own_along - positions_ref[0:1, to : to + LANES]
                delta_side = own_side - positions_ref[1:2, to : to + LANES]
                square = jnp.maximum(delta_along * delta_along + delta_side * delta_side, 1e-30)
                inverse = lax.rsqrt(square)
                turn = (square * inverse) * (0.5 * width / math.pi)
                turn = turn - jnp.round(turn)
                value = turn * horner(SIN_FINE, turn * turn) * (inverse * (1.0 / width))
                taper_ref[start : start + ROWS, to : to + LANES] = value
                load_ref[start : start + ROWS, to : to + LANES] = jnp.where(hit & (chunk == to // LANES), LOAD, 0.0)


COS_FINE = (0.99999999, -19.7392045, 64.93911746, -85.45013953, 60.16763095, -25.96759925, 6.52865816)


def sums(left, right):
    left_re, left_im = left
    right_re, right_im = right
    norm_left = jnp.sum(left_re * left_re + left_im * left_im, axis=1, keepdims=True)
    norm_right = jnp.sum(right_re * right_re + right_im * right_im, axis=1, keepdims=True)
    gamma_re = jnp.sum(left_re * right_re + left_im * right_im, axis=1, keepdims=True)
    gamma_im = jnp.sum(left_re * right_im - left_im * right_re, axis=1, keepdims=True)
    spread = norm_right - norm_left
    radius = jnp.sqrt(spread * spread + 4.0 * (gamma_re * gamma_re + gamma_im * gamma_im) + 1e-30)
    leading = jnp.sqrt((radius + jnp.abs(spread)) / (2.0 * radius))
    factor = 1.0 / (radius * leading)
    return spread >= 0.0, leading, factor * gamma_re, factor * gamma_im


def rotate_side(left, right, side, sign):
    rising, leading, b_re, b_im = sums(left, right)
    plain = jnp.where(rising, 1, 0) != side
    left_re = jnp.where(plain, leading, b_re)
    left_im = jnp.where(plain, 0.0, b_im)
    right_re = sign * jnp.where(plain, b_re, leading)
    right_im = sign * jnp.where(plain, -b_im, 0.0)
    return (
        left_re * left[0] - left_im * left[1] + right_re * right[0] - right_im * right[1],
        left_re * left[1] + left_im * left[0] + right_re * right[1] + right_im * right[0],
    )


def rotate_both(left, right):
    rising, leading, b_re, b_im = sums(left, right)
    zero = jnp.zeros_like(b_im)

    def combine(left_re, left_im, right_re, right_im):
        return (
            left_re * left[0] - left_im * left[1] + right_re * right[0] - right_im * right[1],
            left_re * left[1] + left_im * left[0] + right_re * right[1] + right_im * right[0],
        )

    new_left = combine(
        jnp.where(rising, leading, b_re),
        jnp.where(rising, zero, b_im),
        jnp.where(rising, -b_re, -leading),
        jnp.where(rising, b_im, zero),
    )
    new_right = combine(
        jnp.where(rising, b_re, leading),
        jnp.where(rising, b_im, zero),
        jnp.where(rising, leading, b_re),
        jnp.where(rising, zero, -b_im),
    )
    return new_left, new_right


def respond_kernel(
    order, meta_ref, blocks_ref, table_ref, taper_ref, load_ref, pick_ref, early_hbm, final_hbm, all_ref, re_ref, im_ref, turn_ref, norm_ref, response_ref, semaphores
):
    block, depth = blocks_ref.shape[1:]
    half = block // 2
    for at, source in enumerate(order):
        all_ref[source * block : (source + 1) * block, :] = blocks_ref[at]
    everything = all_ref[...]

    def block_rows(which):
        return all_ref[pl.ds(pl.multiple_of(meta_ref[which] * block, block), block), :]

    near = dot(pick_ref[:block, :], jnp.concatenate([block_rows(0), block_rows(1)], axis=1), (1, 0))
    rows = jnp.concatenate([near[:, :depth], near[:, depth:], dot(pick_ref[block:, :], block_rows(2), (1, 0))], axis=0)
    sign = jnp.where(lax.broadcasted_iota(jnp.int32, rows.shape, 1) < depth // 2, 1.0, -1.0)
    weights = jnp.concatenate([rows, pltpu.roll(rows, depth // 2, 1) * sign], axis=0).astype(jnp.bfloat16)
    tile = dot(weights, everything, (1, 1))
    taper = taper_ref[...]
    re_ref[...] = tile[: 3 * block] * taper + load_ref[...]
    im_ref[...] = tile[3 * block :] * taper

    def rows_at(start):
        return re_ref[start : start + GROUP, :], im_ref[start : start + GROUP, :]

    def keep(which, start, column):
        turn_ref[which, start : start + GROUP, :] = column[0].astype(jnp.bfloat16)
        turn_ref[which, block + start : block + start + GROUP, :] = column[1].astype(jnp.bfloat16)
        total = jnp.sum(column[0] * column[0] + column[1] * column[1], axis=1, keepdims=True)
        norm_ref[which, start : start + GROUP, :] = jnp.broadcast_to(1.0 / total, (GROUP, LANES))

    def respond(which, projected):
        z_re = projected[:block, :BEAMS] + projected[block:, BEAMS:]
        z_im = projected[block:, :BEAMS] - projected[:block, BEAMS:]
        inverse = jnp.concatenate([norm_ref[which]] * (BEAMS // LANES), axis=1)
        response_ref[which] = (z_re * z_re + z_im * z_im) * inverse

    for at in range(0, half, GROUP):
        top, bottom = rotate_both(rows_at(at), rows_at(half + at))
        keep(0, at, top)
        keep(0, half + at, bottom)
    early = dot(turn_ref[0], table_ref[...], (1, 0))
    lower_side, upper_side = meta_ref[3], meta_ref[4]
    lower_sign = (2 * lower_side - 1).astype(jnp.float32)
    upper_sign = (2 * upper_side - 1).astype(jnp.float32)
    for at in range(0, half, GROUP):
        moved_top = rotate_side(rows_at(block + at), rows_at(block + half + at), lower_side, lower_sign)
        moved_bottom = rotate_side(rows_at(2 * block + at), rows_at(2 * block + half + at), upper_side, upper_sign)
        top, bottom = rotate_both(moved_top, moved_bottom)
        keep(1, at, top)
        keep(1, half + at, bottom)
    respond(0, early)
    respond(1, dot(turn_ref[1], table_ref[...], (1, 0)))
    fetch(((response_ref.at[0], early_hbm), (response_ref.at[1], final_hbm)), semaphores)


def send_order(peers):
    ends = [at // 2 if at % 2 == 0 else peers - 1 - at // 2 for at in range(peers)]
    return [peers // 2] + [peer for peer in ends if peer != peers // 2]


def pinned(array):
    return pltpu.with_memory_space_constraint(array, pltpu.HBM)


def per_device(spectra, valid_mask, pairing, positions, wavenumber):
    blocks = lax.axis_size("sens")
    position = lax.axis_index("sens")
    block = valid_mask.shape[1]
    depth = spectra.shape[0]
    sensors = positions.shape[1]
    copies = pl.pallas_call(
        spread_kernel,
        out_shape=pltpu.VMEM((blocks, block, depth), jnp.bfloat16),
        in_specs=[HBM, HBM],
        out_specs=VMEM,
        scratch_shapes=[
            pltpu.VMEM((block, depth), spectra.dtype),
            pltpu.VMEM(valid_mask.shape, valid_mask.dtype),
            pltpu.SemaphoreType.DMA((2,)),
        ],
        compiler_params=small(2),
        name="spread",
    )(pinned(spectra.T), pinned(valid_mask))
    order = send_order(blocks)
    numbers = [
        position,
        jnp.maximum(position - 1, 0),
        jnp.minimum(position + 1, blocks - 1),
        position == 1,
        position < blocks - 1,
    ]
    meta = jnp.stack([jnp.asarray(number, jnp.int32) for number in numbers])
    prepared = pl.pallas_call(
        functools.partial(prepare_kernel, block),
        out_shape=(
            jax.ShapeDtypeStruct((sensors, 2 * BEAMS), jnp.bfloat16),
            jax.ShapeDtypeStruct((3 * block, sensors), jnp.float32),
            jax.ShapeDtypeStruct((3 * block, sensors), jnp.float32),
            jax.ShapeDtypeStruct((2 * block, block), jnp.bfloat16),
        ),
        in_specs=[SMEM, SMEM, HBM, HBM],
        out_specs=(VMEM, VMEM, VMEM, VMEM),
        scratch_shapes=[
            pltpu.SMEM(pairing.shape, pairing.dtype),
            pltpu.VMEM(positions.shape, positions.dtype),
            pltpu.SemaphoreType.DMA((2,)),
        ],
        compiler_params=small(4),
        name="prepare",
    )(meta, wavenumber, pinned(pairing), pinned(positions))
    gathered = lax.all_to_all(copies, "sens", split_axis=0, concat_axis=0, axis_index_groups=[order])
    out = jax.ShapeDtypeStruct((block, BEAMS), jnp.float32)
    return pl.pallas_call(
        functools.partial(respond_kernel, order),
        out_shape=(out, out),
        in_specs=[SMEM, VMEM, VMEM, VMEM, VMEM, VMEM],
        out_specs=(HBM, HBM),
        scratch_shapes=[
            pltpu.VMEM((sensors, depth), jnp.bfloat16),
            pltpu.VMEM((3 * block, sensors), jnp.float32),
            pltpu.VMEM((3 * block, sensors), jnp.float32),
            pltpu.VMEM((2, 2 * block, sensors), jnp.bfloat16),
            pltpu.VMEM((2, block, LANES), jnp.float32),
            pltpu.VMEM((2, block, BEAMS), jnp.float32),
            pltpu.SemaphoreType.DMA((2,)),
        ],
        compiler_params=small(4 + sensors * block // 2**13),
        name="respond",
    )(meta, gathered, *prepared)


def solution(mesh):
    in_specs = (P("bin", "sens"), P(None, "sens"), P(), P(), P("bin"))
    out_specs = (P("sens", "bin"), P("sens", "bin"))
    return jax.shard_map(
        per_device, mesh=mesh, in_specs=in_specs, out_specs=out_specs, check_vma=False
    )
```

```python
import functools
import math

import jax
import jax.numpy as jnp
from jax import lax
from jax.experimental import pallas as pl
from jax.experimental.pallas import tpu as pltpu
from jax.sharding import PartitionSpec as P

BEAMS = 256
LOAD = 0.5
LANES = 128
ROWS = 8
GROUP = 16
VMEM = pl.BlockSpec(memory_space=pltpu.VMEM)
SMEM = pl.BlockSpec(memory_space=pltpu.SMEM)
HBM = pl.BlockSpec(memory_space=pltpu.HBM)

COS = (0.99999921, -19.73898036, 64.92865742, -85.27162153, 58.79049212, -21.07110563)
SIN = (6.28318492, -41.34158923, 81.59994333, -76.61447253, 41.34288235, -12.47124354)
SIN_FINE = (6.2831853, -41.34170041, 81.60513139, -76.70301535, 42.02592699, -14.89984667, 3.23813751)


def small(mebibytes):
    return pltpu.CompilerParams(vmem_limit_bytes=mebibytes * 2**20)


def fetch(pairs, semaphores):
    copies = [pltpu.make_async_copy(*pair, semaphores.at[i]) for i, pair in enumerate(pairs)]
    for copy in copies:
        copy.start()
    for copy in copies:
        copy.wait()


def horner(coefficients, at):
    value = coefficients[-1]
    for coefficient in coefficients[-2::-1]:
        value = value * at + coefficient
    return value


def dot(left, right, contract):
    return lax.dot_general(left, right, ((contract[:1], contract[1:]), ((), ())), preferred_element_type=jnp.float32)


def spread_kernel(spectra_hbm, mask_hbm, copies_ref, spectra_ref, mask_ref, semaphores):
    fetch(((spectra_hbm, spectra_ref), (mask_hbm, mask_ref)), semaphores)
    segments, block = mask_ref.shape
    depth = spectra_ref.shape[1]
    row = lax.broadcasted_iota(jnp.int32, (segments, depth), 0)
    lane = lax.broadcasted_iota(jnp.int32, (segments, depth), 1)
    twice = jnp.where((row == lane) | (row + segments == lane), 1.0, 0.0).astype(jnp.bfloat16)
    validity = dot(mask_ref[...].astype(jnp.float32).astype(jnp.bfloat16), twice, (0, 0))
    counts = 0.5 * jnp.sum(validity, axis=1, keepdims=True)
    scaled = (spectra_ref[...].astype(jnp.float32) * validity * (1.0 / jnp.sqrt(counts))).astype(jnp.bfloat16)
    for peer in range(copies_ref.shape[0]):
        copies_ref[peer] = scaled


def prepare_kernel(
    block, meta_ref, wavenumber_ref, pairing_hbm, positions_hbm, table_ref, taper_ref, load_ref, pick_ref,
    pairing_ref, positions_ref, semaphores
):
    fetch(((pairing_hbm, pairing_ref), (positions_hbm, positions_ref)), semaphores)
    sensors = positions_ref.shape[1]
    half = block // 2
    width = 3.0 / block

    beam = lax.broadcasted_iota(jnp.int32, (ROWS, BEAMS), 1).astype(jnp.float32)
    turns = (beam + 0.5) * (0.5 / BEAMS)
    square = turns * turns
    cos_beam = horner(COS_FINE, square)
    sin_beam = turns * horner(SIN_FINE, square)
    scale = wavenumber_ref[0] * (0.5 / math.pi)
    for at in range(0, sensors, LANES):
        along, side = (
            jnp.transpose(jnp.broadcast_to(positions_ref[axis : axis + 1, at : at + LANES] * scale, (LANES, LANES)))
            for axis in (0, 1)
        )
        for row in range(0, LANES, GROUP):
            for lane in range(0, BEAMS, LANES):
                cos_part = cos_beam[:1, lane : lane + LANES]
                sin_part = sin_beam[:1, lane : lane + LANES]
                phase = along[row : row + GROUP] * cos_part + side[row : row + GROUP] * sin_part
                phase = phase - jnp.round(phase)
                square = phase * phase
                rows = slice(at + row, at + row + GROUP)
                table_ref[rows, lane : lane + LANES] = horner(COS, square).astype(jnp.bfloat16)
                table_ref[rows, BEAMS + lane : BEAMS + lane + LANES] = (phase * horner(SIN, square)).astype(jnp.bfloat16)

    sub = lax.broadcasted_iota(jnp.int32, (ROWS, LANES), 0)
    lane = lax.broadcasted_iota(jnp.int32, (ROWS, LANES), 1)

    def column(numbers):
        value = jnp.zeros((ROWS, LANES), jnp.int32)
        for i, number in enumerate(numbers):
            value = jnp.where(sub == i, number, value)
        return value

    order, later = [], []
    for at in range(0, half, ROWS):
        order.append(sub + at)
        later.append(column([pairing_ref[1, at + i] for i in range(ROWS)]))
    for at in range(0, half, ROWS):
        order.append(column([half + pairing_ref[0, at + i] for i in range(ROWS)]))
        later.append(column([half + pairing_ref[0, pairing_ref[1, at + i]] for i in range(ROWS)]))
    for which, rows in enumerate((order, later)):
        for at in range(0, len(rows), 2):
            pair = jnp.concatenate(rows[at : at + 2], axis=0)
            lanes = jnp.concatenate([lane, lane], axis=0)
            start = which * block + at * ROWS
            pick_ref[start : start + GROUP, :] = jnp.where(pair == lanes, 1.0, 0.0)[:, :block].astype(jnp.bfloat16)

    for which, rows in enumerate((order, order, later)):
        number = meta_ref[which]
        chunk = number // (LANES // block)
        shift = (number - chunk * (LANES // block)) * block
        for at, row in enumerate(rows):
            start = which * block + at * ROWS
            hit = row + shift == lane
            near = positions_ref[:, pl.ds(pl.multiple_of(chunk * LANES, LANES), LANES)]
            own_along = jnp.sum(jnp.where(hit, near[0:1], 0.0), axis=1, keepdims=True)
            own_side = jnp.sum(jnp.where(hit, near[1:2], 0.0), axis=1, keepdims=True)
            for to in range(0, sensors, LANES):
                delta_along = own_along - positions_ref[0:1, to : to + LANES]
                delta_side = own_side - positions_ref[1:2, to : to + LANES]
                square = jnp.maximum(delta_along * delta_along + delta_side * delta_side, 1e-30)
                inverse = lax.rsqrt(square)
                turn = (square * inverse) * (0.5 * width / math.pi)
                turn = turn - jnp.round(turn)
                value = turn * horner(SIN_FINE, turn * turn) * (inverse * (1.0 / width))
                taper_ref[start : start + ROWS, to : to + LANES] = value
                load_ref[start : start + ROWS, to : to + LANES] = jnp.where(hit & (chunk == to // LANES), LOAD, 0.0)


COS_FINE = (0.99999999, -19.7392045, 64.93911746, -85.45013953, 60.16763095, -25.96759925, 6.52865816)


def sums(left, right):
    left_re, left_im = left
    right_re, right_im = right
    norm_left = jnp.sum(left_re * left_re + left_im * left_im, axis=1, keepdims=True)
    norm_right = jnp.sum(right_re * right_re + right_im * right_im, axis=1, keepdims=True)
    gamma_re = jnp.sum(left_re * right_re + left_im * right_im, axis=1, keepdims=True)
    gamma_im = jnp.sum(left_re * right_im - left_im * right_re, axis=1, keepdims=True)
    spread = norm_right - norm_left
    radius = jnp.sqrt(spread * spread + 4.0 * (gamma_re * gamma_re + gamma_im * gamma_im) + 1e-30)
    leading = jnp.sqrt((radius + jnp.abs(spread)) / (2.0 * radius))
    factor = 1.0 / (radius * leading)
    return spread >= 0.0, leading, factor * gamma_re, factor * gamma_im


def rotate_side(left, right, side, sign):
    rising, leading, b_re, b_im = sums(left, right)
    plain = jnp.where(rising, 1, 0) != side
    left_re = jnp.where(plain, leading, b_re)
    left_im = jnp.where(plain, 0.0, b_im)
    right_re = sign * jnp.where(plain, b_re, leading)
    right_im = sign * jnp.where(plain, -b_im, 0.0)
    return (
        left_re * left[0] - left_im * left[1] + right_re * right[0] - right_im * right[1],
        left_re * left[1] + left_im * left[0] + right_re * right[1] + right_im * right[0],
    )


def rotate_both(left, right):
    rising, leading, b_re, b_im = sums(left, right)
    zero = jnp.zeros_like(b_im)

    def combine(left_re, left_im, right_re, right_im):
        return (
            left_re * left[0] - left_im * left[1] + right_re * right[0] - right_im * right[1],
            left_re * left[1] + left_im * left[0] + right_re * right[1] + right_im * right[0],
        )

    new_left = combine(
        jnp.where(rising, leading, b_re),
        jnp.where(rising, zero, b_im),
        jnp.where(rising, -b_re, -leading),
        jnp.where(rising, b_im, zero),
    )
    new_right = combine(
        jnp.where(rising, b_re, leading),
        jnp.where(rising, b_im, zero),
        jnp.where(rising, leading, b_re),
        jnp.where(rising, zero, -b_im),
    )
    return new_left, new_right


def respond_kernel(
    meta_ref, blocks_ref, table_ref, taper_ref, load_ref, pick_ref, early_hbm, final_hbm, all_ref, re_ref, im_ref, turn_ref, norm_ref, response_ref, semaphores
):
    block, depth = blocks_ref.shape[1:]
    half = block // 2
    for at in range(blocks_ref.shape[0]):
        all_ref[pl.ds(pl.multiple_of(meta_ref[5 + at] * block, block), block), :] = blocks_ref[at]
    everything = all_ref[...]

    def block_rows(which):
        return all_ref[pl.ds(pl.multiple_of(meta_ref[which] * block, block), block), :]

    near = dot(pick_ref[:block, :], jnp.concatenate([block_rows(0), block_rows(1)], axis=1), (1, 0))
    rows = jnp.concatenate([near[:, :depth], near[:, depth:], dot(pick_ref[block:, :], block_rows(2), (1, 0))], axis=0)
    sign = jnp.where(lax.broadcasted_iota(jnp.int32, rows.shape, 1) < depth // 2, 1.0, -1.0)
    weights = jnp.concatenate([rows, pltpu.roll(rows, depth // 2, 1) * sign], axis=0).astype(jnp.bfloat16)
    tile = dot(weights, everything, (1, 1))
    taper = taper_ref[...]
    re_ref[...] = tile[: 3 * block] * taper + load_ref[...]
    im_ref[...] = tile[3 * block :] * taper

    def rows_at(start):
        return re_ref[start : start + GROUP, :], im_ref[start : start + GROUP, :]

    def keep(which, start, column):
        turn_ref[which, start : start + GROUP, :] = column[0].astype(jnp.bfloat16)
        turn_ref[which, block + start : block + start + GROUP, :] = column[1].astype(jnp.bfloat16)
        total = jnp.sum(column[0] * column[0] + column[1] * column[1], axis=1, keepdims=True)
        norm_ref[which, start : start + GROUP, :] = jnp.broadcast_to(1.0 / total, (GROUP, LANES))

    def respond(which, projected):
        z_re = projected[:block, :BEAMS] + projected[block:, BEAMS:]
        z_im = projected[block:, :BEAMS] - projected[:block, BEAMS:]
        inverse = jnp.concatenate([norm_ref[which]] * (BEAMS // LANES), axis=1)
        response_ref[which] = (z_re * z_re + z_im * z_im) * inverse

    for at in range(0, half, GROUP):
        top, bottom = rotate_both(rows_at(at), rows_at(half + at))
        keep(0, at, top)
        keep(0, half + at, bottom)
    early = dot(turn_ref[0], table_ref[...], (1, 0))
    lower_side, upper_side = meta_ref[3], meta_ref[4]
    lower_sign = (2 * lower_side - 1).astype(jnp.float32)
    upper_sign = (2 * upper_side - 1).astype(jnp.float32)
    for at in range(0, half, GROUP):
        moved_top = rotate_side(rows_at(block + at), rows_at(block + half + at), lower_side, lower_sign)
        moved_bottom = rotate_side(rows_at(2 * block + at), rows_at(2 * block + half + at), upper_side, upper_sign)
        top, bottom = rotate_both(moved_top, moved_bottom)
        keep(1, at, top)
        keep(1, half + at, bottom)
    respond(0, early)
    respond(1, dot(turn_ref[1], table_ref[...], (1, 0)))
    fetch(((response_ref.at[0], early_hbm), (response_ref.at[1], final_hbm)), semaphores)


def send_orders(peers):
    ends = [at // 2 if at % 2 == 0 else peers - 1 - at // 2 for at in range(peers)]
    ends.remove(peers // 2)
    return [peers // 2] + ends, [peers // 2] + ends[::-1]


def pinned(array):
    return pltpu.with_memory_space_constraint(array, pltpu.HBM)


def per_device(spectra, valid_mask, pairing, positions, wavenumber):
    blocks = lax.axis_size("sens")
    position = lax.axis_index("sens")
    block = valid_mask.shape[1]
    depth = spectra.shape[0]
    sensors = positions.shape[1]
    copies = pl.pallas_call(
        spread_kernel,
        out_shape=pltpu.VMEM((blocks, block, depth), jnp.bfloat16),
        in_specs=[HBM, HBM],
        out_specs=VMEM,
        scratch_shapes=[
            pltpu.VMEM((block, depth), spectra.dtype),
            pltpu.VMEM(valid_mask.shape, valid_mask.dtype),
            pltpu.SemaphoreType.DMA((2,)),
        ],
        compiler_params=small(2),
        name="spread",
    )(pinned(spectra.T), pinned(valid_mask))
    orders = send_orders(blocks)
    odd = lax.axis_index("bin") % 2 == 1
    groups = [[bin * blocks + peer for peer in orders[bin % 2]] for bin in range(lax.axis_size("bin"))]
    numbers = [
        position,
        jnp.maximum(position - 1, 0),
        jnp.minimum(position + 1, blocks - 1),
        position == 1,
        position < blocks - 1,
    ]
    numbers += [jnp.where(odd, second, first) for first, second in zip(*orders)]
    meta = jnp.stack([jnp.asarray(number, jnp.int32) for number in numbers])
    prepared = pl.pallas_call(
        functools.partial(prepare_kernel, block),
        out_shape=(
            jax.ShapeDtypeStruct((sensors, 2 * BEAMS), jnp.bfloat16),
            jax.ShapeDtypeStruct((3 * block, sensors), jnp.float32),
            jax.ShapeDtypeStruct((3 * block, sensors), jnp.float32),
            jax.ShapeDtypeStruct((2 * block, block), jnp.bfloat16),
        ),
        in_specs=[SMEM, SMEM, HBM, HBM],
        out_specs=(VMEM, VMEM, VMEM, VMEM),
        scratch_shapes=[
            pltpu.SMEM(pairing.shape, pairing.dtype),
            pltpu.VMEM(positions.shape, positions.dtype),
            pltpu.SemaphoreType.DMA((2,)),
        ],
        compiler_params=small(4),
        name="prepare",
    )(meta, wavenumber, pinned(pairing), pinned(positions))
    gathered = lax.all_to_all(copies, ("bin", "sens"), split_axis=0, concat_axis=0, axis_index_groups=groups)
    out = jax.ShapeDtypeStruct((block, BEAMS), jnp.float32)
    return pl.pallas_call(
        respond_kernel,
        out_shape=(out, out),
        in_specs=[SMEM, VMEM, VMEM, VMEM, VMEM, VMEM],
        out_specs=(HBM, HBM),
        scratch_shapes=[
            pltpu.VMEM((sensors, depth), jnp.bfloat16),
            pltpu.VMEM((3 * block, sensors), jnp.float32),
            pltpu.VMEM((3 * block, sensors), jnp.float32),
            pltpu.VMEM((2, 2 * block, sensors), jnp.bfloat16),
            pltpu.VMEM((2, block, LANES), jnp.float32),
            pltpu.VMEM((2, block, BEAMS), jnp.float32),
            pltpu.SemaphoreType.DMA((2,)),
        ],
        compiler_params=small(4 + sensors * block // 2**13),
        name="respond",
    )(meta, gathered, *prepared)


def solution(mesh):
    in_specs = (P("bin", "sens"), P(None, "sens"), P(), P(), P("bin"))
    out_specs = (P("sens", "bin"), P("sens", "bin"))
    return jax.shard_map(
        per_device, mesh=mesh, in_specs=in_specs, out_specs=out_specs, check_vma=False
    )
```

```python
import functools
import math

import jax
import jax.numpy as jnp
from jax import lax
from jax.experimental import pallas as pl
from jax.experimental.pallas import tpu as pltpu
from jax.sharding import PartitionSpec as P

BEAMS = 256
LOAD = 0.5
LANES = 128
ROWS = 8
GROUP = 16
VMEM = pl.BlockSpec(memory_space=pltpu.VMEM)
SMEM = pl.BlockSpec(memory_space=pltpu.SMEM)
HBM = pl.BlockSpec(memory_space=pltpu.HBM)

COS = (0.99999921, -19.73898036, 64.92865742, -85.27162153, 58.79049212, -21.07110563)
SIN = (6.28318492, -41.34158923, 81.59994333, -76.61447253, 41.34288235, -12.47124354)
SIN_FINE = (6.2831853, -41.34170041, 81.60513139, -76.70301535, 42.02592699, -14.89984667, 3.23813751)


def small(mebibytes):
    return pltpu.CompilerParams(vmem_limit_bytes=mebibytes * 2**20)


def fetch(pairs, semaphores):
    copies = [pltpu.make_async_copy(*pair, semaphores.at[i]) for i, pair in enumerate(pairs)]
    for copy in copies:
        copy.start()
    for copy in copies:
        copy.wait()


def horner(coefficients, at):
    value = coefficients[-1]
    for coefficient in coefficients[-2::-1]:
        value = value * at + coefficient
    return value


def dot(left, right, contract):
    return lax.dot_general(left, right, ((contract[:1], contract[1:]), ((), ())), preferred_element_type=jnp.float32)


def spread_kernel(spectra_hbm, mask_hbm, copies_ref, spectra_ref, mask_ref, semaphores):
    fetch(((spectra_hbm, spectra_ref), (mask_hbm, mask_ref)), semaphores)
    segments, block = mask_ref.shape
    depth = spectra_ref.shape[1]
    row = lax.broadcasted_iota(jnp.int32, (segments, depth), 0)
    lane = lax.broadcasted_iota(jnp.int32, (segments, depth), 1)
    twice = jnp.where((row == lane) | (row + segments == lane), 1.0, 0.0)
    both = jnp.concatenate([twice, jnp.ones_like(twice)], axis=1).astype(jnp.bfloat16)
    result = dot(mask_ref[...].astype(jnp.float32).astype(jnp.bfloat16), both, (0, 0))
    validity, counts = result[:, :depth], result[:, depth:]
    scaled = (spectra_ref[...].astype(jnp.float32) * validity * lax.rsqrt(counts)).astype(jnp.bfloat16)
    for peer in range(copies_ref.shape[0]):
        copies_ref[peer] = scaled


def prepare_kernel(
    block, meta_ref, wavenumber_ref, pairing_hbm, positions_hbm, table_ref, taper_ref, load_ref, pick_ref,
    pairing_ref, positions_ref, semaphores
):
    fetch(((pairing_hbm, pairing_ref), (positions_hbm, positions_ref)), semaphores)
    sensors = positions_ref.shape[1]
    half = block // 2
    width = 3.0 / block

    beam = lax.broadcasted_iota(jnp.int32, (ROWS, BEAMS), 1).astype(jnp.float32)
    turns = (beam + 0.5) * (0.5 / BEAMS)
    square = turns * turns
    cos_beam = horner(COS_FINE, square)
    sin_beam = turns * horner(SIN_FINE, square)
    scale = wavenumber_ref[0] * (0.5 / math.pi)
    for at in range(0, sensors, LANES):
        along, side = (
            jnp.transpose(jnp.broadcast_to(positions_ref[axis : axis + 1, at : at + LANES] * scale, (LANES, LANES)))
            for axis in (0, 1)
        )
        for row in range(0, LANES, GROUP):
            for lane in range(0, BEAMS, LANES):
                cos_part = cos_beam[:1, lane : lane + LANES]
                sin_part = sin_beam[:1, lane : lane + LANES]
                phase = along[row : row + GROUP] * cos_part + side[row : row + GROUP] * sin_part
                phase = phase - jnp.round(phase)
                square = phase * phase
                rows = slice(at + row, at + row + GROUP)
                table_ref[rows, lane : lane + LANES] = horner(COS, square).astype(jnp.bfloat16)
                table_ref[rows, BEAMS + lane : BEAMS + lane + LANES] = (phase * horner(SIN, square)).astype(jnp.bfloat16)

    sub = lax.broadcasted_iota(jnp.int32, (ROWS, LANES), 0)
    lane = lax.broadcasted_iota(jnp.int32, (ROWS, LANES), 1)

    def column(numbers):
        value = jnp.zeros((ROWS, LANES), jnp.int32)
        for i, number in enumerate(numbers):
            value = jnp.where(sub == i, number, value)
        return value

    order, later = [], []
    for at in range(0, half, ROWS):
        order.append(sub + at)
        later.append(column([pairing_ref[1, at + i] for i in range(ROWS)]))
    for at in range(0, half, ROWS):
        order.append(column([half + pairing_ref[0, at + i] for i in range(ROWS)]))
        later.append(column([half + pairing_ref[0, pairing_ref[1, at + i]] for i in range(ROWS)]))
    for which, rows in enumerate((order, later)):
        for at in range(0, len(rows), 2):
            pair = jnp.concatenate(rows[at : at + 2], axis=0)
            lanes = jnp.concatenate([lane, lane], axis=0)
            start = which * block + at * ROWS
            pick_ref[start : start + GROUP, :] = jnp.where(pair == lanes, 1.0, 0.0)[:, :block].astype(jnp.bfloat16)

    for which, rows in enumerate((order, order, later)):
        number = meta_ref[which]
        chunk = number // (LANES // block)
        shift = (number - chunk * (LANES // block)) * block
        for at, row in enumerate(rows):
            start = which * block + at * ROWS
            hit = row + shift == lane
            near = positions_ref[:, pl.ds(pl.multiple_of(chunk * LANES, LANES), LANES)]
            own_along = jnp.sum(jnp.where(hit, near[0:1], 0.0), axis=1, keepdims=True)
            own_side = jnp.sum(jnp.where(hit, near[1:2], 0.0), axis=1, keepdims=True)
            for to in range(0, sensors, LANES):
                delta_along = own_along - positions_ref[0:1, to : to + LANES]
                delta_side = own_side - positions_ref[1:2, to : to + LANES]
                square = jnp.maximum(delta_along * delta_along + delta_side * delta_side, 1e-30)
                inverse = lax.rsqrt(square)
                turn = (square * inverse) * (0.5 * width / math.pi)
                turn = turn - jnp.round(turn)
                value = turn * horner(SIN_FINE, turn * turn) * (inverse * (1.0 / width))
                taper_ref[start : start + ROWS, to : to + LANES] = value
                load_ref[start : start + ROWS, to : to + LANES] = jnp.where(hit & (chunk == to // LANES), LOAD, 0.0)


COS_FINE = (0.99999999, -19.7392045, 64.93911746, -85.45013953, 60.16763095, -25.96759925, 6.52865816)


def chunks(array):
    return [array[:, at : at + LANES] for at in range(0, array.shape[1], LANES)]


def lane_total(parts):
    return jnp.broadcast_to(jnp.sum(sum(parts[1:], parts[0]), axis=1, keepdims=True), parts[0].shape)


def sums(left, right):
    terms = list(zip(*left, *right))
    norm_left = lane_total([p_re * p_re + p_im * p_im for p_re, p_im, _, _ in terms])
    norm_right = lane_total([q_re * q_re + q_im * q_im for _, _, q_re, q_im in terms])
    gamma_re = lane_total([p_re * q_re + p_im * q_im for p_re, p_im, q_re, q_im in terms])
    gamma_im = lane_total([p_re * q_im - p_im * q_re for p_re, p_im, q_re, q_im in terms])
    spread = norm_right - norm_left
    inverse = lax.rsqrt(spread * spread + 4.0 * (gamma_re * gamma_re + gamma_im * gamma_im) + 1e-30)
    square = 0.5 + 0.5 * (jnp.abs(spread) * inverse)
    shrink = lax.rsqrt(square)
    factor = inverse * shrink
    return spread >= 0.0, square * shrink, factor * gamma_re, factor * gamma_im


def combine(left, right, left_re, left_im, right_re, right_im):
    terms = list(zip(*left, *right))
    return (
        [left_re * p_re - left_im * p_im + right_re * q_re - right_im * q_im for p_re, p_im, q_re, q_im in terms],
        [left_re * p_im + left_im * p_re + right_re * q_im + right_im * q_re for p_re, p_im, q_re, q_im in terms],
    )


def rotate_side(left, right, side, sign):
    rising, leading, b_re, b_im = sums(left, right)
    plain = jnp.where(rising, 1, 0) != side
    return combine(
        left,
        right,
        jnp.where(plain, leading, b_re),
        jnp.where(plain, 0.0, b_im),
        sign * jnp.where(plain, b_re, leading),
        sign * jnp.where(plain, -b_im, 0.0),
    )


def rotate_both(left, right):
    rising, leading, b_re, b_im = sums(left, right)
    new_left = combine(
        left,
        right,
        jnp.where(rising, leading, b_re),
        jnp.where(rising, 0.0, b_im),
        jnp.where(rising, -b_re, -leading),
        jnp.where(rising, b_im, 0.0),
    )
    new_right = combine(
        left,
        right,
        jnp.where(rising, b_re, leading),
        jnp.where(rising, b_im, 0.0),
        jnp.where(rising, leading, b_re),
        jnp.where(rising, 0.0, -b_im),
    )
    return new_left, new_right


def respond_kernel(
    order, meta_ref, blocks_ref, table_ref, taper_ref, load_ref, pick_ref, early_hbm, final_hbm, all_ref, re_ref, im_ref, turn_ref, norm_ref, response_ref, semaphores
):
    block, depth = blocks_ref.shape[1:]
    half = block // 2
    for at, source in enumerate(order):
        all_ref[source * block : (source + 1) * block, :] = blocks_ref[at]
    everything = all_ref[...]

    def block_rows(which):
        return all_ref[pl.ds(pl.multiple_of(meta_ref[which] * block, block), block), :]

    near = dot(pick_ref[:block, :], jnp.concatenate([block_rows(0), block_rows(1)], axis=1), (1, 0))
    rows = jnp.concatenate([near[:, :depth], near[:, depth:], dot(pick_ref[block:, :], block_rows(2), (1, 0))], axis=0)
    sign = jnp.where(lax.broadcasted_iota(jnp.int32, rows.shape, 1) < depth // 2, 1.0, -1.0)
    turned = pltpu.roll(rows, depth // 2, 1) * sign
    parts = []
    for at in range(0, 3 * block, block):
        parts += [rows[at : at + block], turned[at : at + block]]
    tile = dot(jnp.concatenate(parts, axis=0).astype(jnp.bfloat16), everything, (1, 1))
    for at in range(0, 3 * block, block):
        taper = taper_ref[at : at + block, :]
        re_ref[at : at + block, :] = tile[2 * at : 2 * at + block] * taper + load_ref[at : at + block, :]
        im_ref[at : at + block, :] = tile[2 * at + block : 2 * at + 2 * block] * taper

    def rows_at(start):
        return chunks(re_ref[start : start + GROUP, :]), chunks(im_ref[start : start + GROUP, :])

    def keep(which, start, column):
        turn_ref[which, start : start + GROUP, :] = jnp.concatenate(column[0], axis=1).astype(jnp.bfloat16)
        turn_ref[which, block + start : block + start + GROUP, :] = jnp.concatenate(column[1], axis=1).astype(jnp.bfloat16)
        norm_ref[which, start : start + GROUP, :] = 1.0 / lane_total([re * re + im * im for re, im in zip(*column)])

    def respond(which, projected):
        z_re = projected[:block, :BEAMS] + projected[block:, BEAMS:]
        z_im = projected[block:, :BEAMS] - projected[:block, BEAMS:]
        inverse = jnp.concatenate([norm_ref[which]] * (BEAMS // LANES), axis=1)
        response_ref[which] = (z_re * z_re + z_im * z_im) * inverse

    for at in range(0, half, GROUP):
        top, bottom = rotate_both(rows_at(at), rows_at(half + at))
        keep(0, at, top)
        keep(0, half + at, bottom)
    early = dot(turn_ref[0], table_ref[...], (1, 0))
    lower_side, upper_side = meta_ref[3], meta_ref[4]
    lower_sign = (2 * lower_side - 1).astype(jnp.float32)
    upper_sign = (2 * upper_side - 1).astype(jnp.float32)
    for at in range(0, half, GROUP):
        moved_top = rotate_side(rows_at(block + at), rows_at(block + half + at), lower_side, lower_sign)
        moved_bottom = rotate_side(rows_at(2 * block + at), rows_at(2 * block + half + at), upper_side, upper_sign)
        top, bottom = rotate_both(moved_top, moved_bottom)
        keep(1, at, top)
        keep(1, half + at, bottom)
    respond(0, early)
    respond(1, dot(turn_ref[1], table_ref[...], (1, 0)))
    fetch(((response_ref.at[0], early_hbm), (response_ref.at[1], final_hbm)), semaphores)


def send_order(peers):
    ends = [at // 2 if at % 2 == 0 else peers - 1 - at // 2 for at in range(peers)]
    return [peers // 2] + [peer for peer in ends if peer != peers // 2]


def pinned(array):
    return pltpu.with_memory_space_constraint(array, pltpu.HBM)


def per_device(spectra, valid_mask, pairing, positions, wavenumber):
    blocks = lax.axis_size("sens")
    position = lax.axis_index("sens")
    block = valid_mask.shape[1]
    depth = spectra.shape[0]
    sensors = positions.shape[1]
    copies = pl.pallas_call(
        spread_kernel,
        out_shape=pltpu.VMEM((blocks, block, depth), jnp.bfloat16),
        in_specs=[HBM, HBM],
        out_specs=VMEM,
        scratch_shapes=[
            pltpu.VMEM((block, depth), spectra.dtype),
            pltpu.VMEM(valid_mask.shape, valid_mask.dtype),
            pltpu.SemaphoreType.DMA((2,)),
        ],
        compiler_params=small(2),
        name="spread",
    )(pinned(spectra.T), pinned(valid_mask))
    order = send_order(blocks)
    numbers = [
        position,
        jnp.maximum(position - 1, 0),
        jnp.minimum(position + 1, blocks - 1),
        position == 1,
        position < blocks - 1,
    ]
    meta = jnp.stack([jnp.asarray(number, jnp.int32) for number in numbers])
    prepared = pl.pallas_call(
        functools.partial(prepare_kernel, block),
        out_shape=(
            jax.ShapeDtypeStruct((sensors, 2 * BEAMS), jnp.bfloat16),
            jax.ShapeDtypeStruct((3 * block, sensors), jnp.float32),
            jax.ShapeDtypeStruct((3 * block, sensors), jnp.float32),
            jax.ShapeDtypeStruct((2 * block, block), jnp.bfloat16),
        ),
        in_specs=[SMEM, SMEM, HBM, HBM],
        out_specs=(VMEM, VMEM, VMEM, VMEM),
        scratch_shapes=[
            pltpu.SMEM(pairing.shape, pairing.dtype),
            pltpu.VMEM(positions.shape, positions.dtype),
            pltpu.SemaphoreType.DMA((2,)),
        ],
        compiler_params=small(4),
        name="prepare",
    )(meta, wavenumber, pinned(pairing), pinned(positions))
    gathered = lax.all_to_all(copies, "sens", split_axis=0, concat_axis=0, axis_index_groups=[order])
    out = jax.ShapeDtypeStruct((block, BEAMS), jnp.float32)
    return pl.pallas_call(
        functools.partial(respond_kernel, order),
        out_shape=(out, out),
        in_specs=[SMEM, VMEM, VMEM, VMEM, VMEM, VMEM],
        out_specs=(HBM, HBM),
        scratch_shapes=[
            pltpu.VMEM((sensors, depth), jnp.bfloat16),
            pltpu.VMEM((3 * block, sensors), jnp.float32),
            pltpu.VMEM((3 * block, sensors), jnp.float32),
            pltpu.VMEM((2, 2 * block, sensors), jnp.bfloat16),
            pltpu.VMEM((2, block, LANES), jnp.float32),
            pltpu.VMEM((2, block, BEAMS), jnp.float32),
            pltpu.SemaphoreType.DMA((2,)),
        ],
        compiler_params=small(4 + sensors * block // 2**13),
        name="respond",
    )(meta, gathered, *prepared)


def solution(mesh):
    in_specs = (P("bin", "sens"), P(None, "sens"), P(), P(), P("bin"))
    out_specs = (P("sens", "bin"), P("sens", "bin"))
    return jax.shard_map(
        per_device, mesh=mesh, in_specs=in_specs, out_specs=out_specs, check_vma=False
    )
```

```python
import functools
import math

import jax
import jax.numpy as jnp
from jax import lax
from jax.experimental import pallas as pl
from jax.experimental.pallas import tpu as pltpu
from jax.sharding import PartitionSpec as P

BEAMS = 256
LOAD = 0.5
LANES = 128
ROWS = 8
GROUP = 16
VMEM = pl.BlockSpec(memory_space=pltpu.VMEM)
SMEM = pl.BlockSpec(memory_space=pltpu.SMEM)
HBM = pl.BlockSpec(memory_space=pltpu.HBM)

COS = (0.99999921, -19.73898036, 64.92865742, -85.27162153, 58.79049212, -21.07110563)
SIN = (6.28318492, -41.34158923, 81.59994333, -76.61447253, 41.34288235, -12.47124354)
SIN_FINE = (6.2831853, -41.34170041, 81.60513139, -76.70301535, 42.02592699, -14.89984667, 3.23813751)


def small(mebibytes):
    return pltpu.CompilerParams(vmem_limit_bytes=mebibytes * 2**20)


def fetch(pairs, semaphores):
    copies = [pltpu.make_async_copy(*pair, semaphores.at[i]) for i, pair in enumerate(pairs)]
    for copy in copies:
        copy.start()
    for copy in copies:
        copy.wait()


def horner(coefficients, at):
    value = coefficients[-1]
    for coefficient in coefficients[-2::-1]:
        value = value * at + coefficient
    return value


def dot(left, right, contract):
    return lax.dot_general(left, right, ((contract[:1], contract[1:]), ((), ())), preferred_element_type=jnp.float32)


def spread_kernel(spectra_hbm, mask_hbm, copies_ref, spectra_ref, mask_ref, semaphores):
    fetch(((spectra_hbm, spectra_ref), (mask_hbm, mask_ref)), semaphores)
    segments, block = mask_ref.shape
    depth = spectra_ref.shape[1]
    row = lax.broadcasted_iota(jnp.int32, (segments, depth), 0)
    lane = lax.broadcasted_iota(jnp.int32, (segments, depth), 1)
    twice = jnp.where((row == lane) | (row + segments == lane), 1.0, 0.0)
    both = jnp.concatenate([twice, jnp.ones_like(twice)], axis=1).astype(jnp.bfloat16)
    result = dot(mask_ref[...].astype(jnp.float32).astype(jnp.bfloat16), both, (0, 0))
    validity, counts = result[:, :depth], result[:, depth:]
    scaled = (spectra_ref[...].astype(jnp.float32) * validity * lax.rsqrt(counts)).astype(jnp.bfloat16)
    for peer in range(copies_ref.shape[0]):
        copies_ref[peer] = scaled


def place_of(order, number):
    place = jnp.int32(0)
    for at, source in enumerate(order):
        place = jnp.where(number == source, at, place)
    return place


def prepare_kernel(
    block, order, meta_ref, wavenumber_ref, pairing_hbm, positions_hbm, table_ref, taper_ref, load_ref, pick_ref,
    pairing_ref, positions_ref, semaphores
):
    fetch(((pairing_hbm, pairing_ref), (positions_hbm, positions_ref)), semaphores)
    sensors = positions_ref.shape[1]
    half = block // 2
    width = 3.0 / block

    beam = lax.broadcasted_iota(jnp.int32, (ROWS, BEAMS), 1).astype(jnp.float32)
    turns = (beam + 0.5) * (0.5 / BEAMS)
    square = turns * turns
    cos_beam = horner(COS_FINE, square)
    sin_beam = turns * horner(SIN_FINE, square)
    scale = wavenumber_ref[0] * (0.5 / math.pi)
    for at in range(0, sensors, LANES):
        along, side = (
            jnp.transpose(jnp.broadcast_to(positions_ref[axis : axis + 1, at : at + LANES] * scale, (LANES, LANES)))
            for axis in (0, 1)
        )
        for row in range(0, LANES, GROUP):
            for lane in range(0, BEAMS, LANES):
                cos_part = cos_beam[:1, lane : lane + LANES]
                sin_part = sin_beam[:1, lane : lane + LANES]
                phase = along[row : row + GROUP] * cos_part + side[row : row + GROUP] * sin_part
                phase = phase - jnp.round(phase)
                square = phase * phase
                start = order.index((at + row) // block) * block + row % block
                rows = slice(start, start + GROUP)
                table_ref[rows, lane : lane + LANES] = horner(COS, square).astype(jnp.bfloat16)
                table_ref[rows, BEAMS + lane : BEAMS + lane + LANES] = (phase * horner(SIN, square)).astype(jnp.bfloat16)

    sub = lax.broadcasted_iota(jnp.int32, (ROWS, LANES), 0)
    lane = lax.broadcasted_iota(jnp.int32, (ROWS, LANES), 1)

    def column(numbers):
        value = jnp.zeros((ROWS, LANES), jnp.int32)
        for i, number in enumerate(numbers):
            value = jnp.where(sub == i, number, value)
        return value

    first, later = [], []
    for at in range(0, half, ROWS):
        first.append(sub + at)
        later.append(column([pairing_ref[1, at + i] for i in range(ROWS)]))
    for at in range(0, half, ROWS):
        first.append(column([half + pairing_ref[0, at + i] for i in range(ROWS)]))
        later.append(column([half + pairing_ref[0, pairing_ref[1, at + i]] for i in range(ROWS)]))
    for which, rows in enumerate((first, later)):
        for at in range(0, len(rows), 2):
            pair = jnp.concatenate(rows[at : at + 2], axis=0)
            lanes = jnp.concatenate([lane, lane], axis=0)
            start = which * block + at * ROWS
            pick_ref[start : start + GROUP, :] = jnp.where(pair == lanes, 1.0, 0.0)[:, :block].astype(jnp.bfloat16)

    arrived = jnp.concatenate([positions_ref[:, peer * block : (peer + 1) * block] for peer in order], axis=1)
    for which, rows in enumerate((first, first, later)):
        number = meta_ref[which]
        chunk = number // (LANES // block)
        shift = (number - chunk * (LANES // block)) * block
        place = place_of(order, number)
        place_chunk = place // (LANES // block)
        place_shift = (place - place_chunk * (LANES // block)) * block
        for at, row in enumerate(rows):
            start = which * block + at * ROWS
            hit = row + shift == lane
            near = positions_ref[:, pl.ds(pl.multiple_of(chunk * LANES, LANES), LANES)]
            own_along = jnp.sum(jnp.where(hit, near[0:1], 0.0), axis=1, keepdims=True)
            own_side = jnp.sum(jnp.where(hit, near[1:2], 0.0), axis=1, keepdims=True)
            for to in range(0, sensors, LANES):
                delta_along = own_along - arrived[0:1, to : to + LANES]
                delta_side = own_side - arrived[1:2, to : to + LANES]
                square = jnp.maximum(delta_along * delta_along + delta_side * delta_side, 1e-30)
                inverse = lax.rsqrt(square)
                turn = (square * inverse) * (0.5 * width / math.pi)
                turn = turn - jnp.round(turn)
                value = turn * horner(SIN_FINE, turn * turn) * (inverse * (1.0 / width))
                taper_ref[start : start + ROWS, to : to + LANES] = value
                load_ref[start : start + ROWS, to : to + LANES] = jnp.where((row + place_shift == lane) & (place_chunk == to // LANES), LOAD, 0.0)


COS_FINE = (0.99999999, -19.7392045, 64.93911746, -85.45013953, 60.16763095, -25.96759925, 6.52865816)


def chunks(array):
    return [array[:, at : at + LANES] for at in range(0, array.shape[1], LANES)]


def lane_total(parts):
    return jnp.broadcast_to(jnp.sum(sum(parts[1:], parts[0]), axis=1, keepdims=True), parts[0].shape)


def sums(left, right):
    terms = list(zip(*left, *right))
    norm_left = lane_total([p_re * p_re + p_im * p_im for p_re, p_im, _, _ in terms])
    norm_right = lane_total([q_re * q_re + q_im * q_im for _, _, q_re, q_im in terms])
    gamma_re = lane_total([p_re * q_re + p_im * q_im for p_re, p_im, q_re, q_im in terms])
    gamma_im = lane_total([p_re * q_im - p_im * q_re for p_re, p_im, q_re, q_im in terms])
    spread = norm_right - norm_left
    inverse = lax.rsqrt(spread * spread + 4.0 * (gamma_re * gamma_re + gamma_im * gamma_im) + 1e-30)
    square = 0.5 + 0.5 * (jnp.abs(spread) * inverse)
    shrink = lax.rsqrt(square)
    factor = inverse * shrink
    return spread >= 0.0, square * shrink, factor * gamma_re, factor * gamma_im


def combine(left, right, left_re, left_im, right_re, right_im):
    terms = list(zip(*left, *right))
    return (
        [left_re * p_re - left_im * p_im + right_re * q_re - right_im * q_im for p_re, p_im, q_re, q_im in terms],
        [left_re * p_im + left_im * p_re + right_re * q_im + right_im * q_re for p_re, p_im, q_re, q_im in terms],
    )


def rotate_side(left, right, side, sign):
    rising, leading, b_re, b_im = sums(left, right)
    plain = jnp.where(rising, 1, 0) != side
    return combine(
        left,
        right,
        jnp.where(plain, leading, b_re),
        jnp.where(plain, 0.0, b_im),
        sign * jnp.where(plain, b_re, leading),
        sign * jnp.where(plain, -b_im, 0.0),
    )


def rotate_both(left, right):
    rising, leading, b_re, b_im = sums(left, right)
    new_left = combine(
        left,
        right,
        jnp.where(rising, leading, b_re),
        jnp.where(rising, 0.0, b_im),
        jnp.where(rising, -b_re, -leading),
        jnp.where(rising, b_im, 0.0),
    )
    new_right = combine(
        left,
        right,
        jnp.where(rising, b_re, leading),
        jnp.where(rising, b_im, 0.0),
        jnp.where(rising, leading, b_re),
        jnp.where(rising, 0.0, -b_im),
    )
    return new_left, new_right


def respond_kernel(
    order, meta_ref, blocks_ref, table_ref, taper_ref, load_ref, pick_ref, early_hbm, final_hbm, re_ref, im_ref, turn_ref, norm_ref, response_ref, semaphores
):
    block, depth = blocks_ref.shape[1:]
    half = block // 2
    everything = blocks_ref[...].reshape(-1, depth)

    def block_rows(which):
        return blocks_ref[place_of(order, meta_ref[which])]

    near = dot(pick_ref[:block, :], jnp.concatenate([block_rows(0), block_rows(1)], axis=1), (1, 0))
    rows = jnp.concatenate([near[:, :depth], near[:, depth:], dot(pick_ref[block:, :], block_rows(2), (1, 0))], axis=0)
    sign = jnp.where(lax.broadcasted_iota(jnp.int32, rows.shape, 1) < depth // 2, 1.0, -1.0)
    turned = pltpu.roll(rows, depth // 2, 1) * sign
    parts = []
    starts = (block, 2 * block, 0)
    for at in starts:
        parts += [rows[at : at + block], turned[at : at + block]]
    tile = dot(jnp.concatenate(parts, axis=0).astype(jnp.bfloat16), everything, (1, 1))
    for i, at in enumerate(starts):
        taper = taper_ref[at : at + block, :]
        re_ref[at : at + block, :] = tile[2 * i * block : (2 * i + 1) * block] * taper + load_ref[at : at + block, :]
        im_ref[at : at + block, :] = tile[(2 * i + 1) * block : (2 * i + 2) * block] * taper

    def rows_at(start):
        return chunks(re_ref[start : start + GROUP, :]), chunks(im_ref[start : start + GROUP, :])

    def keep(which, start, column):
        turn_ref[which, start : start + GROUP, :] = jnp.concatenate(column[0], axis=1).astype(jnp.bfloat16)
        turn_ref[which, block + start : block + start + GROUP, :] = jnp.concatenate(column[1], axis=1).astype(jnp.bfloat16)
        norm_ref[which, start : start + GROUP, :] = 1.0 / lane_total([re * re + im * im for re, im in zip(*column)])

    def respond(which, projected):
        z_re = projected[:block, :BEAMS] + projected[block:, BEAMS:]
        z_im = projected[block:, :BEAMS] - projected[:block, BEAMS:]
        inverse = jnp.concatenate([norm_ref[which]] * (BEAMS // LANES), axis=1)
        response_ref[which] = (z_re * z_re + z_im * z_im) * inverse

    lower_side, upper_side = meta_ref[3], meta_ref[4]
    lower_sign = (2 * lower_side - 1).astype(jnp.float32)
    upper_sign = (2 * upper_side - 1).astype(jnp.float32)
    for at in range(0, half, GROUP):
        moved_top = rotate_side(rows_at(block + at), rows_at(block + half + at), lower_side, lower_sign)
        moved_bottom = rotate_side(rows_at(2 * block + at), rows_at(2 * block + half + at), upper_side, upper_sign)
        top, bottom = rotate_both(rows_at(at), rows_at(half + at))
        keep(0, at, top)
        keep(0, half + at, bottom)
        top, bottom = rotate_both(moved_top, moved_bottom)
        keep(1, at, top)
        keep(1, half + at, bottom)
    copies = []
    for which, result_hbm in enumerate((early_hbm, final_hbm)):
        respond(which, dot(turn_ref[which], table_ref[...], (1, 0)))
        copies.append(pltpu.make_async_copy(response_ref.at[which], result_hbm, semaphores.at[which]))
        copies[-1].start()
    for copy in copies:
        copy.wait()


def send_order(peers):
    ends = [at // 2 if at % 2 == 0 else peers - 1 - at // 2 for at in range(peers)]
    return [peers // 2] + [peer for peer in ends if peer != peers // 2]


def pinned(array):
    return pltpu.with_memory_space_constraint(array, pltpu.HBM)


def per_device(spectra, valid_mask, pairing, positions, wavenumber):
    blocks = lax.axis_size("sens")
    position = lax.axis_index("sens")
    block = valid_mask.shape[1]
    depth = spectra.shape[0]
    sensors = positions.shape[1]
    copies = pl.pallas_call(
        spread_kernel,
        out_shape=pltpu.VMEM((blocks, block, depth), jnp.bfloat16),
        in_specs=[HBM, HBM],
        out_specs=VMEM,
        scratch_shapes=[
            pltpu.VMEM((block, depth), spectra.dtype),
            pltpu.VMEM(valid_mask.shape, valid_mask.dtype),
            pltpu.SemaphoreType.DMA((2,)),
        ],
        compiler_params=small(2),
        name="spread",
    )(pinned(spectra.T), pinned(valid_mask))
    order = send_order(blocks)
    numbers = [
        position,
        jnp.maximum(position - 1, 0),
        jnp.minimum(position + 1, blocks - 1),
        position == 1,
        position < blocks - 1,
    ]
    meta = jnp.stack([jnp.asarray(number, jnp.int32) for number in numbers])
    prepared = pl.pallas_call(
        functools.partial(prepare_kernel, block, order),
        out_shape=(
            jax.ShapeDtypeStruct((sensors, 2 * BEAMS), jnp.bfloat16),
            jax.ShapeDtypeStruct((3 * block, sensors), jnp.float32),
            jax.ShapeDtypeStruct((3 * block, sensors), jnp.float32),
            jax.ShapeDtypeStruct((2 * block, block), jnp.bfloat16),
        ),
        in_specs=[SMEM, SMEM, HBM, HBM],
        out_specs=(VMEM, VMEM, VMEM, VMEM),
        scratch_shapes=[
            pltpu.SMEM(pairing.shape, pairing.dtype),
            pltpu.VMEM(positions.shape, positions.dtype),
            pltpu.SemaphoreType.DMA((2,)),
        ],
        compiler_params=small(4),
        name="prepare",
    )(meta, wavenumber, pinned(pairing), pinned(positions))
    gathered = lax.all_to_all(copies, "sens", split_axis=0, concat_axis=0, axis_index_groups=[order])
    out = jax.ShapeDtypeStruct((block, BEAMS), jnp.float32)
    return pl.pallas_call(
        functools.partial(respond_kernel, order),
        out_shape=(out, out),
        in_specs=[SMEM, VMEM, VMEM, VMEM, VMEM, VMEM],
        out_specs=(HBM, HBM),
        scratch_shapes=[
            pltpu.VMEM((3 * block, sensors), jnp.float32),
            pltpu.VMEM((3 * block, sensors), jnp.float32),
            pltpu.VMEM((2, 2 * block, sensors), jnp.bfloat16),
            pltpu.VMEM((2, block, LANES), jnp.float32),
            pltpu.VMEM((2, block, BEAMS), jnp.float32),
            pltpu.SemaphoreType.DMA((2,)),
        ],
        compiler_params=small(4 + sensors * block // 2**13),
        name="respond",
    )(meta, gathered, *prepared)


def solution(mesh):
    in_specs = (P("bin", "sens"), P(None, "sens"), P(), P(), P("bin"))
    out_specs = (P("sens", "bin"), P("sens", "bin"))
    return jax.shard_map(
        per_device, mesh=mesh, in_specs=in_specs, out_specs=out_specs, check_vma=False
    )
```

```python
import functools
import math

import jax
import jax.numpy as jnp
from jax import lax
from jax.experimental import pallas as pl
from jax.experimental.pallas import tpu as pltpu
from jax.sharding import PartitionSpec as P

BEAMS = 256
LOAD = 0.5
LANES = 128
ROWS = 8
GROUP = 16
VMEM = pl.BlockSpec(memory_space=pltpu.VMEM)
SMEM = pl.BlockSpec(memory_space=pltpu.SMEM)
HBM = pl.BlockSpec(memory_space=pltpu.HBM)

COS = (0.99999921, -19.73898036, 64.92865742, -85.27162153, 58.79049212, -21.07110563)
SIN = (6.28318492, -41.34158923, 81.59994333, -76.61447253, 41.34288235, -12.47124354)
SIN_FINE = (6.2831853, -41.34170041, 81.60513139, -76.70301535, 42.02592699, -14.89984667, 3.23813751)


def small(mebibytes):
    return pltpu.CompilerParams(vmem_limit_bytes=mebibytes * 2**20)


def fetch(pairs, semaphores):
    copies = [pltpu.make_async_copy(*pair, semaphores.at[i]) for i, pair in enumerate(pairs)]
    for copy in copies:
        copy.start()
    for copy in copies:
        copy.wait()


def horner(coefficients, at):
    value = coefficients[-1]
    for coefficient in coefficients[-2::-1]:
        value = value * at + coefficient
    return value


def dot(left, right, contract):
    return lax.dot_general(left, right, ((contract[:1], contract[1:]), ((), ())), preferred_element_type=jnp.float32)


def spread_kernel(spectra_hbm, mask_hbm, copies_ref, spectra_ref, mask_ref, semaphores):
    fetch(((spectra_hbm, spectra_ref), (mask_hbm, mask_ref)), semaphores)
    segments, block = mask_ref.shape
    depth = spectra_ref.shape[1]
    row = lax.broadcasted_iota(jnp.int32, (segments, depth), 0)
    lane = lax.broadcasted_iota(jnp.int32, (segments, depth), 1)
    twice = jnp.where((row == lane) | (row + segments == lane), 1.0, 0.0)
    both = jnp.concatenate([twice, jnp.ones_like(twice)], axis=1).astype(jnp.bfloat16)
    result = dot(mask_ref[...].astype(jnp.float32).astype(jnp.bfloat16), both, (0, 0))
    validity, counts = result[:, :depth], result[:, depth:]
    scaled = (spectra_ref[...].astype(jnp.float32) * validity * lax.rsqrt(counts)).astype(jnp.bfloat16)
    for peer in range(copies_ref.shape[0]):
        copies_ref[peer] = scaled


def neighbourhood(peers):
    position = lax.axis_index("sens")
    numbers = position, jnp.maximum(position - 1, 0), jnp.minimum(position + 1, peers - 1)
    return numbers, jnp.where(position == 1, 1, 0), jnp.where(position < peers - 1, 1, 0)


def place_of(order, number):
    place = jnp.int32(0)
    for at, source in enumerate(order):
        place = jnp.where(number == source, at, place)
    return place


def prepare_kernel(
    block, order, wavenumber_ref, pairing_hbm, positions_hbm, table_ref, taper_ref, load_ref, pick_ref,
    pairing_ref, positions_ref, semaphores
):
    fetch(((pairing_hbm, pairing_ref), (positions_hbm, positions_ref)), semaphores)
    sensors = positions_ref.shape[1]
    half = block // 2
    width = 3.0 / block

    beam = lax.broadcasted_iota(jnp.int32, (ROWS, BEAMS), 1).astype(jnp.float32)
    turns = (beam + 0.5) * (0.5 / BEAMS)
    square = turns * turns
    cos_beam = horner(COS_FINE, square)
    sin_beam = turns * horner(SIN_FINE, square)
    scale = wavenumber_ref[0] * (0.5 / math.pi)
    for at in range(0, sensors, LANES):
        along, side = (
            jnp.transpose(jnp.broadcast_to(positions_ref[axis : axis + 1, at : at + LANES] * scale, (LANES, LANES)))
            for axis in (0, 1)
        )
        for row in range(0, LANES, GROUP):
            for lane in range(0, BEAMS, LANES):
                cos_part = cos_beam[:1, lane : lane + LANES]
                sin_part = sin_beam[:1, lane : lane + LANES]
                phase = along[row : row + GROUP] * cos_part + side[row : row + GROUP] * sin_part
                phase = phase - jnp.round(phase)
                square = phase * phase
                start = order.index((at + row) // block) * block + row % block
                rows = slice(start, start + GROUP)
                table_ref[rows, lane : lane + LANES] = horner(COS, square).astype(jnp.bfloat16)
                table_ref[rows, BEAMS + lane : BEAMS + lane + LANES] = (phase * horner(SIN, square)).astype(jnp.bfloat16)

    sub = lax.broadcasted_iota(jnp.int32, (ROWS, LANES), 0)
    lane = lax.broadcasted_iota(jnp.int32, (ROWS, LANES), 1)

    def column(numbers):
        value = jnp.zeros((ROWS, LANES), jnp.int32)
        for i, number in enumerate(numbers):
            value = jnp.where(sub == i, number, value)
        return value

    first, later = [], []
    for at in range(0, half, ROWS):
        first.append(sub + at)
        later.append(column([pairing_ref[1, at + i] for i in range(ROWS)]))
    for at in range(0, half, ROWS):
        first.append(column([half + pairing_ref[0, at + i] for i in range(ROWS)]))
        later.append(column([half + pairing_ref[0, pairing_ref[1, at + i]] for i in range(ROWS)]))
    for which, rows in enumerate((first, later)):
        for at in range(0, len(rows), 2):
            pair = jnp.concatenate(rows[at : at + 2], axis=0)
            lanes = jnp.concatenate([lane, lane], axis=0)
            start = which * block + at * ROWS
            pick_ref[start : start + GROUP, :] = jnp.where(pair == lanes, 1.0, 0.0)[:, :block].astype(jnp.bfloat16)

    arrived = jnp.concatenate([positions_ref[:, peer * block : (peer + 1) * block] for peer in order], axis=1)
    for which, (rows, number) in enumerate(zip((first, first, later), neighbourhood(len(order))[0])):
        chunk = number // (LANES // block)
        shift = (number - chunk * (LANES // block)) * block
        place = place_of(order, number)
        place_chunk = place // (LANES // block)
        place_shift = (place - place_chunk * (LANES // block)) * block
        for at, row in enumerate(rows):
            start = which * block + at * ROWS
            hit = row + shift == lane
            near = positions_ref[:, pl.ds(pl.multiple_of(chunk * LANES, LANES), LANES)]
            own_along = jnp.sum(jnp.where(hit, near[0:1], 0.0), axis=1, keepdims=True)
            own_side = jnp.sum(jnp.where(hit, near[1:2], 0.0), axis=1, keepdims=True)
            for to in range(0, sensors, LANES):
                delta_along = own_along - arrived[0:1, to : to + LANES]
                delta_side = own_side - arrived[1:2, to : to + LANES]
                square = jnp.maximum(delta_along * delta_along + delta_side * delta_side, 1e-30)
                inverse = lax.rsqrt(square)
                turn = (square * inverse) * (0.5 * width / math.pi)
                turn = turn - jnp.round(turn)
                value = turn * horner(SIN_FINE, turn * turn) * (inverse * (1.0 / width))
                taper_ref[start : start + ROWS, to : to + LANES] = value
                load_ref[start : start + ROWS, to : to + LANES] = jnp.where((row + place_shift == lane) & (place_chunk == to // LANES), LOAD, 0.0)


COS_FINE = (0.99999999, -19.7392045, 64.93911746, -85.45013953, 60.16763095, -25.96759925, 6.52865816)


def chunks(array):
    return [array[:, at : at + LANES] for at in range(0, array.shape[1], LANES)]


def lane_total(parts):
    return jnp.broadcast_to(jnp.sum(sum(parts[1:], parts[0]), axis=1, keepdims=True), parts[0].shape)


def sums(left, right):
    terms = list(zip(*left, *right))
    norm_left = lane_total([p_re * p_re + p_im * p_im for p_re, p_im, _, _ in terms])
    norm_right = lane_total([q_re * q_re + q_im * q_im for _, _, q_re, q_im in terms])
    gamma_re = lane_total([p_re * q_re + p_im * q_im for p_re, p_im, q_re, q_im in terms])
    gamma_im = lane_total([p_re * q_im - p_im * q_re for p_re, p_im, q_re, q_im in terms])
    spread = norm_right - norm_left
    inverse = lax.rsqrt(spread * spread + 4.0 * (gamma_re * gamma_re + gamma_im * gamma_im) + 1e-30)
    square = 0.5 + 0.5 * (jnp.abs(spread) * inverse)
    shrink = lax.rsqrt(square)
    factor = inverse * shrink
    return spread >= 0.0, square * shrink, factor * gamma_re, factor * gamma_im


def combine(left, right, left_re, left_im, right_re, right_im):
    terms = list(zip(*left, *right))
    return (
        [left_re * p_re - left_im * p_im + right_re * q_re - right_im * q_im for p_re, p_im, q_re, q_im in terms],
        [left_re * p_im + left_im * p_re + right_re * q_im + right_im * q_re for p_re, p_im, q_re, q_im in terms],
    )


def rotate_side(left, right, side, sign):
    rising, leading, b_re, b_im = sums(left, right)
    plain = jnp.where(rising, 1, 0) != side
    return combine(
        left,
        right,
        jnp.where(plain, leading, b_re),
        jnp.where(plain, 0.0, b_im),
        sign * jnp.where(plain, b_re, leading),
        sign * jnp.where(plain, -b_im, 0.0),
    )


def rotate_both(left, right):
    rising, leading, b_re, b_im = sums(left, right)
    new_left = combine(
        left,
        right,
        jnp.where(rising, leading, b_re),
        jnp.where(rising, 0.0, b_im),
        jnp.where(rising, -b_re, -leading),
        jnp.where(rising, b_im, 0.0),
    )
    new_right = combine(
        left,
        right,
        jnp.where(rising, b_re, leading),
        jnp.where(rising, b_im, 0.0),
        jnp.where(rising, leading, b_re),
        jnp.where(rising, 0.0, -b_im),
    )
    return new_left, new_right


def respond_kernel(
    order, blocks_ref, table_ref, taper_ref, load_ref, pick_ref, early_hbm, final_hbm, re_ref, im_ref, turn_ref, norm_ref, response_ref, semaphores
):
    block, depth = blocks_ref.shape[1:]
    half = block // 2
    everything = blocks_ref[...].reshape(-1, depth)

    numbers, lower_side, upper_side = neighbourhood(len(order))

    def block_rows(which):
        return blocks_ref[place_of(order, numbers[which])]

    near = dot(pick_ref[:block, :], jnp.concatenate([block_rows(0), block_rows(1)], axis=1), (1, 0))
    rows = jnp.concatenate([near[:, :depth], near[:, depth:], dot(pick_ref[block:, :], block_rows(2), (1, 0))], axis=0)
    sign = jnp.where(lax.broadcasted_iota(jnp.int32, rows.shape, 1) < depth // 2, 1.0, -1.0)
    turned = pltpu.roll(rows, depth // 2, 1) * sign
    parts = []
    starts = (block, 2 * block, 0)
    for at in starts:
        parts += [rows[at : at + block], turned[at : at + block]]
    tile = dot(jnp.concatenate(parts, axis=0).astype(jnp.bfloat16), everything, (1, 1))
    for i, at in enumerate(starts):
        taper = taper_ref[at : at + block, :]
        re_ref[at : at + block, :] = tile[2 * i * block : (2 * i + 1) * block] * taper + load_ref[at : at + block, :]
        im_ref[at : at + block, :] = tile[(2 * i + 1) * block : (2 * i + 2) * block] * taper

    def rows_at(start):
        return chunks(re_ref[start : start + GROUP, :]), chunks(im_ref[start : start + GROUP, :])

    def keep(which, start, column):
        turn_ref[which, start : start + GROUP, :] = jnp.concatenate(column[0], axis=1).astype(jnp.bfloat16)
        turn_ref[which, block + start : block + start + GROUP, :] = jnp.concatenate(column[1], axis=1).astype(jnp.bfloat16)
        norm_ref[which, start : start + GROUP, :] = 1.0 / lane_total([re * re + im * im for re, im in zip(*column)])

    def respond(which, projected):
        z_re = projected[:block, :BEAMS] + projected[block:, BEAMS:]
        z_im = projected[block:, :BEAMS] - projected[:block, BEAMS:]
        inverse = jnp.concatenate([norm_ref[which]] * (BEAMS // LANES), axis=1)
        response_ref[which] = (z_re * z_re + z_im * z_im) * inverse

    lower_sign = (2 * lower_side - 1).astype(jnp.float32)
    upper_sign = (2 * upper_side - 1).astype(jnp.float32)
    for at in range(0, half, GROUP):
        moved_top = rotate_side(rows_at(block + at), rows_at(block + half + at), lower_side, lower_sign)
        moved_bottom = rotate_side(rows_at(2 * block + at), rows_at(2 * block + half + at), upper_side, upper_sign)
        top, bottom = rotate_both(rows_at(at), rows_at(half + at))
        keep(0, at, top)
        keep(0, half + at, bottom)
        top, bottom = rotate_both(moved_top, moved_bottom)
        keep(1, at, top)
        keep(1, half + at, bottom)
    copies = []
    for which, result_hbm in enumerate((early_hbm, final_hbm)):
        respond(which, dot(turn_ref[which], table_ref[...], (1, 0)))
        copies.append(pltpu.make_async_copy(response_ref.at[which], result_hbm, semaphores.at[which]))
        copies[-1].start()
    for copy in copies:
        copy.wait()


def send_order(peers):
    ends = [at // 2 if at % 2 == 0 else peers - 1 - at // 2 for at in range(peers)]
    return [peers // 2] + [peer for peer in ends if peer != peers // 2]


def pinned(array):
    return pltpu.with_memory_space_constraint(array, pltpu.HBM)


def per_device(spectra, valid_mask, pairing, positions, wavenumber):
    blocks = lax.axis_size("sens")
    block = valid_mask.shape[1]
    depth = spectra.shape[0]
    sensors = positions.shape[1]
    copies = pl.pallas_call(
        spread_kernel,
        out_shape=pltpu.VMEM((blocks, block, depth), jnp.bfloat16),
        in_specs=[HBM, HBM],
        out_specs=VMEM,
        scratch_shapes=[
            pltpu.VMEM((block, depth), spectra.dtype),
            pltpu.VMEM(valid_mask.shape, valid_mask.dtype),
            pltpu.SemaphoreType.DMA((2,)),
        ],
        compiler_params=small(2),
        name="spread",
    )(pinned(spectra.T), pinned(valid_mask))
    order = send_order(blocks)
    prepared = pl.pallas_call(
        functools.partial(prepare_kernel, block, order),
        out_shape=(
            jax.ShapeDtypeStruct((sensors, 2 * BEAMS), jnp.bfloat16),
            jax.ShapeDtypeStruct((3 * block, sensors), jnp.float32),
            jax.ShapeDtypeStruct((3 * block, sensors), jnp.float32),
            jax.ShapeDtypeStruct((2 * block, block), jnp.bfloat16),
        ),
        in_specs=[SMEM, HBM, HBM],
        out_specs=(VMEM, VMEM, VMEM, VMEM),
        scratch_shapes=[
            pltpu.SMEM(pairing.shape, pairing.dtype),
            pltpu.VMEM(positions.shape, positions.dtype),
            pltpu.SemaphoreType.DMA((2,)),
        ],
        compiler_params=small(4),
        name="prepare",
    )(wavenumber, pinned(pairing), pinned(positions))
    gathered = lax.all_to_all(copies, "sens", split_axis=0, concat_axis=0, axis_index_groups=[order])
    out = jax.ShapeDtypeStruct((block, BEAMS), jnp.float32)
    return pl.pallas_call(
        functools.partial(respond_kernel, order),
        out_shape=(out, out),
        in_specs=[VMEM, VMEM, VMEM, VMEM, VMEM],
        out_specs=(HBM, HBM),
        scratch_shapes=[
            pltpu.VMEM((3 * block, sensors), jnp.float32),
            pltpu.VMEM((3 * block, sensors), jnp.float32),
            pltpu.VMEM((2, 2 * block, sensors), jnp.bfloat16),
            pltpu.VMEM((2, block, LANES), jnp.float32),
            pltpu.VMEM((2, block, BEAMS), jnp.float32),
            pltpu.SemaphoreType.DMA((2,)),
        ],
        compiler_params=small(4 + sensors * block // 2**13),
        name="respond",
    )(gathered, *prepared)


def solution(mesh):
    in_specs = (P("bin", "sens"), P(None, "sens"), P(), P(), P("bin"))
    out_specs = (P("sens", "bin"), P("sens", "bin"))
    return jax.shard_map(
        per_device, mesh=mesh, in_specs=in_specs, out_specs=out_specs, check_vma=False
    )
```

```python
import functools
import math

import jax
import jax.numpy as jnp
from jax import lax
from jax.experimental import pallas as pl
from jax.experimental.pallas import tpu as pltpu
from jax.sharding import PartitionSpec as P

BEAMS = 256
LOAD = 0.5
LANES = 128
ROWS = 8
GROUP = 16
VMEM = pl.BlockSpec(memory_space=pltpu.VMEM)
SMEM = pl.BlockSpec(memory_space=pltpu.SMEM)
HBM = pl.BlockSpec(memory_space=pltpu.HBM)

COS = (0.99999921, -19.73898036, 64.92865742, -85.27162153, 58.79049212, -21.07110563)
SIN = (6.28318492, -41.34158923, 81.59994333, -76.61447253, 41.34288235, -12.47124354)
SIN_FINE = (6.2831853, -41.34170041, 81.60513139, -76.70301535, 42.02592699, -14.89984667, 3.23813751)


def small(mebibytes):
    return pltpu.CompilerParams(vmem_limit_bytes=mebibytes * 2**20)


def fetch(pairs, semaphores):
    copies = [pltpu.make_async_copy(*pair, semaphores.at[i]) for i, pair in enumerate(pairs)]
    for copy in copies:
        copy.start()
    for copy in copies:
        copy.wait()


def horner(coefficients, at):
    value = coefficients[-1]
    for coefficient in coefficients[-2::-1]:
        value = value * at + coefficient
    return value


def dot(left, right, contract):
    return lax.dot_general(left, right, ((contract[:1], contract[1:]), ((), ())), preferred_element_type=jnp.float32)


def spread_kernel(spectra_hbm, mask_hbm, copies_hbm, spectra_ref, mask_ref, scaled_ref, semaphores, sent):
    fetch(((spectra_hbm, spectra_ref), (mask_hbm, mask_ref)), semaphores)
    segments, block = mask_ref.shape
    depth = spectra_ref.shape[1]
    row = lax.broadcasted_iota(jnp.int32, (segments, depth), 0)
    lane = lax.broadcasted_iota(jnp.int32, (segments, depth), 1)
    twice = jnp.where((row == lane) | (row + segments == lane), 1.0, 0.0)
    both = jnp.concatenate([twice, jnp.ones_like(twice)], axis=1).astype(jnp.bfloat16)
    result = dot(mask_ref[...].astype(jnp.float32).astype(jnp.bfloat16), both, (0, 0))
    validity, counts = result[:, :depth], result[:, depth:]
    scaled_ref[...] = (spectra_ref[...].astype(jnp.float32) * validity * lax.rsqrt(counts)).astype(jnp.bfloat16)
    fetch([(scaled_ref, copies_hbm.at[peer]) for peer in range(copies_hbm.shape[0])], sent)


def neighbourhood(peers):
    position = lax.axis_index("sens")
    numbers = position, jnp.maximum(position - 1, 0), jnp.minimum(position + 1, peers - 1)
    return numbers, jnp.where(position == 1, 1, 0), jnp.where(position < peers - 1, 1, 0)


def place_of(order, number):
    place = jnp.int32(0)
    for at, source in enumerate(order):
        place = jnp.where(number == source, at, place)
    return place


def prepare_kernel(
    block, order, wavenumber_ref, pairing_hbm, positions_hbm, table_ref, taper_ref, load_ref, pick_ref,
    pairing_ref, positions_ref, semaphores
):
    fetch(((pairing_hbm, pairing_ref), (positions_hbm, positions_ref)), semaphores)
    sensors = positions_ref.shape[1]
    half = block // 2
    width = 3.0 / block

    beam = lax.broadcasted_iota(jnp.int32, (ROWS, BEAMS), 1).astype(jnp.float32)
    turns = (beam + 0.5) * (0.5 / BEAMS)
    square = turns * turns
    cos_beam = horner(COS_FINE, square)
    sin_beam = turns * horner(SIN_FINE, square)
    scale = wavenumber_ref[0] * (0.5 / math.pi)
    for at in range(0, sensors, LANES):
        along, side = (
            jnp.transpose(jnp.broadcast_to(positions_ref[axis : axis + 1, at : at + LANES] * scale, (LANES, LANES)))
            for axis in (0, 1)
        )
        for row in range(0, LANES, GROUP):
            for lane in range(0, BEAMS, LANES):
                cos_part = cos_beam[:1, lane : lane + LANES]
                sin_part = sin_beam[:1, lane : lane + LANES]
                phase = along[row : row + GROUP] * cos_part + side[row : row + GROUP] * sin_part
                phase = phase - jnp.round(phase)
                square = phase * phase
                start = order.index((at + row) // block) * block + row % block
                rows = slice(start, start + GROUP)
                table_ref[rows, lane : lane + LANES] = horner(COS, square).astype(jnp.bfloat16)
                table_ref[rows, BEAMS + lane : BEAMS + lane + LANES] = (phase * horner(SIN, square)).astype(jnp.bfloat16)

    sub = lax.broadcasted_iota(jnp.int32, (ROWS, LANES), 0)
    lane = lax.broadcasted_iota(jnp.int32, (ROWS, LANES), 1)

    def column(numbers):
        value = jnp.zeros((ROWS, LANES), jnp.int32)
        for i, number in enumerate(numbers):
            value = jnp.where(sub == i, number, value)
        return value

    first, later = [], []
    for at in range(0, half, ROWS):
        first.append(sub + at)
        later.append(column([pairing_ref[1, at + i] for i in range(ROWS)]))
    for at in range(0, half, ROWS):
        first.append(column([half + pairing_ref[0, at + i] for i in range(ROWS)]))
        later.append(column([half + pairing_ref[0, pairing_ref[1, at + i]] for i in range(ROWS)]))
    for which, rows in enumerate((first, later)):
        for at in range(0, len(rows), 2):
            pair = jnp.concatenate(rows[at : at + 2], axis=0)
            lanes = jnp.concatenate([lane, lane], axis=0)
            start = which * block + at * ROWS
            pick_ref[start : start + GROUP, :] = jnp.where(pair == lanes, 1.0, 0.0)[:, :block].astype(jnp.bfloat16)

    arrived = jnp.concatenate([positions_ref[:, peer * block : (peer + 1) * block] for peer in order], axis=1)
    for which, (rows, number) in enumerate(zip((first, first, later), neighbourhood(len(order))[0])):
        chunk = number // (LANES // block)
        shift = (number - chunk * (LANES // block)) * block
        place = place_of(order, number)
        place_chunk = place // (LANES // block)
        place_shift = (place - place_chunk * (LANES // block)) * block
        for at, row in enumerate(rows):
            start = which * block + at * ROWS
            hit = row + shift == lane
            near = positions_ref[:, pl.ds(pl.multiple_of(chunk * LANES, LANES), LANES)]
            own_along = jnp.sum(jnp.where(hit, near[0:1], 0.0), axis=1, keepdims=True)
            own_side = jnp.sum(jnp.where(hit, near[1:2], 0.0), axis=1, keepdims=True)
            for to in range(0, sensors, LANES):
                delta_along = own_along - arrived[0:1, to : to + LANES]
                delta_side = own_side - arrived[1:2, to : to + LANES]
                square = jnp.maximum(delta_along * delta_along + delta_side * delta_side, 1e-30)
                inverse = lax.rsqrt(square)
                turn = (square * inverse) * (0.5 * width / math.pi)
                turn = turn - jnp.round(turn)
                value = turn * horner(SIN_FINE, turn * turn) * (inverse * (1.0 / width))
                taper_ref[start : start + ROWS, to : to + LANES] = value
                load_ref[start : start + ROWS, to : to + LANES] = jnp.where((row + place_shift == lane) & (place_chunk == to // LANES), LOAD, 0.0)


COS_FINE = (0.99999999, -19.7392045, 64.93911746, -85.45013953, 60.16763095, -25.96759925, 6.52865816)


def chunks(array):
    return [array[:, at : at + LANES] for at in range(0, array.shape[1], LANES)]


def lane_total(parts):
    return jnp.broadcast_to(jnp.sum(sum(parts[1:], parts[0]), axis=1, keepdims=True), parts[0].shape)


def sums(left, right):
    terms = list(zip(*left, *right))
    norm_left = lane_total([p_re * p_re + p_im * p_im for p_re, p_im, _, _ in terms])
    norm_right = lane_total([q_re * q_re + q_im * q_im for _, _, q_re, q_im in terms])
    gamma_re = lane_total([p_re * q_re + p_im * q_im for p_re, p_im, q_re, q_im in terms])
    gamma_im = lane_total([p_re * q_im - p_im * q_re for p_re, p_im, q_re, q_im in terms])
    spread = norm_right - norm_left
    inverse = lax.rsqrt(spread * spread + 4.0 * (gamma_re * gamma_re + gamma_im * gamma_im) + 1e-30)
    square = 0.5 + 0.5 * (jnp.abs(spread) * inverse)
    shrink = lax.rsqrt(square)
    factor = inverse * shrink
    return spread >= 0.0, square * shrink, factor * gamma_re, factor * gamma_im


def combine(left, right, left_re, left_im, right_re, right_im):
    terms = list(zip(*left, *right))
    return (
        [left_re * p_re - left_im * p_im + right_re * q_re - right_im * q_im for p_re, p_im, q_re, q_im in terms],
        [left_re * p_im + left_im * p_re + right_re * q_im + right_im * q_re for p_re, p_im, q_re, q_im in terms],
    )


def rotate_side(left, right, side, sign):
    rising, leading, b_re, b_im = sums(left, right)
    plain = jnp.where(rising, 1, 0) != side
    return combine(
        left,
        right,
        jnp.where(plain, leading, b_re),
        jnp.where(plain, 0.0, b_im),
        sign * jnp.where(plain, b_re, leading),
        sign * jnp.where(plain, -b_im, 0.0),
    )


def rotate_both(left, right):
    rising, leading, b_re, b_im = sums(left, right)
    new_left = combine(
        left,
        right,
        jnp.where(rising, leading, b_re),
        jnp.where(rising, 0.0, b_im),
        jnp.where(rising, -b_re, -leading),
        jnp.where(rising, b_im, 0.0),
    )
    new_right = combine(
        left,
        right,
        jnp.where(rising, b_re, leading),
        jnp.where(rising, b_im, 0.0),
        jnp.where(rising, leading, b_re),
        jnp.where(rising, 0.0, -b_im),
    )
    return new_left, new_right


def respond_kernel(
    order, blocks_ref, table_ref, taper_ref, load_ref, pick_ref, early_hbm, final_hbm, re_ref, im_ref, turn_ref, norm_ref, response_ref, semaphores
):
    block, depth = blocks_ref.shape[1:]
    half = block // 2
    everything = blocks_ref[...].reshape(-1, depth)

    numbers, lower_side, upper_side = neighbourhood(len(order))

    def block_rows(which):
        return blocks_ref[place_of(order, numbers[which])]

    near = dot(pick_ref[:block, :], jnp.concatenate([block_rows(0), block_rows(1)], axis=1), (1, 0))
    rows = jnp.concatenate([near[:, :depth], near[:, depth:], dot(pick_ref[block:, :], block_rows(2), (1, 0))], axis=0)
    sign = jnp.where(lax.broadcasted_iota(jnp.int32, rows.shape, 1) < depth // 2, 1.0, -1.0)
    turned = pltpu.roll(rows, depth // 2, 1) * sign
    parts = []
    starts = (block, 2 * block, 0)
    for at in starts:
        parts += [rows[at : at + block], turned[at : at + block]]
    tile = dot(jnp.concatenate(parts, axis=0).astype(jnp.bfloat16), everything, (1, 1))
    for i, at in enumerate(starts):
        taper = taper_ref[at : at + block, :]
        re_ref[at : at + block, :] = tile[2 * i * block : (2 * i + 1) * block] * taper + load_ref[at : at + block, :]
        im_ref[at : at + block, :] = tile[(2 * i + 1) * block : (2 * i + 2) * block] * taper

    def rows_at(start):
        return chunks(re_ref[start : start + GROUP, :]), chunks(im_ref[start : start + GROUP, :])

    def keep(which, start, column):
        turn_ref[which, start : start + GROUP, :] = jnp.concatenate(column[0], axis=1).astype(jnp.bfloat16)
        turn_ref[which, block + start : block + start + GROUP, :] = jnp.concatenate(column[1], axis=1).astype(jnp.bfloat16)
        norm_ref[which, start : start + GROUP, :] = 1.0 / lane_total([re * re + im * im for re, im in zip(*column)])

    def respond(which, projected):
        z_re = projected[:block, :BEAMS] + projected[block:, BEAMS:]
        z_im = projected[block:, :BEAMS] - projected[:block, BEAMS:]
        inverse = jnp.concatenate([norm_ref[which]] * (BEAMS // LANES), axis=1)
        response_ref[which] = (z_re * z_re + z_im * z_im) * inverse

    lower_sign = (2 * lower_side - 1).astype(jnp.float32)
    upper_sign = (2 * upper_side - 1).astype(jnp.float32)
    for at in range(0, half, GROUP):
        moved_top = rotate_side(rows_at(block + at), rows_at(block + half + at), lower_side, lower_sign)
        moved_bottom = rotate_side(rows_at(2 * block + at), rows_at(2 * block + half + at), upper_side, upper_sign)
        top, bottom = rotate_both(rows_at(at), rows_at(half + at))
        keep(0, at, top)
        keep(0, half + at, bottom)
        top, bottom = rotate_both(moved_top, moved_bottom)
        keep(1, at, top)
        keep(1, half + at, bottom)
    copies = []
    for which, result_hbm in enumerate((early_hbm, final_hbm)):
        respond(which, dot(turn_ref[which], table_ref[...], (1, 0)))
        for i in range(block // GROUP):
            rows = pl.ds(i * GROUP, GROUP)
            copies.append(pltpu.make_async_copy(response_ref.at[which, rows], result_hbm.at[rows], semaphores.at[which, i]))
            copies[-1].start()
    for copy in copies:
        copy.wait()


def send_order(peers):
    ends = [at // 2 if at % 2 == 0 else peers - 1 - at // 2 for at in range(peers)]
    return [peers // 2] + [peer for peer in ends if peer != peers // 2]


def pinned(array):
    return pltpu.with_memory_space_constraint(array, pltpu.HBM)


def per_device(spectra, valid_mask, pairing, positions, wavenumber):
    blocks = lax.axis_size("sens")
    block = valid_mask.shape[1]
    depth = spectra.shape[0]
    sensors = positions.shape[1]
    copies = pl.pallas_call(
        spread_kernel,
        out_shape=jax.ShapeDtypeStruct((blocks, block, depth), jnp.bfloat16),
        in_specs=[HBM, HBM],
        out_specs=HBM,
        scratch_shapes=[
            pltpu.VMEM((block, depth), spectra.dtype),
            pltpu.VMEM(valid_mask.shape, valid_mask.dtype),
            pltpu.VMEM((block, depth), jnp.bfloat16),
            pltpu.SemaphoreType.DMA((2,)),
            pltpu.SemaphoreType.DMA((blocks,)),
        ],
        compiler_params=small(2),
        name="spread",
    )(pinned(spectra.T), pinned(valid_mask))
    order = send_order(blocks)
    prepared = pl.pallas_call(
        functools.partial(prepare_kernel, block, order),
        out_shape=(
            jax.ShapeDtypeStruct((sensors, 2 * BEAMS), jnp.bfloat16),
            jax.ShapeDtypeStruct((3 * block, sensors), jnp.float32),
            jax.ShapeDtypeStruct((3 * block, sensors), jnp.float32),
            jax.ShapeDtypeStruct((2 * block, block), jnp.bfloat16),
        ),
        in_specs=[SMEM, HBM, HBM],
        out_specs=(VMEM, VMEM, VMEM, VMEM),
        scratch_shapes=[
            pltpu.SMEM(pairing.shape, pairing.dtype),
            pltpu.VMEM(positions.shape, positions.dtype),
            pltpu.SemaphoreType.DMA((2,)),
        ],
        compiler_params=small(4),
        name="prepare",
    )(wavenumber, pinned(pairing), pinned(positions))
    gathered = lax.all_to_all(copies, "sens", split_axis=0, concat_axis=0, axis_index_groups=[order])
    out = jax.ShapeDtypeStruct((block, BEAMS), jnp.float32)
    return pl.pallas_call(
        functools.partial(respond_kernel, order),
        out_shape=(out, out),
        in_specs=[VMEM, VMEM, VMEM, VMEM, VMEM],
        out_specs=(HBM, HBM),
        scratch_shapes=[
            pltpu.VMEM((3 * block, sensors), jnp.float32),
            pltpu.VMEM((3 * block, sensors), jnp.float32),
            pltpu.VMEM((2, 2 * block, sensors), jnp.bfloat16),
            pltpu.VMEM((2, block, LANES), jnp.float32),
            pltpu.VMEM((2, block, BEAMS), jnp.float32),
            pltpu.SemaphoreType.DMA((2, block // GROUP)),
        ],
        compiler_params=small(4 + sensors * block // 2**13),
        name="respond",
    )(gathered, *prepared)


def solution(mesh):
    in_specs = (P("bin", "sens"), P(None, "sens"), P(), P(), P("bin"))
    out_specs = (P("sens", "bin"), P("sens", "bin"))
    return jax.shard_map(
        per_device, mesh=mesh, in_specs=in_specs, out_specs=out_specs, check_vma=False
    )
```

```python
import functools
import math

import jax
import jax.numpy as jnp
from jax import lax
from jax.experimental import pallas as pl
from jax.experimental.pallas import tpu as pltpu
from jax.sharding import PartitionSpec as P

BEAMS = 256
LOAD = 0.5
LANES = 128
ROWS = 8
GROUP = 16
VMEM = pl.BlockSpec(memory_space=pltpu.VMEM)
SMEM = pl.BlockSpec(memory_space=pltpu.SMEM)
HBM = pl.BlockSpec(memory_space=pltpu.HBM)

COS = (0.99999921, -19.73898036, 64.92865742, -85.27162153, 58.79049212, -21.07110563)
SIN = (6.28318492, -41.34158923, 81.59994333, -76.61447253, 41.34288235, -12.47124354)
SIN_FINE = (6.2831853, -41.34170041, 81.60513139, -76.70301535, 42.02592699, -14.89984667, 3.23813751)


def small(mebibytes):
    return pltpu.CompilerParams(vmem_limit_bytes=mebibytes * 2**20)


def fetch(pairs, semaphores):
    copies = [pltpu.make_async_copy(*pair, semaphores.at[i]) for i, pair in enumerate(pairs)]
    for copy in copies:
        copy.start()
    for copy in copies:
        copy.wait()


def horner(coefficients, at):
    value = coefficients[-1]
    for coefficient in coefficients[-2::-1]:
        value = value * at + coefficient
    return value


def dot(left, right, contract):
    return lax.dot_general(left, right, ((contract[:1], contract[1:]), ((), ())), preferred_element_type=jnp.float32)


def spread_kernel(spectra_hbm, mask_hbm, copies_ref, spectra_ref, mask_ref, semaphores):
    fetch(((spectra_hbm, spectra_ref), (mask_hbm, mask_ref)), semaphores)
    segments, block = mask_ref.shape
    depth = spectra_ref.shape[1]
    row = lax.broadcasted_iota(jnp.int32, (segments, depth), 0)
    lane = lax.broadcasted_iota(jnp.int32, (segments, depth), 1)
    twice = jnp.where((row == lane) | (row + segments == lane), 1.0, 0.0)
    both = jnp.concatenate([twice, jnp.ones_like(twice)], axis=1).astype(jnp.bfloat16)
    result = dot(mask_ref[...].astype(jnp.float32).astype(jnp.bfloat16), both, (0, 0))
    validity, counts = result[:, :depth], result[:, depth:]
    scaled = (spectra_ref[...].astype(jnp.float32) * validity * lax.rsqrt(counts)).astype(jnp.bfloat16)
    for peer in range(copies_ref.shape[0]):
        copies_ref[peer] = scaled


def neighbourhood(peers):
    position = lax.axis_index("sens")
    numbers = position, jnp.maximum(position - 1, 0), jnp.minimum(position + 1, peers - 1)
    return numbers, jnp.where(position == 1, 1, 0), jnp.where(position < peers - 1, 1, 0)


def place_of(order, number):
    place = jnp.int32(0)
    for at, source in enumerate(order):
        place = jnp.where(number == source, at, place)
    return place


def prepare_kernel(
    block, order, wavenumber_ref, pairing_hbm, positions_hbm, table_ref, taper_ref, load_ref, pick_ref,
    pairing_ref, positions_ref, semaphores
):
    fetch(((pairing_hbm, pairing_ref), (positions_hbm, positions_ref)), semaphores)
    sensors = positions_ref.shape[1]
    half = block // 2
    width = 3.0 / block

    beam = lax.broadcasted_iota(jnp.int32, (ROWS, BEAMS), 1).astype(jnp.float32)
    turns = (beam + 0.5) * (0.5 / BEAMS)
    square = turns * turns
    cos_beam = horner(COS_FINE, square)
    sin_beam = turns * horner(SIN_FINE, square)
    scale = wavenumber_ref[0] * (0.5 / math.pi)
    for at in range(0, sensors, LANES):
        along, side = (
            jnp.transpose(jnp.broadcast_to(positions_ref[axis : axis + 1, at : at + LANES] * scale, (LANES, LANES)))
            for axis in (0, 1)
        )
        for row in range(0, LANES, GROUP):
            for lane in range(0, BEAMS, LANES):
                cos_part = cos_beam[:1, lane : lane + LANES]
                sin_part = sin_beam[:1, lane : lane + LANES]
                phase = along[row : row + GROUP] * cos_part + side[row : row + GROUP] * sin_part
                phase = phase - jnp.round(phase)
                square = phase * phase
                start = order.index((at + row) // block) * block + row % block
                rows = slice(start, start + GROUP)
                table_ref[rows, lane : lane + LANES] = horner(COS, square).astype(jnp.bfloat16)
                table_ref[rows, BEAMS + lane : BEAMS + lane + LANES] = (phase * horner(SIN, square)).astype(jnp.bfloat16)

    sub = lax.broadcasted_iota(jnp.int32, (ROWS, LANES), 0)
    lane = lax.broadcasted_iota(jnp.int32, (ROWS, LANES), 1)

    def column(numbers):
        value = jnp.zeros((ROWS, LANES), jnp.int32)
        for i, number in enumerate(numbers):
            value = jnp.where(sub == i, number, value)
        return value

    first, later = [], []
    for at in range(0, half, ROWS):
        first.append(sub + at)
        later.append(column([pairing_ref[1, at + i] for i in range(ROWS)]))
    for at in range(0, half, ROWS):
        first.append(column([half + pairing_ref[0, at + i] for i in range(ROWS)]))
        later.append(column([half + pairing_ref[0, pairing_ref[1, at + i]] for i in range(ROWS)]))
    for which, rows in enumerate((first, later)):
        for at in range(0, len(rows), 2):
            pair = jnp.concatenate(rows[at : at + 2], axis=0)
            lanes = jnp.concatenate([lane, lane], axis=0)
            start = which * block + at * ROWS
            pick_ref[start : start + GROUP, :] = jnp.where(pair == lanes, 1.0, 0.0)[:, :block].astype(jnp.bfloat16)

    arrived = jnp.concatenate([positions_ref[:, peer * block : (peer + 1) * block] for peer in order], axis=1)
    for which, (rows, number) in enumerate(zip((first, first, later), neighbourhood(len(order))[0])):
        chunk = number // (LANES // block)
        shift = (number - chunk * (LANES // block)) * block
        place = place_of(order, number)
        place_chunk = place // (LANES // block)
        place_shift = (place - place_chunk * (LANES // block)) * block
        for at, row in enumerate(rows):
            start = which * block + at * ROWS
            hit = row + shift == lane
            near = positions_ref[:, pl.ds(pl.multiple_of(chunk * LANES, LANES), LANES)]
            own_along = jnp.sum(jnp.where(hit, near[0:1], 0.0), axis=1, keepdims=True)
            own_side = jnp.sum(jnp.where(hit, near[1:2], 0.0), axis=1, keepdims=True)
            for to in range(0, sensors, LANES):
                delta_along = own_along - arrived[0:1, to : to + LANES]
                delta_side = own_side - arrived[1:2, to : to + LANES]
                square = jnp.maximum(delta_along * delta_along + delta_side * delta_side, 1e-30)
                inverse = lax.rsqrt(square)
                turn = (square * inverse) * (0.5 * width / math.pi)
                turn = turn - jnp.round(turn)
                value = turn * horner(SIN_FINE, turn * turn) * (inverse * (1.0 / width))
                taper_ref[start : start + ROWS, to : to + LANES] = value
                load_ref[start : start + ROWS, to : to + LANES] = jnp.where((row + place_shift == lane) & (place_chunk == to // LANES), LOAD, 0.0)


COS_FINE = (0.99999999, -19.7392045, 64.93911746, -85.45013953, 60.16763095, -25.96759925, 6.52865816)


def chunks(array):
    return [array[:, at : at + LANES] for at in range(0, array.shape[1], LANES)]


def lane_total(parts):
    return jnp.broadcast_to(jnp.sum(sum(parts[1:], parts[0]), axis=1, keepdims=True), parts[0].shape)


def sums(left, right):
    terms = list(zip(*left, *right))
    norm_left = lane_total([p_re * p_re + p_im * p_im for p_re, p_im, _, _ in terms])
    norm_right = lane_total([q_re * q_re + q_im * q_im for _, _, q_re, q_im in terms])
    gamma_re = lane_total([p_re * q_re + p_im * q_im for p_re, p_im, q_re, q_im in terms])
    gamma_im = lane_total([p_re * q_im - p_im * q_re for p_re, p_im, q_re, q_im in terms])
    spread = norm_right - norm_left
    inverse = lax.rsqrt(spread * spread + 4.0 * (gamma_re * gamma_re + gamma_im * gamma_im) + 1e-30)
    square = 0.5 + 0.5 * (jnp.abs(spread) * inverse)
    shrink = lax.rsqrt(square)
    factor = inverse * shrink
    return spread >= 0.0, square * shrink, factor * gamma_re, factor * gamma_im


def combine(left, right, left_re, left_im, right_re, right_im):
    terms = list(zip(*left, *right))
    return (
        [left_re * p_re - left_im * p_im + right_re * q_re - right_im * q_im for p_re, p_im, q_re, q_im in terms],
        [left_re * p_im + left_im * p_re + right_re * q_im + right_im * q_re for p_re, p_im, q_re, q_im in terms],
    )


def rotate_side(left, right, side, sign):
    rising, leading, b_re, b_im = sums(left, right)
    plain = jnp.where(rising, 1, 0) != side
    return combine(
        left,
        right,
        jnp.where(plain, leading, b_re),
        jnp.where(plain, 0.0, b_im),
        sign * jnp.where(plain, b_re, leading),
        sign * jnp.where(plain, -b_im, 0.0),
    )


def rotate_both(left, right):
    rising, leading, b_re, b_im = sums(left, right)
    new_left = combine(
        left,
        right,
        jnp.where(rising, leading, b_re),
        jnp.where(rising, 0.0, b_im),
        jnp.where(rising, -b_re, -leading),
        jnp.where(rising, b_im, 0.0),
    )
    new_right = combine(
        left,
        right,
        jnp.where(rising, b_re, leading),
        jnp.where(rising, b_im, 0.0),
        jnp.where(rising, leading, b_re),
        jnp.where(rising, 0.0, -b_im),
    )
    return new_left, new_right


def respond_kernel(
    order, blocks_ref, table_ref, taper_ref, load_ref, pick_ref, early_hbm, final_hbm, re_ref, im_ref, turn_ref, norm_ref, response_ref, semaphores
):
    block, depth = blocks_ref.shape[1:]
    half = block // 2
    everything = blocks_ref[...].reshape(-1, depth)

    numbers, lower_side, upper_side = neighbourhood(len(order))

    def block_rows(which):
        return blocks_ref[place_of(order, numbers[which])]

    near = dot(pick_ref[:block, :], jnp.concatenate([block_rows(0), block_rows(1)], axis=1), (1, 0))
    far = dot(pick_ref[block:, :], block_rows(2), (1, 0))
    rows = jnp.concatenate([near[:, depth:], far, near[:, :depth]], axis=0).astype(jnp.bfloat16)
    sign = jnp.where(lax.broadcasted_iota(jnp.int32, everything.shape, 1) < depth // 2, -1.0, 1.0)
    turned = (pltpu.roll(everything.astype(jnp.float32), depth // 2, 1) * sign).astype(jnp.bfloat16)
    tile_re = dot(rows, everything, (1, 1))
    tile_im = dot(rows, turned, (1, 1))
    for i, at in enumerate((block, 2 * block, 0)):
        taper = taper_ref[at : at + block, :]
        re_ref[at : at + block, :] = tile_re[i * block : (i + 1) * block] * taper + load_ref[at : at + block, :]
        im_ref[at : at + block, :] = tile_im[i * block : (i + 1) * block] * taper

    def rows_at(start):
        return chunks(re_ref[start : start + GROUP, :]), chunks(im_ref[start : start + GROUP, :])

    def keep(which, start, column):
        turn_ref[which, start : start + GROUP, :] = jnp.concatenate(column[0], axis=1).astype(jnp.bfloat16)
        turn_ref[which, block + start : block + start + GROUP, :] = jnp.concatenate(column[1], axis=1).astype(jnp.bfloat16)
        norm_ref[which, start : start + GROUP, :] = 1.0 / lane_total([re * re + im * im for re, im in zip(*column)])

    def respond(which, projected):
        z_re = projected[:block, :BEAMS] + projected[block:, BEAMS:]
        z_im = projected[block:, :BEAMS] - projected[:block, BEAMS:]
        inverse = jnp.concatenate([norm_ref[which]] * (BEAMS // LANES), axis=1)
        response_ref[which] = (z_re * z_re + z_im * z_im) * inverse

    lower_sign = (2 * lower_side - 1).astype(jnp.float32)
    upper_sign = (2 * upper_side - 1).astype(jnp.float32)
    for at in range(0, half, GROUP):
        moved_top = rotate_side(rows_at(block + at), rows_at(block + half + at), lower_side, lower_sign)
        moved_bottom = rotate_side(rows_at(2 * block + at), rows_at(2 * block + half + at), upper_side, upper_sign)
        top, bottom = rotate_both(rows_at(at), rows_at(half + at))
        keep(0, at, top)
        keep(0, half + at, bottom)
        top, bottom = rotate_both(moved_top, moved_bottom)
        keep(1, at, top)
        keep(1, half + at, bottom)
    copies = []
    for which, result_hbm in enumerate((early_hbm, final_hbm)):
        respond(which, dot(turn_ref[which], table_ref[...], (1, 0)))
        copies.append(pltpu.make_async_copy(response_ref.at[which], result_hbm, semaphores.at[which]))
        copies[-1].start()
    for copy in copies:
        copy.wait()


def send_order(peers):
    ends = [at // 2 if at % 2 == 0 else peers - 1 - at // 2 for at in range(peers)]
    return [peers // 2] + [peer for peer in ends if peer != peers // 2]


def pinned(array):
    return pltpu.with_memory_space_constraint(array, pltpu.HBM)


def per_device(spectra, valid_mask, pairing, positions, wavenumber):
    blocks = lax.axis_size("sens")
    block = valid_mask.shape[1]
    depth = spectra.shape[0]
    sensors = positions.shape[1]
    copies = pl.pallas_call(
        spread_kernel,
        out_shape=pltpu.VMEM((blocks, block, depth), jnp.bfloat16),
        in_specs=[HBM, HBM],
        out_specs=VMEM,
        scratch_shapes=[
            pltpu.VMEM((block, depth), spectra.dtype),
            pltpu.VMEM(valid_mask.shape, valid_mask.dtype),
            pltpu.SemaphoreType.DMA((2,)),
        ],
        compiler_params=small(2),
        name="spread",
    )(pinned(spectra.T), pinned(valid_mask))
    order = send_order(blocks)
    prepared = pl.pallas_call(
        functools.partial(prepare_kernel, block, order),
        out_shape=(
            jax.ShapeDtypeStruct((sensors, 2 * BEAMS), jnp.bfloat16),
            jax.ShapeDtypeStruct((3 * block, sensors), jnp.float32),
            jax.ShapeDtypeStruct((3 * block, sensors), jnp.float32),
            jax.ShapeDtypeStruct((2 * block, block), jnp.bfloat16),
        ),
        in_specs=[SMEM, HBM, HBM],
        out_specs=(VMEM, VMEM, VMEM, VMEM),
        scratch_shapes=[
            pltpu.SMEM(pairing.shape, pairing.dtype),
            pltpu.VMEM(positions.shape, positions.dtype),
            pltpu.SemaphoreType.DMA((2,)),
        ],
        compiler_params=small(4),
        name="prepare",
    )(wavenumber, pinned(pairing), pinned(positions))
    gathered = lax.all_to_all(copies, "sens", split_axis=0, concat_axis=0, axis_index_groups=[order])
    out = jax.ShapeDtypeStruct((block, BEAMS), jnp.float32)
    return pl.pallas_call(
        functools.partial(respond_kernel, order),
        out_shape=(out, out),
        in_specs=[VMEM, VMEM, VMEM, VMEM, VMEM],
        out_specs=(HBM, HBM),
        scratch_shapes=[
            pltpu.VMEM((3 * block, sensors), jnp.float32),
            pltpu.VMEM((3 * block, sensors), jnp.float32),
            pltpu.VMEM((2, 2 * block, sensors), jnp.bfloat16),
            pltpu.VMEM((2, block, LANES), jnp.float32),
            pltpu.VMEM((2, block, BEAMS), jnp.float32),
            pltpu.SemaphoreType.DMA((2,)),
        ],
        compiler_params=small(4 + sensors * block // 2**13),
        name="respond",
    )(gathered, *prepared)


def solution(mesh):
    in_specs = (P("bin", "sens"), P(None, "sens"), P(), P(), P("bin"))
    out_specs = (P("sens", "bin"), P("sens", "bin"))
    return jax.shard_map(
        per_device, mesh=mesh, in_specs=in_specs, out_specs=out_specs, check_vma=False
    )
```

```python
import functools
import math

import jax
import jax.numpy as jnp
from jax import lax
from jax.experimental import pallas as pl
from jax.experimental.pallas import tpu as pltpu
from jax.sharding import PartitionSpec as P

BEAMS = 256
LOAD = 0.5
LANES = 128
ROWS = 8
GROUP = 16
VMEM = pl.BlockSpec(memory_space=pltpu.VMEM)
SMEM = pl.BlockSpec(memory_space=pltpu.SMEM)
HBM = pl.BlockSpec(memory_space=pltpu.HBM)

COS = (0.99999921, -19.73898036, 64.92865742, -85.27162153, 58.79049212, -21.07110563)
SIN = (6.28318492, -41.34158923, 81.59994333, -76.61447253, 41.34288235, -12.47124354)
SIN_FINE = (6.2831853, -41.34170041, 81.60513139, -76.70301535, 42.02592699, -14.89984667, 3.23813751)


def small(mebibytes):
    return pltpu.CompilerParams(vmem_limit_bytes=mebibytes * 2**20)


def fetch(pairs, semaphores):
    copies = [pltpu.make_async_copy(*pair, semaphores.at[i]) for i, pair in enumerate(pairs)]
    for copy in copies:
        copy.start()
    for copy in copies:
        copy.wait()


def horner(coefficients, at):
    value = coefficients[-1]
    for coefficient in coefficients[-2::-1]:
        value = value * at + coefficient
    return value


def dot(left, right, contract):
    return lax.dot_general(left, right, ((contract[:1], contract[1:]), ((), ())), preferred_element_type=jnp.float32)


def spread_kernel(spectra_hbm, mask_hbm, copies_ref, spectra_ref, mask_ref, semaphores):
    fetch(((spectra_hbm, spectra_ref), (mask_hbm, mask_ref)), semaphores)
    segments, block = mask_ref.shape
    depth = spectra_ref.shape[1]
    row = lax.broadcasted_iota(jnp.int32, (segments, depth), 0)
    lane = lax.broadcasted_iota(jnp.int32, (segments, depth), 1)
    twice = jnp.where((row == lane) | (row + segments == lane), 1.0, 0.0)
    both = jnp.concatenate([twice, jnp.ones_like(twice)], axis=1).astype(jnp.bfloat16)
    result = dot(mask_ref[...].astype(jnp.float32).astype(jnp.bfloat16), both, (0, 0))
    validity, counts = result[:, :depth], result[:, depth:]
    scaled = (spectra_ref[...].astype(jnp.float32) * validity * lax.rsqrt(counts)).astype(jnp.bfloat16)
    for peer in range(copies_ref.shape[0]):
        copies_ref[peer] = scaled


def neighbourhood(peers):
    position = lax.axis_index("sens")
    numbers = position, jnp.maximum(position - 1, 0), jnp.minimum(position + 1, peers - 1)
    return numbers, jnp.where(position == 1, 1, 0), jnp.where(position < peers - 1, 1, 0)


def place_of(order, number):
    place = jnp.int32(0)
    for at, source in enumerate(order):
        place = jnp.where(number == source, at, place)
    return place


def prepare_kernel(
    block, order, wavenumber_ref, pairing_hbm, positions_hbm, table_ref, taper_ref, load_ref, pick_ref,
    pairing_ref, positions_ref, semaphores
):
    fetch(((pairing_hbm, pairing_ref), (positions_hbm, positions_ref)), semaphores)
    sensors = positions_ref.shape[1]
    half = block // 2
    width = 3.0 / block

    beam = lax.broadcasted_iota(jnp.int32, (ROWS, BEAMS), 1).astype(jnp.float32)
    turns = (beam + 0.5) * (0.5 / BEAMS)
    square = turns * turns
    cos_beam = horner(COS_FINE, square)
    sin_beam = turns * horner(SIN_FINE, square)
    scale = wavenumber_ref[0] * (0.5 / math.pi)
    for at in range(0, sensors, LANES):
        along, side = (
            jnp.transpose(jnp.broadcast_to(positions_ref[axis : axis + 1, at : at + LANES] * scale, (LANES, LANES)))
            for axis in (0, 1)
        )
        for row in range(0, LANES, GROUP):
            for lane in range(0, BEAMS, LANES):
                cos_part = cos_beam[:1, lane : lane + LANES]
                sin_part = sin_beam[:1, lane : lane + LANES]
                phase = along[row : row + GROUP] * cos_part + side[row : row + GROUP] * sin_part
                phase = phase - jnp.round(phase)
                square = phase * phase
                start = order.index((at + row) // block) * block + row % block
                rows = slice(start, start + GROUP)
                table_ref[rows, lane : lane + LANES] = horner(COS, square).astype(jnp.bfloat16)
                table_ref[rows, BEAMS + lane : BEAMS + lane + LANES] = (phase * horner(SIN, square)).astype(jnp.bfloat16)

    sub = lax.broadcasted_iota(jnp.int32, (ROWS, LANES), 0)
    lane = lax.broadcasted_iota(jnp.int32, (ROWS, LANES), 1)

    def column(numbers):
        value = jnp.zeros((ROWS, LANES), jnp.int32)
        for i, number in enumerate(numbers):
            value = jnp.where(sub == i, number, value)
        return value

    first, later = [], []
    for at in range(0, half, ROWS):
        first.append(sub + at)
        later.append(column([pairing_ref[1, at + i] for i in range(ROWS)]))
    for at in range(0, half, ROWS):
        first.append(column([half + pairing_ref[0, at + i] for i in range(ROWS)]))
        later.append(column([half + pairing_ref[0, pairing_ref[1, at + i]] for i in range(ROWS)]))
    for which, rows in enumerate((first, later)):
        for at in range(0, len(rows), 2):
            pair = jnp.concatenate(rows[at : at + 2], axis=0)
            lanes = jnp.concatenate([lane, lane], axis=0)
            start = which * block + at * ROWS
            pick_ref[start : start + GROUP, :] = jnp.where(pair == lanes, 1.0, 0.0)[:, :block].astype(jnp.bfloat16)

    arrived = jnp.concatenate([positions_ref[:, peer * block : (peer + 1) * block] for peer in order], axis=1)
    for which, (rows, number) in enumerate(zip((first, first, later), neighbourhood(len(order))[0])):
        chunk = number // (LANES // block)
        shift = (number - chunk * (LANES // block)) * block
        place = place_of(order, number)
        place_chunk = place // (LANES // block)
        place_shift = (place - place_chunk * (LANES // block)) * block
        for at, row in enumerate(rows):
            start = which * block + at * ROWS
            hit = row + shift == lane
            near = positions_ref[:, pl.ds(pl.multiple_of(chunk * LANES, LANES), LANES)]
            own_along = jnp.sum(jnp.where(hit, near[0:1], 0.0), axis=1, keepdims=True)
            own_side = jnp.sum(jnp.where(hit, near[1:2], 0.0), axis=1, keepdims=True)
            for to in range(0, sensors, LANES):
                delta_along = own_along - arrived[0:1, to : to + LANES]
                delta_side = own_side - arrived[1:2, to : to + LANES]
                square = jnp.maximum(delta_along * delta_along + delta_side * delta_side, 1e-30)
                inverse = lax.rsqrt(square)
                turn = (square * inverse) * (0.5 * width / math.pi)
                turn = turn - jnp.round(turn)
                value = turn * horner(SIN_FINE, turn * turn) * (inverse * (1.0 / width))
                taper_ref[start : start + ROWS, to : to + LANES] = value
                load_ref[start : start + ROWS, to : to + LANES] = jnp.where((row + place_shift == lane) & (place_chunk == to // LANES), LOAD, 0.0)


COS_FINE = (0.99999999, -19.7392045, 64.93911746, -85.45013953, 60.16763095, -25.96759925, 6.52865816)


def chunks(array):
    return [array[:, at : at + LANES] for at in range(0, array.shape[1], LANES)]


def lane_total(parts):
    return jnp.broadcast_to(jnp.sum(sum(parts[1:], parts[0]), axis=1, keepdims=True), parts[0].shape)


def sums(left, right):
    terms = list(zip(*left, *right))
    norm_left = lane_total([p_re * p_re + p_im * p_im for p_re, p_im, _, _ in terms])
    norm_right = lane_total([q_re * q_re + q_im * q_im for _, _, q_re, q_im in terms])
    gamma_re = lane_total([p_re * q_re + p_im * q_im for p_re, p_im, q_re, q_im in terms])
    gamma_im = lane_total([p_re * q_im - p_im * q_re for p_re, p_im, q_re, q_im in terms])
    spread = norm_right - norm_left
    inverse = lax.rsqrt(spread * spread + 4.0 * (gamma_re * gamma_re + gamma_im * gamma_im) + 1e-30)
    square = 0.5 + 0.5 * (jnp.abs(spread) * inverse)
    shrink = lax.rsqrt(square)
    factor = inverse * shrink
    return spread >= 0.0, square * shrink, factor * gamma_re, factor * gamma_im


def combine(left, right, left_re, left_im, right_re, right_im):
    terms = list(zip(*left, *right))
    return (
        [left_re * p_re - left_im * p_im + right_re * q_re - right_im * q_im for p_re, p_im, q_re, q_im in terms],
        [left_re * p_im + left_im * p_re + right_re * q_im + right_im * q_re for p_re, p_im, q_re, q_im in terms],
    )


def rotate_side(left, right, side, sign):
    rising, leading, b_re, b_im = sums(left, right)
    plain = jnp.where(rising, 1, 0) != side
    return combine(
        left,
        right,
        jnp.where(plain, leading, b_re),
        jnp.where(plain, 0.0, b_im),
        sign * jnp.where(plain, b_re, leading),
        sign * jnp.where(plain, -b_im, 0.0),
    )


def rotate_both(left, right):
    rising, leading, b_re, b_im = sums(left, right)
    new_left = combine(
        left,
        right,
        jnp.where(rising, leading, b_re),
        jnp.where(rising, 0.0, b_im),
        jnp.where(rising, -b_re, -leading),
        jnp.where(rising, b_im, 0.0),
    )
    new_right = combine(
        left,
        right,
        jnp.where(rising, b_re, leading),
        jnp.where(rising, b_im, 0.0),
        jnp.where(rising, leading, b_re),
        jnp.where(rising, 0.0, -b_im),
    )
    return new_left, new_right


def respond_kernel(
    order, blocks_ref, table_ref, taper_ref, load_ref, pick_ref, early_hbm, final_hbm, re_ref, im_ref, turn_ref, norm_ref, response_ref, semaphores
):
    block, depth = blocks_ref.shape[1:]
    half = block // 2
    everything = blocks_ref[...].reshape(-1, depth)

    numbers, lower_side, upper_side = neighbourhood(len(order))

    def block_rows(which):
        return blocks_ref[place_of(order, numbers[which])]

    near = dot(pick_ref[:block, :], jnp.concatenate([block_rows(0), block_rows(1)], axis=1), (1, 0))
    far = dot(pick_ref[block:, :], block_rows(2), (1, 0))
    rows = jnp.concatenate([near[:, depth:], far, near[:, :depth]], axis=0).astype(jnp.bfloat16)
    sign = jnp.where(lax.broadcasted_iota(jnp.int32, everything.shape, 1) < depth // 2, -1.0, 1.0)
    turned = (pltpu.roll(everything.astype(jnp.float32), depth // 2, 1) * sign).astype(jnp.bfloat16)
    tile_re = dot(rows, everything, (1, 1))
    tile_im = dot(rows, turned, (1, 1))
    for i, at in enumerate((block, 2 * block, 0)):
        taper = taper_ref[at : at + block, :]
        re_ref[at : at + block, :] = tile_re[i * block : (i + 1) * block] * taper + load_ref[at : at + block, :]
        im_ref[at : at + block, :] = tile_im[i * block : (i + 1) * block] * taper

    def rows_at(start):
        return chunks(re_ref[start : start + GROUP, :]), chunks(im_ref[start : start + GROUP, :])

    def keep(which, start, column):
        turn_ref[which, start : start + GROUP, :] = jnp.concatenate(column[0], axis=1).astype(jnp.bfloat16)
        turn_ref[which, block + start : block + start + GROUP, :] = jnp.concatenate(column[1], axis=1).astype(jnp.bfloat16)
        norm_ref[which, start : start + GROUP, :] = 1.0 / lane_total([re * re + im * im for re, im in zip(*column)])

    def respond(which, projected):
        z_re = projected[:block, :BEAMS] + projected[block:, BEAMS:]
        z_im = projected[block:, :BEAMS] - projected[:block, BEAMS:]
        inverse = jnp.concatenate([norm_ref[which]] * (BEAMS // LANES), axis=1)
        response_ref[which] = (z_re * z_re + z_im * z_im) * inverse

    lower_sign = (2 * lower_side - 1).astype(jnp.float32)
    upper_sign = (2 * upper_side - 1).astype(jnp.float32)
    for at in range(0, half, GROUP):
        moved_top = rotate_side(rows_at(block + at), rows_at(block + half + at), lower_side, lower_sign)
        moved_bottom = rotate_side(rows_at(2 * block + at), rows_at(2 * block + half + at), upper_side, upper_sign)
        top, bottom = rotate_both(rows_at(at), rows_at(half + at))
        keep(0, at, top)
        keep(0, half + at, bottom)
        top, bottom = rotate_both(moved_top, moved_bottom)
        keep(1, at, top)
        keep(1, half + at, bottom)
    copies = []
    for which, result_hbm in enumerate((early_hbm, final_hbm)):
        respond(which, dot(turn_ref[which], table_ref[...], (1, 0)))
        copies.append(pltpu.make_async_copy(response_ref.at[which], result_hbm, semaphores.at[which]))
        copies[-1].start()
    for copy in copies:
        copy.wait()


def send_order(peers):
    ends = [at // 2 if at % 2 == 0 else peers - 1 - at // 2 for at in range(peers)]
    return [peers - 2] + [peer for peer in ends if peer != peers - 2]


def pinned(array):
    return pltpu.with_memory_space_constraint(array, pltpu.HBM)


def per_device(spectra, valid_mask, pairing, positions, wavenumber):
    blocks = lax.axis_size("sens")
    block = valid_mask.shape[1]
    depth = spectra.shape[0]
    sensors = positions.shape[1]
    copies = pl.pallas_call(
        spread_kernel,
        out_shape=pltpu.VMEM((blocks, block, depth), jnp.bfloat16),
        in_specs=[HBM, HBM],
        out_specs=VMEM,
        scratch_shapes=[
            pltpu.VMEM((block, depth), spectra.dtype),
            pltpu.VMEM(valid_mask.shape, valid_mask.dtype),
            pltpu.SemaphoreType.DMA((2,)),
        ],
        compiler_params=small(2),
        name="spread",
    )(pinned(spectra.T), pinned(valid_mask))
    order = send_order(blocks)
    prepared = pl.pallas_call(
        functools.partial(prepare_kernel, block, order),
        out_shape=(
            jax.ShapeDtypeStruct((sensors, 2 * BEAMS), jnp.bfloat16),
            jax.ShapeDtypeStruct((3 * block, sensors), jnp.float32),
            jax.ShapeDtypeStruct((3 * block, sensors), jnp.float32),
            jax.ShapeDtypeStruct((2 * block, block), jnp.bfloat16),
        ),
        in_specs=[SMEM, HBM, HBM],
        out_specs=(VMEM, VMEM, VMEM, VMEM),
        scratch_shapes=[
            pltpu.SMEM(pairing.shape, pairing.dtype),
            pltpu.VMEM(positions.shape, positions.dtype),
            pltpu.SemaphoreType.DMA((2,)),
        ],
        compiler_params=small(4),
        name="prepare",
    )(wavenumber, pinned(pairing), pinned(positions))
    gathered = lax.all_to_all(copies, "sens", split_axis=0, concat_axis=0, axis_index_groups=[order])
    out = jax.ShapeDtypeStruct((block, BEAMS), jnp.float32)
    return pl.pallas_call(
        functools.partial(respond_kernel, order),
        out_shape=(out, out),
        in_specs=[VMEM, VMEM, VMEM, VMEM, VMEM],
        out_specs=(HBM, HBM),
        scratch_shapes=[
            pltpu.VMEM((3 * block, sensors), jnp.float32),
            pltpu.VMEM((3 * block, sensors), jnp.float32),
            pltpu.VMEM((2, 2 * block, sensors), jnp.bfloat16),
            pltpu.VMEM((2, block, LANES), jnp.float32),
            pltpu.VMEM((2, block, BEAMS), jnp.float32),
            pltpu.SemaphoreType.DMA((2,)),
        ],
        compiler_params=small(4 + sensors * block // 2**13),
        name="respond",
    )(gathered, *prepared)


def solution(mesh):
    in_specs = (P("bin", "sens"), P(None, "sens"), P(), P(), P("bin"))
    out_specs = (P("sens", "bin"), P("sens", "bin"))
    return jax.shard_map(
        per_device, mesh=mesh, in_specs=in_specs, out_specs=out_specs, check_vma=False
    )
```

```python
import functools
import math

import jax
import jax.numpy as jnp
from jax import lax
from jax.experimental import pallas as pl
from jax.experimental.pallas import tpu as pltpu
from jax.sharding import PartitionSpec as P

BEAMS = 256
LOAD = 0.5
LANES = 128
ROWS = 8
GROUP = 16
VMEM = pl.BlockSpec(memory_space=pltpu.VMEM)
SMEM = pl.BlockSpec(memory_space=pltpu.SMEM)
HBM = pl.BlockSpec(memory_space=pltpu.HBM)

COS = (0.99999921, -19.73898036, 64.92865742, -85.27162153, 58.79049212, -21.07110563)
SIN = (6.28318492, -41.34158923, 81.59994333, -76.61447253, 41.34288235, -12.47124354)
SIN_FINE = (6.2831853, -41.34170041, 81.60513139, -76.70301535, 42.02592699, -14.89984667, 3.23813751)


def small(mebibytes):
    return pltpu.CompilerParams(vmem_limit_bytes=mebibytes * 2**20)


def fetch(pairs, semaphores):
    copies = [pltpu.make_async_copy(*pair, semaphores.at[i]) for i, pair in enumerate(pairs)]
    for copy in copies:
        copy.start()
    for copy in copies:
        copy.wait()


def horner(coefficients, at):
    value = coefficients[-1]
    for coefficient in coefficients[-2::-1]:
        value = value * at + coefficient
    return value


def dot(left, right, contract):
    return lax.dot_general(left, right, ((contract[:1], contract[1:]), ((), ())), preferred_element_type=jnp.float32)


def spread_kernel(spectra_hbm, mask_hbm, copies_ref, spectra_ref, mask_ref, semaphores):
    fetch(((spectra_hbm, spectra_ref), (mask_hbm, mask_ref)), semaphores)
    segments, block = mask_ref.shape
    depth = spectra_ref.shape[1]
    row = lax.broadcasted_iota(jnp.int32, (segments, depth), 0)
    lane = lax.broadcasted_iota(jnp.int32, (segments, depth), 1)
    twice = jnp.where((row == lane) | (row + segments == lane), 1.0, 0.0)
    both = jnp.concatenate([twice, jnp.ones_like(twice)], axis=1).astype(jnp.bfloat16)
    result = dot(mask_ref[...].astype(jnp.float32).astype(jnp.bfloat16), both, (0, 0))
    validity, counts = result[:, :depth], result[:, depth:]
    scaled = (spectra_ref[...].astype(jnp.float32) * validity * lax.rsqrt(counts)).astype(jnp.bfloat16)
    for peer in range(copies_ref.shape[0]):
        copies_ref[peer] = scaled


def neighbourhood(peers):
    position = lax.axis_index("sens")
    numbers = position, jnp.maximum(position - 1, 0), jnp.minimum(position + 1, peers - 1)
    return numbers, jnp.where(position == 1, 1, 0), jnp.where(position < peers - 1, 1, 0)


def place_of(order, number):
    place = jnp.int32(0)
    for at, source in enumerate(order):
        place = jnp.where(number == source, at, place)
    return place


def prepare_kernel(
    block, order, wavenumber_ref, pairing_hbm, positions_hbm, table_ref, taper_ref, load_ref, pick_ref,
    pairing_ref, positions_ref, semaphores
):
    fetch(((pairing_hbm, pairing_ref), (positions_hbm, positions_ref)), semaphores)
    sensors = positions_ref.shape[1]
    half = block // 2
    width = 3.0 / block

    beam = lax.broadcasted_iota(jnp.int32, (ROWS, BEAMS), 1).astype(jnp.float32)
    turns = (beam + 0.5) * (0.5 / BEAMS)
    square = turns * turns
    cos_beam = horner(COS_FINE, square)
    sin_beam = turns * horner(SIN_FINE, square)
    scale = wavenumber_ref[0] * (0.5 / math.pi)
    for at in range(0, sensors, LANES):
        along, side = (
            jnp.transpose(jnp.broadcast_to(positions_ref[axis : axis + 1, at : at + LANES] * scale, (LANES, LANES)))
            for axis in (0, 1)
        )
        for row in range(0, LANES, GROUP):
            for lane in range(0, BEAMS, LANES):
                cos_part = cos_beam[:1, lane : lane + LANES]
                sin_part = sin_beam[:1, lane : lane + LANES]
                phase = along[row : row + GROUP] * cos_part + side[row : row + GROUP] * sin_part
                phase = phase - jnp.round(phase)
                square = phase * phase
                start = order.index((at + row) // block) * block + row % block
                rows = slice(start, start + GROUP)
                table_ref[rows, lane : lane + LANES] = horner(COS, square).astype(jnp.bfloat16)
                table_ref[rows, BEAMS + lane : BEAMS + lane + LANES] = (phase * horner(SIN, square)).astype(jnp.bfloat16)

    sub = lax.broadcasted_iota(jnp.int32, (ROWS, LANES), 0)
    lane = lax.broadcasted_iota(jnp.int32, (ROWS, LANES), 1)

    def column(numbers):
        value = jnp.zeros((ROWS, LANES), jnp.int32)
        for i, number in enumerate(numbers):
            value = jnp.where(sub == i, number, value)
        return value

    first, later = [], []
    for at in range(0, half, ROWS):
        first.append(sub + at)
        later.append(column([pairing_ref[1, at + i] for i in range(ROWS)]))
    for at in range(0, half, ROWS):
        first.append(column([half + pairing_ref[0, at + i] for i in range(ROWS)]))
        later.append(column([half + pairing_ref[0, pairing_ref[1, at + i]] for i in range(ROWS)]))
    for which, rows in enumerate((first, later)):
        for at in range(0, len(rows), 2):
            pair = jnp.concatenate(rows[at : at + 2], axis=0)
            lanes = jnp.concatenate([lane, lane], axis=0)
            start = which * block + at * ROWS
            pick_ref[start : start + GROUP, :] = jnp.where(pair == lanes, 1.0, 0.0)[:, :block].astype(jnp.bfloat16)

    arrived = jnp.concatenate([positions_ref[:, peer * block : (peer + 1) * block] for peer in order], axis=1)
    for which, (rows, number) in enumerate(zip((first, first, later), neighbourhood(len(order))[0])):
        chunk = number // (LANES // block)
        shift = (number - chunk * (LANES // block)) * block
        place = place_of(order, number)
        place_chunk = place // (LANES // block)
        place_shift = (place - place_chunk * (LANES // block)) * block
        for at, row in enumerate(rows):
            start = which * block + at * ROWS
            hit = row + shift == lane
            near = positions_ref[:, pl.ds(pl.multiple_of(chunk * LANES, LANES), LANES)]
            own_along = jnp.sum(jnp.where(hit, near[0:1], 0.0), axis=1, keepdims=True)
            own_side = jnp.sum(jnp.where(hit, near[1:2], 0.0), axis=1, keepdims=True)
            for to in range(0, sensors, LANES):
                delta_along = own_along - arrived[0:1, to : to + LANES]
                delta_side = own_side - arrived[1:2, to : to + LANES]
                square = jnp.maximum(delta_along * delta_along + delta_side * delta_side, 1e-30)
                inverse = lax.rsqrt(square)
                turn = (square * inverse) * (0.5 * width / math.pi)
                turn = turn - jnp.round(turn)
                value = turn * horner(SIN_FINE, turn * turn) * (inverse * (1.0 / width))
                taper_ref[start : start + ROWS, to : to + LANES] = value
                load_ref[start : start + ROWS, to : to + LANES] = jnp.where((row + place_shift == lane) & (place_chunk == to // LANES), LOAD, 0.0)


COS_FINE = (0.99999999, -19.7392045, 64.93911746, -85.45013953, 60.16763095, -25.96759925, 6.52865816)


def chunks(array):
    return [array[:, at : at + LANES] for at in range(0, array.shape[1], LANES)]


def lane_total(parts):
    return jnp.broadcast_to(jnp.sum(sum(parts[1:], parts[0]), axis=1, keepdims=True), parts[0].shape)


def sums(left, right):
    terms = list(zip(*left, *right))
    norm_left = lane_total([p_re * p_re + p_im * p_im for p_re, p_im, _, _ in terms])
    norm_right = lane_total([q_re * q_re + q_im * q_im for _, _, q_re, q_im in terms])
    gamma_re = lane_total([p_re * q_re + p_im * q_im for p_re, p_im, q_re, q_im in terms])
    gamma_im = lane_total([p_re * q_im - p_im * q_re for p_re, p_im, q_re, q_im in terms])
    spread = norm_right - norm_left
    inverse = lax.rsqrt(spread * spread + 4.0 * (gamma_re * gamma_re + gamma_im * gamma_im) + 1e-30)
    square = 0.5 + 0.5 * (jnp.abs(spread) * inverse)
    shrink = lax.rsqrt(square)
    factor = inverse * shrink
    return spread >= 0.0, square * shrink, factor * gamma_re, factor * gamma_im


def combine(left, right, left_re, left_im, right_re, right_im):
    terms = list(zip(*left, *right))
    return (
        [left_re * p_re - left_im * p_im + right_re * q_re - right_im * q_im for p_re, p_im, q_re, q_im in terms],
        [left_re * p_im + left_im * p_re + right_re * q_im + right_im * q_re for p_re, p_im, q_re, q_im in terms],
    )


def rotate_side(left, right, side, sign):
    rising, leading, b_re, b_im = sums(left, right)
    plain = jnp.where(rising, 1, 0) != side
    return combine(
        left,
        right,
        jnp.where(plain, leading, b_re),
        jnp.where(plain, 0.0, b_im),
        sign * jnp.where(plain, b_re, leading),
        sign * jnp.where(plain, -b_im, 0.0),
    )


def rotate_both(left, right):
    rising, leading, b_re, b_im = sums(left, right)
    new_left = combine(
        left,
        right,
        jnp.where(rising, leading, b_re),
        jnp.where(rising, 0.0, b_im),
        jnp.where(rising, -b_re, -leading),
        jnp.where(rising, b_im, 0.0),
    )
    new_right = combine(
        left,
        right,
        jnp.where(rising, b_re, leading),
        jnp.where(rising, b_im, 0.0),
        jnp.where(rising, leading, b_re),
        jnp.where(rising, 0.0, -b_im),
    )
    return new_left, new_right


def respond_kernel(
    order, blocks_ref, table_ref, taper_ref, load_ref, pick_ref, early_hbm, final_hbm, re_ref, im_ref, turn_ref, norm_ref, response_ref, semaphores
):
    block, depth = blocks_ref.shape[1:]
    half = block // 2
    everything = blocks_ref[...].reshape(-1, depth)

    numbers, lower_side, upper_side = neighbourhood(len(order))

    def block_rows(which):
        return blocks_ref[place_of(order, numbers[which])]

    near = dot(pick_ref[:block, :], jnp.concatenate([block_rows(0), block_rows(1)], axis=1), (1, 0))
    far = dot(pick_ref[block:, :], block_rows(2), (1, 0))
    rows = jnp.concatenate([near[:, depth:], far, near[:, :depth]], axis=0).astype(jnp.bfloat16)
    sign = jnp.where(lax.broadcasted_iota(jnp.int32, everything.shape, 1) < depth // 2, -1.0, 1.0)
    turned = (pltpu.roll(everything.astype(jnp.float32), depth // 2, 1) * sign).astype(jnp.bfloat16)
    tile_re = dot(rows, everything, (1, 1))
    tile_im = dot(rows, turned, (1, 1))
    for i, at in enumerate((block, 2 * block, 0)):
        taper = taper_ref[at : at + block, :]
        re_ref[at : at + block, :] = tile_re[i * block : (i + 1) * block] * taper + load_ref[at : at + block, :]
        im_ref[at : at + block, :] = tile_im[i * block : (i + 1) * block] * taper

    def rows_at(start):
        return chunks(re_ref[start : start + ROWS, :]), chunks(im_ref[start : start + ROWS, :])

    def keep(which, start, columns):
        for part, offset in ((0, 0), (1, block)):
            stacked = jnp.concatenate([jnp.concatenate(column[part], axis=1) for column in columns], axis=0)
            turn_ref[which, offset + start : offset + start + GROUP, :] = stacked.astype(jnp.bfloat16)
        for i, column in enumerate(columns):
            total = lane_total([re * re + im * im for re, im in zip(*column)])
            norm_ref[which, start + i * ROWS : start + (i + 1) * ROWS, :] = 1.0 / total

    def respond(which, projected):
        z_re = projected[:block, :BEAMS] + projected[block:, BEAMS:]
        z_im = projected[block:, :BEAMS] - projected[:block, BEAMS:]
        inverse = jnp.concatenate([norm_ref[which]] * (BEAMS // LANES), axis=1)
        response_ref[which] = (z_re * z_re + z_im * z_im) * inverse

    lower_sign = (2 * lower_side - 1).astype(jnp.float32)
    upper_sign = (2 * upper_side - 1).astype(jnp.float32)
    for at in range(0, half, GROUP):
        early, final = [], []
        for row in range(at, at + GROUP, ROWS):
            moved_top = rotate_side(rows_at(block + row), rows_at(block + half + row), lower_side, lower_sign)
            moved_bottom = rotate_side(rows_at(2 * block + row), rows_at(2 * block + half + row), upper_side, upper_sign)
            early.append(rotate_both(rows_at(row), rows_at(half + row)))
            final.append(rotate_both(moved_top, moved_bottom))
        for which, pairs in enumerate((early, final)):
            keep(which, at, [top for top, _ in pairs])
            keep(which, half + at, [bottom for _, bottom in pairs])
    copies = []
    for which, result_hbm in enumerate((early_hbm, final_hbm)):
        respond(which, dot(turn_ref[which], table_ref[...], (1, 0)))
        copies.append(pltpu.make_async_copy(response_ref.at[which], result_hbm, semaphores.at[which]))
        copies[-1].start()
    for copy in copies:
        copy.wait()


def send_order(peers):
    ends = [at // 2 if at % 2 == 0 else peers - 1 - at // 2 for at in range(peers)]
    return [peers // 2] + [peer for peer in ends if peer != peers // 2]


def pinned(array):
    return pltpu.with_memory_space_constraint(array, pltpu.HBM)


def per_device(spectra, valid_mask, pairing, positions, wavenumber):
    blocks = lax.axis_size("sens")
    block = valid_mask.shape[1]
    depth = spectra.shape[0]
    sensors = positions.shape[1]
    copies = pl.pallas_call(
        spread_kernel,
        out_shape=pltpu.VMEM((blocks, block, depth), jnp.bfloat16),
        in_specs=[HBM, HBM],
        out_specs=VMEM,
        scratch_shapes=[
            pltpu.VMEM((block, depth), spectra.dtype),
            pltpu.VMEM(valid_mask.shape, valid_mask.dtype),
            pltpu.SemaphoreType.DMA((2,)),
        ],
        compiler_params=small(2),
        name="spread",
    )(pinned(spectra.T), pinned(valid_mask))
    order = send_order(blocks)
    prepared = pl.pallas_call(
        functools.partial(prepare_kernel, block, order),
        out_shape=(
            jax.ShapeDtypeStruct((sensors, 2 * BEAMS), jnp.bfloat16),
            jax.ShapeDtypeStruct((3 * block, sensors), jnp.float32),
            jax.ShapeDtypeStruct((3 * block, sensors), jnp.float32),
            jax.ShapeDtypeStruct((2 * block, block), jnp.bfloat16),
        ),
        in_specs=[SMEM, HBM, HBM],
        out_specs=(VMEM, VMEM, VMEM, VMEM),
        scratch_shapes=[
            pltpu.SMEM(pairing.shape, pairing.dtype),
            pltpu.VMEM(positions.shape, positions.dtype),
            pltpu.SemaphoreType.DMA((2,)),
        ],
        compiler_params=small(4),
        name="prepare",
    )(wavenumber, pinned(pairing), pinned(positions))
    gathered = lax.all_to_all(copies, "sens", split_axis=0, concat_axis=0, axis_index_groups=[order])
    out = jax.ShapeDtypeStruct((block, BEAMS), jnp.float32)
    return pl.pallas_call(
        functools.partial(respond_kernel, order),
        out_shape=(out, out),
        in_specs=[VMEM, VMEM, VMEM, VMEM, VMEM],
        out_specs=(HBM, HBM),
        scratch_shapes=[
            pltpu.VMEM((3 * block, sensors), jnp.float32),
            pltpu.VMEM((3 * block, sensors), jnp.float32),
            pltpu.VMEM((2, 2 * block, sensors), jnp.bfloat16),
            pltpu.VMEM((2, block, LANES), jnp.float32),
            pltpu.VMEM((2, block, BEAMS), jnp.float32),
            pltpu.SemaphoreType.DMA((2,)),
        ],
        compiler_params=small(4 + sensors * block // 2**13),
        name="respond",
    )(gathered, *prepared)


def solution(mesh):
    in_specs = (P("bin", "sens"), P(None, "sens"), P(), P(), P("bin"))
    out_specs = (P("sens", "bin"), P("sens", "bin"))
    return jax.shard_map(
        per_device, mesh=mesh, in_specs=in_specs, out_specs=out_specs, check_vma=False
    )
```

```python
import functools
import math

import jax
import jax.numpy as jnp
from jax import lax
from jax.experimental import pallas as pl
from jax.experimental.pallas import tpu as pltpu
from jax.sharding import PartitionSpec as P

BEAMS = 256
LOAD = 0.5
LANES = 128
ROWS = 8
GROUP = 16
VMEM = pl.BlockSpec(memory_space=pltpu.VMEM)
SMEM = pl.BlockSpec(memory_space=pltpu.SMEM)
HBM = pl.BlockSpec(memory_space=pltpu.HBM)

COS = (0.99999921, -19.73898036, 64.92865742, -85.27162153, 58.79049212, -21.07110563)
SIN = (6.28318492, -41.34158923, 81.59994333, -76.61447253, 41.34288235, -12.47124354)
SIN_FINE = (6.2831853, -41.34170041, 81.60513139, -76.70301535, 42.02592699, -14.89984667, 3.23813751)


def small(mebibytes):
    return pltpu.CompilerParams(vmem_limit_bytes=mebibytes * 2**20)


def fetch(pairs, semaphores):
    copies = [pltpu.make_async_copy(*pair, semaphores.at[i]) for i, pair in enumerate(pairs)]
    for copy in copies:
        copy.start()
    for copy in copies:
        copy.wait()


def horner(coefficients, at):
    value = coefficients[-1]
    for coefficient in coefficients[-2::-1]:
        value = value * at + coefficient
    return value


def dot(left, right, contract):
    return lax.dot_general(left, right, ((contract[:1], contract[1:]), ((), ())), preferred_element_type=jnp.float32)


def spread_kernel(spectra_hbm, mask_hbm, copies_ref, spectra_ref, mask_ref, semaphores):
    fetch(((spectra_hbm, spectra_ref), (mask_hbm, mask_ref)), semaphores)
    segments, block = mask_ref.shape
    depth = spectra_ref.shape[1]
    row = lax.broadcasted_iota(jnp.int32, (segments, depth), 0)
    lane = lax.broadcasted_iota(jnp.int32, (segments, depth), 1)
    twice = jnp.where((row == lane) | (row + segments == lane), 1.0, 0.0)
    both = jnp.concatenate([twice, jnp.ones_like(twice)], axis=1).astype(jnp.bfloat16)
    result = dot(mask_ref[...].astype(jnp.float32).astype(jnp.bfloat16), both, (0, 0))
    validity, counts = result[:, :depth], result[:, depth:]
    scaled = (spectra_ref[...].astype(jnp.float32) * validity * lax.rsqrt(counts)).astype(jnp.bfloat16)
    for peer in range(copies_ref.shape[0]):
        copies_ref[peer] = scaled


def neighbourhood(peers):
    position = lax.axis_index("sens")
    numbers = position, jnp.maximum(position - 1, 0), jnp.minimum(position + 1, peers - 1)
    return numbers, jnp.where(position == 1, 1, 0), jnp.where(position < peers - 1, 1, 0)


def place_of(order, number):
    place = jnp.int32(0)
    for at, source in enumerate(order):
        place = jnp.where(number == source, at, place)
    return place


def prepare_kernel(
    block, order, wavenumber_ref, pairing_hbm, positions_hbm, table_ref, taper_ref, load_ref, pick_ref,
    pairing_ref, positions_ref, semaphores
):
    fetch(((pairing_hbm, pairing_ref), (positions_hbm, positions_ref)), semaphores)
    sensors = positions_ref.shape[1]
    half = block // 2
    width = 3.0 / block

    beam = lax.broadcasted_iota(jnp.int32, (ROWS, BEAMS), 1).astype(jnp.float32)
    turns = (beam + 0.5) * (0.5 / BEAMS)
    square = turns * turns
    cos_beam = horner(COS_FINE, square)
    sin_beam = turns * horner(SIN_FINE, square)
    scale = wavenumber_ref[0] * (0.5 / math.pi)
    for at in range(0, sensors, LANES):
        along, side = (
            jnp.transpose(jnp.broadcast_to(positions_ref[axis : axis + 1, at : at + LANES] * scale, (LANES, LANES)))
            for axis in (0, 1)
        )
        for row in range(0, LANES, GROUP):
            for lane in range(0, BEAMS, LANES):
                cos_part = cos_beam[:1, lane : lane + LANES]
                sin_part = sin_beam[:1, lane : lane + LANES]
                phase = along[row : row + GROUP] * cos_part + side[row : row + GROUP] * sin_part
                phase = phase - jnp.round(phase)
                square = phase * phase
                start = order.index((at + row) // block) * block + row % block
                rows = slice(start, start + GROUP)
                table_ref[rows, lane : lane + LANES] = horner(COS, square).astype(jnp.bfloat16)
                table_ref[rows, BEAMS + lane : BEAMS + lane + LANES] = (phase * horner(SIN, square)).astype(jnp.bfloat16)

    sub = lax.broadcasted_iota(jnp.int32, (ROWS, LANES), 0)
    lane = lax.broadcasted_iota(jnp.int32, (ROWS, LANES), 1)

    def column(numbers):
        value = jnp.zeros((ROWS, LANES), jnp.int32)
        for i, number in enumerate(numbers):
            value = jnp.where(sub == i, number, value)
        return value

    first, later = [], []
    for at in range(0, half, ROWS):
        first.append(sub + at)
        later.append(column([pairing_ref[1, at + i] for i in range(ROWS)]))
    for at in range(0, half, ROWS):
        first.append(column([half + pairing_ref[0, at + i] for i in range(ROWS)]))
        later.append(column([half + pairing_ref[0, pairing_ref[1, at + i]] for i in range(ROWS)]))
    for which, rows in enumerate((first, later)):
        for at in range(0, len(rows), 2):
            pair = jnp.concatenate(rows[at : at + 2], axis=0)
            lanes = jnp.concatenate([lane, lane], axis=0)
            start = which * block + at * ROWS
            pick_ref[start : start + GROUP, :] = jnp.where(pair == lanes, 1.0, 0.0)[:, :block].astype(jnp.bfloat16)

    arrived = jnp.concatenate([positions_ref[:, peer * block : (peer + 1) * block] for peer in order], axis=1)
    for which, (rows, number) in enumerate(zip((first, first, later), neighbourhood(len(order))[0])):
        chunk = number // (LANES // block)
        shift = (number - chunk * (LANES // block)) * block
        place = place_of(order, number)
        place_chunk = place // (LANES // block)
        place_shift = (place - place_chunk * (LANES // block)) * block
        for at, row in enumerate(rows):
            start = which * block + at * ROWS
            hit = row + shift == lane
            near = positions_ref[:, pl.ds(pl.multiple_of(chunk * LANES, LANES), LANES)]
            own_along = jnp.sum(jnp.where(hit, near[0:1], 0.0), axis=1, keepdims=True)
            own_side = jnp.sum(jnp.where(hit, near[1:2], 0.0), axis=1, keepdims=True)
            for to in range(0, sensors, LANES):
                delta_along = own_along - arrived[0:1, to : to + LANES]
                delta_side = own_side - arrived[1:2, to : to + LANES]
                square = jnp.maximum(delta_along * delta_along + delta_side * delta_side, 1e-30)
                inverse = lax.rsqrt(square)
                turn = (square * inverse) * (0.5 * width / math.pi)
                turn = turn - jnp.round(turn)
                value = turn * horner(SIN_FINE, turn * turn) * (inverse * (1.0 / width))
                taper_ref[start : start + ROWS, to : to + LANES] = value
                load_ref[start : start + ROWS, to : to + LANES] = jnp.where((row + place_shift == lane) & (place_chunk == to // LANES), LOAD, 0.0)


COS_FINE = (0.99999999, -19.7392045, 64.93911746, -85.45013953, 60.16763095, -25.96759925, 6.52865816)


def chunks(array):
    return [array[:, at : at + LANES] for at in range(0, array.shape[1], LANES)]


def lane_total(parts):
    return jnp.broadcast_to(jnp.sum(sum(parts[1:], parts[0]), axis=1, keepdims=True), parts[0].shape)


def sums(left, right):
    terms = list(zip(*left, *right))
    norm_left = lane_total([p_re * p_re + p_im * p_im for p_re, p_im, _, _ in terms])
    norm_right = lane_total([q_re * q_re + q_im * q_im for _, _, q_re, q_im in terms])
    gamma_re = lane_total([p_re * q_re + p_im * q_im for p_re, p_im, q_re, q_im in terms])
    gamma_im = lane_total([p_re * q_im - p_im * q_re for p_re, p_im, q_re, q_im in terms])
    spread = norm_right - norm_left
    inverse = lax.rsqrt(spread * spread + 4.0 * (gamma_re * gamma_re + gamma_im * gamma_im) + 1e-30)
    square = 0.5 + 0.5 * (jnp.abs(spread) * inverse)
    shrink = lax.rsqrt(square)
    factor = inverse * shrink
    return spread >= 0.0, square * shrink, factor * gamma_re, factor * gamma_im


def combine(left, right, left_re, left_im, right_re, right_im):
    terms = list(zip(*left, *right))
    return (
        [left_re * p_re - left_im * p_im + right_re * q_re - right_im * q_im for p_re, p_im, q_re, q_im in terms],
        [left_re * p_im + left_im * p_re + right_re * q_im + right_im * q_re for p_re, p_im, q_re, q_im in terms],
    )


def rotate_side(left, right, side, sign):
    rising, leading, b_re, b_im = sums(left, right)
    plain = jnp.where(rising, 1, 0) != side
    return combine(
        left,
        right,
        jnp.where(plain, leading, b_re),
        jnp.where(plain, 0.0, b_im),
        sign * jnp.where(plain, b_re, leading),
        sign * jnp.where(plain, -b_im, 0.0),
    )


def rotate_both(left, right):
    rising, leading, b_re, b_im = sums(left, right)
    new_left = combine(
        left,
        right,
        jnp.where(rising, leading, b_re),
        jnp.where(rising, 0.0, b_im),
        jnp.where(rising, -b_re, -leading),
        jnp.where(rising, b_im, 0.0),
    )
    new_right = combine(
        left,
        right,
        jnp.where(rising, b_re, leading),
        jnp.where(rising, b_im, 0.0),
        jnp.where(rising, leading, b_re),
        jnp.where(rising, 0.0, -b_im),
    )
    return new_left, new_right


def respond_kernel(
    orders, blocks_ref, table_ref, taper_ref, load_ref, pick_ref, early_hbm, final_hbm, all_ref, re_ref, im_ref, turn_ref, norm_ref, response_ref, semaphores
):
    block, depth = blocks_ref.shape[1:]
    half = block // 2
    odd = lax.axis_index("bin") % 2 == 1
    for at, (first, second) in enumerate(zip(*orders)):
        start = pl.multiple_of(jnp.where(odd, second, first) * block, block)
        all_ref[pl.ds(start, block), :] = blocks_ref[at]
    everything = all_ref[...]
    numbers, lower_side, upper_side = neighbourhood(blocks_ref.shape[0])

    def block_rows(which):
        return all_ref[pl.ds(pl.multiple_of(numbers[which] * block, block), block), :]

    near = dot(pick_ref[:block, :], jnp.concatenate([block_rows(0), block_rows(1)], axis=1), (1, 0))
    far = dot(pick_ref[block:, :], block_rows(2), (1, 0))
    rows = jnp.concatenate([near[:, depth:], far, near[:, :depth]], axis=0).astype(jnp.bfloat16)
    sign = jnp.where(lax.broadcasted_iota(jnp.int32, everything.shape, 1) < depth // 2, -1.0, 1.0)
    turned = (pltpu.roll(everything.astype(jnp.float32), depth // 2, 1) * sign).astype(jnp.bfloat16)
    tile_re = dot(rows, everything, (1, 1))
    tile_im = dot(rows, turned, (1, 1))
    for i, at in enumerate((block, 2 * block, 0)):
        taper = taper_ref[at : at + block, :]
        re_ref[at : at + block, :] = tile_re[i * block : (i + 1) * block] * taper + load_ref[at : at + block, :]
        im_ref[at : at + block, :] = tile_im[i * block : (i + 1) * block] * taper

    def rows_at(start):
        return chunks(re_ref[start : start + GROUP, :]), chunks(im_ref[start : start + GROUP, :])

    def keep(which, start, column):
        turn_ref[which, start : start + GROUP, :] = jnp.concatenate(column[0], axis=1).astype(jnp.bfloat16)
        turn_ref[which, block + start : block + start + GROUP, :] = jnp.concatenate(column[1], axis=1).astype(jnp.bfloat16)
        norm_ref[which, start : start + GROUP, :] = 1.0 / lane_total([re * re + im * im for re, im in zip(*column)])

    def respond(which, projected):
        z_re = projected[:block, :BEAMS] + projected[block:, BEAMS:]
        z_im = projected[block:, :BEAMS] - projected[:block, BEAMS:]
        inverse = jnp.concatenate([norm_ref[which]] * (BEAMS // LANES), axis=1)
        response_ref[which] = (z_re * z_re + z_im * z_im) * inverse

    lower_sign = (2 * lower_side - 1).astype(jnp.float32)
    upper_sign = (2 * upper_side - 1).astype(jnp.float32)
    for at in range(0, half, GROUP):
        moved_top = rotate_side(rows_at(block + at), rows_at(block + half + at), lower_side, lower_sign)
        moved_bottom = rotate_side(rows_at(2 * block + at), rows_at(2 * block + half + at), upper_side, upper_sign)
        top, bottom = rotate_both(rows_at(at), rows_at(half + at))
        keep(0, at, top)
        keep(0, half + at, bottom)
        top, bottom = rotate_both(moved_top, moved_bottom)
        keep(1, at, top)
        keep(1, half + at, bottom)
    copies = []
    for which, result_hbm in enumerate((early_hbm, final_hbm)):
        respond(which, dot(turn_ref[which], table_ref[...], (1, 0)))
        copies.append(pltpu.make_async_copy(response_ref.at[which], result_hbm, semaphores.at[which]))
        copies[-1].start()
    for copy in copies:
        copy.wait()


def send_orders(peers):
    middle = peers // 2
    ends = [at // 2 if at % 2 == 0 else peers - 1 - at // 2 for at in range(peers)]
    down = list(range(peers))[::-1]
    return tuple([middle] + [peer for peer in order if peer != middle] for order in (ends, down))


def pinned(array):
    return pltpu.with_memory_space_constraint(array, pltpu.HBM)


def per_device(spectra, valid_mask, pairing, positions, wavenumber):
    blocks = lax.axis_size("sens")
    block = valid_mask.shape[1]
    depth = spectra.shape[0]
    sensors = positions.shape[1]
    copies = pl.pallas_call(
        spread_kernel,
        out_shape=pltpu.VMEM((blocks, block, depth), jnp.bfloat16),
        in_specs=[HBM, HBM],
        out_specs=VMEM,
        scratch_shapes=[
            pltpu.VMEM((block, depth), spectra.dtype),
            pltpu.VMEM(valid_mask.shape, valid_mask.dtype),
            pltpu.SemaphoreType.DMA((2,)),
        ],
        compiler_params=small(2),
        name="spread",
    )(pinned(spectra.T), pinned(valid_mask))
    order, orders = list(range(blocks)), send_orders(blocks)
    groups = [[bin * blocks + peer for peer in orders[bin % 2]] for bin in range(lax.axis_size("bin"))]
    prepared = pl.pallas_call(
        functools.partial(prepare_kernel, block, order),
        out_shape=(
            jax.ShapeDtypeStruct((sensors, 2 * BEAMS), jnp.bfloat16),
            jax.ShapeDtypeStruct((3 * block, sensors), jnp.float32),
            jax.ShapeDtypeStruct((3 * block, sensors), jnp.float32),
            jax.ShapeDtypeStruct((2 * block, block), jnp.bfloat16),
        ),
        in_specs=[SMEM, HBM, HBM],
        out_specs=(VMEM, VMEM, VMEM, VMEM),
        scratch_shapes=[
            pltpu.SMEM(pairing.shape, pairing.dtype),
            pltpu.VMEM(positions.shape, positions.dtype),
            pltpu.SemaphoreType.DMA((2,)),
        ],
        compiler_params=small(4),
        name="prepare",
    )(wavenumber, pinned(pairing), pinned(positions))
    gathered = lax.all_to_all(copies, ("bin", "sens"), split_axis=0, concat_axis=0, axis_index_groups=groups)
    out = jax.ShapeDtypeStruct((block, BEAMS), jnp.float32)
    return pl.pallas_call(
        functools.partial(respond_kernel, orders),
        out_shape=(out, out),
        in_specs=[VMEM, VMEM, VMEM, VMEM, VMEM],
        out_specs=(HBM, HBM),
        scratch_shapes=[
            pltpu.VMEM((sensors, depth), jnp.bfloat16),
            pltpu.VMEM((3 * block, sensors), jnp.float32),
            pltpu.VMEM((3 * block, sensors), jnp.float32),
            pltpu.VMEM((2, 2 * block, sensors), jnp.bfloat16),
            pltpu.VMEM((2, block, LANES), jnp.float32),
            pltpu.VMEM((2, block, BEAMS), jnp.float32),
            pltpu.SemaphoreType.DMA((2,)),
        ],
        compiler_params=small(4 + sensors * block // 2**13),
        name="respond",
    )(gathered, *prepared)


def solution(mesh):
    in_specs = (P("bin", "sens"), P(None, "sens"), P(), P(), P("bin"))
    out_specs = (P("sens", "bin"), P("sens", "bin"))
    return jax.shard_map(
        per_device, mesh=mesh, in_specs=in_specs, out_specs=out_specs, check_vma=False
    )
```

```python
import functools
import math

import jax
import jax.numpy as jnp
from jax import lax
from jax.experimental import pallas as pl
from jax.experimental.pallas import tpu as pltpu
from jax.sharding import PartitionSpec as P

BEAMS = 256
LOAD = 0.5
LANES = 128
ROWS = 8
GROUP = 16
VMEM = pl.BlockSpec(memory_space=pltpu.VMEM)
SMEM = pl.BlockSpec(memory_space=pltpu.SMEM)
HBM = pl.BlockSpec(memory_space=pltpu.HBM)

COS = (0.99999921, -19.73898036, 64.92865742, -85.27162153, 58.79049212, -21.07110563)
SIN = (6.28318492, -41.34158923, 81.59994333, -76.61447253, 41.34288235, -12.47124354)
SIN_FINE = (6.2831853, -41.34170041, 81.60513139, -76.70301535, 42.02592699, -14.89984667, 3.23813751)


def small(mebibytes):
    return pltpu.CompilerParams(vmem_limit_bytes=mebibytes * 2**20)


def fetch(pairs, semaphores):
    copies = [pltpu.make_async_copy(*pair, semaphores.at[i]) for i, pair in enumerate(pairs)]
    for copy in copies:
        copy.start()
    for copy in copies:
        copy.wait()


def horner(coefficients, at):
    value = coefficients[-1]
    for coefficient in coefficients[-2::-1]:
        value = value * at + coefficient
    return value


def dot(left, right, contract):
    return lax.dot_general(left, right, ((contract[:1], contract[1:]), ((), ())), preferred_element_type=jnp.float32)


def spread_kernel(spectra_hbm, mask_hbm, copies_ref, spectra_ref, mask_ref, semaphores):
    fetch(((spectra_hbm, spectra_ref), (mask_hbm, mask_ref)), semaphores)
    segments, block = mask_ref.shape
    depth = spectra_ref.shape[1]
    row = lax.broadcasted_iota(jnp.int32, (segments, depth), 0)
    lane = lax.broadcasted_iota(jnp.int32, (segments, depth), 1)
    twice = jnp.where((row == lane) | (row + segments == lane), 1.0, 0.0)
    both = jnp.concatenate([twice, jnp.ones_like(twice)], axis=1).astype(jnp.bfloat16)
    result = dot(mask_ref[...].astype(jnp.float32).astype(jnp.bfloat16), both, (0, 0))
    validity, counts = result[:, :depth], result[:, depth:]
    scaled = (spectra_ref[...].astype(jnp.float32) * validity * lax.rsqrt(counts)).astype(jnp.bfloat16)
    for peer in range(copies_ref.shape[0]):
        copies_ref[peer] = scaled


def neighbourhood(peers):
    position = lax.axis_index("sens")
    numbers = position, jnp.maximum(position - 1, 0), jnp.minimum(position + 1, peers - 1)
    return numbers, jnp.where(position == 1, 1, 0), jnp.where(position < peers - 1, 1, 0)


def place_of(order, number):
    place = jnp.int32(0)
    for at, source in enumerate(order):
        place = jnp.where(number == source, at, place)
    return place


def prepare_kernel(
    block, order, wavenumber_ref, pairing_hbm, positions_hbm, table_ref, taper_ref, load_ref, pick_ref,
    pairing_ref, positions_ref, semaphores
):
    fetch(((pairing_hbm, pairing_ref), (positions_hbm, positions_ref)), semaphores)
    sensors = positions_ref.shape[1]
    half = block // 2
    width = 3.0 / block

    beam = lax.broadcasted_iota(jnp.int32, (ROWS, BEAMS), 1).astype(jnp.float32)
    turns = (beam + 0.5) * (0.5 / BEAMS)
    square = turns * turns
    cos_beam = horner(COS_FINE, square)
    sin_beam = turns * horner(SIN_FINE, square)
    scale = wavenumber_ref[0] * (0.5 / math.pi)
    for at in range(0, sensors, LANES):
        along, side = (
            jnp.transpose(jnp.broadcast_to(positions_ref[axis : axis + 1, at : at + LANES] * scale, (LANES, LANES)))
            for axis in (0, 1)
        )
        for row in range(0, LANES, GROUP):
            for lane in range(0, BEAMS, LANES):
                cos_part = cos_beam[:1, lane : lane + LANES]
                sin_part = sin_beam[:1, lane : lane + LANES]
                phase = along[row : row + GROUP] * cos_part + side[row : row + GROUP] * sin_part
                phase = phase - jnp.round(phase)
                square = phase * phase
                start = order.index((at + row) // block) * block + row % block
                rows = slice(start, start + GROUP)
                table_ref[rows, lane : lane + LANES] = horner(COS, square).astype(jnp.bfloat16)
                table_ref[rows, BEAMS + lane : BEAMS + lane + LANES] = (phase * horner(SIN, square)).astype(jnp.bfloat16)

    sub = lax.broadcasted_iota(jnp.int32, (ROWS, LANES), 0)
    lane = lax.broadcasted_iota(jnp.int32, (ROWS, LANES), 1)

    def column(numbers):
        value = jnp.zeros((ROWS, LANES), jnp.int32)
        for i, number in enumerate(numbers):
            value = jnp.where(sub == i, number, value)
        return value

    first, later = [], []
    for at in range(0, half, ROWS):
        first.append(sub + at)
        later.append(column([pairing_ref[1, at + i] for i in range(ROWS)]))
    for at in range(0, half, ROWS):
        first.append(column([half + pairing_ref[0, at + i] for i in range(ROWS)]))
        later.append(column([half + pairing_ref[0, pairing_ref[1, at + i]] for i in range(ROWS)]))
    for which, rows in enumerate((first, later)):
        for at in range(0, len(rows), 2):
            pair = jnp.concatenate(rows[at : at + 2], axis=0)
            lanes = jnp.concatenate([lane, lane], axis=0)
            start = which * block + at * ROWS
            pick_ref[start : start + GROUP, :] = jnp.where(pair == lanes, 1.0, 0.0)[:, :block].astype(jnp.bfloat16)

    arrived = jnp.concatenate([positions_ref[:, peer * block : (peer + 1) * block] for peer in order], axis=1)
    for which, (rows, number) in enumerate(zip((first, first, later), neighbourhood(len(order))[0])):
        chunk = number // (LANES // block)
        shift = (number - chunk * (LANES // block)) * block
        place = place_of(order, number)
        place_chunk = place // (LANES // block)
        place_shift = (place - place_chunk * (LANES // block)) * block
        for at, row in enumerate(rows):
            start = which * block + at * ROWS
            hit = row + shift == lane
            near = positions_ref[:, pl.ds(pl.multiple_of(chunk * LANES, LANES), LANES)]
            own_along = jnp.sum(jnp.where(hit, near[0:1], 0.0), axis=1, keepdims=True)
            own_side = jnp.sum(jnp.where(hit, near[1:2], 0.0), axis=1, keepdims=True)
            for to in range(0, sensors, LANES):
                delta_along = own_along - arrived[0:1, to : to + LANES]
                delta_side = own_side - arrived[1:2, to : to + LANES]
                square = jnp.maximum(delta_along * delta_along + delta_side * delta_side, 1e-30)
                inverse = lax.rsqrt(square)
                turn = (square * inverse) * (0.5 * width / math.pi)
                turn = turn - jnp.round(turn)
                value = turn * horner(SIN_FINE, turn * turn) * (inverse * (1.0 / width))
                taper_ref[start : start + ROWS, to : to + LANES] = value
                load_ref[start : start + ROWS, to : to + LANES] = jnp.where((row + place_shift == lane) & (place_chunk == to // LANES), LOAD, 0.0)


COS_FINE = (0.99999999, -19.7392045, 64.93911746, -85.45013953, 60.16763095, -25.96759925, 6.52865816)


def chunks(array):
    return [array[:, at : at + LANES] for at in range(0, array.shape[1], LANES)]


def lane_total(parts):
    return jnp.broadcast_to(jnp.sum(sum(parts[1:], parts[0]), axis=1, keepdims=True), parts[0].shape)


def sums(left, right):
    terms = list(zip(*left, *right))
    norm_left = lane_total([p_re * p_re + p_im * p_im for p_re, p_im, _, _ in terms])
    norm_right = lane_total([q_re * q_re + q_im * q_im for _, _, q_re, q_im in terms])
    gamma_re = lane_total([p_re * q_re + p_im * q_im for p_re, p_im, q_re, q_im in terms])
    gamma_im = lane_total([p_re * q_im - p_im * q_re for p_re, p_im, q_re, q_im in terms])
    spread = norm_right - norm_left
    inverse = lax.rsqrt(spread * spread + 4.0 * (gamma_re * gamma_re + gamma_im * gamma_im) + 1e-30)
    square = 0.5 + 0.5 * (jnp.abs(spread) * inverse)
    shrink = lax.rsqrt(square)
    factor = inverse * shrink
    return spread >= 0.0, square * shrink, factor * gamma_re, factor * gamma_im


def combine(left, right, left_re, left_im, right_re, right_im):
    terms = list(zip(*left, *right))
    return (
        [left_re * p_re - left_im * p_im + right_re * q_re - right_im * q_im for p_re, p_im, q_re, q_im in terms],
        [left_re * p_im + left_im * p_re + right_re * q_im + right_im * q_re for p_re, p_im, q_re, q_im in terms],
    )


def rotate_side(left, right, side, sign):
    rising, leading, b_re, b_im = sums(left, right)
    plain = jnp.where(rising, 1, 0) != side
    return combine(
        left,
        right,
        jnp.where(plain, leading, b_re),
        jnp.where(plain, 0.0, b_im),
        sign * jnp.where(plain, b_re, leading),
        sign * jnp.where(plain, -b_im, 0.0),
    )


def rotate_both(left, right):
    rising, leading, b_re, b_im = sums(left, right)
    new_left = combine(
        left,
        right,
        jnp.where(rising, leading, b_re),
        jnp.where(rising, 0.0, b_im),
        jnp.where(rising, -b_re, -leading),
        jnp.where(rising, b_im, 0.0),
    )
    new_right = combine(
        left,
        right,
        jnp.where(rising, b_re, leading),
        jnp.where(rising, b_im, 0.0),
        jnp.where(rising, leading, b_re),
        jnp.where(rising, 0.0, -b_im),
    )
    return new_left, new_right


def respond_kernel(
    order, blocks_ref, table_ref, taper_ref, load_ref, pick_ref, early_hbm, final_hbm, re_ref, im_ref, turn_ref, norm_ref, response_ref, semaphores
):
    block, depth = blocks_ref.shape[1:]
    half = block // 2
    everything = blocks_ref[...].reshape(-1, depth)

    numbers, lower_side, upper_side = neighbourhood(len(order))

    def block_rows(which):
        return blocks_ref[place_of(order, numbers[which])]

    near = dot(pick_ref[:block, :], jnp.concatenate([block_rows(0), block_rows(1)], axis=1), (1, 0))
    rows = jnp.concatenate([near[:, :depth], near[:, depth:], dot(pick_ref[block:, :], block_rows(2), (1, 0))], axis=0)
    sign = jnp.where(lax.broadcasted_iota(jnp.int32, rows.shape, 1) < depth // 2, 1.0, -1.0)
    turned = pltpu.roll(rows, depth // 2, 1) * sign
    parts = []
    starts = (block, 2 * block, 0)
    for at in starts:
        parts += [rows[at : at + block], turned[at : at + block]]
    tile = dot(jnp.concatenate(parts, axis=0).astype(jnp.bfloat16), everything, (1, 1))
    for i, at in enumerate(starts):
        taper = taper_ref[at : at + block, :]
        re_ref[at : at + block, :] = tile[2 * i * block : (2 * i + 1) * block] * taper + load_ref[at : at + block, :]
        im_ref[at : at + block, :] = tile[(2 * i + 1) * block : (2 * i + 2) * block] * taper

    def rows_at(start):
        return chunks(re_ref[start : start + GROUP, :]), chunks(im_ref[start : start + GROUP, :])

    def keep(which, start, column):
        turn_ref[which, start : start + GROUP, :] = jnp.concatenate(column[0], axis=1).astype(jnp.bfloat16)
        turn_ref[which, block + start : block + start + GROUP, :] = jnp.concatenate(column[1], axis=1).astype(jnp.bfloat16)
        norm_ref[which, start : start + GROUP, :] = 1.0 / lane_total([re * re + im * im for re, im in zip(*column)])

    def respond(which, projected):
        z_re = projected[:block, :BEAMS] + projected[block:, BEAMS:]
        z_im = projected[block:, :BEAMS] - projected[:block, BEAMS:]
        inverse = jnp.concatenate([norm_ref[which]] * (BEAMS // LANES), axis=1)
        response_ref[which] = (z_re * z_re + z_im * z_im) * inverse

    lower_sign = (2 * lower_side - 1).astype(jnp.float32)
    upper_sign = (2 * upper_side - 1).astype(jnp.float32)
    for at in range(0, half, GROUP):
        moved_top = rotate_side(rows_at(block + at), rows_at(block + half + at), lower_side, lower_sign)
        moved_bottom = rotate_side(rows_at(2 * block + at), rows_at(2 * block + half + at), upper_side, upper_sign)
        top, bottom = rotate_both(rows_at(at), rows_at(half + at))
        keep(0, at, top)
        keep(0, half + at, bottom)
        top, bottom = rotate_both(moved_top, moved_bottom)
        keep(1, at, top)
        keep(1, half + at, bottom)
    copies = []
    for which, result_hbm in enumerate((early_hbm, final_hbm)):
        respond(which, dot(turn_ref[which], table_ref[...], (1, 0)))
        copies.append(pltpu.make_async_copy(response_ref.at[which], result_hbm, semaphores.at[which]))
        copies[-1].start()
    for copy in copies:
        copy.wait()


def send_order(peers):
    root = peers // 2 + 1
    ends = [at // 2 if at % 2 == 0 else peers - 1 - at // 2 for at in range(peers)]
    return [root] + [peer for peer in ends if peer != root]


def pinned(array):
    return pltpu.with_memory_space_constraint(array, pltpu.HBM)


def per_device(spectra, valid_mask, pairing, positions, wavenumber):
    blocks = lax.axis_size("sens")
    block = valid_mask.shape[1]
    depth = spectra.shape[0]
    sensors = positions.shape[1]
    copies = pl.pallas_call(
        spread_kernel,
        out_shape=pltpu.VMEM((blocks, block, depth), jnp.bfloat16),
        in_specs=[HBM, HBM],
        out_specs=VMEM,
        scratch_shapes=[
            pltpu.VMEM((block, depth), spectra.dtype),
            pltpu.VMEM(valid_mask.shape, valid_mask.dtype),
            pltpu.SemaphoreType.DMA((2,)),
        ],
        compiler_params=small(2),
        name="spread",
    )(pinned(spectra.T), pinned(valid_mask))
    order = send_order(blocks)
    prepared = pl.pallas_call(
        functools.partial(prepare_kernel, block, order),
        out_shape=(
            jax.ShapeDtypeStruct((sensors, 2 * BEAMS), jnp.bfloat16),
            jax.ShapeDtypeStruct((3 * block, sensors), jnp.float32),
            jax.ShapeDtypeStruct((3 * block, sensors), jnp.float32),
            jax.ShapeDtypeStruct((2 * block, block), jnp.bfloat16),
        ),
        in_specs=[SMEM, HBM, HBM],
        out_specs=(VMEM, VMEM, VMEM, VMEM),
        scratch_shapes=[
            pltpu.SMEM(pairing.shape, pairing.dtype),
            pltpu.VMEM(positions.shape, positions.dtype),
            pltpu.SemaphoreType.DMA((2,)),
        ],
        compiler_params=small(4),
        name="prepare",
    )(wavenumber, pinned(pairing), pinned(positions))
    gathered = lax.all_to_all(copies, "sens", split_axis=0, concat_axis=0, axis_index_groups=[order])
    out = jax.ShapeDtypeStruct((block, BEAMS), jnp.float32)
    return pl.pallas_call(
        functools.partial(respond_kernel, order),
        out_shape=(out, out),
        in_specs=[VMEM, VMEM, VMEM, VMEM, VMEM],
        out_specs=(HBM, HBM),
        scratch_shapes=[
            pltpu.VMEM((3 * block, sensors), jnp.float32),
            pltpu.VMEM((3 * block, sensors), jnp.float32),
            pltpu.VMEM((2, 2 * block, sensors), jnp.bfloat16),
            pltpu.VMEM((2, block, LANES), jnp.float32),
            pltpu.VMEM((2, block, BEAMS), jnp.float32),
            pltpu.SemaphoreType.DMA((2,)),
        ],
        compiler_params=small(4 + sensors * block // 2**13),
        name="respond",
    )(gathered, *prepared)


def solution(mesh):
    in_specs = (P("bin", "sens"), P(None, "sens"), P(), P(), P("bin"))
    out_specs = (P("sens", "bin"), P("sens", "bin"))
    return jax.shard_map(
        per_device, mesh=mesh, in_specs=in_specs, out_specs=out_specs, check_vma=False
    )
```

```python
import functools
import math

import jax
import jax.numpy as jnp
from jax import lax
from jax.experimental import pallas as pl
from jax.experimental.pallas import tpu as pltpu
from jax.sharding import PartitionSpec as P

BEAMS = 256
LOAD = 0.5
LANES = 128
ROWS = 8
GROUP = 16
VMEM = pl.BlockSpec(memory_space=pltpu.VMEM)
SMEM = pl.BlockSpec(memory_space=pltpu.SMEM)
HBM = pl.BlockSpec(memory_space=pltpu.HBM)

COS = (0.99999921, -19.73898036, 64.92865742, -85.27162153, 58.79049212, -21.07110563)
SIN = (6.28318492, -41.34158923, 81.59994333, -76.61447253, 41.34288235, -12.47124354)
SIN_FINE = (6.2831853, -41.34170041, 81.60513139, -76.70301535, 42.02592699, -14.89984667, 3.23813751)


def small(mebibytes):
    return pltpu.CompilerParams(vmem_limit_bytes=mebibytes * 2**20)


def fetch(pairs, semaphores):
    copies = [pltpu.make_async_copy(*pair, semaphores.at[i]) for i, pair in enumerate(pairs)]
    for copy in copies:
        copy.start()
    for copy in copies:
        copy.wait()


def horner(coefficients, at):
    value = coefficients[-1]
    for coefficient in coefficients[-2::-1]:
        value = value * at + coefficient
    return value


def dot(left, right, contract):
    return lax.dot_general(left, right, ((contract[:1], contract[1:]), ((), ())), preferred_element_type=jnp.float32)


def spread_kernel(spectra_hbm, mask_hbm, copies_ref, spectra_ref, mask_ref, semaphores):
    fetch(((spectra_hbm, spectra_ref), (mask_hbm, mask_ref)), semaphores)
    segments, block = mask_ref.shape
    depth = spectra_ref.shape[1]
    row = lax.broadcasted_iota(jnp.int32, (segments, depth), 0)
    lane = lax.broadcasted_iota(jnp.int32, (segments, depth), 1)
    twice = jnp.where((row == lane) | (row + segments == lane), 1.0, 0.0)
    both = jnp.concatenate([twice, jnp.ones_like(twice)], axis=1).astype(jnp.bfloat16)
    result = dot(mask_ref[...].astype(jnp.float32).astype(jnp.bfloat16), both, (0, 0))
    validity, counts = result[:, :depth], result[:, depth:]
    scaled = (spectra_ref[...].astype(jnp.float32) * validity * lax.rsqrt(counts)).astype(jnp.bfloat16)
    copies_ref[...] = jnp.zeros_like(copies_ref)
    copies_ref[lax.axis_index("sens")] = scaled


def neighbourhood(peers):
    position = lax.axis_index("sens")
    numbers = position, jnp.maximum(position - 1, 0), jnp.minimum(position + 1, peers - 1)
    return numbers, jnp.where(position == 1, 1, 0), jnp.where(position < peers - 1, 1, 0)


def place_of(order, number):
    place = jnp.int32(0)
    for at, source in enumerate(order):
        place = jnp.where(number == source, at, place)
    return place


def prepare_kernel(
    block, order, wavenumber_ref, pairing_hbm, positions_hbm, table_ref, taper_ref, load_ref, pick_ref,
    pairing_ref, positions_ref, semaphores
):
    fetch(((pairing_hbm, pairing_ref), (positions_hbm, positions_ref)), semaphores)
    sensors = positions_ref.shape[1]
    half = block // 2
    width = 3.0 / block

    beam = lax.broadcasted_iota(jnp.int32, (ROWS, BEAMS), 1).astype(jnp.float32)
    turns = (beam + 0.5) * (0.5 / BEAMS)
    square = turns * turns
    cos_beam = horner(COS_FINE, square)
    sin_beam = turns * horner(SIN_FINE, square)
    scale = wavenumber_ref[0] * (0.5 / math.pi)
    for at in range(0, sensors, LANES):
        along, side = (
            jnp.transpose(jnp.broadcast_to(positions_ref[axis : axis + 1, at : at + LANES] * scale, (LANES, LANES)))
            for axis in (0, 1)
        )
        for row in range(0, LANES, GROUP):
            for lane in range(0, BEAMS, LANES):
                cos_part = cos_beam[:1, lane : lane + LANES]
                sin_part = sin_beam[:1, lane : lane + LANES]
                phase = along[row : row + GROUP] * cos_part + side[row : row + GROUP] * sin_part
                phase = phase - jnp.round(phase)
                square = phase * phase
                start = order.index((at + row) // block) * block + row % block
                rows = slice(start, start + GROUP)
                table_ref[rows, lane : lane + LANES] = horner(COS, square).astype(jnp.bfloat16)
                table_ref[rows, BEAMS + lane : BEAMS + lane + LANES] = (phase * horner(SIN, square)).astype(jnp.bfloat16)

    sub = lax.broadcasted_iota(jnp.int32, (ROWS, LANES), 0)
    lane = lax.broadcasted_iota(jnp.int32, (ROWS, LANES), 1)

    def column(numbers):
        value = jnp.zeros((ROWS, LANES), jnp.int32)
        for i, number in enumerate(numbers):
            value = jnp.where(sub == i, number, value)
        return value

    first, later = [], []
    for at in range(0, half, ROWS):
        first.append(sub + at)
        later.append(column([pairing_ref[1, at + i] for i in range(ROWS)]))
    for at in range(0, half, ROWS):
        first.append(column([half + pairing_ref[0, at + i] for i in range(ROWS)]))
        later.append(column([half + pairing_ref[0, pairing_ref[1, at + i]] for i in range(ROWS)]))
    for which, rows in enumerate((first, later)):
        for at in range(0, len(rows), 2):
            pair = jnp.concatenate(rows[at : at + 2], axis=0)
            lanes = jnp.concatenate([lane, lane], axis=0)
            start = which * block + at * ROWS
            pick_ref[start : start + GROUP, :] = jnp.where(pair == lanes, 1.0, 0.0)[:, :block].astype(jnp.bfloat16)

    arrived = jnp.concatenate([positions_ref[:, peer * block : (peer + 1) * block] for peer in order], axis=1)
    for which, (rows, number) in enumerate(zip((first, first, later), neighbourhood(len(order))[0])):
        chunk = number // (LANES // block)
        shift = (number - chunk * (LANES // block)) * block
        place = place_of(order, number)
        place_chunk = place // (LANES // block)
        place_shift = (place - place_chunk * (LANES // block)) * block
        for at, row in enumerate(rows):
            start = which * block + at * ROWS
            hit = row + shift == lane
            near = positions_ref[:, pl.ds(pl.multiple_of(chunk * LANES, LANES), LANES)]
            own_along = jnp.sum(jnp.where(hit, near[0:1], 0.0), axis=1, keepdims=True)
            own_side = jnp.sum(jnp.where(hit, near[1:2], 0.0), axis=1, keepdims=True)
            for to in range(0, sensors, LANES):
                delta_along = own_along - arrived[0:1, to : to + LANES]
                delta_side = own_side - arrived[1:2, to : to + LANES]
                square = jnp.maximum(delta_along * delta_along + delta_side * delta_side, 1e-30)
                inverse = lax.rsqrt(square)
                turn = (square * inverse) * (0.5 * width / math.pi)
                turn = turn - jnp.round(turn)
                value = turn * horner(SIN_FINE, turn * turn) * (inverse * (1.0 / width))
                taper_ref[start : start + ROWS, to : to + LANES] = value
                load_ref[start : start + ROWS, to : to + LANES] = jnp.where((row + place_shift == lane) & (place_chunk == to // LANES), LOAD, 0.0)


COS_FINE = (0.99999999, -19.7392045, 64.93911746, -85.45013953, 60.16763095, -25.96759925, 6.52865816)


def chunks(array):
    return [array[:, at : at + LANES] for at in range(0, array.shape[1], LANES)]


def lane_total(parts):
    return jnp.broadcast_to(jnp.sum(sum(parts[1:], parts[0]), axis=1, keepdims=True), parts[0].shape)


def sums(left, right):
    terms = list(zip(*left, *right))
    norm_left = lane_total([p_re * p_re + p_im * p_im for p_re, p_im, _, _ in terms])
    norm_right = lane_total([q_re * q_re + q_im * q_im for _, _, q_re, q_im in terms])
    gamma_re = lane_total([p_re * q_re + p_im * q_im for p_re, p_im, q_re, q_im in terms])
    gamma_im = lane_total([p_re * q_im - p_im * q_re for p_re, p_im, q_re, q_im in terms])
    spread = norm_right - norm_left
    inverse = lax.rsqrt(spread * spread + 4.0 * (gamma_re * gamma_re + gamma_im * gamma_im) + 1e-30)
    square = 0.5 + 0.5 * (jnp.abs(spread) * inverse)
    shrink = lax.rsqrt(square)
    factor = inverse * shrink
    return spread >= 0.0, square * shrink, factor * gamma_re, factor * gamma_im


def combine(left, right, left_re, left_im, right_re, right_im):
    terms = list(zip(*left, *right))
    return (
        [left_re * p_re - left_im * p_im + right_re * q_re - right_im * q_im for p_re, p_im, q_re, q_im in terms],
        [left_re * p_im + left_im * p_re + right_re * q_im + right_im * q_re for p_re, p_im, q_re, q_im in terms],
    )


def rotate_side(left, right, side, sign):
    rising, leading, b_re, b_im = sums(left, right)
    plain = jnp.where(rising, 1, 0) != side
    return combine(
        left,
        right,
        jnp.where(plain, leading, b_re),
        jnp.where(plain, 0.0, b_im),
        sign * jnp.where(plain, b_re, leading),
        sign * jnp.where(plain, -b_im, 0.0),
    )


def rotate_both(left, right):
    rising, leading, b_re, b_im = sums(left, right)
    new_left = combine(
        left,
        right,
        jnp.where(rising, leading, b_re),
        jnp.where(rising, 0.0, b_im),
        jnp.where(rising, -b_re, -leading),
        jnp.where(rising, b_im, 0.0),
    )
    new_right = combine(
        left,
        right,
        jnp.where(rising, b_re, leading),
        jnp.where(rising, b_im, 0.0),
        jnp.where(rising, leading, b_re),
        jnp.where(rising, 0.0, -b_im),
    )
    return new_left, new_right


def respond_kernel(
    order, blocks_ref, table_ref, taper_ref, load_ref, pick_ref, early_hbm, final_hbm, re_ref, im_ref, turn_ref, norm_ref, response_ref, semaphores
):
    block, depth = blocks_ref.shape[1:]
    half = block // 2
    everything = blocks_ref[...].reshape(-1, depth)

    numbers, lower_side, upper_side = neighbourhood(len(order))

    def block_rows(which):
        return blocks_ref[place_of(order, numbers[which])]

    near = dot(pick_ref[:block, :], jnp.concatenate([block_rows(0), block_rows(1)], axis=1), (1, 0))
    rows = jnp.concatenate([near[:, :depth], near[:, depth:], dot(pick_ref[block:, :], block_rows(2), (1, 0))], axis=0)
    sign = jnp.where(lax.broadcasted_iota(jnp.int32, rows.shape, 1) < depth // 2, 1.0, -1.0)
    turned = pltpu.roll(rows, depth // 2, 1) * sign
    parts = []
    starts = (block, 2 * block, 0)
    for at in starts:
        parts += [rows[at : at + block], turned[at : at + block]]
    tile = dot(jnp.concatenate(parts, axis=0).astype(jnp.bfloat16), everything, (1, 1))
    for i, at in enumerate(starts):
        taper = taper_ref[at : at + block, :]
        re_ref[at : at + block, :] = tile[2 * i * block : (2 * i + 1) * block] * taper + load_ref[at : at + block, :]
        im_ref[at : at + block, :] = tile[(2 * i + 1) * block : (2 * i + 2) * block] * taper

    def rows_at(start):
        return chunks(re_ref[start : start + GROUP, :]), chunks(im_ref[start : start + GROUP, :])

    def keep(which, start, column):
        turn_ref[which, start : start + GROUP, :] = jnp.concatenate(column[0], axis=1).astype(jnp.bfloat16)
        turn_ref[which, block + start : block + start + GROUP, :] = jnp.concatenate(column[1], axis=1).astype(jnp.bfloat16)
        norm_ref[which, start : start + GROUP, :] = 1.0 / lane_total([re * re + im * im for re, im in zip(*column)])

    def respond(which, projected):
        z_re = projected[:block, :BEAMS] + projected[block:, BEAMS:]
        z_im = projected[block:, :BEAMS] - projected[:block, BEAMS:]
        inverse = jnp.concatenate([norm_ref[which]] * (BEAMS // LANES), axis=1)
        response_ref[which] = (z_re * z_re + z_im * z_im) * inverse

    lower_sign = (2 * lower_side - 1).astype(jnp.float32)
    upper_sign = (2 * upper_side - 1).astype(jnp.float32)
    for at in range(0, half, GROUP):
        moved_top = rotate_side(rows_at(block + at), rows_at(block + half + at), lower_side, lower_sign)
        moved_bottom = rotate_side(rows_at(2 * block + at), rows_at(2 * block + half + at), upper_side, upper_sign)
        top, bottom = rotate_both(rows_at(at), rows_at(half + at))
        keep(0, at, top)
        keep(0, half + at, bottom)
        top, bottom = rotate_both(moved_top, moved_bottom)
        keep(1, at, top)
        keep(1, half + at, bottom)
    copies = []
    for which, result_hbm in enumerate((early_hbm, final_hbm)):
        respond(which, dot(turn_ref[which], table_ref[...], (1, 0)))
        copies.append(pltpu.make_async_copy(response_ref.at[which], result_hbm, semaphores.at[which]))
        copies[-1].start()
    for copy in copies:
        copy.wait()


def pinned(array):
    return pltpu.with_memory_space_constraint(array, pltpu.HBM)


def per_device(spectra, valid_mask, pairing, positions, wavenumber):
    blocks = lax.axis_size("sens")
    block = valid_mask.shape[1]
    depth = spectra.shape[0]
    sensors = positions.shape[1]
    copies = pl.pallas_call(
        spread_kernel,
        out_shape=pltpu.VMEM((blocks, block, depth), jnp.bfloat16),
        in_specs=[HBM, HBM],
        out_specs=VMEM,
        scratch_shapes=[
            pltpu.VMEM((block, depth), spectra.dtype),
            pltpu.VMEM(valid_mask.shape, valid_mask.dtype),
            pltpu.SemaphoreType.DMA((2,)),
        ],
        compiler_params=small(2),
        name="spread",
    )(pinned(spectra.T), pinned(valid_mask))
    order = list(range(blocks))
    prepared = pl.pallas_call(
        functools.partial(prepare_kernel, block, order),
        out_shape=(
            jax.ShapeDtypeStruct((sensors, 2 * BEAMS), jnp.bfloat16),
            jax.ShapeDtypeStruct((3 * block, sensors), jnp.float32),
            jax.ShapeDtypeStruct((3 * block, sensors), jnp.float32),
            jax.ShapeDtypeStruct((2 * block, block), jnp.bfloat16),
        ),
        in_specs=[SMEM, HBM, HBM],
        out_specs=(VMEM, VMEM, VMEM, VMEM),
        scratch_shapes=[
            pltpu.SMEM(pairing.shape, pairing.dtype),
            pltpu.VMEM(positions.shape, positions.dtype),
            pltpu.SemaphoreType.DMA((2,)),
        ],
        compiler_params=small(4),
        name="prepare",
    )(wavenumber, pinned(pairing), pinned(positions))
    gathered = lax.psum(copies, "sens")
    out = jax.ShapeDtypeStruct((block, BEAMS), jnp.float32)
    return pl.pallas_call(
        functools.partial(respond_kernel, order),
        out_shape=(out, out),
        in_specs=[VMEM, VMEM, VMEM, VMEM, VMEM],
        out_specs=(HBM, HBM),
        scratch_shapes=[
            pltpu.VMEM((3 * block, sensors), jnp.float32),
            pltpu.VMEM((3 * block, sensors), jnp.float32),
            pltpu.VMEM((2, 2 * block, sensors), jnp.bfloat16),
            pltpu.VMEM((2, block, LANES), jnp.float32),
            pltpu.VMEM((2, block, BEAMS), jnp.float32),
            pltpu.SemaphoreType.DMA((2,)),
        ],
        compiler_params=small(4 + sensors * block // 2**13),
        name="respond",
    )(gathered, *prepared)


def solution(mesh):
    in_specs = (P("bin", "sens"), P(None, "sens"), P(), P(), P("bin"))
    out_specs = (P("sens", "bin"), P("sens", "bin"))
    return jax.shard_map(
        per_device, mesh=mesh, in_specs=in_specs, out_specs=out_specs, check_vma=False
    )
```

```python
import functools
import math

import jax
import jax.numpy as jnp
from jax import lax
from jax.experimental import pallas as pl
from jax.experimental.pallas import tpu as pltpu
from jax.sharding import PartitionSpec as P

BEAMS = 256
LOAD = 0.5
LANES = 128
ROWS = 8
GROUP = 16
VMEM = pl.BlockSpec(memory_space=pltpu.VMEM)
SMEM = pl.BlockSpec(memory_space=pltpu.SMEM)
HBM = pl.BlockSpec(memory_space=pltpu.HBM)

COS = (0.99999921, -19.73898036, 64.92865742, -85.27162153, 58.79049212, -21.07110563)
SIN = (6.28318492, -41.34158923, 81.59994333, -76.61447253, 41.34288235, -12.47124354)
SIN_FINE = (6.2831853, -41.34170041, 81.60513139, -76.70301535, 42.02592699, -14.89984667, 3.23813751)


def small(mebibytes):
    return pltpu.CompilerParams(vmem_limit_bytes=mebibytes * 2**20)


def fetch(pairs, semaphores):
    copies = [pltpu.make_async_copy(*pair, semaphores.at[i]) for i, pair in enumerate(pairs)]
    for copy in copies:
        copy.start()
    for copy in copies:
        copy.wait()


def horner(coefficients, at):
    value = coefficients[-1]
    for coefficient in coefficients[-2::-1]:
        value = value * at + coefficient
    return value


def dot(left, right, contract):
    return lax.dot_general(left, right, ((contract[:1], contract[1:]), ((), ())), preferred_element_type=jnp.float32)


def spread_kernel(spectra_hbm, mask_hbm, copies_ref, spectra_ref, mask_ref, semaphores):
    fetch(((spectra_hbm, spectra_ref), (mask_hbm, mask_ref)), semaphores)
    segments, block = mask_ref.shape
    depth = spectra_ref.shape[1]
    row = lax.broadcasted_iota(jnp.int32, (segments, depth), 0)
    lane = lax.broadcasted_iota(jnp.int32, (segments, depth), 1)
    twice = jnp.where((row == lane) | (row + segments == lane), 1.0, 0.0)
    both = jnp.concatenate([twice, jnp.ones_like(twice)], axis=1).astype(jnp.bfloat16)
    result = dot(mask_ref[...].astype(jnp.float32).astype(jnp.bfloat16), both, (0, 0))
    validity, counts = result[:, :depth], result[:, depth:]
    scaled = (spectra_ref[...].astype(jnp.float32) * validity * lax.rsqrt(counts)).astype(jnp.bfloat16)
    for peer in range(copies_ref.shape[0]):
        copies_ref[peer] = scaled


def neighbourhood(peers):
    position = lax.axis_index("sens")
    numbers = position, jnp.maximum(position - 1, 0), jnp.minimum(position + 1, peers - 1)
    return numbers, jnp.where(position == 1, 1, 0), jnp.where(position < peers - 1, 1, 0)


def place_of(order, number):
    place = jnp.int32(0)
    for at, source in enumerate(order):
        place = jnp.where(number == source, at, place)
    return place


def prepare_kernel(
    block, order, wavenumber_ref, pairing_hbm, positions_hbm, table_ref, taper_ref, load_ref, pick_ref,
    pairing_ref, positions_ref, semaphores
):
    fetch(((pairing_hbm, pairing_ref), (positions_hbm, positions_ref)), semaphores)
    sensors = positions_ref.shape[1]
    half = block // 2
    width = 3.0 / block

    beam = lax.broadcasted_iota(jnp.int32, (ROWS, BEAMS), 1).astype(jnp.float32)
    turns = (beam + 0.5) * (0.5 / BEAMS)
    square = turns * turns
    cos_beam = horner(COS_FINE, square)
    sin_beam = turns * horner(SIN_FINE, square)
    scale = wavenumber_ref[0] * (0.5 / math.pi)
    for at in range(0, sensors, LANES):
        along, side = (
            jnp.transpose(jnp.broadcast_to(positions_ref[axis : axis + 1, at : at + LANES] * scale, (LANES, LANES)))
            for axis in (0, 1)
        )
        for row in range(0, LANES, GROUP):
            for lane in range(0, BEAMS, LANES):
                cos_part = cos_beam[:1, lane : lane + LANES]
                sin_part = sin_beam[:1, lane : lane + LANES]
                phase = along[row : row + GROUP] * cos_part + side[row : row + GROUP] * sin_part
                phase = phase - jnp.round(phase)
                square = phase * phase
                start = order.index((at + row) // block) * block + row % block
                rows = slice(start, start + GROUP)
                table_ref[rows, lane : lane + LANES] = horner(COS, square).astype(jnp.bfloat16)
                table_ref[rows, BEAMS + lane : BEAMS + lane + LANES] = (phase * horner(SIN, square)).astype(jnp.bfloat16)

    sub = lax.broadcasted_iota(jnp.int32, (ROWS, LANES), 0)
    lane = lax.broadcasted_iota(jnp.int32, (ROWS, LANES), 1)

    def column(numbers):
        value = jnp.zeros((ROWS, LANES), jnp.int32)
        for i, number in enumerate(numbers):
            value = jnp.where(sub == i, number, value)
        return value

    first, later = [], []
    for at in range(0, half, ROWS):
        first.append(sub + at)
        later.append(column([pairing_ref[1, at + i] for i in range(ROWS)]))
    for at in range(0, half, ROWS):
        first.append(column([half + pairing_ref[0, at + i] for i in range(ROWS)]))
        later.append(column([half + pairing_ref[0, pairing_ref[1, at + i]] for i in range(ROWS)]))
    for which, rows in enumerate((first, later)):
        for at in range(0, len(rows), 2):
            pair = jnp.concatenate(rows[at : at + 2], axis=0)
            lanes = jnp.concatenate([lane, lane], axis=0)
            start = which * block + at * ROWS
            pick_ref[start : start + GROUP, :] = jnp.where(pair == lanes, 1.0, 0.0)[:, :block].astype(jnp.bfloat16)

    arrived = jnp.concatenate([positions_ref[:, peer * block : (peer + 1) * block] for peer in order], axis=1)
    for which, (rows, number) in enumerate(zip((first, first, later), neighbourhood(len(order))[0])):
        chunk = number // (LANES // block)
        shift = (number - chunk * (LANES // block)) * block
        place = place_of(order, number)
        place_chunk = place // (LANES // block)
        place_shift = (place - place_chunk * (LANES // block)) * block
        for at, row in enumerate(rows):
            start = which * block + at * ROWS
            hit = row + shift == lane
            near = positions_ref[:, pl.ds(pl.multiple_of(chunk * LANES, LANES), LANES)]
            own_along = jnp.sum(jnp.where(hit, near[0:1], 0.0), axis=1, keepdims=True)
            own_side = jnp.sum(jnp.where(hit, near[1:2], 0.0), axis=1, keepdims=True)
            for to in range(0, sensors, LANES):
                delta_along = own_along - arrived[0:1, to : to + LANES]
                delta_side = own_side - arrived[1:2, to : to + LANES]
                square = jnp.maximum(delta_along * delta_along + delta_side * delta_side, 1e-30)
                inverse = lax.rsqrt(square)
                turn = (square * inverse) * (0.5 * width / math.pi)
                turn = turn - jnp.round(turn)
                value = turn * horner(SIN_FINE, turn * turn) * (inverse * (1.0 / width))
                taper_ref[start : start + ROWS, to : to + LANES] = value
                load_ref[start : start + ROWS, to : to + LANES] = jnp.where((row + place_shift == lane) & (place_chunk == to // LANES), LOAD, 0.0)


COS_FINE = (0.99999999, -19.7392045, 64.93911746, -85.45013953, 60.16763095, -25.96759925, 6.52865816)


def chunks(array):
    return [array[:, at : at + LANES] for at in range(0, array.shape[1], LANES)]


def lane_total(parts):
    return jnp.broadcast_to(jnp.sum(sum(parts[1:], parts[0]), axis=1, keepdims=True), parts[0].shape)


def sums(left, right):
    terms = list(zip(*left, *right))
    norm_left = lane_total([p_re * p_re + p_im * p_im for p_re, p_im, _, _ in terms])
    norm_right = lane_total([q_re * q_re + q_im * q_im for _, _, q_re, q_im in terms])
    gamma_re = lane_total([p_re * q_re + p_im * q_im for p_re, p_im, q_re, q_im in terms])
    gamma_im = lane_total([p_re * q_im - p_im * q_re for p_re, p_im, q_re, q_im in terms])
    spread = norm_right - norm_left
    inverse = lax.rsqrt(spread * spread + 4.0 * (gamma_re * gamma_re + gamma_im * gamma_im) + 1e-30)
    square = 0.5 + 0.5 * (jnp.abs(spread) * inverse)
    shrink = lax.rsqrt(square)
    factor = inverse * shrink
    return spread >= 0.0, square * shrink, factor * gamma_re, factor * gamma_im


def weights_of(left, right):
    rising, leading, b_re, b_im = sums(left, right)
    alpha = jnp.where(rising, b_re, leading), jnp.where(rising, b_im, 0.0)
    beta = jnp.where(rising, leading, b_re), jnp.where(rising, 0.0, -b_im)
    return alpha, beta


def combine(left, right, on_left, on_right):
    (p_scale, p_turn), (q_scale, q_turn) = on_left, on_right
    terms = list(zip(*left, *right))
    return (
        [p_scale * p_re - p_turn * p_im + q_scale * q_re - q_turn * q_im for p_re, p_im, q_re, q_im in terms],
        [p_scale * p_im + p_turn * p_re + q_scale * q_im + q_turn * q_re for p_re, p_im, q_re, q_im in terms],
    )


def smaller(alpha, beta):
    return (beta[0], -beta[1]), (-alpha[0], alpha[1])


def rotate_side(left, right, side):
    alpha, beta = weights_of(left, right)
    on_left, on_right = smaller(alpha, beta)
    chosen = [
        tuple(jnp.where(side == 1, large, small) for large, small in zip(*pair))
        for pair in ((alpha, on_left), (beta, on_right))
    ]
    return combine(left, right, *chosen)


def rotate_both(left, right):
    alpha, beta = weights_of(left, right)
    return combine(left, right, *smaller(alpha, beta)), combine(left, right, alpha, beta)


def respond_kernel(
    order, blocks_ref, table_ref, taper_ref, load_ref, pick_ref, early_hbm, final_hbm, turn_ref, norm_ref, response_ref, semaphores
):
    block, depth = blocks_ref.shape[1:]
    half = block // 2
    everything = blocks_ref[...].reshape(-1, depth)

    numbers, lower_side, upper_side = neighbourhood(len(order))

    def block_rows(which):
        return blocks_ref[place_of(order, numbers[which])]

    near = dot(pick_ref[:block, :], jnp.concatenate([block_rows(0), block_rows(1)], axis=1), (1, 0))
    rows = jnp.concatenate([near[:, :depth], near[:, depth:], dot(pick_ref[block:, :], block_rows(2), (1, 0))], axis=0)
    sign = jnp.where(lax.broadcasted_iota(jnp.int32, rows.shape, 1) < depth // 2, 1.0, -1.0)
    turned = pltpu.roll(rows, depth // 2, 1) * sign
    parts = []
    starts = (block, 2 * block, 0)
    for at in starts:
        parts += [rows[at : at + block], turned[at : at + block]]
    tile = dot(jnp.concatenate(parts, axis=0).astype(jnp.bfloat16), everything, (1, 1))
    columns = {}
    for i, at in enumerate(starts):
        taper = taper_ref[at : at + block, :]
        real = tile[2 * i * block : (2 * i + 1) * block] * taper + load_ref[at : at + block, :]
        columns[at] = real, tile[(2 * i + 1) * block : (2 * i + 2) * block] * taper

    def rows_at(start):
        row = start % block
        return tuple(chunks(part[row : row + GROUP, :]) for part in columns[start - row])

    def keep(which, start, column):
        turn_ref[which, start : start + GROUP, :] = jnp.concatenate(column[0], axis=1).astype(jnp.bfloat16)
        turn_ref[which, block + start : block + start + GROUP, :] = jnp.concatenate(column[1], axis=1).astype(jnp.bfloat16)
        norm_ref[which, start : start + GROUP, :] = 1.0 / lane_total([re * re + im * im for re, im in zip(*column)])

    def respond(which, projected):
        z_re = projected[:block, :BEAMS] + projected[block:, BEAMS:]
        z_im = projected[block:, :BEAMS] - projected[:block, BEAMS:]
        inverse = jnp.concatenate([norm_ref[which]] * (BEAMS // LANES), axis=1)
        response_ref[which] = (z_re * z_re + z_im * z_im) * inverse

    for at in range(0, half, GROUP):
        moved_top = rotate_side(rows_at(block + at), rows_at(block + half + at), lower_side)
        moved_bottom = rotate_side(rows_at(2 * block + at), rows_at(2 * block + half + at), upper_side)
        top, bottom = rotate_both(rows_at(at), rows_at(half + at))
        keep(0, at, top)
        keep(0, half + at, bottom)
        top, bottom = rotate_both(moved_top, moved_bottom)
        keep(1, at, top)
        keep(1, half + at, bottom)
    copies = []
    for which, result_hbm in enumerate((early_hbm, final_hbm)):
        respond(which, dot(turn_ref[which], table_ref[...], (1, 0)))
        copies.append(pltpu.make_async_copy(response_ref.at[which], result_hbm, semaphores.at[which]))
        copies[-1].start()
    for copy in copies:
        copy.wait()


def send_order(peers):
    ends = [at // 2 if at % 2 == 0 else peers - 1 - at // 2 for at in range(peers)]
    return [peers // 2] + [peer for peer in ends if peer != peers // 2]


def pinned(array):
    return pltpu.with_memory_space_constraint(array, pltpu.HBM)


def per_device(spectra, valid_mask, pairing, positions, wavenumber):
    blocks = lax.axis_size("sens")
    block = valid_mask.shape[1]
    depth = spectra.shape[0]
    sensors = positions.shape[1]
    copies = pl.pallas_call(
        spread_kernel,
        out_shape=pltpu.VMEM((blocks, block, depth), jnp.bfloat16),
        in_specs=[HBM, HBM],
        out_specs=VMEM,
        scratch_shapes=[
            pltpu.VMEM((block, depth), spectra.dtype),
            pltpu.VMEM(valid_mask.shape, valid_mask.dtype),
            pltpu.SemaphoreType.DMA((2,)),
        ],
        compiler_params=small(2),
        name="spread",
    )(pinned(spectra.T), pinned(valid_mask))
    order = send_order(blocks)
    prepared = pl.pallas_call(
        functools.partial(prepare_kernel, block, order),
        out_shape=(
            jax.ShapeDtypeStruct((sensors, 2 * BEAMS), jnp.bfloat16),
            jax.ShapeDtypeStruct((3 * block, sensors), jnp.float32),
            jax.ShapeDtypeStruct((3 * block, sensors), jnp.float32),
            jax.ShapeDtypeStruct((2 * block, block), jnp.bfloat16),
        ),
        in_specs=[SMEM, HBM, HBM],
        out_specs=(VMEM, VMEM, VMEM, VMEM),
        scratch_shapes=[
            pltpu.SMEM(pairing.shape, pairing.dtype),
            pltpu.VMEM(positions.shape, positions.dtype),
            pltpu.SemaphoreType.DMA((2,)),
        ],
        compiler_params=small(4),
        name="prepare",
    )(wavenumber, pinned(pairing), pinned(positions))
    gathered = lax.all_to_all(copies, "sens", split_axis=0, concat_axis=0, axis_index_groups=[order])
    out = jax.ShapeDtypeStruct((block, BEAMS), jnp.float32)
    return pl.pallas_call(
        functools.partial(respond_kernel, order),
        out_shape=(out, out),
        in_specs=[VMEM, VMEM, VMEM, VMEM, VMEM],
        out_specs=(HBM, HBM),
        scratch_shapes=[
            pltpu.VMEM((2, 2 * block, sensors), jnp.bfloat16),
            pltpu.VMEM((2, block, LANES), jnp.float32),
            pltpu.VMEM((2, block, BEAMS), jnp.float32),
            pltpu.SemaphoreType.DMA((2,)),
        ],
        compiler_params=small(4 + sensors * block // 2**13),
        name="respond",
    )(gathered, *prepared)


def solution(mesh):
    in_specs = (P("bin", "sens"), P(None, "sens"), P(), P(), P("bin"))
    out_specs = (P("sens", "bin"), P("sens", "bin"))
    return jax.shard_map(
        per_device, mesh=mesh, in_specs=in_specs, out_specs=out_specs, check_vma=False
    )
```

```python
import functools
import math

import jax
import jax.numpy as jnp
from jax import lax
from jax.experimental import pallas as pl
from jax.experimental.pallas import tpu as pltpu
from jax.sharding import PartitionSpec as P

BEAMS = 256
LOAD = 0.5
LANES = 128
ROWS = 8
GROUP = 16
VMEM = pl.BlockSpec(memory_space=pltpu.VMEM)
SMEM = pl.BlockSpec(memory_space=pltpu.SMEM)
HBM = pl.BlockSpec(memory_space=pltpu.HBM)

COS = (0.99999921, -19.73898036, 64.92865742, -85.27162153, 58.79049212, -21.07110563)
SIN = (6.28318492, -41.34158923, 81.59994333, -76.61447253, 41.34288235, -12.47124354)
SIN_FINE = (6.2831853, -41.34170041, 81.60513139, -76.70301535, 42.02592699, -14.89984667, 3.23813751)


def small(mebibytes):
    return pltpu.CompilerParams(vmem_limit_bytes=mebibytes * 2**20)


def fetch(pairs, semaphores):
    copies = [pltpu.make_async_copy(*pair, semaphores.at[i]) for i, pair in enumerate(pairs)]
    for copy in copies:
        copy.start()
    for copy in copies:
        copy.wait()


def horner(coefficients, at):
    value = coefficients[-1]
    for coefficient in coefficients[-2::-1]:
        value = value * at + coefficient
    return value


def dot(left, right, contract):
    return lax.dot_general(left, right, ((contract[:1], contract[1:]), ((), ())), preferred_element_type=jnp.float32)


def spread_kernel(spectra_hbm, mask_hbm, copies_ref, spectra_ref, mask_ref, semaphores):
    fetch(((spectra_hbm, spectra_ref), (mask_hbm, mask_ref)), semaphores)
    segments, block = mask_ref.shape
    depth = spectra_ref.shape[1]
    row = lax.broadcasted_iota(jnp.int32, (segments, depth), 0)
    lane = lax.broadcasted_iota(jnp.int32, (segments, depth), 1)
    twice = jnp.where((row == lane) | (row + segments == lane), 1.0, 0.0)
    both = jnp.concatenate([twice, jnp.ones_like(twice)], axis=1).astype(jnp.bfloat16)
    result = dot(mask_ref[...].astype(jnp.float32).astype(jnp.bfloat16), both, (0, 0))
    validity, counts = result[:, :depth], result[:, depth:]
    scaled = (spectra_ref[...].astype(jnp.float32) * validity * lax.rsqrt(counts)).astype(jnp.bfloat16)
    for peer in range(copies_ref.shape[0]):
        copies_ref[peer] = scaled


def neighbourhood(peers):
    position = lax.axis_index("sens")
    numbers = position, jnp.maximum(position - 1, 0), jnp.minimum(position + 1, peers - 1)
    return numbers, jnp.where(position == 1, 1, 0), jnp.where(position < peers - 1, 1, 0)


def place_of(order, number):
    place = jnp.int32(0)
    for at, source in enumerate(order):
        place = jnp.where(number == source, at, place)
    return place


def prepare_kernel(
    block, order, wavenumber_ref, pairing_hbm, positions_hbm, table_ref, taper_ref, load_ref, pick_ref,
    pairing_ref, positions_ref, semaphores
):
    fetch(((pairing_hbm, pairing_ref), (positions_hbm, positions_ref)), semaphores)
    sensors = positions_ref.shape[1]
    half = block // 2
    width = 3.0 / block

    beam = lax.broadcasted_iota(jnp.int32, (ROWS, BEAMS), 1).astype(jnp.float32)
    turns = (beam + 0.5) * (0.5 / BEAMS)
    square = turns * turns
    cos_beam = horner(COS_FINE, square)
    sin_beam = turns * horner(SIN_FINE, square)
    scale = wavenumber_ref[0] * (0.5 / math.pi)
    for at in range(0, sensors, LANES):
        along, side = (
            jnp.transpose(jnp.broadcast_to(positions_ref[axis : axis + 1, at : at + LANES] * scale, (LANES, LANES)))
            for axis in (0, 1)
        )
        for row in range(0, LANES, GROUP):
            for lane in range(0, BEAMS, LANES):
                cos_part = cos_beam[:1, lane : lane + LANES]
                sin_part = sin_beam[:1, lane : lane + LANES]
                phase = along[row : row + GROUP] * cos_part + side[row : row + GROUP] * sin_part
                phase = phase - jnp.round(phase)
                square = phase * phase
                start = order.index((at + row) // block) * block + row % block
                rows = slice(start, start + GROUP)
                table_ref[rows, lane : lane + LANES] = horner(COS, square).astype(jnp.bfloat16)
                table_ref[rows, BEAMS + lane : BEAMS + lane + LANES] = (phase * horner(SIN, square)).astype(jnp.bfloat16)

    sub = lax.broadcasted_iota(jnp.int32, (ROWS, LANES), 0)
    lane = lax.broadcasted_iota(jnp.int32, (ROWS, LANES), 1)

    def column(numbers):
        value = jnp.zeros((ROWS, LANES), jnp.int32)
        for i, number in enumerate(numbers):
            value = jnp.where(sub == i, number, value)
        return value

    first, later = [], []
    for at in range(0, half, ROWS):
        first.append(sub + at)
        later.append(column([pairing_ref[1, at + i] for i in range(ROWS)]))
    for at in range(0, half, ROWS):
        first.append(column([half + pairing_ref[0, at + i] for i in range(ROWS)]))
        later.append(column([half + pairing_ref[0, pairing_ref[1, at + i]] for i in range(ROWS)]))
    for which, rows in enumerate((first, later)):
        for at in range(0, len(rows), 2):
            pair = jnp.concatenate(rows[at : at + 2], axis=0)
            lanes = jnp.concatenate([lane, lane], axis=0)
            start = which * block + at * ROWS
            pick_ref[start : start + GROUP, :] = jnp.where(pair == lanes, 1.0, 0.0)[:, :block].astype(jnp.bfloat16)

    arrived = jnp.concatenate([positions_ref[:, peer * block : (peer + 1) * block] for peer in order], axis=1)
    for which, (rows, number) in enumerate(zip((first, first, later), neighbourhood(len(order))[0])):
        chunk = number // (LANES // block)
        shift = (number - chunk * (LANES // block)) * block
        place = place_of(order, number)
        place_chunk = place // (LANES // block)
        place_shift = (place - place_chunk * (LANES // block)) * block
        for at, row in enumerate(rows):
            start = which * block + at * ROWS
            hit = row + shift == lane
            near = positions_ref[:, pl.ds(pl.multiple_of(chunk * LANES, LANES), LANES)]
            own_along = jnp.sum(jnp.where(hit, near[0:1], 0.0), axis=1, keepdims=True)
            own_side = jnp.sum(jnp.where(hit, near[1:2], 0.0), axis=1, keepdims=True)
            for to in range(0, sensors, LANES):
                delta_along = own_along - arrived[0:1, to : to + LANES]
                delta_side = own_side - arrived[1:2, to : to + LANES]
                square = jnp.maximum(delta_along * delta_along + delta_side * delta_side, 1e-30)
                inverse = lax.rsqrt(square)
                turn = (square * inverse) * (0.5 * width / math.pi)
                turn = turn - jnp.round(turn)
                value = turn * horner(SIN_FINE, turn * turn) * (inverse * (1.0 / width))
                taper_ref[start : start + ROWS, to : to + LANES] = value
                load_ref[start : start + ROWS, to : to + LANES] = jnp.where((row + place_shift == lane) & (place_chunk == to // LANES), LOAD, 0.0)


COS_FINE = (0.99999999, -19.7392045, 64.93911746, -85.45013953, 60.16763095, -25.96759925, 6.52865816)


def chunks(array):
    return [array[:, at : at + LANES] for at in range(0, array.shape[1], LANES)]


def lane_total(parts):
    return jnp.broadcast_to(jnp.sum(sum(parts[1:], parts[0]), axis=1, keepdims=True), parts[0].shape)


def lane_totals(many):
    partial = jnp.concatenate([sum(parts[1:], parts[0]) for parts in many], axis=0)
    pieces = []
    for _ in range(3):
        pieces.append(partial.astype(jnp.bfloat16))
        partial = partial - pieces[-1].astype(jnp.float32)
    total = dot(jnp.concatenate(pieces, axis=1), jnp.ones((3 * LANES, LANES), jnp.bfloat16), (1, 0))
    return [total[at : at + GROUP] for at in range(0, total.shape[0], GROUP)]


def sums(left, right):
    terms = list(zip(*left, *right))
    norm_left, norm_right, gamma_re, gamma_im = lane_totals(
        [
            [p_re * p_re + p_im * p_im for p_re, p_im, _, _ in terms],
            [q_re * q_re + q_im * q_im for _, _, q_re, q_im in terms],
            [p_re * q_re + p_im * q_im for p_re, p_im, q_re, q_im in terms],
            [p_re * q_im - p_im * q_re for p_re, p_im, q_re, q_im in terms],
        ]
    )
    spread = norm_right - norm_left
    inverse = lax.rsqrt(spread * spread + 4.0 * (gamma_re * gamma_re + gamma_im * gamma_im) + 1e-30)
    square = 0.5 + 0.5 * (jnp.abs(spread) * inverse)
    shrink = lax.rsqrt(square)
    factor = inverse * shrink
    return spread >= 0.0, square * shrink, factor * gamma_re, factor * gamma_im


def weights_of(left, right):
    rising, leading, b_re, b_im = sums(left, right)
    alpha = jnp.where(rising, b_re, leading), jnp.where(rising, b_im, 0.0)
    beta = jnp.where(rising, leading, b_re), jnp.where(rising, 0.0, -b_im)
    return alpha, beta


def combine(left, right, on_left, on_right):
    (p_scale, p_turn), (q_scale, q_turn) = on_left, on_right
    terms = list(zip(*left, *right))
    return (
        [p_scale * p_re - p_turn * p_im + q_scale * q_re - q_turn * q_im for p_re, p_im, q_re, q_im in terms],
        [p_scale * p_im + p_turn * p_re + q_scale * q_im + q_turn * q_re for p_re, p_im, q_re, q_im in terms],
    )


def smaller(alpha, beta):
    return (beta[0], -beta[1]), (-alpha[0], alpha[1])


def rotate_side(left, right, side):
    alpha, beta = weights_of(left, right)
    on_left, on_right = smaller(alpha, beta)
    chosen = [
        tuple(jnp.where(side == 1, large, small) for large, small in zip(*pair))
        for pair in ((alpha, on_left), (beta, on_right))
    ]
    return combine(left, right, *chosen)


def rotate_both(left, right):
    alpha, beta = weights_of(left, right)
    return combine(left, right, *smaller(alpha, beta)), combine(left, right, alpha, beta)


def respond_kernel(
    order, blocks_ref, table_ref, taper_ref, load_ref, pick_ref, early_hbm, final_hbm, turn_ref, norm_ref, response_ref, semaphores
):
    block, depth = blocks_ref.shape[1:]
    half = block // 2
    everything = blocks_ref[...].reshape(-1, depth)

    numbers, lower_side, upper_side = neighbourhood(len(order))

    def block_rows(which):
        return blocks_ref[place_of(order, numbers[which])]

    near = dot(pick_ref[:block, :], jnp.concatenate([block_rows(0), block_rows(1)], axis=1), (1, 0))
    rows = jnp.concatenate([near[:, :depth], near[:, depth:], dot(pick_ref[block:, :], block_rows(2), (1, 0))], axis=0)
    sign = jnp.where(lax.broadcasted_iota(jnp.int32, rows.shape, 1) < depth // 2, 1.0, -1.0)
    turned = pltpu.roll(rows, depth // 2, 1) * sign
    parts = []
    starts = (block, 2 * block, 0)
    for at in starts:
        parts += [rows[at : at + block], turned[at : at + block]]
    tile = dot(jnp.concatenate(parts, axis=0).astype(jnp.bfloat16), everything, (1, 1))
    columns = {}
    for i, at in enumerate(starts):
        taper = taper_ref[at : at + block, :]
        real = tile[2 * i * block : (2 * i + 1) * block] * taper + load_ref[at : at + block, :]
        columns[at] = real, tile[(2 * i + 1) * block : (2 * i + 2) * block] * taper

    def rows_at(start):
        row = start % block
        return tuple(chunks(part[row : row + GROUP, :]) for part in columns[start - row])

    def keep(which, start, column):
        turn_ref[which, start : start + GROUP, :] = jnp.concatenate(column[0], axis=1).astype(jnp.bfloat16)
        turn_ref[which, block + start : block + start + GROUP, :] = jnp.concatenate(column[1], axis=1).astype(jnp.bfloat16)
        norm_ref[which, start : start + GROUP, :] = 1.0 / lane_total([re * re + im * im for re, im in zip(*column)])

    def respond(which, projected):
        z_re = projected[:block, :BEAMS] + projected[block:, BEAMS:]
        z_im = projected[block:, :BEAMS] - projected[:block, BEAMS:]
        inverse = jnp.concatenate([norm_ref[which]] * (BEAMS // LANES), axis=1)
        response_ref[which] = (z_re * z_re + z_im * z_im) * inverse

    for at in range(0, half, GROUP):
        moved_top = rotate_side(rows_at(block + at), rows_at(block + half + at), lower_side)
        moved_bottom = rotate_side(rows_at(2 * block + at), rows_at(2 * block + half + at), upper_side)
        top, bottom = rotate_both(rows_at(at), rows_at(half + at))
        keep(0, at, top)
        keep(0, half + at, bottom)
        top, bottom = rotate_both(moved_top, moved_bottom)
        keep(1, at, top)
        keep(1, half + at, bottom)
    copies = []
    for which, result_hbm in enumerate((early_hbm, final_hbm)):
        respond(which, dot(turn_ref[which], table_ref[...], (1, 0)))
        copies.append(pltpu.make_async_copy(response_ref.at[which], result_hbm, semaphores.at[which]))
        copies[-1].start()
    for copy in copies:
        copy.wait()


def send_order(peers):
    ends = [at // 2 if at % 2 == 0 else peers - 1 - at // 2 for at in range(peers)]
    return [peers // 2] + [peer for peer in ends if peer != peers // 2]


def pinned(array):
    return pltpu.with_memory_space_constraint(array, pltpu.HBM)


def per_device(spectra, valid_mask, pairing, positions, wavenumber):
    blocks = lax.axis_size("sens")
    block = valid_mask.shape[1]
    depth = spectra.shape[0]
    sensors = positions.shape[1]
    copies = pl.pallas_call(
        spread_kernel,
        out_shape=pltpu.VMEM((blocks, block, depth), jnp.bfloat16),
        in_specs=[HBM, HBM],
        out_specs=VMEM,
        scratch_shapes=[
            pltpu.VMEM((block, depth), spectra.dtype),
            pltpu.VMEM(valid_mask.shape, valid_mask.dtype),
            pltpu.SemaphoreType.DMA((2,)),
        ],
        compiler_params=small(2),
        name="spread",
    )(pinned(spectra.T), pinned(valid_mask))
    order = send_order(blocks)
    prepared = pl.pallas_call(
        functools.partial(prepare_kernel, block, order),
        out_shape=(
            jax.ShapeDtypeStruct((sensors, 2 * BEAMS), jnp.bfloat16),
            jax.ShapeDtypeStruct((3 * block, sensors), jnp.float32),
            jax.ShapeDtypeStruct((3 * block, sensors), jnp.float32),
            jax.ShapeDtypeStruct((2 * block, block), jnp.bfloat16),
        ),
        in_specs=[SMEM, HBM, HBM],
        out_specs=(VMEM, VMEM, VMEM, VMEM),
        scratch_shapes=[
            pltpu.SMEM(pairing.shape, pairing.dtype),
            pltpu.VMEM(positions.shape, positions.dtype),
            pltpu.SemaphoreType.DMA((2,)),
        ],
        compiler_params=small(4),
        name="prepare",
    )(wavenumber, pinned(pairing), pinned(positions))
    gathered = lax.all_to_all(copies, "sens", split_axis=0, concat_axis=0, axis_index_groups=[order])
    out = jax.ShapeDtypeStruct((block, BEAMS), jnp.float32)
    return pl.pallas_call(
        functools.partial(respond_kernel, order),
        out_shape=(out, out),
        in_specs=[VMEM, VMEM, VMEM, VMEM, VMEM],
        out_specs=(HBM, HBM),
        scratch_shapes=[
            pltpu.VMEM((2, 2 * block, sensors), jnp.bfloat16),
            pltpu.VMEM((2, block, LANES), jnp.float32),
            pltpu.VMEM((2, block, BEAMS), jnp.float32),
            pltpu.SemaphoreType.DMA((2,)),
        ],
        compiler_params=small(4 + sensors * block // 2**13),
        name="respond",
    )(gathered, *prepared)


def solution(mesh):
    in_specs = (P("bin", "sens"), P(None, "sens"), P(), P(), P("bin"))
    out_specs = (P("sens", "bin"), P("sens", "bin"))
    return jax.shard_map(
        per_device, mesh=mesh, in_specs=in_specs, out_specs=out_specs, check_vma=False
    )
```

```python
import functools
import math

import jax
import jax.numpy as jnp
from jax import lax
from jax.experimental import pallas as pl
from jax.experimental.pallas import tpu as pltpu
from jax.sharding import PartitionSpec as P

BEAMS = 256
LOAD = 0.5
LANES = 128
ROWS = 8
GROUP = 16
VMEM = pl.BlockSpec(memory_space=pltpu.VMEM)
SMEM = pl.BlockSpec(memory_space=pltpu.SMEM)
HBM = pl.BlockSpec(memory_space=pltpu.HBM)

COS = (0.99999921, -19.73898036, 64.92865742, -85.27162153, 58.79049212, -21.07110563)
SIN = (6.28318492, -41.34158923, 81.59994333, -76.61447253, 41.34288235, -12.47124354)
SIN_FINE = (6.2831853, -41.34170041, 81.60513139, -76.70301535, 42.02592699, -14.89984667, 3.23813751)


def small(mebibytes):
    return pltpu.CompilerParams(vmem_limit_bytes=mebibytes * 2**20)


def fetch(pairs, semaphores):
    copies = [pltpu.make_async_copy(*pair, semaphores.at[i]) for i, pair in enumerate(pairs)]
    for copy in copies:
        copy.start()
    for copy in copies:
        copy.wait()


def horner(coefficients, at):
    value = coefficients[-1]
    for coefficient in coefficients[-2::-1]:
        value = value * at + coefficient
    return value


def dot(left, right, contract):
    return lax.dot_general(left, right, ((contract[:1], contract[1:]), ((), ())), preferred_element_type=jnp.float32)


def spread_kernel(spectra_hbm, mask_hbm, copies_ref, spectra_ref, mask_ref, semaphores):
    fetch(((mask_hbm, mask_ref), (spectra_hbm, spectra_ref)), semaphores)
    block = mask_ref.shape[1]
    depth = spectra_ref.shape[1]
    validity = mask_ref[...].astype(jnp.float32)
    counts = jnp.broadcast_to(jnp.sum(validity, axis=0, keepdims=True), (depth, block))
    stacked = jnp.concatenate([validity, validity, counts], axis=0).astype(jnp.bfloat16)
    row = lax.broadcasted_iota(jnp.int32, (block, block), 0)
    lane = lax.broadcasted_iota(jnp.int32, (block, block), 1)
    result = dot(jnp.where(row == lane, 1.0, 0.0).astype(jnp.bfloat16), stacked, (1, 1))
    validity, counts = result[:, :depth], result[:, depth:]
    scaled = (spectra_ref[...].astype(jnp.float32) * validity * lax.rsqrt(counts)).astype(jnp.bfloat16)
    for peer in range(copies_ref.shape[0]):
        copies_ref[peer] = scaled


def neighbourhood(peers):
    position = lax.axis_index("sens")
    numbers = position, jnp.maximum(position - 1, 0), jnp.minimum(position + 1, peers - 1)
    return numbers, jnp.where(position == 1, 1, 0), jnp.where(position < peers - 1, 1, 0)


def place_of(order, number):
    place = jnp.int32(0)
    for at, source in enumerate(order):
        place = jnp.where(number == source, at, place)
    return place


def prepare_kernel(
    block, order, wavenumber_ref, pairing_hbm, positions_hbm, table_ref, taper_ref, load_ref, pick_ref,
    pairing_ref, positions_ref, semaphores
):
    fetch(((pairing_hbm, pairing_ref), (positions_hbm, positions_ref)), semaphores)
    sensors = positions_ref.shape[1]
    half = block // 2
    width = 3.0 / block

    beam = lax.broadcasted_iota(jnp.int32, (ROWS, BEAMS), 1).astype(jnp.float32)
    turns = (beam + 0.5) * (0.5 / BEAMS)
    square = turns * turns
    cos_beam = horner(COS_FINE, square)
    sin_beam = turns * horner(SIN_FINE, square)
    scale = wavenumber_ref[0] * (0.5 / math.pi)
    for at in range(0, sensors, LANES):
        along, side = (
            jnp.transpose(jnp.broadcast_to(positions_ref[axis : axis + 1, at : at + LANES] * scale, (LANES, LANES)))
            for axis in (0, 1)
        )
        for row in range(0, LANES, GROUP):
            for lane in range(0, BEAMS, LANES):
                cos_part = cos_beam[:1, lane : lane + LANES]
                sin_part = sin_beam[:1, lane : lane + LANES]
                phase = along[row : row + GROUP] * cos_part + side[row : row + GROUP] * sin_part
                phase = phase - jnp.round(phase)
                square = phase * phase
                start = order.index((at + row) // block) * block + row % block
                rows = slice(start, start + GROUP)
                table_ref[rows, lane : lane + LANES] = horner(COS, square).astype(jnp.bfloat16)
                table_ref[rows, BEAMS + lane : BEAMS + lane + LANES] = (phase * horner(SIN, square)).astype(jnp.bfloat16)

    sub = lax.broadcasted_iota(jnp.int32, (ROWS, LANES), 0)
    lane = lax.broadcasted_iota(jnp.int32, (ROWS, LANES), 1)

    def column(numbers):
        value = jnp.zeros((ROWS, LANES), jnp.int32)
        for i, number in enumerate(numbers):
            value = jnp.where(sub == i, number, value)
        return value

    first, later = [], []
    for at in range(0, half, ROWS):
        first.append(sub + at)
        later.append(column([pairing_ref[1, at + i] for i in range(ROWS)]))
    for at in range(0, half, ROWS):
        first.append(column([half + pairing_ref[0, at + i] for i in range(ROWS)]))
        later.append(column([half + pairing_ref[0, pairing_ref[1, at + i]] for i in range(ROWS)]))
    for which, rows in enumerate((first, later)):
        for at in range(0, len(rows), 2):
            pair = jnp.concatenate(rows[at : at + 2], axis=0)
            lanes = jnp.concatenate([lane, lane], axis=0)
            start = which * block + at * ROWS
            pick_ref[start : start + GROUP, :] = jnp.where(pair == lanes, 1.0, 0.0)[:, :block].astype(jnp.bfloat16)

    arrived = jnp.concatenate([positions_ref[:, peer * block : (peer + 1) * block] for peer in order], axis=1)
    for which, (rows, number) in enumerate(zip((first, first, later), neighbourhood(len(order))[0])):
        chunk = number // (LANES // block)
        shift = (number - chunk * (LANES // block)) * block
        place = place_of(order, number)
        place_chunk = place // (LANES // block)
        place_shift = (place - place_chunk * (LANES // block)) * block
        for at, row in enumerate(rows):
            start = which * block + at * ROWS
            hit = row + shift == lane
            near = positions_ref[:, pl.ds(pl.multiple_of(chunk * LANES, LANES), LANES)]
            own_along = jnp.sum(jnp.where(hit, near[0:1], 0.0), axis=1, keepdims=True)
            own_side = jnp.sum(jnp.where(hit, near[1:2], 0.0), axis=1, keepdims=True)
            for to in range(0, sensors, LANES):
                delta_along = own_along - arrived[0:1, to : to + LANES]
                delta_side = own_side - arrived[1:2, to : to + LANES]
                square = jnp.maximum(delta_along * delta_along + delta_side * delta_side, 1e-30)
                inverse = lax.rsqrt(square)
                turn = (square * inverse) * (0.5 * width / math.pi)
                turn = turn - jnp.round(turn)
                value = turn * horner(SIN_FINE, turn * turn) * (inverse * (1.0 / width))
                taper_ref[start : start + ROWS, to : to + LANES] = value
                load_ref[start : start + ROWS, to : to + LANES] = jnp.where((row + place_shift == lane) & (place_chunk == to // LANES), LOAD, 0.0)


COS_FINE = (0.99999999, -19.7392045, 64.93911746, -85.45013953, 60.16763095, -25.96759925, 6.52865816)


def chunks(array):
    return [array[:, at : at + LANES] for at in range(0, array.shape[1], LANES)]


def lane_total(parts):
    return jnp.broadcast_to(jnp.sum(sum(parts[1:], parts[0]), axis=1, keepdims=True), parts[0].shape)


def sums(left, right):
    terms = list(zip(*left, *right))
    norm_left = lane_total([p_re * p_re + p_im * p_im for p_re, p_im, _, _ in terms])
    norm_right = lane_total([q_re * q_re + q_im * q_im for _, _, q_re, q_im in terms])
    gamma_re = lane_total([p_re * q_re + p_im * q_im for p_re, p_im, q_re, q_im in terms])
    gamma_im = lane_total([p_re * q_im - p_im * q_re for p_re, p_im, q_re, q_im in terms])
    spread = norm_right - norm_left
    inverse = lax.rsqrt(spread * spread + 4.0 * (gamma_re * gamma_re + gamma_im * gamma_im) + 1e-30)
    square = 0.5 + 0.5 * (jnp.abs(spread) * inverse)
    shrink = lax.rsqrt(square)
    factor = inverse * shrink
    return spread >= 0.0, square * shrink, factor * gamma_re, factor * gamma_im


def combine(left, right, left_re, left_im, right_re, right_im):
    terms = list(zip(*left, *right))
    return (
        [left_re * p_re - left_im * p_im + right_re * q_re - right_im * q_im for p_re, p_im, q_re, q_im in terms],
        [left_re * p_im + left_im * p_re + right_re * q_im + right_im * q_re for p_re, p_im, q_re, q_im in terms],
    )


def rotate_side(left, right, side, sign):
    rising, leading, b_re, b_im = sums(left, right)
    plain = jnp.where(rising, 1, 0) != side
    return combine(
        left,
        right,
        jnp.where(plain, leading, b_re),
        jnp.where(plain, 0.0, b_im),
        sign * jnp.where(plain, b_re, leading),
        sign * jnp.where(plain, -b_im, 0.0),
    )


def rotate_both(left, right):
    rising, leading, b_re, b_im = sums(left, right)
    new_left = combine(
        left,
        right,
        jnp.where(rising, leading, b_re),
        jnp.where(rising, 0.0, b_im),
        jnp.where(rising, -b_re, -leading),
        jnp.where(rising, b_im, 0.0),
    )
    new_right = combine(
        left,
        right,
        jnp.where(rising, b_re, leading),
        jnp.where(rising, b_im, 0.0),
        jnp.where(rising, leading, b_re),
        jnp.where(rising, 0.0, -b_im),
    )
    return new_left, new_right


def respond_kernel(
    order, blocks_ref, table_ref, taper_ref, load_ref, pick_ref, early_hbm, final_hbm, re_ref, im_ref, turn_ref, norm_ref, response_ref, semaphores
):
    block, depth = blocks_ref.shape[1:]
    half = block // 2
    everything = blocks_ref[...].reshape(-1, depth)

    numbers, lower_side, upper_side = neighbourhood(len(order))

    def block_rows(which):
        return blocks_ref[place_of(order, numbers[which])]

    near = dot(pick_ref[:block, :], jnp.concatenate([block_rows(0), block_rows(1)], axis=1), (1, 0))
    far = dot(pick_ref[block:, :], block_rows(2), (1, 0))
    rows = jnp.concatenate([near[:, depth:], far, near[:, :depth]], axis=0).astype(jnp.bfloat16)
    sign = jnp.where(lax.broadcasted_iota(jnp.int32, everything.shape, 1) < depth // 2, -1.0, 1.0)
    turned = (pltpu.roll(everything.astype(jnp.float32), depth // 2, 1) * sign).astype(jnp.bfloat16)
    tile_re = dot(rows, everything, (1, 1))
    tile_im = dot(rows, turned, (1, 1))
    for i, at in enumerate((block, 2 * block, 0)):
        taper = taper_ref[at : at + block, :]
        re_ref[at : at + block, :] = tile_re[i * block : (i + 1) * block] * taper + load_ref[at : at + block, :]
        im_ref[at : at + block, :] = tile_im[i * block : (i + 1) * block] * taper

    def rows_at(start):
        return chunks(re_ref[start : start + GROUP, :]), chunks(im_ref[start : start + GROUP, :])

    def keep(which, start, column):
        turn_ref[which, start : start + GROUP, :] = jnp.concatenate(column[0], axis=1).astype(jnp.bfloat16)
        turn_ref[which, block + start : block + start + GROUP, :] = jnp.concatenate(column[1], axis=1).astype(jnp.bfloat16)
        norm_ref[which, start : start + GROUP, :] = 1.0 / lane_total([re * re + im * im for re, im in zip(*column)])

    def respond(which, projected):
        z_re = projected[:block, :BEAMS] + projected[block:, BEAMS:]
        z_im = projected[block:, :BEAMS] - projected[:block, BEAMS:]
        inverse = jnp.concatenate([norm_ref[which]] * (BEAMS // LANES), axis=1)
        response_ref[which] = (z_re * z_re + z_im * z_im) * inverse

    lower_sign = (2 * lower_side - 1).astype(jnp.float32)
    upper_sign = (2 * upper_side - 1).astype(jnp.float32)
    for at in range(0, half, GROUP):
        moved_top = rotate_side(rows_at(block + at), rows_at(block + half + at), lower_side, lower_sign)
        moved_bottom = rotate_side(rows_at(2 * block + at), rows_at(2 * block + half + at), upper_side, upper_sign)
        top, bottom = rotate_both(rows_at(at), rows_at(half + at))
        keep(0, at, top)
        keep(0, half + at, bottom)
        top, bottom = rotate_both(moved_top, moved_bottom)
        keep(1, at, top)
        keep(1, half + at, bottom)
    copies = []
    for which, result_hbm in enumerate((early_hbm, final_hbm)):
        respond(which, dot(turn_ref[which], table_ref[...], (1, 0)))
        copies.append(pltpu.make_async_copy(response_ref.at[which], result_hbm, semaphores.at[which]))
        copies[-1].start()
    for copy in copies:
        copy.wait()


def send_order(peers):
    ends = [at // 2 if at % 2 == 0 else peers - 1 - at // 2 for at in range(peers)]
    return [peers // 2] + [peer for peer in ends if peer != peers // 2]


def pinned(array):
    return pltpu.with_memory_space_constraint(array, pltpu.HBM)


def per_device(spectra, valid_mask, pairing, positions, wavenumber):
    blocks = lax.axis_size("sens")
    block = valid_mask.shape[1]
    depth = spectra.shape[0]
    sensors = positions.shape[1]
    copies = pl.pallas_call(
        spread_kernel,
        out_shape=pltpu.VMEM((blocks, block, depth), jnp.bfloat16),
        in_specs=[HBM, HBM],
        out_specs=VMEM,
        scratch_shapes=[
            pltpu.VMEM((block, depth), spectra.dtype),
            pltpu.VMEM(valid_mask.shape, valid_mask.dtype),
            pltpu.SemaphoreType.DMA((2,)),
        ],
        compiler_params=small(2),
        name="spread",
    )(pinned(spectra.T), pinned(valid_mask))
    order = send_order(blocks)
    prepared = pl.pallas_call(
        functools.partial(prepare_kernel, block, order),
        out_shape=(
            jax.ShapeDtypeStruct((sensors, 2 * BEAMS), jnp.bfloat16),
            jax.ShapeDtypeStruct((3 * block, sensors), jnp.float32),
            jax.ShapeDtypeStruct((3 * block, sensors), jnp.float32),
            jax.ShapeDtypeStruct((2 * block, block), jnp.bfloat16),
        ),
        in_specs=[SMEM, HBM, HBM],
        out_specs=(VMEM, VMEM, VMEM, VMEM),
        scratch_shapes=[
            pltpu.SMEM(pairing.shape, pairing.dtype),
            pltpu.VMEM(positions.shape, positions.dtype),
            pltpu.SemaphoreType.DMA((2,)),
        ],
        compiler_params=small(4),
        name="prepare",
    )(wavenumber, pinned(pairing), pinned(positions))
    gathered = lax.all_to_all(copies, "sens", split_axis=0, concat_axis=0, axis_index_groups=[order])
    out = jax.ShapeDtypeStruct((block, BEAMS), jnp.float32)
    return pl.pallas_call(
        functools.partial(respond_kernel, order),
        out_shape=(out, out),
        in_specs=[VMEM, VMEM, VMEM, VMEM, VMEM],
        out_specs=(HBM, HBM),
        scratch_shapes=[
            pltpu.VMEM((3 * block, sensors), jnp.float32),
            pltpu.VMEM((3 * block, sensors), jnp.float32),
            pltpu.VMEM((2, 2 * block, sensors), jnp.bfloat16),
            pltpu.VMEM((2, block, LANES), jnp.float32),
            pltpu.VMEM((2, block, BEAMS), jnp.float32),
            pltpu.SemaphoreType.DMA((2,)),
        ],
        compiler_params=small(4 + sensors * block // 2**13),
        name="respond",
    )(gathered, *prepared)


def solution(mesh):
    in_specs = (P("bin", "sens"), P(None, "sens"), P(), P(), P("bin"))
    out_specs = (P("sens", "bin"), P("sens", "bin"))
    return jax.shard_map(
        per_device, mesh=mesh, in_specs=in_specs, out_specs=out_specs, check_vma=False
    )
```

```python
import functools
import math

import jax
import jax.numpy as jnp
from jax import lax
from jax.experimental import pallas as pl
from jax.experimental.pallas import tpu as pltpu
from jax.sharding import PartitionSpec as P

BEAMS = 256
LOAD = 0.5
LANES = 128
ROWS = 8
GROUP = 16
VMEM = pl.BlockSpec(memory_space=pltpu.VMEM)
SMEM = pl.BlockSpec(memory_space=pltpu.SMEM)
HBM = pl.BlockSpec(memory_space=pltpu.HBM)

COS = (0.99999921, -19.73898036, 64.92865742, -85.27162153, 58.79049212, -21.07110563)
SIN = (6.28318492, -41.34158923, 81.59994333, -76.61447253, 41.34288235, -12.47124354)
SIN_FINE = (6.2831853, -41.34170041, 81.60513139, -76.70301535, 42.02592699, -14.89984667, 3.23813751)


def small(mebibytes):
    return pltpu.CompilerParams(vmem_limit_bytes=mebibytes * 2**20)


def fetch(pairs, semaphores):
    copies = [pltpu.make_async_copy(*pair, semaphores.at[i]) for i, pair in enumerate(pairs)]
    for copy in copies:
        copy.start()
    for copy in copies:
        copy.wait()


def horner(coefficients, at):
    value = coefficients[-1]
    for coefficient in coefficients[-2::-1]:
        value = value * at + coefficient
    return value


def dot(left, right, contract):
    return lax.dot_general(left, right, ((contract[:1], contract[1:]), ((), ())), preferred_element_type=jnp.float32)


def spread_kernel(spectra_hbm, mask_hbm, copies_ref, spectra_ref, mask_ref, semaphores):
    fetch(((mask_hbm, mask_ref), (spectra_hbm, spectra_ref)), semaphores)
    block = mask_ref.shape[1]
    depth = spectra_ref.shape[1]
    validity = mask_ref[...].astype(jnp.float32)
    counts = jnp.broadcast_to(jnp.sum(validity, axis=0, keepdims=True), (depth, block))
    stacked = jnp.concatenate([validity, validity, counts], axis=0).astype(jnp.bfloat16)
    row = lax.broadcasted_iota(jnp.int32, (block, block), 0)
    lane = lax.broadcasted_iota(jnp.int32, (block, block), 1)
    result = dot(jnp.where(row == lane, 1.0, 0.0).astype(jnp.bfloat16), stacked, (1, 1))
    validity, counts = result[:, :depth], result[:, depth:]
    scaled = (spectra_ref[...].astype(jnp.float32) * validity * lax.rsqrt(counts)).astype(jnp.bfloat16)
    for peer in range(copies_ref.shape[0]):
        copies_ref[peer] = scaled


def neighbourhood(peers):
    position = lax.axis_index("sens")
    numbers = position, jnp.maximum(position - 1, 0), jnp.minimum(position + 1, peers - 1)
    return numbers, jnp.where(position == 1, 1, 0), jnp.where(position < peers - 1, 1, 0)


def place_of(order, number):
    place = jnp.int32(0)
    for at, source in enumerate(order):
        place = jnp.where(number == source, at, place)
    return place


def prepare_kernel(
    block, order, wavenumber_ref, pairing_hbm, positions_hbm, table_ref, taper_ref, load_ref, pick_ref,
    pairing_ref, positions_ref, semaphores
):
    fetch(((pairing_hbm, pairing_ref), (positions_hbm, positions_ref)), semaphores)
    sensors = positions_ref.shape[1]
    half = block // 2
    width = 3.0 / block

    beam = lax.broadcasted_iota(jnp.int32, (ROWS, BEAMS), 1).astype(jnp.float32)
    turns = (beam + 0.5) * (0.5 / BEAMS)
    square = turns * turns
    cos_beam = horner(COS_FINE, square)
    sin_beam = turns * horner(SIN_FINE, square)
    scale = wavenumber_ref[0] * (0.5 / math.pi)
    for at in range(0, sensors, LANES):
        along, side = (
            jnp.transpose(jnp.broadcast_to(positions_ref[axis : axis + 1, at : at + LANES] * scale, (LANES, LANES)))
            for axis in (0, 1)
        )
        for row in range(0, LANES, GROUP):
            for lane in range(0, BEAMS, LANES):
                cos_part = cos_beam[:1, lane : lane + LANES]
                sin_part = sin_beam[:1, lane : lane + LANES]
                phase = along[row : row + GROUP] * cos_part + side[row : row + GROUP] * sin_part
                phase = phase - jnp.round(phase)
                square = phase * phase
                start = order.index((at + row) // block) * block + row % block
                rows = slice(start, start + GROUP)
                table_ref[rows, lane : lane + LANES] = horner(COS, square).astype(jnp.bfloat16)
                table_ref[rows, BEAMS + lane : BEAMS + lane + LANES] = (phase * horner(SIN, square)).astype(jnp.bfloat16)

    sub = lax.broadcasted_iota(jnp.int32, (ROWS, LANES), 0)
    lane = lax.broadcasted_iota(jnp.int32, (ROWS, LANES), 1)

    def column(numbers):
        value = jnp.zeros((ROWS, LANES), jnp.int32)
        for i, number in enumerate(numbers):
            value = jnp.where(sub == i, number, value)
        return value

    first, later = [], []
    for at in range(0, half, ROWS):
        first.append(sub + at)
        later.append(column([pairing_ref[1, at + i] for i in range(ROWS)]))
    for at in range(0, half, ROWS):
        first.append(column([half + pairing_ref[0, at + i] for i in range(ROWS)]))
        later.append(column([half + pairing_ref[0, pairing_ref[1, at + i]] for i in range(ROWS)]))
    for which, rows in enumerate((first, later)):
        for at in range(0, len(rows), 2):
            pair = jnp.concatenate(rows[at : at + 2], axis=0)
            lanes = jnp.concatenate([lane, lane], axis=0)
            start = which * block + at * ROWS
            pick_ref[start : start + GROUP, :] = jnp.where(pair == lanes, 1.0, 0.0)[:, :block].astype(jnp.bfloat16)

    arrived = jnp.concatenate([positions_ref[:, peer * block : (peer + 1) * block] for peer in order], axis=1)
    for which, (rows, number) in enumerate(zip((first, first, later), neighbourhood(len(order))[0])):
        chunk = number // (LANES // block)
        shift = (number - chunk * (LANES // block)) * block
        place = place_of(order, number)
        place_chunk = place // (LANES // block)
        place_shift = (place - place_chunk * (LANES // block)) * block
        for at, row in enumerate(rows):
            start = which * block + at * ROWS
            hit = row + shift == lane
            near = positions_ref[:, pl.ds(pl.multiple_of(chunk * LANES, LANES), LANES)]
            own_along = jnp.sum(jnp.where(hit, near[0:1], 0.0), axis=1, keepdims=True)
            own_side = jnp.sum(jnp.where(hit, near[1:2], 0.0), axis=1, keepdims=True)
            for to in range(0, sensors, LANES):
                delta_along = own_along - arrived[0:1, to : to + LANES]
                delta_side = own_side - arrived[1:2, to : to + LANES]
                square = jnp.maximum(delta_along * delta_along + delta_side * delta_side, 1e-30)
                inverse = lax.rsqrt(square)
                turn = (square * inverse) * (0.5 * width / math.pi)
                turn = turn - jnp.round(turn)
                value = turn * horner(SIN_FINE, turn * turn) * (inverse * (1.0 / width))
                taper_ref[start : start + ROWS, to : to + LANES] = value
                load_ref[start : start + ROWS, to : to + LANES] = jnp.where((row + place_shift == lane) & (place_chunk == to // LANES), LOAD, 0.0)


COS_FINE = (0.99999999, -19.7392045, 64.93911746, -85.45013953, 60.16763095, -25.96759925, 6.52865816)


def chunks(array):
    return [array[:, at : at + LANES] for at in range(0, array.shape[1], LANES)]


def lane_total(parts):
    return jnp.broadcast_to(jnp.sum(sum(parts[1:], parts[0]), axis=1, keepdims=True), parts[0].shape)


def sums(left, right):
    terms = list(zip(*left, *right))
    norm_left = lane_total([p_re * p_re + p_im * p_im for p_re, p_im, _, _ in terms])
    norm_right = lane_total([q_re * q_re + q_im * q_im for _, _, q_re, q_im in terms])
    gamma_re = lane_total([p_re * q_re + p_im * q_im for p_re, p_im, q_re, q_im in terms])
    gamma_im = lane_total([p_re * q_im - p_im * q_re for p_re, p_im, q_re, q_im in terms])
    spread = norm_right - norm_left
    inverse = lax.rsqrt(spread * spread + 4.0 * (gamma_re * gamma_re + gamma_im * gamma_im) + 1e-30)
    square = 0.5 + 0.5 * (jnp.abs(spread) * inverse)
    shrink = lax.rsqrt(square)
    factor = inverse * shrink
    return spread >= 0.0, square * shrink, factor * gamma_re, factor * gamma_im


def combine(left, right, left_re, left_im, right_re, right_im):
    terms = list(zip(*left, *right))
    return (
        [left_re * p_re - left_im * p_im + right_re * q_re - right_im * q_im for p_re, p_im, q_re, q_im in terms],
        [left_re * p_im + left_im * p_re + right_re * q_im + right_im * q_re for p_re, p_im, q_re, q_im in terms],
    )


def rotate_side(left, right, side, sign):
    rising, leading, b_re, b_im = sums(left, right)
    plain = jnp.where(rising, 1, 0) != side
    return combine(
        left,
        right,
        jnp.where(plain, leading, b_re),
        jnp.where(plain, 0.0, b_im),
        sign * jnp.where(plain, b_re, leading),
        sign * jnp.where(plain, -b_im, 0.0),
    )


def rotate_both(left, right):
    rising, leading, b_re, b_im = sums(left, right)
    new_left = combine(
        left,
        right,
        jnp.where(rising, leading, b_re),
        jnp.where(rising, 0.0, b_im),
        jnp.where(rising, -b_re, -leading),
        jnp.where(rising, b_im, 0.0),
    )
    new_right = combine(
        left,
        right,
        jnp.where(rising, b_re, leading),
        jnp.where(rising, b_im, 0.0),
        jnp.where(rising, leading, b_re),
        jnp.where(rising, 0.0, -b_im),
    )
    return new_left, new_right


def respond_kernel(
    order, blocks_ref, table_ref, taper_ref, load_ref, pick_ref, early_hbm, final_hbm, re_ref, im_ref, turn_ref, norm_ref, response_ref, semaphores
):
    block, depth = blocks_ref.shape[1:]
    half = block // 2
    everything = blocks_ref[...].reshape(-1, depth)

    numbers, lower_side, upper_side = neighbourhood(len(order))

    def block_rows(which):
        return blocks_ref[place_of(order, numbers[which])]

    near = dot(pick_ref[:block, :], jnp.concatenate([block_rows(0), block_rows(1)], axis=1), (1, 0))
    far = dot(pick_ref[block:, :], block_rows(2), (1, 0))
    rows = jnp.concatenate([near[:, depth:], far, near[:, :depth]], axis=0).astype(jnp.bfloat16)
    sign = jnp.where(lax.broadcasted_iota(jnp.int32, everything.shape, 1) < depth // 2, -1.0, 1.0)
    turned = (pltpu.roll(everything.astype(jnp.float32), depth // 2, 1) * sign).astype(jnp.bfloat16)
    tile_re = dot(rows, everything, (1, 1))
    tile_im = dot(rows, turned, (1, 1))
    for i, at in enumerate((block, 2 * block, 0)):
        taper = taper_ref[at : at + block, :]
        re_ref[at : at + block, :] = tile_re[i * block : (i + 1) * block] * taper + load_ref[at : at + block, :]
        im_ref[at : at + block, :] = tile_im[i * block : (i + 1) * block] * taper

    def rows_at(start):
        return chunks(re_ref[start : start + GROUP, :]), chunks(im_ref[start : start + GROUP, :])

    def keep(which, start, column):
        turn_ref[which, start : start + GROUP, :] = jnp.concatenate(column[0], axis=1).astype(jnp.bfloat16)
        turn_ref[which, block + start : block + start + GROUP, :] = jnp.concatenate(column[1], axis=1).astype(jnp.bfloat16)
        norm_ref[which, start : start + GROUP, :] = 1.0 / lane_total([re * re + im * im for re, im in zip(*column)])

    def respond(which, projected):
        z_re = projected[:block, :BEAMS] + projected[block:, BEAMS:]
        z_im = projected[block:, :BEAMS] - projected[:block, BEAMS:]
        inverse = jnp.concatenate([norm_ref[which]] * (BEAMS // LANES), axis=1)
        response_ref[which] = (z_re * z_re + z_im * z_im) * inverse

    lower_sign = (2 * lower_side - 1).astype(jnp.float32)
    upper_sign = (2 * upper_side - 1).astype(jnp.float32)
    groups = range(0, half, GROUP)
    moved = [
        (
            rotate_side(rows_at(block + at), rows_at(block + half + at), lower_side, lower_sign),
            rotate_side(rows_at(2 * block + at), rows_at(2 * block + half + at), upper_side, upper_sign),
        )
        for at in groups
    ]
    for at in groups:
        top, bottom = rotate_both(rows_at(at), rows_at(half + at))
        keep(0, at, top)
        keep(0, half + at, bottom)
    early = dot(turn_ref[0], table_ref[...], (1, 0))
    for at, pair in zip(groups, moved):
        top, bottom = rotate_both(*pair)
        keep(1, at, top)
        keep(1, half + at, bottom)
    final = dot(turn_ref[1], table_ref[...], (1, 0))
    copies = []
    for which, projected, result_hbm in ((1, final, final_hbm), (0, early, early_hbm)):
        respond(which, projected)
        copies.append(pltpu.make_async_copy(response_ref.at[which], result_hbm, semaphores.at[which]))
        copies[-1].start()
    for copy in copies:
        copy.wait()


def send_order(peers):
    ends = [at // 2 if at % 2 == 0 else peers - 1 - at // 2 for at in range(peers)]
    return [peers // 2] + [peer for peer in ends if peer != peers // 2]


def pinned(array):
    return pltpu.with_memory_space_constraint(array, pltpu.HBM)


def per_device(spectra, valid_mask, pairing, positions, wavenumber):
    blocks = lax.axis_size("sens")
    block = valid_mask.shape[1]
    depth = spectra.shape[0]
    sensors = positions.shape[1]
    copies = pl.pallas_call(
        spread_kernel,
        out_shape=pltpu.VMEM((blocks, block, depth), jnp.bfloat16),
        in_specs=[HBM, HBM],
        out_specs=VMEM,
        scratch_shapes=[
            pltpu.VMEM((block, depth), spectra.dtype),
            pltpu.VMEM(valid_mask.shape, valid_mask.dtype),
            pltpu.SemaphoreType.DMA((2,)),
        ],
        compiler_params=small(2),
        name="spread",
    )(pinned(spectra.T), pinned(valid_mask))
    order = send_order(blocks)
    prepared = pl.pallas_call(
        functools.partial(prepare_kernel, block, order),
        out_shape=(
            jax.ShapeDtypeStruct((sensors, 2 * BEAMS), jnp.bfloat16),
            jax.ShapeDtypeStruct((3 * block, sensors), jnp.float32),
            jax.ShapeDtypeStruct((3 * block, sensors), jnp.float32),
            jax.ShapeDtypeStruct((2 * block, block), jnp.bfloat16),
        ),
        in_specs=[SMEM, HBM, HBM],
        out_specs=(VMEM, VMEM, VMEM, VMEM),
        scratch_shapes=[
            pltpu.SMEM(pairing.shape, pairing.dtype),
            pltpu.VMEM(positions.shape, positions.dtype),
            pltpu.SemaphoreType.DMA((2,)),
        ],
        compiler_params=small(4),
        name="prepare",
    )(wavenumber, pinned(pairing), pinned(positions))
    gathered = lax.all_to_all(copies, "sens", split_axis=0, concat_axis=0, axis_index_groups=[order])
    out = jax.ShapeDtypeStruct((block, BEAMS), jnp.float32)
    return pl.pallas_call(
        functools.partial(respond_kernel, order),
        out_shape=(out, out),
        in_specs=[VMEM, VMEM, VMEM, VMEM, VMEM],
        out_specs=(HBM, HBM),
        scratch_shapes=[
            pltpu.VMEM((3 * block, sensors), jnp.float32),
            pltpu.VMEM((3 * block, sensors), jnp.float32),
            pltpu.VMEM((2, 2 * block, sensors), jnp.bfloat16),
            pltpu.VMEM((2, block, LANES), jnp.float32),
            pltpu.VMEM((2, block, BEAMS), jnp.float32),
            pltpu.SemaphoreType.DMA((2,)),
        ],
        compiler_params=small(4 + sensors * block // 2**13),
        name="respond",
    )(gathered, *prepared)


def solution(mesh):
    in_specs = (P("bin", "sens"), P(None, "sens"), P(), P(), P("bin"))
    out_specs = (P("sens", "bin"), P("sens", "bin"))
    return jax.shard_map(
        per_device, mesh=mesh, in_specs=in_specs, out_specs=out_specs, check_vma=False
    )
```
